32 devices in a mesh: dp: 16 (over z, y, core), mod: 2 (over x).
Axes of the slice: x: 2, y: 2, z: 4, core: 2. Of those that a mesh axis runs over, the one named last changes fastest.
Arguments:
- tokens: bfloat16 [32, 256, 1152], P(('dp', 'mod')), may hold values from -6 to 6
- cond: bfloat16 [256, 1152], P('dp'), may hold values from -6 to 6
- segment_ids: int32 [32, 256], P(('dp', 'mod')), may hold values from 0 to 7, never falling along the last dimension, each value on 1 to 64 neighbouring positions
- crop_slot: int32 [16, 16], P('dp'), may hold values from 0 to 15, each once within a row
- ada_weight: bfloat16 [1152, 6912], P(None, 'mod'), may hold values from -0.1875 to 0.1875
- ada_bias: bfloat16 [6, 1152], P('mod'), may hold values from -3 to 3
- attn_weight: bfloat16 [4608, 1152], P(('dp', 'mod'))
- fc_in: bfloat16 [4608, 1152], P(('dp', 'mod')), may hold values from -0.1875 to 0.1875
- fc_out: bfloat16 [4608, 1152], P(('dp', 'mod')), may hold values from -0.09375 to 0.09375
- biases: bfloat16 [9216], P(('dp', 'mod')), may hold values from -2 to 2
- out_grad: bfloat16 [32, 256, 1152], P(('dp', 'mod')), may hold values from -6 to 6
Outputs:
- out: bfloat16 [32, 256, 1152], P(('dp', 'mod'))
- tokens_grad: float32 [32, 256, 1152], P(('dp', 'mod'))
- cond_grad: float32 [256, 1152], P(('dp', 'mod'))
- ada_weight_grad: float32 [1152, 6912], P('dp', 'mod')
- ada_bias_grad: float32 [6, 1152], P('mod', 'dp')
- attn_weight_grad: float32 [4608, 1152], P(('dp', 'mod'))
- fc_in_grad: float32 [4608, 1152], P(('dp', 'mod'))
- fc_out_grad: float32 [4608, 1152], P(('dp', 'mod'))
- biases_grad: float32 [9216], P(('dp', 'mod'))
The draws below stay inside these ranges and needn't reach their ends.
Inputs may be any that keep to these rules, and one draw needn't show every extreme that they name: `segment_ids`: within each sequence the crop numbers never fall, every crop has 1 to 64 tokens, and some crop has exactly 64. Each row holds every number once; crop c of sequence p * 2 + m uses conditioning row p * 2 * 8 + crop_slot[p, m * 8 + c].
All inputs are finite; a program needn't handle non-finite values.
Results may differ from the reference program's by a relative error of at most 0.015.
The reference program's roundings to bfloat16 on the way count: a program that leaves them out, or rounds other values in their place, can miss the bound.
Values may be sent and summed in bfloat16 or wider, within the bound.
No kernel may reach another device: no remote copies, remote signals or barrier semaphores. Data moves between devices by JAX's collectives and lax.ppermute only.
A program may use at most 384 MiB of HBM per device.

```python
import math
from functools import partial
import jax
import jax.numpy as jnp
import numpy as np
from jax import lax

D = 1152
HEADS = 16
FF = 4608
HEAD_DIM = 72
TOK_DEV = 256
CROP_MAX = 64
CROPS_SEQ = 8
SEQS = 32
CONDS = 256
N_MOD = 2


def draw_attn_weight(key, part):
    key = jax.random.fold_in(key, 5)
    values = jax.random.normal(key, (4 * D, D), jnp.float32)
    rows = jnp.arange(4 * D)
    factor = jnp.where(rows < 3 * D, 1.0, 4.0)
    return (values * factor[:, None] / math.sqrt(D)).astype(jnp.bfloat16)


def block_scale(own_key, shape, shards, low, top_value):
    gain = 1.0
    for axis_at, blocks in shards:
        steps = jax.random.uniform(jax.random.fold_in(jax.random.fold_in(own_key, 6), axis_at), (blocks,), jnp.float32, low / len(shards), top_value / len(shards))
        gain = gain * jnp.repeat(jnp.exp(steps), shape[axis_at] // blocks).reshape((-1,) + (1,) * (len(shape) - 1 - axis_at))
    return gain


def length_profile(amount, total, reach, skew):
    weights = [(1 << 20) // math.isqrt(grade ** skew) + 1 for grade in range(2, amount + 1)]
    surplus, given = total - reach - (amount - 1), [1] * (amount - 1)
    while surplus > 0:
        candidates = [i for i in range(amount - 1) if given[i] < reach]
        mass, left = sum([weights[i] for i in candidates]), surplus
        for i in candidates:
            addition = min(reach - given[i], max(1, left * weights[i] // mass), surplus)
            given[i] = given[i] + addition
            surplus = surplus - addition
    return np.array([reach] + given)


def ragged_sizes(stream_key, count, total, most, skew):
    if count == 2:
        one = jax.random.randint(stream_key, (), max(1, total - most), min(most, total - 1) + 1)
        return jnp.stack([one, total - one])
    sizes = jnp.asarray(length_profile(count, total, most, skew), jnp.int32)
    twos = (count - 1) // 2
    donor, taker = sizes[1:1 + 2 * twos:2], sizes[2:2 + 2 * twos:2]
    room = jnp.minimum(donor - 1, most - taker)
    moved = jax.random.randint(jax.random.fold_in(stream_key, 1), (twos,), 0, 1 << 20) % (room + 1)
    sizes = sizes.at[1:1 + 2 * twos:2].set(donor - moved).at[2:2 + 2 * twos:2].set(taker + moved)
    return sizes[jax.random.permutation(jax.random.fold_in(stream_key, 2), count)]


def bell_draw(rng, extent, scale, reach, pieces=(), kind=jnp.bfloat16):
    values = scale * jax.random.normal(rng, extent, jnp.float32)
    if pieces:
        values = values * block_scale(rng, extent, pieces, -0.22, 0.18)
    return jnp.clip(values, -reach, reach).astype(kind)


def setup_inputs(seed: int = 0) -> dict:
    keys = jax.random.split(jax.random.key(seed), 12)
    return {
        "tokens": bell_draw(keys[0], (SEQS, TOK_DEV, D), 1.0, 6.0, ((0, 32),)),
        "cond": bell_draw(keys[1], (CONDS, D), 1.0, 6.0, ((0, 16),)),
        "segment_ids": jax.vmap(lambda own: jnp.searchsorted(jnp.cumsum(ragged_sizes(own, CROPS_SEQ, TOK_DEV, CROP_MAX, 1)), jnp.arange(TOK_DEV), side="right"))(jax.random.split(keys[2], SEQS)).reshape((SEQS, TOK_DEV)).astype(jnp.int32),
        "crop_slot": jax.vmap(lambda own: jax.random.permutation(own, N_MOD * CROPS_SEQ))(jax.random.split(keys[3], (SEQS // N_MOD))).reshape((SEQS // N_MOD, N_MOD * CROPS_SEQ)).astype(jnp.int32),
        "ada_weight": bell_draw(keys[4], (D, 6 * D), D ** -0.5, 0.1875, ((1, 2),)),
        "ada_bias": bell_draw(keys[5], (6, D), 0.5, 3.0, ((0, 2),)),
        "attn_weight": draw_attn_weight(jax.random.fold_in(keys[11], 71), 0),
        "fc_in": bell_draw(keys[7], (FF, D), D ** -0.5, 0.1875, ((0, 32),)),
        "fc_out": bell_draw(keys[8], (FF, D), FF ** -0.5, 0.09375, ((0, 32),)),
        "biases": bell_draw(keys[9], (4 * D + FF,), 0.3, 2.0, ((0, 32),)),
        "out_grad": bell_draw(keys[10], (SEQS, TOK_DEV, D), 1.0, 6.0, ((0, 32),)),
    }


@jax.custom_vjp
def low(v):
    return lax.optimization_barrier(v.astype(jnp.bfloat16)).astype(jnp.float32)

@jax.custom_vjp
def low_back(v):
    return v

def low_keep(v):
    return (low(v), None)

def low_pass(kept, grad):
    return (grad,)

def back_keep(v):
    return (v, None)

def back_low(kept, grad):
    return (low(grad),)
low.defvjp(low_keep, low_pass)
low_back.defvjp(back_keep, back_low)
highest = lax.Precision.HIGHEST
norm_eps = 1e-06

def layer_norm(values):
    center = values - lax.optimization_barrier(jnp.mean(values, axis=-1, keepdims=True))
    return center * lax.rsqrt(lax.optimization_barrier(jnp.mean(center * center, axis=-1, keepdims=True)) + norm_eps)

def block_one(weights, inputs):
    attn_weight, fc_in, fc_out, biases = weights
    resid, crop_mod, seg_ids = inputs
    token_mod = crop_mod[seg_ids]
    shift_a, scale_a, gate_a, shift_m, scale_m, gate_m = jnp.split(token_mod, 6, axis=1)
    attn_in = low(layer_norm(resid) * (1.0 + scale_a) + shift_a)
    qkv_bias = jnp.concatenate([biases[:D], jnp.zeros((D,), jnp.float32), biases[D:2 * D]])
    qkv = low_back(low(jnp.dot(attn_in, attn_weight[:3 * D].T, precision=highest) + qkv_bias))
    query = qkv[:, :D].reshape(TOK_DEV, HEADS, HEAD_DIM)
    key_part = qkv[:, D:2 * D].reshape(TOK_DEV, HEADS, HEAD_DIM)
    value = qkv[:, 2 * D:].reshape(TOK_DEV, HEADS, HEAD_DIM)
    scores = jnp.einsum('qhd,khd->hqk', query, key_part, precision=highest) * HEAD_DIM ** (-0.5)
    same_crop = seg_ids[:, None] == seg_ids[None, :]
    scores = low_back(jnp.where(same_crop[None], scores, -1e+30))
    probs = low(jax.nn.softmax(scores, axis=-1))
    context = jnp.einsum('hqk,khd->qhd', probs, value, precision=highest).reshape(TOK_DEV, D)
    context = low_back(low(context))
    attn_out = low_back(jnp.dot(context, attn_weight[3 * D:].T, precision=highest) + biases[2 * D:3 * D])
    mid = resid + gate_a * attn_out
    mlp_in = low(layer_norm(mid) * (1.0 + scale_m) + shift_m)
    hidden = low_back(jnp.dot(mlp_in, fc_in.T, precision=highest) + biases[4 * D:])
    act = low(jax.nn.gelu(hidden, approximate=True))
    mlp_out = low_back(jnp.dot(act, fc_out, precision=highest) + biases[3 * D:4 * D])
    return mid + gate_m * mlp_out

def reference(tokens, cond, segment_ids, crop_slot, ada_weight, ada_bias, attn_weight, fc_in, fc_out, biases, out_grad):
    pair_base = jnp.arange(SEQS // N_MOD, dtype=jnp.int32) * (N_MOD * CROPS_SEQ)
    slot_rows = (crop_slot + pair_base[:, None]).reshape(SEQS, CROPS_SEQ).astype(jnp.int32)

    def forward(token_vals, cond_vals, ada_w, ada_b, attn_w, fcin_w, fcout_w, bias_vals):
        silu_cond = low(jax.nn.silu(cond_vals))
        modulation = low_back(low(jnp.dot(silu_cond, ada_w, precision=highest) + ada_b.reshape(6 * D)))
        crop_mod = modulation[slot_rows]
        step_fn = jax.checkpoint(partial(block_one, (attn_w, fcin_w, fcout_w, bias_vals)))
        return lax.map(step_fn, (token_vals, crop_mod, segment_ids))
    primals = (tokens.astype(jnp.float32), cond.astype(jnp.float32), ada_weight.astype(jnp.float32), ada_bias.astype(jnp.float32), attn_weight.astype(jnp.float32), fc_in.astype(jnp.float32), fc_out.astype(jnp.float32), biases.astype(jnp.float32))
    result, pullback = jax.vjp(forward, *primals)
    grads = pullback(out_grad.astype(jnp.float32))
    return (result.astype(jnp.bfloat16), grads[0], grads[1], grads[2], grads[3], grads[4], grads[5], grads[6], grads[7])
```

```python
import jax
import jax.numpy as jnp
from jax import lax
from jax.experimental import pallas as pl
from jax.experimental.pallas import tpu as pltpu
from jax.sharding import PartitionSpec as P

HEADS = 16
highest = lax.Precision.HIGHEST
norm_eps = 1e-06
bf16 = jnp.bfloat16
f32 = jnp.float32


def layer_norm(values):
    center = values - jnp.mean(values, axis=-1, keepdims=True)
    inverse = lax.rsqrt(jnp.mean(center * center, axis=-1, keepdims=True) + norm_eps)
    return (center * inverse, inverse)


def norm_back(grad_in, normed, inverse):
    centered = grad_in - jnp.mean(grad_in, axis=-1, keepdims=True)
    return (centered - normed * jnp.mean(grad_in * normed, axis=-1, keepdims=True)) * inverse


def times_rows(left, right):
    return lax.dot_general(left, right, (((1,), (1,)), ((), ())), preferred_element_type=f32)


def contract_rows(left, right):
    return lax.dot_general(left, right, (((0,), (0,)), ((), ())), preferred_element_type=f32)


def times(left, right):
    return jnp.dot(left, right, preferred_element_type=f32)


def gelu_tanh(values):
    return jax.nn.gelu(values, approximate=True)


class Net:
    def __init__(self):
        self.dp = lax.axis_size("dp")
        self.mod = lax.axis_size("mod")
        self.bits = self.dp.bit_length() - 1
        self.dp_rank = lax.axis_index("dp")
        self.mod_rank = lax.axis_index("mod")
        self.chips = self.dp // 2 * self.mod

    def swap(self, value, dim):
        if dim == "mod":
            return lax.ppermute(value, "mod", [(i, i ^ 1) for i in range(self.mod)])
        return lax.ppermute(value, "dp", [(i, i ^ (1 << dim)) for i in range(self.dp)])

    def mask(self, order, j):
        dp_mask, mod_mask = 0, 0
        for step, dim in enumerate(order):
            if j >> step & 1:
                if dim == "mod":
                    mod_mask ^= 1
                else:
                    dp_mask ^= 1 << dim
        return dp_mask, mod_mask

    def device(self, order, j, core):
        dp_mask, mod_mask = self.mask(order, j)
        return (self.dp_rank ^ (dp_mask ^ core)) * self.mod + (self.mod_rank ^ mod_mask)

    def gather(self, value, order):
        for dim in order[:-1]:
            value = jnp.concatenate([value, self.swap(value, dim)], axis=0)
        return value, self.swap(value, order[-1])

    def scatter(self, own, other, order):
        for step in range(len(order) - 1, -1, -1):
            got = self.swap(other, order[step])
            total = own.astype(f32) + got.astype(f32)
            if step == 0:
                return total
            total = total.astype(bf16)
            half = total.shape[0] // 2
            own, other = total[:half], total[half:]


def copy_kernel(moves, *refs):
    index_ref, refs, sems = refs[0], refs[1:-1], refs[-1]
    copies = []
    for n, (source, source_at, target, target_at, rows) in enumerate(moves):
        if source_at is None:
            source_at = pl.multiple_of(index_ref[n] * rows, rows)
        if target_at is None:
            target_at = pl.multiple_of(index_ref[n] * rows, rows)
        copies.append(
            pltpu.make_async_copy(
                refs[source].at[pl.ds(source_at, rows)],
                refs[target].at[pl.ds(target_at, rows)],
                sems.at[n],
            )
        )
    for copy in copies:
        copy.start()
    for copy in copies:
        copy.wait()


def move_blocks(arrays, shapes, moves, index):
    any_spec = pl.BlockSpec(memory_space=pl.ANY)
    return pl.pallas_call(
        lambda *refs: copy_kernel(moves, *refs),
        grid_spec=pltpu.PrefetchScalarGridSpec(
            num_scalar_prefetch=1,
            grid=(1,),
            in_specs=[any_spec] * len(arrays),
            out_specs=[any_spec] * len(shapes),
            scratch_shapes=[pltpu.SemaphoreType.DMA((len(moves),))],
        ),
        out_shape=[jax.ShapeDtypeStruct(s, bf16) for s in shapes],
        compiler_params=pltpu.CompilerParams(vmem_limit_bytes=4 * 1024 * 1024),
        name="move_blocks",
    )(index, *arrays)


def on_device(
    tokens,
    cond,
    segment_ids,
    crop_slot,
    ada_weight,
    ada_bias,
    attn_weight,
    fc_in,
    fc_out,
    biases,
    out_grad,
):
    net = Net()
    model_width = tokens.shape[2]
    tok_len = tokens.shape[1]
    head_count = HEADS
    head_dim = model_width // head_count
    score_scale = head_dim ** (-0.5)
    dp_count, mod_count = net.dp, net.mod
    crop_count = crop_slot.shape[1] // mod_count
    mod_rank = net.mod_rank
    high = list(range(net.bits - 1, 1, -1))
    order_a = ["mod"] + high + [1]
    order_b = [1] + high + ["mod"]
    attn_orders = [[high[0], "mod"] + high[1:] + [1], high[1:] + [high[0], 1, "mod"], [high[0], 1, "mod"] + high[1:]]
    shard = attn_weight.shape[0]
    chips = net.chips
    third = shard // 3
    attn_cut = [third, third, third]
    part_a = shard * 5 // 9 // 16 * 16 if shard % 16 == 0 else shard // 2
    fc_cut = [part_a, shard - part_a]
    fc_orders = [order_a, order_b]

    attn_parts = []
    for n in range(3):
        attn_parts.append(net.gather(attn_weight[n * third : (n + 1) * third], attn_orders[n]))
    attn_other = [tuple(net.swap(piece, 0) for piece in pair) for pair in attn_parts]
    fcin_pieces, fcout_pieces, fc_order_of = [], [], []
    for weight, pieces in ((fc_in, fcin_pieces), (fc_out, fcout_pieces)):
        start = 0
        for rows, order in zip(fc_cut, fc_orders):
            pieces.extend(net.gather(weight[start : start + rows], order))
            start += rows

    arrays, moves, index = [], [], []
    for core in range(2):
        for n in range(3):
            for side in range(2):
                arrays.append((attn_parts, attn_other)[core][n][side])
                for j in range(chips // 2):
                    moves.append((len(arrays) - 1, j * third, None, None, third))
                    index.append(net.device(attn_orders[n], j + side * (chips // 2), core) * 3 + n)
    index = jnp.stack(index).astype(jnp.int32)
    blocky = third % 16 == 0
    if blocky:
        to_natural = [(s, sa, 12, ta, r) for s, sa, _, ta, r in moves]
        (attn_w,) = move_blocks(arrays, [(shard * dp_count * mod_count, model_width)], to_natural, index)
    else:
        spread = jnp.concatenate(arrays)

        def place(n, whole):
            block = lax.dynamic_slice_in_dim(spread, n * third, third)
            return lax.dynamic_update_slice_in_dim(whole, block, index[n] * third, 0)

        attn_w = lax.fori_loop(0, len(moves), place, jnp.zeros_like(spread))

    silu_cond = jax.nn.silu(cond.astype(f32)).astype(bf16)
    mod_part = times(silu_cond, ada_weight) + ada_bias.reshape(-1).astype(f32)
    mod_own = mod_part.astype(bf16)
    mod_other = net.swap(mod_own, "mod")
    modulation = jnp.concatenate(
        [jnp.where(mod_rank == 0, mod_own, mod_other), jnp.where(mod_rank == 0, mod_other, mod_own)], axis=1
    )
    seg_ids = segment_ids[0]
    slots = lax.dynamic_slice_in_dim(crop_slot[0], mod_rank * crop_count, crop_count)
    crop_onehot = seg_ids[:, None] == jnp.arange(crop_count, dtype=jnp.int32)[None, :]
    token_slot = jnp.sum(jnp.where(crop_onehot, slots[None, :], 0), axis=1)
    slot_pick = token_slot[:, None] == jnp.arange(cond.shape[0], dtype=jnp.int32)[None, :]
    slot_pick = slot_pick.astype(bf16)
    token_mod = times(slot_pick, modulation)
    shift_a, scale_a, gate_a, shift_m, scale_m, gate_m = jnp.split(token_mod, 6, axis=1)

    bias_all = lax.all_gather(biases, ("dp", "mod"), axis=0, tiled=True)
    bias_query = bias_all[:model_width].astype(f32)
    bias_value = bias_all[model_width : 2 * model_width].astype(f32)
    bias_proj = bias_all[2 * model_width : 3 * model_width].astype(f32)
    bias_out = bias_all[3 * model_width : 4 * model_width].astype(f32)
    bias_in = bias_all[4 * model_width :].reshape(dp_count * mod_count, shard)
    bias_pieces, picks = [], []
    start = 0
    for rows, order in zip(fc_cut, fc_orders):
        for side in range(2):
            devices = jnp.stack([net.device(order, j + side * (chips // 2), 0) for j in range(chips // 2)])
            pick = (devices[:, None] == jnp.arange(dp_count * mod_count)[None, :]).astype(bf16)
            picks.append(pick)
            bias_pieces.append(times(pick, bias_in[:, start : start + rows]).reshape(-1))
        start += rows

    qkv_weight = attn_w[: 3 * model_width]
    proj_weight = attn_w[3 * model_width :]
    resid = tokens[0].astype(f32)
    normed_a, inverse_a = layer_norm(resid)
    attn_in = (normed_a * (1.0 + scale_a) + shift_a).astype(bf16)
    qkv_bias = jnp.concatenate([bias_query, jnp.zeros_like(bias_query), bias_value])
    qkv = (times_rows(attn_in, qkv_weight) + qkv_bias).astype(bf16)
    query = qkv[:, :model_width].reshape(tok_len, head_count, head_dim)
    key_part = qkv[:, model_width : 2 * model_width].reshape(tok_len, head_count, head_dim)
    value = qkv[:, 2 * model_width :].reshape(tok_len, head_count, head_dim)
    same_crop = seg_ids[:, None] == seg_ids[None, :]

    def scores_of(left, right):
        raw = jnp.einsum("qhd,khd->hqk", left, right, preferred_element_type=f32) * score_scale
        return jnp.where(same_crop[None], raw, -1e30)

    scores = scores_of(query, key_part)
    row_max = jnp.max(scores, axis=-1, keepdims=True)
    log_total = row_max + jnp.log(jnp.sum(jnp.exp(scores - row_max), axis=-1, keepdims=True))
    probs = jnp.exp(scores - log_total).astype(bf16)
    context = jnp.einsum("hqk,khd->qhd", probs, value, preferred_element_type=f32)
    context = context.reshape(tok_len, model_width).astype(bf16)
    attn_out = times_rows(context, proj_weight) + bias_proj
    mid = resid + gate_a * attn_out
    normed_m, inverse_m = layer_norm(mid)
    mlp_in = (normed_m * (1.0 + scale_m) + shift_m).astype(bf16)
    grad_out = out_grad[0].astype(f32)
    grad_mlp = (gate_m * grad_out).astype(bf16)

    mlp_both = jnp.concatenate([mlp_in, net.swap(mlp_in, 0)], axis=0)
    grad_both = jnp.concatenate([grad_mlp, net.swap(grad_mlp, 0)], axis=0)
    out_sum, back_sum = 0.0, 0.0
    fcin_grads, fcout_grads, grad_bias_in = [], [], 0.0
    hiddens, acts = [], []
    start = 0
    for n, (w_in, b_in) in enumerate(zip(fcin_pieces, bias_pieces)):
        hidden = times_rows(mlp_both, w_in) + b_in
        act = gelu_tanh(hidden).astype(bf16)
        hiddens.append(hidden)
        acts.append(act)
        fcout_grads.append(contract_rows(act, grad_both).astype(bf16))
    for n, (w_in, w_out) in enumerate(zip(fcin_pieces, fcout_pieces)):
        out_sum = out_sum + times(acts[n], w_out)
        gelu_back = jax.vjp(gelu_tanh, hiddens[n])[1]
        grad_hidden = gelu_back(times_rows(grad_both, w_out))[0].astype(bf16)
        fcin_grads.append(contract_rows(grad_hidden, mlp_both).astype(bf16))
        back_sum = back_sum + times(grad_hidden, w_in)
        rows = fc_cut[n // 2]
        column = jnp.sum(grad_hidden.astype(f32), axis=0).reshape(chips // 2, rows)
        placed = jnp.dot(picks[n].astype(f32).T, column, precision=highest)
        lead = 0 if n < 2 else fc_cut[0]
        grad_bias_in = grad_bias_in + jnp.pad(placed, ((0, 0), (lead, shard - lead - rows)))
    mlp_out = out_sum[:tok_len] + net.swap(out_sum[tok_len:], 0) + bias_out
    grad_mlp_in = back_sum[:tok_len] + net.swap(back_sum[tok_len:], 0)

    result = (mid + gate_m * mlp_out).astype(bf16)
    grad_gate_m = grad_out * mlp_out
    grad_scale_m = grad_mlp_in * normed_m
    grad_mid = grad_out + norm_back(grad_mlp_in * (1.0 + scale_m), normed_m, inverse_m)
    grad_gate_a = grad_mid * attn_out
    grad_attn = (gate_a * grad_mid).astype(bf16)
    grad_proj = contract_rows(grad_attn, context)
    grad_context = times(grad_attn, proj_weight)
    grad_context = grad_context.astype(bf16).reshape(tok_len, head_count, head_dim)
    scores_again = scores_of(query, key_part)
    probs_full = jnp.exp(scores_again - log_total)
    probs_low = probs_full.astype(bf16)
    grad_probs = jnp.einsum("qhd,khd->hqk", grad_context, value, preferred_element_type=f32)
    grad_scores = probs_full * (grad_probs - jnp.sum(grad_probs * probs_full, axis=-1, keepdims=True))
    grad_scores = grad_scores.astype(bf16)
    grad_query = jnp.einsum("hqk,khd->qhd", grad_scores, key_part, preferred_element_type=f32) * score_scale
    grad_keys = jnp.einsum("hqk,qhd->khd", grad_scores, query, preferred_element_type=f32) * score_scale
    grad_value = jnp.einsum("hqk,qhd->khd", probs_low, grad_context, preferred_element_type=f32)
    grad_qkv = jnp.concatenate(
        [
            grad_query.reshape(tok_len, model_width),
            grad_keys.reshape(tok_len, model_width),
            grad_value.reshape(tok_len, model_width),
        ],
        axis=1,
    ).astype(bf16)
    grad_qkv_w = contract_rows(grad_qkv, attn_in)
    grad_attn_in = times(grad_qkv, qkv_weight)
    grad_scale_a = grad_attn_in * normed_a
    grad_tokens = grad_mid + norm_back(grad_attn_in * (1.0 + scale_a), normed_a, inverse_a)
    grad_qkv_wide = grad_qkv.astype(f32)
    grad_bias = jnp.concatenate(
        [
            jnp.sum(grad_qkv_wide[:, :model_width], axis=0),
            jnp.sum(grad_qkv_wide[:, 2 * model_width :], axis=0),
            jnp.sum(grad_attn.astype(f32), axis=0),
            jnp.sum(grad_mlp.astype(f32), axis=0),
            grad_bias_in.reshape(-1),
        ]
    )
    bias_sum = lax.psum_scatter(grad_bias, ("dp", "mod"), scatter_dimension=0, tiled=True)

    grad_token_mod = jnp.concatenate(
        [grad_attn_in, grad_scale_a, grad_gate_a, grad_mlp_in, grad_scale_m, grad_gate_m], axis=1
    )
    token_high = lax.reduce_precision(grad_token_mod, 8, 7)
    token_low = (grad_token_mod - token_high).astype(bf16)
    grad_pair = contract_rows(slot_pick, token_high.astype(bf16)) + contract_rows(slot_pick, token_low)
    grad_pair = grad_pair.astype(bf16)
    width = grad_pair.shape[1] // 2
    pair_own = jnp.where(mod_rank == 0, grad_pair[:, :width], grad_pair[:, width:])
    pair_send = jnp.where(mod_rank == 0, grad_pair[:, width:], grad_pair[:, :width])
    grad_mod = (pair_own.astype(f32) + net.swap(pair_send, "mod").astype(f32)).astype(bf16)
    grad_silu = times_rows(grad_mod, ada_weight)
    silu_own = jnp.where(mod_rank == 0, grad_silu[:crop_count], grad_silu[crop_count:])
    silu_send = jnp.where(mod_rank == 0, grad_silu[crop_count:], grad_silu[:crop_count])
    grad_silu = silu_own + net.swap(silu_send.astype(bf16), "mod").astype(f32)
    own_cond = lax.dynamic_slice_in_dim(cond, mod_rank * crop_count, crop_count, 0).astype(f32)
    silu_back = jax.vjp(jax.nn.silu, own_cond)[1]
    grad_cond = silu_back(grad_silu)[0]
    ada_order = [1] + high + [0]
    mod_rows = jnp.concatenate(net.gather(grad_mod, ada_order), axis=0)
    cond_rows = jnp.concatenate(net.gather(silu_cond, ada_order), axis=0)
    own_rows = model_width // dp_count
    cond_cols = lax.dynamic_slice_in_dim(cond_rows, net.dp_rank * own_rows, own_rows, 1)
    ada_w_sum = contract_rows(cond_cols, mod_rows)
    ada_b_sum = jnp.sum(mod_rows.astype(f32), axis=0).reshape(ada_bias.shape[0], model_width)
    ada_b_sum = lax.dynamic_slice_in_dim(ada_b_sum, net.dp_rank * own_rows, own_rows, 1)

    start = 0
    fc_sums = []
    for grads in (fcout_grads, fcin_grads):
        fc_sums.append(
            jnp.concatenate(
                [net.scatter(grads[2 * n], grads[2 * n + 1], fc_orders[n]) for n in range(2)], axis=0
            )
        )
    fcout_sum, fcin_sum = fc_sums
    attn_grad = jnp.concatenate([grad_qkv_w, grad_proj], axis=0).astype(bf16)
    if blocky:
        shapes = [a.shape for a in arrays]
        from_natural = [(0, None, s + 1, sa, r) for s, sa, _, ta, r in moves]
        grads = move_blocks([attn_grad], shapes, from_natural, index)
    else:
        def take(n, whole):
            block = lax.dynamic_slice_in_dim(attn_grad, index[n] * third, third)
            return lax.dynamic_update_slice_in_dim(whole, block, n * third, 0)

        grads = jnp.split(lax.fori_loop(0, len(moves), take, jnp.zeros_like(attn_grad)), 12)
    attn_sum = []
    for n in range(3):
        pair = [
            (grads[2 * n + s].astype(f32) + net.swap(grads[6 + 2 * n + s], 0).astype(f32)).astype(bf16)
            for s in range(2)
        ]
        attn_sum.append(net.scatter(pair[0], pair[1], attn_orders[n]))
    attn_sum = jnp.concatenate(attn_sum, axis=0)
    return (
        result[None],
        grad_tokens[None],
        grad_cond,
        ada_w_sum,
        ada_b_sum,
        attn_sum,
        fcin_sum,
        fcout_sum,
        bias_sum,
    )


def solution(mesh):
    placed = (
        P(("dp", "mod"), None, None),
        P("dp", None),
        P(("dp", "mod"), None),
        P("dp", None),
        P(None, "mod"),
        P("mod", None),
        P(("dp", "mod"), None),
        P(("dp", "mod"), None),
        P(("dp", "mod"), None),
        P(("dp", "mod")),
        P(("dp", "mod"), None, None),
    )
    return jax.shard_map(
        on_device,
        mesh=mesh,
        in_specs=placed,
        out_specs=(
            P(("dp", "mod"), None, None),
            P(("dp", "mod"), None, None),
            P(("dp", "mod"), None),
            P("dp", "mod"),
            P("mod", "dp"),
            P(("dp", "mod"), None),
            P(("dp", "mod"), None),
            P(("dp", "mod"), None),
            P(("dp", "mod")),
        ),
        check_vma=False,
    )
```

```python
import jax
import jax.numpy as jnp
import numpy as np
from jax import lax
from jax.experimental import pallas as pl
from jax.experimental.pallas import tpu as pltpu
from jax.sharding import PartitionSpec as P

HEADS = 16
highest = lax.Precision.HIGHEST
norm_eps = 1e-06
bf16 = jnp.bfloat16
f32 = jnp.float32


def layer_norm(values):
    center = values - jnp.mean(values, axis=-1, keepdims=True)
    inverse = lax.rsqrt(jnp.mean(center * center, axis=-1, keepdims=True) + norm_eps)
    return (center * inverse, inverse)


def norm_back(grad_in, normed, inverse):
    centered = grad_in - jnp.mean(grad_in, axis=-1, keepdims=True)
    return (centered - normed * jnp.mean(grad_in * normed, axis=-1, keepdims=True)) * inverse


def times_rows(left, right):
    return lax.dot_general(left, right, (((1,), (1,)), ((), ())), preferred_element_type=f32)


def contract_rows(left, right):
    return lax.dot_general(left, right, (((0,), (0,)), ((), ())), preferred_element_type=f32)


def times(left, right):
    return jnp.dot(left, right, preferred_element_type=f32)


def gelu_tanh(values):
    return jax.nn.gelu(values, approximate=True)


class Net:
    def __init__(self):
        self.dp = lax.axis_size("dp")
        self.mod = lax.axis_size("mod")
        self.bits = self.dp.bit_length() - 1
        self.dp_rank = lax.axis_index("dp")
        self.mod_rank = lax.axis_index("mod")
        self.chips = self.dp // 2 * self.mod
        self.lead = list(range(self.bits - 1, 2, -1))
        last = ["mod", 1, 2]
        self.turns = [last[n:] + last[:n] for n in range(3)]
        self.orders = [self.lead + turn for turn in self.turns]

    def swap(self, value, dim):
        if dim == "mod":
            return lax.ppermute(value, "mod", [(i, i ^ 1) for i in range(self.mod)])
        return lax.ppermute(value, "dp", [(i, i ^ (1 << dim)) for i in range(self.dp)])

    def mask(self, order, j):
        dp_mask, mod_mask = 0, 0
        for step, dim in enumerate(order):
            if j >> step & 1:
                if dim == "mod":
                    mod_mask ^= 1
                else:
                    dp_mask ^= 1 << dim
        return dp_mask, mod_mask

    def devices(self, order, core, chunks):
        masks = np.array([self.mask(order, j) for j in chunks], np.int32)
        return (self.dp_rank ^ (masks[:, 0] ^ core)) * self.mod + (self.mod_rank ^ masks[:, 1])

    def gather(self, value, order):
        for dim in order[:-1]:
            value = jnp.concatenate([value, self.swap(value, dim)], axis=0)
        return value, self.swap(value, order[-1])


def after(value, *others):
    return lax.optimization_barrier((value, *others))[0]


class Gather:
    def __init__(self, net, shard):
        self.net, self.count = net, len(net.lead)
        self.third = shard.shape[0] // 3
        self.value, self.got, self.phase = shard, None, 0

    def start(self, *others):
        net, phase = self.net, self.phase
        if phase < self.count:
            value = after(self.value, *others) if others else self.value
            self.value, self.got = value, net.swap(value, net.lead[phase])
        else:
            if phase == self.count:
                whole = self.value.reshape(-1, 3, self.third, self.value.shape[-1])
                self.value = [whole[:, n].reshape(-1, whole.shape[-1]) for n in range(3)]
            if others:
                self.value = list(lax.optimization_barrier((*self.value, *others))[:3])
            step = phase - self.count
            self.got = [net.swap(self.value[n], net.turns[n][step]) for n in range(3)]
        self.phase += 1
        return self

    def finish(self):
        if self.phase <= self.count:
            self.value = jnp.concatenate([self.value, self.got], axis=0)
        elif self.phase < self.count + 3:
            self.value = [jnp.concatenate(pair, axis=0) for pair in zip(self.value, self.got)]
        return self

    def arrived(self):
        return self.got if isinstance(self.got, list) else [self.got]


class Scatter:
    def __init__(self, net, own, other):
        self.net, self.own, self.other = net, own, other
        self.step = 2
        self.lead = len(net.lead) - 1
        self.send()

    def send(self):
        net = self.net
        if self.step >= 0:
            self.got = [net.swap(self.other[n], net.turns[n][self.step]) for n in range(3)]
        else:
            self.got = [net.swap(self.other, net.lead[self.lead])]

    def arrived(self):
        return self.got

    def advance(self):
        if self.step >= 0:
            totals = [(a.astype(f32) + b.astype(f32)).astype(bf16) for a, b in zip(self.own, self.got)]
            self.step -= 1
            if self.step >= 0:
                half = totals[0].shape[0] // 2
                self.own, self.other = [t[:half] for t in totals], [t[half:] for t in totals]
            else:
                width = totals[0].shape[-1]
                count = 1 << len(self.net.lead)
                whole = jnp.concatenate([t.reshape(count, -1, width) for t in totals], axis=1)
                half = count // 2
                self.own, self.other = (
                    whole[:half].reshape(-1, width),
                    whole[half:].reshape(-1, width),
                )
            self.send()
            return
        total = self.own.astype(f32) + self.got[0].astype(f32)
        self.lead -= 1
        if self.lead < 0:
            self.total, self.got = total, []
            return
        total = total.astype(bf16)
        half = total.shape[0] // 2
        self.own, self.other = total[:half], total[half:]
        self.send()

    def rest(self):
        while self.got:
            self.advance()
        return self.total


def copy_kernel(moves, *refs):
    index_ref, refs, sems = refs[0], refs[1:-1], refs[-1]
    copies = []
    for n, (source, source_at, target, target_at, rows) in enumerate(moves):
        if source_at is None:
            source_at = pl.multiple_of(index_ref[n] * rows, rows)
        if target_at is None:
            target_at = pl.multiple_of(index_ref[n] * rows, rows)
        copies.append(
            pltpu.make_async_copy(
                refs[source].at[pl.ds(source_at, rows)],
                refs[target].at[pl.ds(target_at, rows)],
                sems.at[n],
            )
        )
    for copy in copies:
        copy.start()
    for copy in copies:
        copy.wait()


def move_blocks(arrays, shapes, moves, index):
    any_spec = pl.BlockSpec(memory_space=pl.ANY)
    return pl.pallas_call(
        lambda *refs: copy_kernel(moves, *refs),
        grid_spec=pltpu.PrefetchScalarGridSpec(
            num_scalar_prefetch=1,
            grid=(1,),
            in_specs=[any_spec] * len(arrays),
            out_specs=[any_spec] * len(shapes),
            scratch_shapes=[pltpu.SemaphoreType.DMA((len(moves),))],
        ),
        out_shape=[jax.ShapeDtypeStruct(s, bf16) for s in shapes],
        compiler_params=pltpu.CompilerParams(vmem_limit_bytes=4 * 1024 * 1024),
        name="move_blocks",
    )(index, *arrays)


def on_device(
    tokens,
    cond,
    segment_ids,
    crop_slot,
    ada_weight,
    ada_bias,
    attn_weight,
    fc_in,
    fc_out,
    biases,
    out_grad,
):
    net = Net()
    model_width = tokens.shape[2]
    tok_len = tokens.shape[1]
    head_count = HEADS
    head_dim = model_width // head_count
    score_scale = head_dim ** (-0.5)
    dp_count, mod_count = net.dp, net.mod
    crop_count = crop_slot.shape[1] // mod_count
    mod_rank = net.mod_rank
    shard = attn_weight.shape[0]
    chips = net.chips
    third = shard // 3

    g_attn, g_in, g_out = Gather(net, attn_weight), Gather(net, fc_in), Gather(net, fc_out)
    for _ in net.lead:
        g_attn.start().finish()
    g_attn.start()
    for _ in net.lead:
        g_in.start(*g_attn.value).finish()
    g_attn.finish().start()
    for _ in net.lead:
        g_out.start(*g_attn.arrived()).finish()
    g_attn.finish().start()
    attn_own = g_attn.value
    attn_own_other = [net.swap(piece, 0) for piece in attn_own]
    g_in.start(*attn_own)
    attn_got = g_attn.arrived()
    attn_got_other = [net.swap(piece, 0) for piece in attn_got]
    g_in.finish().start(*attn_got)
    attn_parts = list(zip(attn_own, attn_got))
    attn_other = list(zip(attn_own_other, attn_got_other))

    chunks_of = [range(chips // 2), range(chips // 2, chips)]
    arrays, moves, index = [], [], []
    for core in range(2):
        for n in range(3):
            for side in range(2):
                arrays.append((attn_parts, attn_other)[core][n][side])
                for j in range(chips // 2):
                    moves.append((len(arrays) - 1, j * third, None, None, third))
                index.append(net.devices(net.orders[n], core, chunks_of[side]) * 3 + n)
    index = jnp.concatenate(index).astype(jnp.int32)
    blocky = third % 16 == 0
    if blocky:
        to_natural = [(s, sa, 12, ta, r) for s, sa, _, ta, r in moves]
        (attn_w,) = move_blocks(arrays, [(shard * dp_count * mod_count, model_width)], to_natural, index)
    else:
        spread = jnp.concatenate(arrays)

        def place(n, whole):
            block = lax.dynamic_slice_in_dim(spread, n * third, third)
            return lax.dynamic_update_slice_in_dim(whole, block, index[n] * third, 0)

        attn_w = lax.fori_loop(0, len(moves), place, jnp.zeros_like(spread))

    silu_cond = jax.nn.silu(cond.astype(f32)).astype(bf16)
    mod_part = times(silu_cond, ada_weight) + ada_bias.reshape(-1).astype(f32)
    mod_own = mod_part.astype(bf16)
    mod_other = net.swap(mod_own, "mod")
    modulation = jnp.concatenate(
        [jnp.where(mod_rank == 0, mod_own, mod_other), jnp.where(mod_rank == 0, mod_other, mod_own)], axis=1
    )
    seg_ids = segment_ids[0]
    slots = lax.dynamic_slice_in_dim(crop_slot[0], mod_rank * crop_count, crop_count)
    crop_onehot = seg_ids[:, None] == jnp.arange(crop_count, dtype=jnp.int32)[None, :]
    token_slot = jnp.sum(jnp.where(crop_onehot, slots[None, :], 0), axis=1)
    slot_pick = token_slot[:, None] == jnp.arange(cond.shape[0], dtype=jnp.int32)[None, :]
    slot_pick = slot_pick.astype(bf16)
    token_mod = times(slot_pick, modulation)
    shift_a, scale_a, gate_a, shift_m, scale_m, gate_m = jnp.split(token_mod, 6, axis=1)

    bias_all = lax.all_to_all(
        jnp.broadcast_to(biases[None], (dp_count * mod_count, biases.shape[0])),
        ("dp", "mod"),
        split_axis=0,
        concat_axis=0,
        tiled=True,
    ).reshape(-1)
    bias_query = bias_all[:model_width].astype(f32)
    bias_value = bias_all[model_width : 2 * model_width].astype(f32)
    bias_proj = bias_all[2 * model_width : 3 * model_width].astype(f32)
    bias_out = bias_all[3 * model_width : 4 * model_width].astype(f32)
    bias_in = bias_all[4 * model_width :].reshape(dp_count * mod_count, shard)
    bias_pieces, picks = [], []
    for n in range(3):
        for side in range(2):
            devices = net.devices(net.orders[n], 0, chunks_of[side])
            pick = (devices[:, None] == jnp.arange(dp_count * mod_count)[None, :]).astype(bf16)
            picks.append(pick)
            bias_pieces.append(times(pick, bias_in[:, n * third : (n + 1) * third]).reshape(-1))

    qkv_weight = attn_w[: 3 * model_width]
    proj_weight = attn_w[3 * model_width :]
    resid = tokens[0].astype(f32)
    normed_a, inverse_a = layer_norm(resid)
    attn_in = (normed_a * (1.0 + scale_a) + shift_a).astype(bf16)
    attn_in = after(attn_in, *g_in.arrived())
    g_in.finish().start()
    g_out.start()
    qkv_bias = jnp.concatenate([bias_query, jnp.zeros_like(bias_query), bias_value])
    qkv = (times_rows(attn_in, qkv_weight) + qkv_bias).astype(bf16)
    query = qkv[:, :model_width].reshape(tok_len, head_count, head_dim)
    key_part = qkv[:, model_width : 2 * model_width].reshape(tok_len, head_count, head_dim)
    value = qkv[:, 2 * model_width :].reshape(tok_len, head_count, head_dim)
    same_crop = seg_ids[:, None] == seg_ids[None, :]

    def scores_of(left, right):
        raw = jnp.einsum("qhd,khd->hqk", left, right, preferred_element_type=f32) * score_scale
        return jnp.where(same_crop[None], raw, -1e30)

    scores = scores_of(query, key_part)
    row_max = jnp.max(scores, axis=-1, keepdims=True)
    log_total = row_max + jnp.log(jnp.sum(jnp.exp(scores - row_max), axis=-1, keepdims=True))
    probs = jnp.exp(scores - log_total).astype(bf16)
    context = jnp.einsum("hqk,khd->qhd", probs, value, preferred_element_type=f32)
    context = context.reshape(tok_len, model_width).astype(bf16)
    context = after(context, *g_out.arrived())
    g_out.finish().start()
    attn_out = times_rows(context, proj_weight) + bias_proj
    mid = resid + gate_a * attn_out
    normed_m, inverse_m = layer_norm(mid)
    mlp_in = (normed_m * (1.0 + scale_m) + shift_m).astype(bf16)
    grad_out = out_grad[0].astype(f32)
    grad_mlp = (gate_m * grad_out).astype(bf16)

    mlp_both = jnp.concatenate([mlp_in, net.swap(mlp_in, 0)], axis=0)
    grad_both = jnp.concatenate([grad_mlp, net.swap(grad_mlp, 0)], axis=0)
    out_sum, back_sum = 0.0, 0.0
    fcin_grads, fcout_grads, grad_bias_in = [], [], 0.0
    hiddens, acts = [], []
    mlp_both = after(mlp_both, *g_in.arrived(), *g_out.arrived())
    g_out.finish().start()
    fcin_pieces = [piece for pair in zip(g_in.value, g_in.arrived()) for piece in pair]
    fcout_pieces = [piece for pair in zip(g_out.value, g_out.arrived()) for piece in pair]
    for n, (w_in, b_in) in enumerate(zip(fcin_pieces, bias_pieces)):
        hidden = times_rows(mlp_both, w_in) + b_in
        act = gelu_tanh(hidden).astype(bf16)
        hiddens.append(hidden)
        acts.append(act)
        fcout_grads.append(contract_rows(act, grad_both).astype(bf16))
    s_out = Scatter(net, fcout_grads[0::2], fcout_grads[1::2])
    grad_hiddens = []
    for n, w_out in enumerate(fcout_pieces):
        out_sum = out_sum + times(acts[n], w_out)
        gelu_back = jax.vjp(gelu_tanh, hiddens[n])[1]
        grad_hidden = gelu_back(times_rows(grad_both, w_out))[0].astype(bf16)
        grad_hiddens.append(grad_hidden)
    grad_hiddens = lax.optimization_barrier((*grad_hiddens, *s_out.arrived()))[:6]
    s_out.advance()
    for n, w_in in enumerate(fcin_pieces):
        fcin_grads.append(contract_rows(grad_hiddens[n], mlp_both).astype(bf16))
        back_sum = back_sum + times(grad_hiddens[n], w_in)
        column = jnp.sum(grad_hiddens[n].astype(f32), axis=0).reshape(chips // 2, third)
        placed = jnp.dot(picks[n].astype(f32).T, column, precision=highest)
        lead = n // 2 * third
        grad_bias_in = grad_bias_in + jnp.pad(placed, ((0, 0), (lead, shard - lead - third)))
    s_in = Scatter(net, fcin_grads[0::2], fcin_grads[1::2])
    back_sum = after(back_sum, *s_out.arrived())
    s_out.advance()
    mlp_out = out_sum[:tok_len] + net.swap(out_sum[tok_len:], 0) + bias_out
    grad_mlp_in = back_sum[:tok_len] + net.swap(back_sum[tok_len:], 0)

    result = (mid + gate_m * mlp_out).astype(bf16)
    grad_gate_m = grad_out * mlp_out
    grad_scale_m = grad_mlp_in * normed_m
    grad_mid = grad_out + norm_back(grad_mlp_in * (1.0 + scale_m), normed_m, inverse_m)
    grad_gate_a = grad_mid * attn_out
    grad_attn = (gate_a * grad_mid).astype(bf16)
    grad_attn = after(grad_attn, *s_out.arrived(), *s_in.arrived())
    s_out.advance()
    s_in.advance()
    grad_proj = contract_rows(grad_attn, context)
    grad_context = times(grad_attn, proj_weight)
    grad_context = grad_context.astype(bf16).reshape(tok_len, head_count, head_dim)
    scores_again = scores_of(query, key_part)
    probs_full = jnp.exp(scores_again - log_total)
    probs_low = probs_full.astype(bf16)
    grad_probs = jnp.einsum("qhd,khd->hqk", grad_context, value, preferred_element_type=f32)
    grad_scores = probs_full * (grad_probs - jnp.sum(grad_probs * probs_full, axis=-1, keepdims=True))
    grad_scores = grad_scores.astype(bf16)
    grad_scores = after(grad_scores, *s_in.arrived())
    s_in.advance()
    grad_query = jnp.einsum("hqk,khd->qhd", grad_scores, key_part, preferred_element_type=f32) * score_scale
    grad_keys = jnp.einsum("hqk,qhd->khd", grad_scores, query, preferred_element_type=f32) * score_scale
    grad_value = jnp.einsum("hqk,qhd->khd", probs_low, grad_context, preferred_element_type=f32)
    grad_qkv = jnp.concatenate(
        [
            grad_query.reshape(tok_len, model_width),
            grad_keys.reshape(tok_len, model_width),
            grad_value.reshape(tok_len, model_width),
        ],
        axis=1,
    ).astype(bf16)
    grad_qkv = after(grad_qkv, *s_out.arrived(), *s_in.arrived())
    fcout_sum = s_out.rest()
    s_in.advance()
    grad_qkv_w = contract_rows(grad_qkv, attn_in)
    grad_attn_in = times(grad_qkv, qkv_weight)
    grad_scale_a = grad_attn_in * normed_a
    grad_tokens = grad_mid + norm_back(grad_attn_in * (1.0 + scale_a), normed_a, inverse_a)
    grad_qkv_wide = grad_qkv.astype(f32)
    grad_bias = jnp.concatenate(
        [
            jnp.sum(grad_qkv_wide[:, :model_width], axis=0),
            jnp.sum(grad_qkv_wide[:, 2 * model_width :], axis=0),
            jnp.sum(grad_attn.astype(f32), axis=0),
            jnp.sum(grad_mlp.astype(f32), axis=0),
            grad_bias_in.reshape(-1),
        ]
    )
    bias_rows = lax.all_to_all(
        grad_bias.reshape(dp_count * mod_count, -1), ("dp", "mod"), split_axis=0, concat_axis=0, tiled=True
    )
    bias_sum = jnp.sum(bias_rows, axis=0)

    grad_token_mod = jnp.concatenate(
        [grad_attn_in, grad_scale_a, grad_gate_a, grad_mlp_in, grad_scale_m, grad_gate_m], axis=1
    )
    token_high = lax.reduce_precision(grad_token_mod, 8, 7)
    token_low = (grad_token_mod - token_high).astype(bf16)
    grad_pair = contract_rows(slot_pick, token_high.astype(bf16)) + contract_rows(slot_pick, token_low)
    grad_pair = grad_pair.astype(bf16)
    width = grad_pair.shape[1] // 2
    pair_own = jnp.where(mod_rank == 0, grad_pair[:, :width], grad_pair[:, width:])
    pair_send = jnp.where(mod_rank == 0, grad_pair[:, width:], grad_pair[:, :width])
    grad_mod = (pair_own.astype(f32) + net.swap(pair_send, "mod").astype(f32)).astype(bf16)
    grad_silu = times_rows(grad_mod, ada_weight)
    silu_own = jnp.where(mod_rank == 0, grad_silu[:crop_count], grad_silu[crop_count:])
    silu_send = jnp.where(mod_rank == 0, grad_silu[crop_count:], grad_silu[:crop_count])
    grad_silu = silu_own + net.swap(silu_send.astype(bf16), "mod").astype(f32)
    own_cond = lax.dynamic_slice_in_dim(cond, mod_rank * crop_count, crop_count, 0).astype(f32)
    silu_back = jax.vjp(jax.nn.silu, own_cond)[1]
    grad_cond = silu_back(grad_silu)[0]
    ada_order = list(range(1, net.bits)) + [0]
    mod_rows = jnp.concatenate(net.gather(grad_mod, ada_order), axis=0)
    cond_rows = jnp.concatenate(net.gather(silu_cond, ada_order), axis=0)
    own_rows = model_width // dp_count
    cond_cols = lax.dynamic_slice_in_dim(cond_rows, net.dp_rank * own_rows, own_rows, 1)
    ada_w_sum = contract_rows(cond_cols, mod_rows)
    ada_b_sum = jnp.sum(mod_rows.astype(f32), axis=0).reshape(ada_bias.shape[0], model_width)
    ada_b_sum = lax.dynamic_slice_in_dim(ada_b_sum, net.dp_rank * own_rows, own_rows, 1)

    fcin_sum = s_in.rest()
    attn_grad = jnp.concatenate([grad_qkv_w, grad_proj], axis=0).astype(bf16)
    if blocky:
        shapes = [a.shape for a in arrays]
        from_natural = [(0, None, s + 1, sa, r) for s, sa, _, ta, r in moves]
        grads = move_blocks([attn_grad], shapes, from_natural, index)
    else:
        def take(n, whole):
            block = lax.dynamic_slice_in_dim(attn_grad, index[n] * third, third)
            return lax.dynamic_update_slice_in_dim(whole, block, n * third, 0)

        grads = jnp.split(lax.fori_loop(0, len(moves), take, jnp.zeros_like(attn_grad)), 12)
    pairs = [(a.astype(f32) + net.swap(b, 0).astype(f32)).astype(bf16) for a, b in zip(grads[:6], grads[6:])]
    attn_sum = Scatter(net, pairs[0::2], pairs[1::2]).rest()
    return (
        result[None],
        grad_tokens[None],
        grad_cond,
        ada_w_sum,
        ada_b_sum,
        attn_sum,
        fcin_sum,
        fcout_sum,
        bias_sum,
    )


def solution(mesh):
    placed = (
        P(("dp", "mod"), None, None),
        P("dp", None),
        P(("dp", "mod"), None),
        P("dp", None),
        P(None, "mod"),
        P("mod", None),
        P(("dp", "mod"), None),
        P(("dp", "mod"), None),
        P(("dp", "mod"), None),
        P(("dp", "mod")),
        P(("dp", "mod"), None, None),
    )
    return jax.shard_map(
        on_device,
        mesh=mesh,
        in_specs=placed,
        out_specs=(
            P(("dp", "mod"), None, None),
            P(("dp", "mod"), None, None),
            P(("dp", "mod"), None),
            P("dp", "mod"),
            P("mod", "dp"),
            P(("dp", "mod"), None),
            P(("dp", "mod"), None),
            P(("dp", "mod"), None),
            P(("dp", "mod")),
        ),
        check_vma=False,
    )
```

```python
import functools

import jax
import jax.numpy as jnp
import numpy as np
from jax import lax
from jax.experimental import pallas as pl
from jax.experimental.pallas import tpu as pltpu
from jax.sharding import PartitionSpec as P

HEADS = 16
norm_eps = 1e-06
bf16 = jnp.bfloat16
f32 = jnp.float32
MIB = 1024 * 1024


def layer_norm(values):
    center = values - jnp.mean(values, axis=-1, keepdims=True)
    inverse = lax.rsqrt(jnp.mean(center * center, axis=-1, keepdims=True) + norm_eps)
    return (center * inverse, inverse)


def norm_back(grad_in, normed, inverse):
    centered = grad_in - jnp.mean(grad_in, axis=-1, keepdims=True)
    return (centered - normed * jnp.mean(grad_in * normed, axis=-1, keepdims=True)) * inverse


def dot(left, right, left_dim, right_dim):
    return lax.dot_general(left, right, (((left_dim,), (right_dim,)), ((), ())), preferred_element_type=f32)


def times(left, right):
    return dot(left, right, 1, 0)


def times_rows(left, right):
    return dot(left, right, 1, 1)


def contract_rows(left, right):
    return dot(left, right, 0, 0)


def after(value, *others):
    return lax.optimization_barrier((value, *others))[0]


def summed(left, right):
    return (left.astype(f32) + right.astype(f32)).astype(bf16)


class Net:
    def __init__(self):
        self.dp = lax.axis_size("dp")
        self.mod = lax.axis_size("mod")
        self.bits = self.dp.bit_length() - 1
        self.dp_rank = lax.axis_index("dp")
        self.mod_rank = lax.axis_index("mod")
        self.core = self.dp_rank & 1
        self.chips = self.dp // 2 * self.mod
        self.lead = list(range(self.bits - 1, 2, -1))
        last = ["mod", 1, 2]
        self.turns = [last[n:] + last[:n] for n in range(3)]
        self.orders = [self.lead + turn for turn in self.turns]

    def swap(self, value, dim):
        if dim == "mod":
            return lax.ppermute(value, "mod", [(i, i ^ 1) for i in range(self.mod)])
        return lax.ppermute(value, "dp", [(i, i ^ (1 << dim)) for i in range(self.dp)])

    def ranks(self, order, chunks, core=0):
        masks = []
        for j in chunks:
            dp_mask, mod_mask = core, 0
            for step, dim in enumerate(order):
                if j >> step & 1:
                    if dim == "mod":
                        mod_mask ^= 1
                    else:
                        dp_mask ^= 1 << dim
            masks.append((dp_mask, mod_mask))
        masks = np.array(masks, np.int32)
        return self.dp_rank ^ masks[:, 0], self.mod_rank ^ masks[:, 1]

    def devices(self, order, chunks, core=0):
        dp, mod = self.ranks(order, chunks, core)
        return dp * self.mod + mod

    def local(self, order, chunks):
        dp, mod = self.ranks(order, chunks)
        return (dp >> 1) * self.mod + mod


class Gather:
    def __init__(self, net, shard):
        self.net, self.count = net, len(net.lead)
        self.third = shard.shape[1] // 3
        self.value, self.got, self.phase = shard, None, 0

    def start(self, *others):
        net, phase = self.net, self.phase
        if phase < self.count:
            self.value = after(self.value, *others) if others else self.value
            self.got = [net.swap(self.value, net.lead[phase])]
        else:
            if phase == self.count:
                kinds, _, width = self.value.shape
                whole = self.value.reshape(kinds, -1, 3, self.third, width)
                self.value = [whole[:, :, n].reshape(kinds, -1, width) for n in range(3)]
            if others:
                self.value = list(lax.optimization_barrier((*self.value, *others))[:3])
            step = phase - self.count
            self.got = [net.swap(self.value[n], net.turns[n][step]) for n in range(3)]
        self.phase += 1
        return self

    def finish(self):
        if self.phase <= self.count:
            self.value = jnp.concatenate([self.value, self.got[0]], axis=1)
        elif self.phase < self.count + 3:
            self.value = [jnp.concatenate(pair, axis=1) for pair in zip(self.value, self.got)]
        return self


class Scatter:
    def __init__(self, net):
        self.net = net
        self.own, self.got, self.step = [None] * 3, [None] * 3, [2] * 3
        self.whole = None

    def begin(self, n, own, other):
        self.own[n] = own
        self.got[n] = self.net.swap(other, self.net.turns[n][2])

    def arrived(self):
        return [got for got in self.got if got is not None]

    def advance(self, which=(0, 1, 2)):
        net = self.net
        if self.whole is None:
            for n in which:
                own, got = self.own[n], self.got[n]
                self.step[n] -= 1
                if self.step[n] >= 0:
                    half = own.shape[1] // 2
                    other = summed(own[:, half:], got[:, half:])
                    self.own[n] = summed(own[:, :half], got[:, :half])
                    self.got[n] = net.swap(other, net.turns[n][self.step[n]])
                else:
                    self.own[n], self.got[n] = summed(own, got), None
            if self.arrived():
                return self
            kinds, _, width = self.own[0].shape
            count = 1 << len(net.lead)
            whole = jnp.concatenate([own.reshape(kinds, count, -1, width) for own in self.own], axis=2)
            self.whole, self.left = whole.reshape(kinds, -1, width), len(net.lead)
        else:
            total = self.whole.astype(f32) + self.got[0].astype(f32)
            if self.left == 0:
                self.total, self.got = total, []
                return self
            self.whole = total.astype(bf16)
        half = self.whole.shape[1] // 2
        self.left -= 1
        self.got = [net.swap(self.whole[:, half:], net.lead[self.left])]
        self.whole = self.whole[:, :half]
        return self

    def rest(self):
        while self.got:
            self.advance()
        return self.total


any_spec = pl.BlockSpec(memory_space=pl.ANY)
vmem_spec = pl.BlockSpec(memory_space=pltpu.VMEM)


def run_copies(copies):
    for copy in copies:
        copy.start()
    for copy in copies:
        copy.wait()


def assemble_kernel(rows, each, index_ref, *refs):
    pieces, out_ref, hold, sems, last = refs[:-4], *refs[-4:]
    copies = []
    for n, piece in enumerate(pieces):
        for j in range(each):
            at = pl.multiple_of(index_ref[n * each + j] * rows, rows)
            copies.append(
                pltpu.make_async_copy(
                    piece.at[0, pl.ds(j * rows, rows)], hold.at[pl.ds(at, rows)], sems.at[n * each + j]
                )
            )
    run_copies(copies)
    run_copies([pltpu.make_async_copy(hold, out_ref, last)])


def assemble(pieces, index, rows):
    each, width = pieces[0].shape[1] // rows, pieces[0].shape[2]
    total = len(pieces) * each
    return pl.pallas_call(
        functools.partial(assemble_kernel, rows, each),
        grid_spec=pltpu.PrefetchScalarGridSpec(
            num_scalar_prefetch=1,
            grid=(1,),
            in_specs=[any_spec] * len(pieces),
            out_specs=any_spec,
            scratch_shapes=[
                pltpu.VMEM((total * rows, width), bf16),
                pltpu.SemaphoreType.DMA((total,)),
                pltpu.SemaphoreType.DMA,
            ],
        ),
        out_shape=jax.ShapeDtypeStruct((total * rows, width), bf16),
        compiler_params=pltpu.CompilerParams(vmem_limit_bytes=10 * MIB),
        name="assemble",
    )(index, *pieces)


def split_kernel(rows, each, index_ref, first_ref, second_ref, *refs):
    outs, hold, sems, ins = refs[:-3], *refs[-3:]
    top = first_ref.shape[0]
    run_copies(
        [
            pltpu.make_async_copy(first_ref, hold.at[pl.ds(0, top)], ins.at[0]),
            pltpu.make_async_copy(second_ref, hold.at[pl.ds(top, second_ref.shape[0])], ins.at[1]),
        ]
    )
    copies = []
    for n, out in enumerate(outs):
        for j in range(each):
            at = pl.multiple_of(index_ref[n * each + j] * rows, rows)
            copies.append(
                pltpu.make_async_copy(
                    hold.at[pl.ds(at, rows)], out.at[0, pl.ds(j * rows, rows)], sems.at[n * each + j]
                )
            )
    run_copies(copies)


def split_pieces(first, second, index, rows, count):
    total, width = first.shape[0] + second.shape[0], first.shape[1]
    each = total // rows // count
    return pl.pallas_call(
        functools.partial(split_kernel, rows, each),
        grid_spec=pltpu.PrefetchScalarGridSpec(
            num_scalar_prefetch=1,
            grid=(1,),
            in_specs=[any_spec] * 2,
            out_specs=[any_spec] * count,
            scratch_shapes=[
                pltpu.VMEM((total, width), bf16),
                pltpu.SemaphoreType.DMA((each * count,)),
                pltpu.SemaphoreType.DMA((2,)),
            ],
        ),
        out_shape=[jax.ShapeDtypeStruct((1, each * rows, width), bf16)] * count,
        compiler_params=pltpu.CompilerParams(vmem_limit_bytes=10 * MIB),
        name="split_pieces",
    )(index, first, second)


def softmax_t(key, query, same, scale):
    scores = jnp.where(same, dot(key, query, 0, 0) * scale, -1e30)
    weights = jnp.exp(scores - jnp.max(scores, axis=0, keepdims=True))
    return weights * (1.0 / jnp.sum(weights, axis=0, keepdims=True))


def heads_of(block, dim, cols):
    wide = block[:, cols].astype(f32)
    return [wide[n * dim : (n + 1) * dim].astype(bf16) for n in range(wide.shape[0] // dim)]


def attn_forward(dim, scale, row_ref, col_ref, q_ref, k_ref, v_ref, out_ref):
    length = col_ref.shape[0]
    for s in range(row_ref.shape[0]):
        cols = slice(s * length, (s + 1) * length)
        same = row_ref[s : s + 1] == col_ref[:, s : s + 1]
        outs = []
        for q, k, v in zip(*[heads_of(r[0, 0], dim, cols) for r in (q_ref, k_ref, v_ref)]):
            probs = softmax_t(k, q, same, scale).astype(bf16)
            outs.append(dot(v, probs, 1, 0))
        out_ref[0, :, cols] = jnp.concatenate(outs, axis=0).astype(bf16)


def attn_backward(dim, scale, row_ref, col_ref, q_ref, k_ref, v_ref, g_ref, out_ref):
    length = col_ref.shape[0]
    for s in range(row_ref.shape[0]):
        cols = slice(s * length, (s + 1) * length)
        same = row_ref[s : s + 1] == col_ref[:, s : s + 1]
        gq, gk, gv = [], [], []
        qs, ks, vs = [heads_of(r[0, 0], dim, cols) for r in (q_ref, k_ref, v_ref)]
        for q, k, v, g in zip(qs, ks, vs, heads_of(g_ref[0], dim, cols)):
            probs = softmax_t(k, q, same, scale)
            back = dot(v, g, 0, 0)
            back = probs * (back - jnp.sum(back * probs, axis=0, keepdims=True))
            back = back.astype(bf16)
            gq.append(dot(k, back, 1, 0) * scale)
            gk.append(dot(q, back, 1, 1) * scale)
            gv.append(dot(g, probs.astype(bf16), 1, 1))
        for n, parts in enumerate((gq, gk, gv)):
            out_ref[n, 0, :, cols] = jnp.concatenate(parts, axis=0).astype(bf16)


def attention(qkv, ids, dim, grad=None):
    _, groups, rows, tokens = qkv.shape
    scale = dim**-0.5
    ids_t = ids.T
    flops = groups * rows * tokens * ids.shape[1] * 2

    def one(n):
        return pl.BlockSpec((1, 1, rows, tokens), lambda i: (n, i, 0, 0))

    flat = pl.BlockSpec((1, rows, tokens), lambda i: (i, 0, 0))
    args = [ids, ids_t, qkv, qkv, qkv]
    specs = [pl.BlockSpec(a.shape, lambda i: (0, 0)) for a in (ids, ids_t)] + [one(0), one(1), one(2)]
    if grad is None:
        return pl.pallas_call(
            functools.partial(attn_forward, dim, scale),
            grid=(groups,),
            in_specs=specs,
            out_specs=flat,
            out_shape=jax.ShapeDtypeStruct((groups, rows, tokens), bf16),
            cost_estimate=pl.CostEstimate(flops=2 * flops, bytes_accessed=qkv.size * 3, transcendentals=0),
            compiler_params=pltpu.CompilerParams(vmem_limit_bytes=24 * MIB),
            name="attention",
        )(*args)
    return pl.pallas_call(
        functools.partial(attn_backward, dim, scale),
        grid=(groups,),
        in_specs=specs + [flat],
        out_specs=pl.BlockSpec((3, 1, rows, tokens), lambda i: (0, i, 0, 0)),
        out_shape=jax.ShapeDtypeStruct(qkv.shape, bf16),
        cost_estimate=pl.CostEstimate(flops=5 * flops, bytes_accessed=qkv.size * 5, transcendentals=0),
        compiler_params=pltpu.CompilerParams(vmem_limit_bytes=24 * MIB),
        name="attention_back",
    )(*args, grad)


def mlp_kernel(first, x_ref, g_ref, b_ref, *refs):
    if first:
        pieces, sums, before = refs[:2], refs[-4:], [None] * 4
    else:
        pieces, before, sums = refs[:2], refs[2:6], refs[-4:]
    grads, columns = refs[-7:-5], refs[-5]
    x, g = x_ref[...], g_ref[...]
    half = x.shape[0] // 2
    out_sum, back_sum = 0.0, 0.0
    root = 0.7978845608028654
    for n, piece in enumerate(pieces):
        w_in, w_out = piece[0], piece[1]
        hidden = dot(x, w_in, 1, 1) + b_ref[n : n + 1]
        square = hidden * hidden
        tanh = jnp.tanh(root * hidden * (1.0 + 0.044715 * square))
        act = (0.5 * hidden * (1.0 + tanh)).astype(bf16)
        slope = 0.5 * (1.0 + tanh) + 0.5 * hidden * (1.0 - tanh * tanh) * (root * (1.0 + 0.134145 * square))
        back = dot(g, w_out, 1, 1) * slope
        back = back.astype(bf16)
        grads[n][1] = dot(act, g, 0, 0).astype(bf16)
        grads[n][0] = dot(back, x, 0, 0).astype(bf16)
        columns[n : n + 1] = jnp.sum(back.astype(f32), axis=0, keepdims=True)
        out_sum = out_sum + dot(act, w_out, 1, 0)
        back_sum = back_sum + dot(back, w_in, 1, 0)
    for ref, prior, value in zip(
        sums, before, (out_sum[:half], out_sum[half:], back_sum[:half], back_sum[half:])
    ):
        ref[...] = value if prior is None else value + prior[...]


def mlp_part(x, g, bias, own, other, before):
    tokens, width = x.shape
    units = own.shape[1]
    sums = [jax.ShapeDtypeStruct((tokens // 2, width), f32)] * 4
    outs = [jax.ShapeDtypeStruct(own.shape, bf16)] * 2 + [jax.ShapeDtypeStruct((2, units), f32)] + sums
    args = [x, g, bias, own, other, *before]
    return pl.pallas_call(
        functools.partial(mlp_kernel, not before),
        in_specs=[vmem_spec] * len(args),
        out_specs=[vmem_spec] * len(outs),
        out_shape=outs,
        cost_estimate=pl.CostEstimate(
            flops=24 * tokens * width * units, bytes_accessed=units * width * 32, transcendentals=0
        ),
        compiler_params=pltpu.CompilerParams(vmem_limit_bytes=48 * MIB),
        name="mlp_part",
    )(*args)


def on_device(
    tokens,
    cond,
    segment_ids,
    crop_slot,
    ada_weight,
    ada_bias,
    attn_weight,
    fc_in,
    fc_out,
    biases,
    out_grad,
):
    net = Net()
    tok_len, width = tokens.shape[1:]
    head_dim = width // HEADS
    mod_rank, core, chips = net.mod_rank, net.core, net.chips
    device_count = net.dp * net.mod
    crop_count = crop_slot.shape[1] // net.mod
    shard = attn_weight.shape[0]
    third = shard // 3
    chunks_of = [range(chips // 2), range(chips // 2, chips)]
    halves = [(n, side) for n in range(3) for side in range(2)]
    aligned = shard % (2 * head_dim) == 0 and third % 16 == 0 and width % (2 * net.mod * shard) == 0

    g_attn = Gather(net, attn_weight[None])
    g_fc = Gather(net, jnp.stack([fc_in, fc_out]))
    for n in range(g_attn.count):
        g_attn.start().finish()
    g_attn.start()
    for n in range(g_fc.count):
        g_fc.start(*g_attn.value).finish()
    g_attn.finish().start()
    g_attn.finish().start()
    g_fc.start(*g_attn.got)
    attn_pieces = [(g_attn.value, g_attn.got)[side][n] for n, side in halves]

    silu_cond = jax.nn.silu(cond.astype(f32)).astype(bf16)
    mod_part = times(silu_cond, ada_weight) + ada_bias.reshape(-1).astype(f32)
    mod_own = mod_part.astype(bf16)
    mod_other = net.swap(mod_own, "mod")
    modulation = jnp.concatenate(
        [jnp.where(mod_rank == 0, mod_own, mod_other), jnp.where(mod_rank == 0, mod_other, mod_own)], axis=1
    )
    seg_ids = segment_ids[0]
    slots = lax.dynamic_slice_in_dim(crop_slot[0], mod_rank * crop_count, crop_count)
    crop_onehot = seg_ids[:, None] == jnp.arange(crop_count, dtype=jnp.int32)[None, :]
    token_slot = jnp.sum(jnp.where(crop_onehot, slots[None, :], 0), axis=1)
    slot_pick = token_slot[:, None] == jnp.arange(cond.shape[0], dtype=jnp.int32)[None, :]
    slot_pick = slot_pick.astype(bf16)
    token_mod = times(slot_pick, modulation)
    shift_a, scale_a, gate_a, shift_m, scale_m, gate_m = jnp.split(token_mod, 6, axis=1)

    bias_all = lax.all_to_all(
        jnp.broadcast_to(biases[None], (device_count, biases.shape[0])),
        ("dp", "mod"),
        split_axis=0,
        concat_axis=0,
        tiled=True,
    ).reshape(-1)
    bias_query, bias_value, bias_proj, bias_out = [
        bias_all[n * width : (n + 1) * width].astype(f32) for n in range(4)
    ]
    bias_in = bias_all[4 * width :].reshape(device_count, shard)
    bias_pieces, picks = [], []
    for n, side in halves:
        devices = net.devices(net.orders[n], chunks_of[side])
        pick = (devices[:, None] == jnp.arange(device_count)[None, :]).astype(bf16)
        picks.append(pick)
        bias_pieces.append(times(pick, bias_in[:, n * third : (n + 1) * third]).reshape(1, -1))

    def join(own, other):
        own, other = [a.reshape(-1, 1, net.mod * shard, a.shape[-1]) for a in (own, other)]
        both = jnp.where(core == 0, jnp.concatenate([own, other], 1), jnp.concatenate([other, own], 1))
        return both.reshape(-1, both.shape[-1])

    def part(whole):
        whole = whole.reshape(-1, 2, net.mod * shard, whole.shape[-1])
        return [
            jnp.where(core == c, whole[:, 0], whole[:, 1]).reshape(-1, whole.shape[-1]) for c in range(2)
        ]

    resid = tokens[0].astype(f32)
    normed_a, inverse_a = layer_norm(resid)
    attn_in = (normed_a * (1.0 + scale_a) + shift_a).astype(bf16)
    if aligned:
        index = jnp.concatenate([net.local(net.orders[n], chunks_of[side]) * 3 + n for n, side in halves])
        own_weight = assemble(attn_pieces, index, third)
        qkv_rows = own_weight.shape[0] * 3 // 4
        qkv_weight = own_weight[:qkv_rows]
        proj_own = own_weight[qkv_rows:]
        proj_weight = join(proj_own, net.swap(proj_own, 0))
        ids = jnp.stack([seg_ids, net.swap(seg_ids, 0)])
        attn_both = jnp.concatenate([attn_in, net.swap(attn_in, 0)], axis=0)
        own_query, own_value = part(bias_query[:, None])[0], part(bias_value[:, None])[0]
        qkv_bias = jnp.concatenate([own_query, jnp.zeros_like(own_query), own_value], axis=0)
        attn_both = after(attn_both, *g_fc.got)
        g_fc.finish().start()
        qkv = (times_rows(qkv_weight, attn_both) + qkv_bias).astype(bf16)
        qkv = qkv.reshape(3, -1, 2 * head_dim, 2 * tok_len)
        context_both = attention(qkv, ids, head_dim).reshape(-1, 2 * tok_len)
        context_both = after(context_both, *g_fc.got)
        g_fc.finish().start()
        context = join(context_both[:, :tok_len], net.swap(context_both[:, tok_len:], 0))
        attn_out = dot(context, proj_weight, 0, 1) + bias_proj
    else:
        arrays = attn_pieces + [net.swap(piece, 0) for piece in attn_pieces]
        places = jnp.concatenate(
            [net.devices(net.orders[n], chunks_of[side], c) * 3 + n for c in range(2) for n, side in halves]
        )
        spread = jnp.concatenate(arrays, axis=1)[0]

        def place(n, whole):
            block = lax.dynamic_slice_in_dim(spread, n * third, third)
            return lax.dynamic_update_slice_in_dim(whole, block, places[n] * third, 0)

        attn_w = lax.fori_loop(0, places.shape[0], place, jnp.zeros_like(spread))
        g_fc.finish().start()
        g_fc.finish().start()
        qkv_weight, proj_weight = attn_w[: 3 * width], attn_w[3 * width :]
        qkv_bias = jnp.concatenate([bias_query, jnp.zeros_like(bias_query), bias_value])
        qkv = (times_rows(qkv_weight, attn_in) + qkv_bias[:, None]).astype(bf16)
        qkv = qkv.reshape(3, -1, 2 * head_dim, tok_len)
        context = attention(qkv, seg_ids[None], head_dim).reshape(-1, tok_len)
        attn_out = dot(context, proj_weight, 0, 1) + bias_proj
    mid = resid + gate_a * attn_out
    normed_m, inverse_m = layer_norm(mid)
    mlp_in = (normed_m * (1.0 + scale_m) + shift_m).astype(bf16)
    grad_out = out_grad[0].astype(f32)
    grad_mlp = (gate_m * grad_out).astype(bf16)

    mlp_both = jnp.concatenate([mlp_in, net.swap(mlp_in, 0)], axis=0)
    grad_both = jnp.concatenate([grad_mlp, net.swap(grad_mlp, 0)], axis=0)
    s_fc = Scatter(net)
    sums, columns = [], []
    for n in range(3):
        bias = jnp.concatenate(bias_pieces[2 * n : 2 * n + 2], axis=0)
        own, other, column, *sums = mlp_part(mlp_both, grad_both, bias, g_fc.value[n], g_fc.got[n], sums)
        s_fc.begin(n, own, other)
        columns.extend([column[0], column[1]])
    out_own, out_other, back_own, back_other = sums
    mlp_out = out_own + net.swap(out_other, 0) + bias_out
    grad_mlp_in = back_own + net.swap(back_other, 0)
    grad_bias_in = []
    for n in range(3):
        placed = 0.0
        for side in range(2):
            column = columns[2 * n + side].reshape(chips // 2, third)
            placed = placed + jnp.dot(
                picks[2 * n + side].astype(f32).T, column, precision=lax.Precision.HIGHEST
            )
        grad_bias_in.append(placed)
    grad_bias_in = jnp.concatenate(grad_bias_in, axis=1)

    ada_order = list(range(1, net.bits)) + [0]

    def all_rows(value):
        for dim in ada_order:
            value = jnp.concatenate([value, net.swap(value, dim)], axis=0)
        return value

    cond_rows = all_rows(after(silu_cond, mlp_both))

    result = (mid + gate_m * mlp_out).astype(bf16)
    grad_gate_m = grad_out * mlp_out
    grad_scale_m = grad_mlp_in * normed_m
    grad_mid = grad_out + norm_back(grad_mlp_in * (1.0 + scale_m), normed_m, inverse_m)
    grad_gate_a = grad_mid * attn_out
    grad_attn = (gate_a * grad_mid).astype(bf16)
    grad_proj = dot(grad_attn, context, 0, 1).astype(bf16)
    grad_context = dot(proj_weight, grad_attn, 0, 1).astype(bf16)
    s_attn = Scatter(net)
    if aligned:
        proj_mine, proj_other = part(grad_proj)
        proj_mine = summed(proj_mine, net.swap(proj_other, 0))
        mine, other = part(grad_context)
        context_grads = jnp.concatenate([mine, net.swap(other, 0)], axis=1)
        grad_qkv = attention(qkv, ids, head_dim, context_grads.reshape(-1, 2 * head_dim, 2 * tok_len))
        grad_qkv = grad_qkv.reshape(-1, 2 * tok_len)
        grad_qkv = after(grad_qkv, *s_fc.arrived())
        s_fc.advance()
        grad_qkv_w = times(grad_qkv, attn_both).astype(bf16)
        pieces = split_pieces(grad_qkv_w, proj_mine, index, third, 6)
        back_both = contract_rows(grad_qkv, qkv_weight)
        grad_attn_in = back_both[:tok_len] + net.swap(back_both[tok_len:], 0)
        column = jnp.sum(grad_qkv.astype(f32), axis=1, keepdims=True).reshape(3, -1, 1)
        none = jnp.zeros_like(column[0])
        grad_bias_query, grad_bias_value = join(column[0], none)[:, 0], join(column[2], none)[:, 0]
    else:
        grad_qkv = attention(
            qkv, seg_ids[None], head_dim, grad_context.reshape(-1, 2 * head_dim, tok_len)
        ).reshape(-1, tok_len)
        s_fc.advance()
        attn_grad = jnp.concatenate([times(grad_qkv, attn_in).astype(bf16), grad_proj], axis=0)

        def take(n, whole):
            block = lax.dynamic_slice_in_dim(attn_grad, places[n] * third, third)
            return lax.dynamic_update_slice_in_dim(whole, block, n * third, 0)

        grads = lax.fori_loop(0, places.shape[0], take, jnp.zeros_like(attn_grad))
        grads = jnp.split(grads[None], 12, axis=1)
        pieces = [summed(a, net.swap(b, 0)) for a, b in zip(grads[:6], grads[6:])]
        grad_attn_in = contract_rows(grad_qkv, qkv_weight)
        column = jnp.sum(grad_qkv.astype(f32), axis=1).reshape(3, -1)
        grad_bias_query, grad_bias_value = column[0], column[2]
    for n in range(3):
        s_attn.begin(n, pieces[2 * n], pieces[2 * n + 1])
    grad_scale_a = grad_attn_in * normed_a
    grad_tokens = grad_mid + norm_back(grad_attn_in * (1.0 + scale_a), normed_a, inverse_a)
    grad_bias = jnp.concatenate(
        [
            grad_bias_query,
            grad_bias_value,
            jnp.sum(grad_attn.astype(f32), axis=0),
            jnp.sum(grad_mlp.astype(f32), axis=0),
            grad_bias_in.reshape(-1),
        ]
    )
    bias_rows = lax.all_to_all(
        grad_bias.reshape(device_count, -1), ("dp", "mod"), split_axis=0, concat_axis=0, tiled=True
    )
    bias_sum = jnp.sum(bias_rows, axis=0)

    grad_token_mod = jnp.concatenate(
        [grad_attn_in, grad_scale_a, grad_gate_a, grad_mlp_in, grad_scale_m, grad_gate_m], axis=1
    )
    token_high = lax.reduce_precision(grad_token_mod, 8, 7)
    token_low = (grad_token_mod - token_high).astype(bf16)
    grad_pair = contract_rows(slot_pick, token_high.astype(bf16)) + contract_rows(slot_pick, token_low)
    grad_pair = grad_pair.astype(bf16)
    columns = grad_pair.shape[1] // 2
    pair_own = jnp.where(mod_rank == 0, grad_pair[:, :columns], grad_pair[:, columns:])
    pair_send = jnp.where(mod_rank == 0, grad_pair[:, columns:], grad_pair[:, :columns])
    grad_mod = summed(pair_own, net.swap(pair_send, "mod"))
    grad_silu = times_rows(grad_mod, ada_weight)
    silu_own = jnp.where(mod_rank == 0, grad_silu[:crop_count], grad_silu[crop_count:])
    silu_send = jnp.where(mod_rank == 0, grad_silu[crop_count:], grad_silu[:crop_count])
    grad_silu = silu_own + net.swap(silu_send.astype(bf16), "mod").astype(f32)
    own_cond = lax.dynamic_slice_in_dim(cond, mod_rank * crop_count, crop_count, 0).astype(f32)
    silu_back = jax.vjp(jax.nn.silu, own_cond)[1]
    grad_cond = silu_back(grad_silu)[0]
    mod_rows = all_rows(grad_mod)
    own_cols = width // net.dp
    cond_cols = lax.dynamic_slice_in_dim(cond_rows, net.dp_rank * own_cols, own_cols, 1)
    ada_w_sum = contract_rows(cond_cols, mod_rows)
    ada_b_sum = jnp.sum(mod_rows.astype(f32), axis=0).reshape(ada_bias.shape[0], width)
    ada_b_sum = lax.dynamic_slice_in_dim(ada_b_sum, net.dp_rank * own_cols, own_cols, 1)

    fc_sum = s_fc.rest()
    attn_sum = s_attn.rest()[0]
    return (
        result[None],
        grad_tokens[None],
        grad_cond,
        ada_w_sum,
        ada_b_sum,
        attn_sum,
        fc_sum[0],
        fc_sum[1],
        bias_sum,
    )


def solution(mesh):
    placed = (
        P(("dp", "mod"), None, None),
        P("dp", None),
        P(("dp", "mod"), None),
        P("dp", None),
        P(None, "mod"),
        P("mod", None),
        P(("dp", "mod"), None),
        P(("dp", "mod"), None),
        P(("dp", "mod"), None),
        P(("dp", "mod")),
        P(("dp", "mod"), None, None),
    )
    return jax.shard_map(
        on_device,
        mesh=mesh,
        in_specs=placed,
        out_specs=(
            P(("dp", "mod"), None, None),
            P(("dp", "mod"), None, None),
            P(("dp", "mod"), None),
            P("dp", "mod"),
            P("mod", "dp"),
            P(("dp", "mod"), None),
            P(("dp", "mod"), None),
            P(("dp", "mod"), None),
            P(("dp", "mod")),
        ),
        check_vma=False,
    )
```

```python
import functools

import jax
import jax.numpy as jnp
import numpy as np
from jax import lax
from jax.experimental import pallas as pl
from jax.experimental.pallas import tpu as pltpu
from jax.sharding import PartitionSpec as P

HEADS = 16
norm_eps = 1e-06
bf16 = jnp.bfloat16
f32 = jnp.float32
MIB = 1024 * 1024


def layer_norm(values):
    center = values - jnp.mean(values, axis=-1, keepdims=True)
    inverse = lax.rsqrt(jnp.mean(center * center, axis=-1, keepdims=True) + norm_eps)
    return (center * inverse, inverse)


def norm_back(grad_in, normed, inverse):
    centered = grad_in - jnp.mean(grad_in, axis=-1, keepdims=True)
    return (centered - normed * jnp.mean(grad_in * normed, axis=-1, keepdims=True)) * inverse


def dot(left, right, left_dim, right_dim):
    return lax.dot_general(left, right, (((left_dim,), (right_dim,)), ((), ())), preferred_element_type=f32)


def times(left, right):
    return dot(left, right, 1, 0)


def times_rows(left, right):
    return dot(left, right, 1, 1)


def contract_rows(left, right):
    return dot(left, right, 0, 0)


def after(value, *others):
    return lax.optimization_barrier((value, *others))[0]


def summed(left, right):
    return (left.astype(f32) + right.astype(f32)).astype(bf16)


class Net:
    def __init__(self):
        self.dp = lax.axis_size("dp")
        self.mod = lax.axis_size("mod")
        self.bits = self.dp.bit_length() - 1
        self.dp_rank = lax.axis_index("dp")
        self.mod_rank = lax.axis_index("mod")
        self.core = self.dp_rank & 1
        self.chips = self.dp // 2 * self.mod
        self.lead = list(range(self.bits - 1, 2, -1))
        last = ["mod", 1, 2]
        self.turns = [last[n:] + last[:n] for n in range(3)]
        self.orders = [self.lead + turn for turn in self.turns]

    def swap(self, value, dim):
        if dim == "mod":
            return lax.ppermute(value, "mod", [(i, i ^ 1) for i in range(self.mod)])
        return lax.ppermute(value, "dp", [(i, i ^ (1 << dim)) for i in range(self.dp)])

    def ranks(self, order, chunks, core=0):
        masks = []
        for j in chunks:
            dp_mask, mod_mask = core, 0
            for step, dim in enumerate(order):
                if j >> step & 1:
                    if dim == "mod":
                        mod_mask ^= 1
                    else:
                        dp_mask ^= 1 << dim
            masks.append((dp_mask, mod_mask))
        masks = np.array(masks, np.int32)
        return self.dp_rank ^ masks[:, 0], self.mod_rank ^ masks[:, 1]

    def devices(self, order, chunks, core=0):
        dp, mod = self.ranks(order, chunks, core)
        return dp * self.mod + mod

    def local(self, order, chunks):
        dp, mod = self.ranks(order, chunks)
        return (dp >> 1) * self.mod + mod


class Gather:
    def __init__(self, net, shard):
        self.net, self.count = net, len(net.lead)
        self.third = shard.shape[1] // 3
        self.value, self.got, self.phase = shard, None, 0

    def start(self, *others):
        net, phase = self.net, self.phase
        if phase < self.count:
            self.value = after(self.value, *others) if others else self.value
            self.got = [net.swap(self.value, net.lead[phase])]
        else:
            if phase == self.count:
                kinds, _, width = self.value.shape
                whole = self.value.reshape(kinds, -1, 3, self.third, width)
                self.value = [whole[:, :, n].reshape(kinds, -1, width) for n in range(3)]
            if others:
                self.value = list(lax.optimization_barrier((*self.value, *others))[:3])
            step = phase - self.count
            self.got = [net.swap(self.value[n], net.turns[n][step]) for n in range(3)]
        self.phase += 1
        return self

    def finish(self):
        if self.phase <= self.count:
            self.value = jnp.concatenate([self.value, self.got[0]], axis=1)
        elif self.phase < self.count + 3:
            self.value = [jnp.concatenate(pair, axis=1) for pair in zip(self.value, self.got)]
        return self


class Scatter:
    def __init__(self, net):
        self.net = net
        self.own, self.got, self.step = [None] * 3, [None] * 3, [2] * 3
        self.whole = None

    def begin(self, n, own, other):
        self.own[n] = own
        self.got[n] = self.net.swap(other, self.net.turns[n][2])

    def arrived(self):
        return [got for got in self.got if got is not None]

    def advance(self, which=(0, 1, 2)):
        net = self.net
        if self.whole is None:
            for n in which:
                own, got = self.own[n], self.got[n]
                self.step[n] -= 1
                if self.step[n] >= 0:
                    half = own.shape[1] // 2
                    other = summed(own[:, half:], got[:, half:])
                    self.own[n] = summed(own[:, :half], got[:, :half])
                    self.got[n] = net.swap(other, net.turns[n][self.step[n]])
                else:
                    self.own[n], self.got[n] = summed(own, got), None
            if self.arrived():
                return self
            kinds, _, width = self.own[0].shape
            count = 1 << len(net.lead)
            whole = jnp.concatenate([own.reshape(kinds, count, -1, width) for own in self.own], axis=2)
            self.whole, self.left = whole.reshape(kinds, -1, width), len(net.lead)
        else:
            total = self.whole.astype(f32) + self.got[0].astype(f32)
            if self.left == 0:
                self.total, self.got = total, []
                return self
            self.whole = total.astype(bf16)
        half = self.whole.shape[1] // 2
        self.left -= 1
        self.got = [net.swap(self.whole[:, half:], net.lead[self.left])]
        self.whole = self.whole[:, :half]
        return self

    def rest(self):
        while self.got:
            self.advance()
        return self.total


any_spec = pl.BlockSpec(memory_space=pl.ANY)
vmem_spec = pl.BlockSpec(memory_space=pltpu.VMEM)
tiny = pl.CostEstimate(flops=1024, bytes_accessed=1024, transcendentals=0)


def run_copies(copies):
    for copy in copies:
        copy.start()
    for copy in copies:
        copy.wait()


def assemble_kernel(rows, each, index_ref, *refs):
    pieces, out_ref, hold, sems, last = refs[:-4], *refs[-4:]
    copies = []
    for n, piece in enumerate(pieces):
        for j in range(each):
            at = pl.multiple_of(index_ref[n * each + j] * rows, rows)
            copies.append(
                pltpu.make_async_copy(
                    piece.at[0, pl.ds(j * rows, rows)], hold.at[pl.ds(at, rows)], sems.at[n * each + j]
                )
            )
    run_copies(copies)
    run_copies([pltpu.make_async_copy(hold, out_ref, last)])


def assemble(pieces, index, rows):
    each, width = pieces[0].shape[1] // rows, pieces[0].shape[2]
    total = len(pieces) * each
    return pl.pallas_call(
        functools.partial(assemble_kernel, rows, each),
        grid_spec=pltpu.PrefetchScalarGridSpec(
            num_scalar_prefetch=1,
            grid=(1,),
            in_specs=[any_spec] * len(pieces),
            out_specs=any_spec,
            scratch_shapes=[
                pltpu.VMEM((total * rows, width), bf16),
                pltpu.SemaphoreType.DMA((total,)),
                pltpu.SemaphoreType.DMA,
            ],
        ),
        out_shape=jax.ShapeDtypeStruct((total * rows, width), bf16),
        compiler_params=pltpu.CompilerParams(vmem_limit_bytes=10 * MIB),
        name="assemble",
    )(index, *pieces)


def weight_grad_kernel(rows, each, index_ref, grad_ref, x_ref, mine_ref, other_ref, *refs):
    outs, hold, sems = refs[:-2], *refs[-2:]
    top = grad_ref.shape[0]
    step = top // 3
    for n in range(3):
        here = slice(n * step, (n + 1) * step)
        hold[here] = dot(grad_ref[here], x_ref[...], 1, 0).astype(bf16)
    hold[top:] = summed(mine_ref[...], other_ref[...])
    copies = []
    for n, out in enumerate(outs):
        for j in range(each):
            at = pl.multiple_of(index_ref[n * each + j] * rows, rows)
            copies.append(
                pltpu.make_async_copy(
                    hold.at[pl.ds(at, rows)], out.at[0, pl.ds(j * rows, rows)], sems.at[n * each + j]
                )
            )
    run_copies(copies)


def weight_grad(grad, x, mine, other, index, rows, count):
    total, width = grad.shape[0] + mine.shape[0], x.shape[1]
    each = total // rows // count
    return pl.pallas_call(
        functools.partial(weight_grad_kernel, rows, each),
        grid_spec=pltpu.PrefetchScalarGridSpec(
            num_scalar_prefetch=1,
            grid=(1,),
            in_specs=[vmem_spec] * 4,
            out_specs=[any_spec] * count,
            scratch_shapes=[pltpu.VMEM((total, width), bf16), pltpu.SemaphoreType.DMA((each * count,))],
        ),
        out_shape=[jax.ShapeDtypeStruct((1, each * rows, width), bf16)] * count,
        cost_estimate=tiny,
        compiler_params=pltpu.CompilerParams(vmem_limit_bytes=32 * MIB),
        name="weight_grad",
    )(index, grad, x, mine, other)


def by_core(core_ref, group, whole):
    if group is None:
        return [whole]
    picked = []
    for c in range(2):
        rows = []
        for at in range(0, whole.shape[0], 2 * group):
            first, second = whole[at : at + group], whole[at + group : at + 2 * group]
            rows.append(jnp.where(core_ref[0] == c, first, second))
        picked.append(jnp.concatenate(rows, axis=0))
    return picked


def middle_kernel(group, core_ref, *refs):
    back_a, back_b, normed_ref, inverse_ref, grad_out, attn_out, pick, scale, gate, weight, context = refs[:11]
    mid_ref, attn_ref, column_ref = refs[11:14]
    normed = normed_ref[...]
    back = (back_a[...] + back_b[...]) * (1.0 + dot(pick[...], scale[...], 1, 0))
    grad_mid = grad_out[...].astype(f32) + norm_back(back, normed, inverse_ref[...])
    mid_ref[...] = grad_mid
    grad_attn = (dot(pick[...], gate[...], 1, 0) * grad_mid).astype(bf16)
    attn_ref[...] = grad_attn
    column_ref[...] = jnp.sum(grad_attn.astype(f32), axis=0, keepdims=True)
    parts = by_core(core_ref, group, dot(weight[...], grad_attn, 0, 1))
    parts += by_core(core_ref, group, dot(grad_attn, context[...], 0, 1))
    for ref, value in zip(refs[14:], parts):
        ref[...] = value.astype(bf16)


def middle(core, group, *args):
    tokens, width = args[0].shape
    if group is None:
        sizes = [(width, tokens), (width, width)]
    else:
        sizes = [(width // 2, tokens)] * 2 + [(width // 2, width)] * 2
    return pl.pallas_call(
        functools.partial(middle_kernel, group),
        in_specs=[pl.BlockSpec(memory_space=pltpu.SMEM)] + [vmem_spec] * len(args),
        out_specs=[vmem_spec] * (3 + len(sizes)),
        out_shape=[
            jax.ShapeDtypeStruct((tokens, width), f32),
            jax.ShapeDtypeStruct((tokens, width), bf16),
            jax.ShapeDtypeStruct((1, width), f32),
        ]
        + [jax.ShapeDtypeStruct(size, bf16) for size in sizes],
        cost_estimate=tiny,
        compiler_params=pltpu.CompilerParams(vmem_limit_bytes=40 * MIB),
        name="middle",
    )(core.reshape(1), *args)


def slot_sums(pick, blocks, out_ref):
    for n, block in enumerate(blocks):
        high = block.astype(bf16)
        low = (block - high.astype(f32)).astype(bf16)
        total = dot(pick, high, 0, 0) + dot(pick, low, 0, 0)
        out_ref[:, n * block.shape[1] : (n + 1) * block.shape[1]] = total.astype(bf16)


def mlp_end_kernel(*refs):
    back_a, back_b, out_a, out_b, bias, normed, grad_out, mid, pick, gate = refs[:10]
    result_ref, pair_ref = refs[10:]
    mlp_out = out_a[...] + out_b[...] + bias[...]
    result_ref[...] = (mid[...] + dot(pick[...], gate[...], 1, 0) * mlp_out).astype(bf16)
    back = back_a[...] + back_b[...]
    slot_sums(pick[...], (back, back * normed[...], grad_out[...].astype(f32) * mlp_out), pair_ref)


def attn_end_kernel(*refs):
    back_a, back_b, normed_ref, inverse_ref, grad_mid, attn_out, pick, scale = refs[:8]
    tokens_ref, pair_ref = refs[8:]
    back, normed = back_a[...] + back_b[...], normed_ref[...]
    slope = back * (1.0 + dot(pick[...], scale[...], 1, 0))
    tokens_ref[...] = grad_mid[...] + norm_back(slope, normed, inverse_ref[...])
    slot_sums(pick[...], (back, back * normed, grad_mid[...] * attn_out[...]), pair_ref)


def end_call(kernel, dtype, slots, *args):
    tokens, width = args[0].shape
    return pl.pallas_call(
        kernel,
        in_specs=[vmem_spec] * len(args),
        out_specs=[vmem_spec] * 2,
        out_shape=[
            jax.ShapeDtypeStruct((tokens, width), dtype),
            jax.ShapeDtypeStruct((slots, 3 * width), bf16),
        ],
        cost_estimate=tiny,
        compiler_params=pltpu.CompilerParams(vmem_limit_bytes=32 * MIB),
        name=kernel.__name__,
    )(*args)


def rows_kernel(*refs):
    at = 0
    for ref in refs[:-1]:
        refs[-1][at : at + ref.shape[0]] = ref[...]
        at += ref.shape[0]


def stack_rows(*args):
    count = sum(a.shape[0] for a in args)
    return pl.pallas_call(
        rows_kernel,
        in_specs=[vmem_spec] * len(args),
        out_specs=vmem_spec,
        out_shape=jax.ShapeDtypeStruct((count, args[0].shape[1]), f32),
        cost_estimate=tiny,
        name="stack_rows",
    )(*args)


def softmax_t(key, query, same, scale):
    scores = jnp.where(same, dot(key, query, 0, 0) * scale, -1e30)
    weights = jnp.exp(scores - jnp.max(scores, axis=0, keepdims=True))
    return weights * (1.0 / jnp.sum(weights, axis=0, keepdims=True))


def heads_of(block, dim, cols):
    wide = block[:, cols].astype(f32)
    return [wide[n * dim : (n + 1) * dim].astype(bf16) for n in range(wide.shape[0] // dim)]


def attn_forward(dim, scale, row_ref, col_ref, q_ref, k_ref, v_ref, out_ref):
    length = col_ref.shape[0]
    for s in range(row_ref.shape[0]):
        cols = slice(s * length, (s + 1) * length)
        same = row_ref[s : s + 1] == col_ref[:, s : s + 1]
        outs = []
        for q, k, v in zip(*[heads_of(r[0, 0], dim, cols) for r in (q_ref, k_ref, v_ref)]):
            probs = softmax_t(k, q, same, scale).astype(bf16)
            outs.append(dot(v, probs, 1, 0))
        out_ref[0, :, cols] = jnp.concatenate(outs, axis=0).astype(bf16)


def attn_backward(dim, scale, row_ref, col_ref, q_ref, k_ref, v_ref, g_ref, out_ref):
    length = col_ref.shape[0]
    for s in range(row_ref.shape[0]):
        cols = slice(s * length, (s + 1) * length)
        same = row_ref[s : s + 1] == col_ref[:, s : s + 1]
        gq, gk, gv = [], [], []
        qs, ks, vs = [heads_of(r[0, 0], dim, cols) for r in (q_ref, k_ref, v_ref)]
        for q, k, v, g in zip(qs, ks, vs, heads_of(g_ref[0], dim, cols)):
            probs = softmax_t(k, q, same, scale)
            back = dot(v, g, 0, 0)
            back = probs * (back - jnp.sum(back * probs, axis=0, keepdims=True))
            back = back.astype(bf16)
            gq.append(dot(k, back, 1, 0) * scale)
            gk.append(dot(q, back, 1, 1) * scale)
            gv.append(dot(g, probs.astype(bf16), 1, 1))
        for n, parts in enumerate((gq, gk, gv)):
            out_ref[n, 0, :, cols] = jnp.concatenate(parts, axis=0).astype(bf16)


def attention(qkv, ids, dim, grad=None):
    _, groups, rows, tokens = qkv.shape
    scale = dim**-0.5
    ids_t = ids.T

    def one(n):
        return pl.BlockSpec((1, 1, rows, tokens), lambda i: (n, i, 0, 0))

    flat = pl.BlockSpec((1, rows, tokens), lambda i: (i, 0, 0))
    args = [ids, ids_t, qkv, qkv, qkv]
    specs = [pl.BlockSpec(a.shape, lambda i: (0, 0)) for a in (ids, ids_t)] + [one(0), one(1), one(2)]
    if grad is None:
        return pl.pallas_call(
            functools.partial(attn_forward, dim, scale),
            grid=(groups,),
            in_specs=specs,
            out_specs=flat,
            out_shape=jax.ShapeDtypeStruct((groups, rows, tokens), bf16),
            cost_estimate=tiny,
            compiler_params=pltpu.CompilerParams(vmem_limit_bytes=24 * MIB),
            name="attention",
        )(*args)
    return pl.pallas_call(
        functools.partial(attn_backward, dim, scale),
        grid=(groups,),
        in_specs=specs + [flat],
        out_specs=pl.BlockSpec((3, 1, rows, tokens), lambda i: (0, i, 0, 0)),
        out_shape=jax.ShapeDtypeStruct(qkv.shape, bf16),
        cost_estimate=tiny,
        compiler_params=pltpu.CompilerParams(vmem_limit_bytes=24 * MIB),
        name="attention_back",
    )(*args, grad)


def mlp_kernel(number, first, x_ref, g_ref, b_ref, *refs):
    if first:
        pieces, sums, before = refs[:2], refs[-4:], [None] * 4
    else:
        pieces, before, sums = refs[:2], refs[2:6], refs[-4:]
    grads, columns = refs[-7:-5], refs[-5]
    x, g = x_ref[...], g_ref[...]
    half = x.shape[0] // 2
    out_sum, back_sum = 0.0, 0.0
    root = 0.7978845608028654
    for n, piece in enumerate(pieces):
        w_in, w_out = piece[0], piece[1]
        hidden = dot(x, w_in, 1, 1) + b_ref[2 * number + n : 2 * number + n + 1]
        square = hidden * hidden
        tanh = jnp.tanh(root * hidden * (1.0 + 0.044715 * square))
        act = (0.5 * hidden * (1.0 + tanh)).astype(bf16)
        slope = 0.5 * (1.0 + tanh) + 0.5 * hidden * (1.0 - tanh * tanh) * (root * (1.0 + 0.134145 * square))
        back = dot(g, w_out, 1, 1) * slope
        back = back.astype(bf16)
        grads[n][1] = dot(act, g, 0, 0).astype(bf16)
        grads[n][0] = dot(back, x, 0, 0).astype(bf16)
        columns[n : n + 1] = jnp.sum(back.astype(f32), axis=0, keepdims=True)
        out_sum = out_sum + dot(act, w_out, 1, 0)
        back_sum = back_sum + dot(back, w_in, 1, 0)
    for ref, prior, value in zip(
        sums, before, (out_sum[:half], out_sum[half:], back_sum[:half], back_sum[half:])
    ):
        ref[...] = value if prior is None else value + prior[...]


def mlp_part(number, x, g, bias, own, other, before):
    tokens, width = x.shape
    units = own.shape[1]
    sums = [jax.ShapeDtypeStruct((tokens // 2, width), f32)] * 4
    outs = [jax.ShapeDtypeStruct(own.shape, bf16)] * 2 + [jax.ShapeDtypeStruct((2, units), f32)] + sums
    args = [x, g, bias, own, other, *before]
    return pl.pallas_call(
        functools.partial(mlp_kernel, number, not before),
        in_specs=[vmem_spec] * len(args),
        out_specs=[vmem_spec] * len(outs),
        out_shape=outs,
        cost_estimate=tiny,
        compiler_params=pltpu.CompilerParams(vmem_limit_bytes=48 * MIB),
        name="mlp_part",
    )(*args)


def on_device(
    tokens,
    cond,
    segment_ids,
    crop_slot,
    ada_weight,
    ada_bias,
    attn_weight,
    fc_in,
    fc_out,
    biases,
    out_grad,
):
    net = Net()
    tok_len, width = tokens.shape[1:]
    head_dim = width // HEADS
    mod_rank, core, chips = net.mod_rank, net.core, net.chips
    device_count = net.dp * net.mod
    crop_count = crop_slot.shape[1] // net.mod
    shard = attn_weight.shape[0]
    third = shard // 3
    chunks_of = [range(chips // 2), range(chips // 2, chips)]
    halves = [(n, side) for n in range(3) for side in range(2)]
    aligned = shard % (2 * head_dim) == 0 and third % 16 == 0 and width % (2 * net.mod * shard) == 0

    g_attn = Gather(net, attn_weight[None])
    g_fc = Gather(net, jnp.stack([fc_in, fc_out]))
    for n in range(g_attn.count):
        g_attn.start().finish()
    g_attn.start()
    first = g_attn.value
    for n in range(g_fc.count):
        g_fc.start(*first).finish()
    g_attn.finish().start()
    g_attn.finish().start()
    g_fc.start(*g_attn.got)
    attn_pieces = [(g_attn.value, g_attn.got)[side][n] for n, side in halves]

    silu_cond = jax.nn.silu(after(cond, *first).astype(f32)).astype(bf16)
    mod_part = times(silu_cond, ada_weight) + ada_bias.reshape(-1).astype(f32)
    mod_own = mod_part.astype(bf16)
    mod_other = net.swap(mod_own, "mod")
    modulation = jnp.concatenate(
        [jnp.where(mod_rank == 0, mod_own, mod_other), jnp.where(mod_rank == 0, mod_other, mod_own)], axis=1
    )
    seg_ids = segment_ids[0]
    slots = lax.dynamic_slice_in_dim(crop_slot[0], mod_rank * crop_count, crop_count)
    crop_onehot = seg_ids[:, None] == jnp.arange(crop_count, dtype=jnp.int32)[None, :]
    token_slot = jnp.sum(jnp.where(crop_onehot, slots[None, :], 0), axis=1)
    slot_pick = token_slot[:, None] == jnp.arange(cond.shape[0], dtype=jnp.int32)[None, :]
    slot_pick = slot_pick.astype(bf16)
    mods = [modulation[:, n * width : (n + 1) * width] for n in range(6)]
    shift_a, scale_a, gate_a, shift_m, scale_m, gate_m = [times(slot_pick, block) for block in mods]

    slot_count, own_cols = cond.shape[0], width // net.dp
    to_dp = jnp.moveaxis(silu_cond.reshape(slot_count, net.dp, own_cols), 1, 0).reshape(net.dp, 1, -1)
    to_all = jnp.broadcast_to(to_dp, (net.dp, net.mod, slot_count * own_cols)).reshape(device_count, -1)
    sent = jnp.concatenate([jnp.broadcast_to(biases[None], (device_count, biases.shape[0])), to_all], axis=1)
    met = lax.all_to_all(sent, ("dp", "mod"), split_axis=0, concat_axis=0, tiled=True)
    ada_order = list(range(1, net.bits)) + [0]
    dp_order = net.ranks(ada_order, range(net.dp))[0]
    dp_pick = (dp_order[:, None] == jnp.arange(net.dp)[None, :]).astype(bf16)
    cond_cols = times(dp_pick, met.reshape(net.dp, net.mod, -1)[:, 0, biases.shape[0] :]).astype(bf16)
    cond_cols = cond_cols.reshape(-1, own_cols)
    bias_all = met[:, : biases.shape[0]].reshape(-1, width)
    bias_query, bias_value, bias_proj, bias_out = [bias_all[n].astype(f32) for n in range(4)]
    bias_in = bias_all[4:].reshape(device_count, 3, third)
    picks = []
    for n, side in halves:
        devices = net.devices(net.orders[n], chunks_of[side])
        picks.append((devices[:, None] == jnp.arange(device_count)[None, :]).astype(bf16))
    picks = jnp.stack(picks).reshape(3, 2, chips // 2, device_count)
    bias_pieces = jnp.einsum("nsjd,dnr->nsjr", picks, bias_in, preferred_element_type=f32).reshape(6, -1)

    def join(own, other):
        own, other = [a.reshape(-1, 1, net.mod * shard, a.shape[-1]) for a in (own, other)]
        both = jnp.where(core == 0, jnp.concatenate([own, other], 1), jnp.concatenate([other, own], 1))
        return both.reshape(-1, both.shape[-1])

    def part(whole):
        whole = whole.reshape(-1, 2, net.mod * shard, whole.shape[-1])
        return [
            jnp.where(core == c, whole[:, 0], whole[:, 1]).reshape(-1, whole.shape[-1]) for c in range(2)
        ]

    resid = tokens[0].astype(f32)
    normed_a, inverse_a = layer_norm(resid)
    attn_in = (normed_a * (1.0 + scale_a) + shift_a).astype(bf16)
    if aligned:
        index = jnp.concatenate([net.local(net.orders[n], chunks_of[side]) * 3 + n for n, side in halves])
        own_weight = assemble(attn_pieces, index, third)
        qkv_rows = own_weight.shape[0] * 3 // 4
        qkv_weight = own_weight[:qkv_rows]
        proj_own = own_weight[qkv_rows:]
        proj_weight = join(proj_own, net.swap(proj_own, 0))
        ids = jnp.stack([seg_ids, net.swap(seg_ids, 0)])
        attn_both = jnp.concatenate([attn_in, net.swap(attn_in, 0)], axis=0)
        own_query, own_value = part(bias_query[:, None])[0], part(bias_value[:, None])[0]
        qkv_bias = jnp.concatenate([own_query, jnp.zeros_like(own_query), own_value], axis=0)
        attn_both = after(attn_both, *g_fc.got)
        g_fc.finish().start()
        qkv = (times_rows(qkv_weight, attn_both) + qkv_bias).astype(bf16)
        qkv = qkv.reshape(3, -1, 2 * head_dim, 2 * tok_len)
        context_both = attention(qkv, ids, head_dim).reshape(-1, 2 * tok_len)
        context = join(context_both[:, :tok_len], net.swap(context_both[:, tok_len:], 0))
        attn_out = dot(context, proj_weight, 0, 1) + bias_proj
    else:
        arrays = attn_pieces + [net.swap(piece, 0) for piece in attn_pieces]
        places = jnp.concatenate(
            [net.devices(net.orders[n], chunks_of[side], c) * 3 + n for c in range(2) for n, side in halves]
        )
        spread = jnp.concatenate(arrays, axis=1)[0]

        def place(n, whole):
            block = lax.dynamic_slice_in_dim(spread, n * third, third)
            return lax.dynamic_update_slice_in_dim(whole, block, places[n] * third, 0)

        attn_w = lax.fori_loop(0, places.shape[0], place, jnp.zeros_like(spread))
        g_fc.finish().start()
        g_fc.finish().start()
        qkv_weight, proj_weight = attn_w[: 3 * width], attn_w[3 * width :]
        qkv_bias = jnp.concatenate([bias_query, jnp.zeros_like(bias_query), bias_value])
        qkv = (times_rows(qkv_weight, attn_in) + qkv_bias[:, None]).astype(bf16)
        qkv = qkv.reshape(3, -1, 2 * head_dim, tok_len)
        context = attention(qkv, seg_ids[None], head_dim).reshape(-1, tok_len)
        attn_out = dot(context, proj_weight, 0, 1) + bias_proj
    mid = resid + gate_a * attn_out
    normed_m, inverse_m = layer_norm(mid)
    mlp_in = (normed_m * (1.0 + scale_m) + shift_m).astype(bf16)
    if aligned:
        mlp_in = after(mlp_in, *g_fc.got)
        g_fc.finish().start()
    grad_mlp = (gate_m * out_grad[0].astype(f32)).astype(bf16)

    mlp_both = jnp.concatenate([mlp_in, net.swap(mlp_in, 0)], axis=0)
    grad_both = jnp.concatenate([grad_mlp, net.swap(grad_mlp, 0)], axis=0)
    grad_bias_out = jnp.sum(grad_mlp.astype(f32), axis=0, keepdims=True)
    s_fc = Scatter(net)
    sums, columns = [], []
    for n in range(3):
        own, other, column, *sums = mlp_part(
            n, mlp_both, grad_both, bias_pieces, g_fc.value[n], g_fc.got[n], sums
        )
        s_fc.begin(n, own, other)
        columns.append(column)
    out_own, out_other, back_own, back_other = sums
    mlp_back_met = net.swap(back_other, 0)
    out_met = net.swap(after(out_other, mlp_back_met), 0)

    grad_mid, grad_attn, grad_bias_proj, *parts = middle(
        core,
        net.mod * shard if aligned else None,
        back_own,
        mlp_back_met,
        normed_m,
        inverse_m,
        out_grad[0],
        attn_out,
        slot_pick,
        mods[4],
        mods[2],
        proj_weight,
        context,
    )
    s_attn = Scatter(net)
    if aligned:
        mine, other, proj_mine, proj_other = parts
        context_grads = jnp.concatenate([mine, net.swap(other, 0)], axis=1)
        proj_met = net.swap(after(proj_other, context_grads), 0)
        grad_qkv = attention(qkv, ids, head_dim, context_grads.reshape(-1, 2 * head_dim, 2 * tok_len))
        grad_qkv = grad_qkv.reshape(-1, 2 * tok_len)
        grad_qkv = after(grad_qkv, *s_fc.arrived()[:2])
        s_fc.advance((0, 1))
        pieces = weight_grad(grad_qkv, attn_both, proj_mine, proj_met, index, third, 6)
        pieces = lax.optimization_barrier((*pieces, *s_fc.arrived()[2:]))[:6]
        s_fc.advance((2,))
        back_both = contract_rows(grad_qkv, qkv_weight)
        back_own, back_met = back_both[:tok_len], net.swap(back_both[tok_len:], 0)
        column = jnp.sum(grad_qkv.astype(f32), axis=1, keepdims=True).reshape(3, -1, 1)
        none = jnp.zeros_like(column[0])
        grad_bias_query, grad_bias_value = join(column[0], none)[:, 0], join(column[2], none)[:, 0]
    else:
        grad_context, grad_proj = parts
        grad_qkv = attention(
            qkv, seg_ids[None], head_dim, grad_context.reshape(-1, 2 * head_dim, tok_len)
        ).reshape(-1, tok_len)
        s_fc.advance()
        attn_grad = jnp.concatenate([times(grad_qkv, attn_in).astype(bf16), grad_proj], axis=0)

        def take(n, whole):
            block = lax.dynamic_slice_in_dim(attn_grad, places[n] * third, third)
            return lax.dynamic_update_slice_in_dim(whole, block, n * third, 0)

        grads = lax.fori_loop(0, places.shape[0], take, jnp.zeros_like(attn_grad))
        grads = jnp.split(grads[None], 12, axis=1)
        pieces = [summed(a, net.swap(b, 0)) for a, b in zip(grads[:6], grads[6:])]
        back_own = contract_rows(grad_qkv, qkv_weight)
        back_met = jnp.zeros_like(back_own)
        column = jnp.sum(grad_qkv.astype(f32), axis=1).reshape(3, -1)
        grad_bias_query, grad_bias_value = column[0], column[2]
    for n in range(3):
        s_attn.begin(n, pieces[2 * n], pieces[2 * n + 1])
    result, pair_m = end_call(
        mlp_end_kernel,
        bf16,
        slot_count,
        sums[2],
        mlp_back_met,
        out_own,
        out_met,
        bias_out[None],
        normed_m,
        out_grad[0],
        mid,
        slot_pick,
        mods[5],
    )
    grad_tokens, pair_a = end_call(
        attn_end_kernel,
        f32,
        slot_count,
        back_own,
        back_met,
        normed_a,
        inverse_a,
        grad_mid,
        attn_out,
        slot_pick,
        mods[1],
    )
    columns = jnp.concatenate(columns, axis=0).reshape(3, 2, chips // 2, third)
    grad_bias_in = jnp.einsum("nsjd,nsjr->dnr", picks.astype(f32), columns, precision=lax.Precision.HIGHEST)
    grad_bias = stack_rows(
        grad_bias_query[None],
        grad_bias_value[None],
        grad_bias_proj,
        grad_bias_out,
        grad_bias_in.reshape(-1, width),
    )
    bias_rows = lax.all_to_all(
        grad_bias.reshape(device_count, -1), ("dp", "mod"), split_axis=0, concat_axis=0, tiled=True
    )
    bias_sum = jnp.sum(bias_rows, axis=0)

    pair_own = jnp.where(mod_rank == 0, pair_a, pair_m)
    pair_send = jnp.where(mod_rank == 0, pair_m, pair_a)
    grad_mod = summed(pair_own, net.swap(pair_send, "mod"))
    grad_silu = times_rows(grad_mod, ada_weight)
    silu_own = jnp.where(mod_rank == 0, grad_silu[:crop_count], grad_silu[crop_count:])
    silu_send = jnp.where(mod_rank == 0, grad_silu[crop_count:], grad_silu[:crop_count])
    grad_silu = silu_own + net.swap(silu_send.astype(bf16), "mod").astype(f32)
    own_cond = lax.dynamic_slice_in_dim(cond, mod_rank * crop_count, crop_count, 0).astype(f32)
    silu_back = jax.vjp(jax.nn.silu, own_cond)[1]
    grad_cond = silu_back(grad_silu)[0]
    mod_rows = grad_mod
    for dim in ada_order:
        mod_rows = jnp.concatenate([mod_rows, net.swap(mod_rows, dim)], axis=0)
    ada_w_sum = contract_rows(cond_cols, mod_rows)
    ada_b_sum = jnp.sum(mod_rows.astype(f32), axis=0).reshape(ada_bias.shape[0], width)
    ada_b_sum = lax.dynamic_slice_in_dim(ada_b_sum, net.dp_rank * own_cols, own_cols, 1)

    fc_sum = s_fc.rest()
    attn_sum = s_attn.rest()[0]
    return (
        result[None],
        grad_tokens[None],
        grad_cond,
        ada_w_sum,
        ada_b_sum,
        attn_sum,
        fc_sum[0],
        fc_sum[1],
        bias_sum,
    )


def solution(mesh):
    placed = (
        P(("dp", "mod"), None, None),
        P("dp", None),
        P(("dp", "mod"), None),
        P("dp", None),
        P(None, "mod"),
        P("mod", None),
        P(("dp", "mod"), None),
        P(("dp", "mod"), None),
        P(("dp", "mod"), None),
        P(("dp", "mod")),
        P(("dp", "mod"), None, None),
    )
    return jax.shard_map(
        on_device,
        mesh=mesh,
        in_specs=placed,
        out_specs=(
            P(("dp", "mod"), None, None),
            P(("dp", "mod"), None, None),
            P(("dp", "mod"), None),
            P("dp", "mod"),
            P("mod", "dp"),
            P(("dp", "mod"), None),
            P(("dp", "mod"), None),
            P(("dp", "mod"), None),
            P(("dp", "mod")),
        ),
        check_vma=False,
    )
```

```python
import functools

import jax
import jax.numpy as jnp
import numpy as np
from jax import lax
from jax.experimental import pallas as pl
from jax.experimental.pallas import tpu as pltpu
from jax.sharding import PartitionSpec as P

HEADS = 16
norm_eps = 1e-06
bf16 = jnp.bfloat16
f32 = jnp.float32
MIB = 1024 * 1024


def layer_norm(values):
    center = values - jnp.mean(values, axis=-1, keepdims=True)
    inverse = lax.rsqrt(jnp.mean(center * center, axis=-1, keepdims=True) + norm_eps)
    return (center * inverse, inverse)


def norm_back(grad_in, normed, inverse):
    centered = grad_in - jnp.mean(grad_in, axis=-1, keepdims=True)
    return (centered - normed * jnp.mean(grad_in * normed, axis=-1, keepdims=True)) * inverse


def dot(left, right, left_dim, right_dim):
    return lax.dot_general(left, right, (((left_dim,), (right_dim,)), ((), ())), preferred_element_type=f32)


def times(left, right):
    return dot(left, right, 1, 0)


def times_rows(left, right):
    return dot(left, right, 1, 1)


def contract_rows(left, right):
    return dot(left, right, 0, 0)


def after(value, *others):
    return lax.optimization_barrier((value, *others))[0]


def summed(left, right):
    return (left.astype(f32) + right.astype(f32)).astype(bf16)


class Net:
    def __init__(self):
        self.dp = lax.axis_size("dp")
        self.mod = lax.axis_size("mod")
        self.bits = self.dp.bit_length() - 1
        self.dp_rank = lax.axis_index("dp")
        self.mod_rank = lax.axis_index("mod")
        self.core = self.dp_rank & 1
        self.chips = self.dp // 2 * self.mod
        self.lead = list(range(self.bits - 1, 2, -1))
        last = ["mod", 1, 2]
        self.turns = [last[n:] + last[:n] for n in range(3)]
        self.orders = [self.lead + turn for turn in self.turns]

    def swap(self, value, dim):
        if dim == "mod":
            return lax.ppermute(value, "mod", [(i, i ^ 1) for i in range(self.mod)])
        return lax.ppermute(value, "dp", [(i, i ^ (1 << dim)) for i in range(self.dp)])

    def ranks(self, order, chunks, core=0):
        masks = []
        for j in chunks:
            dp_mask, mod_mask = core, 0
            for step, dim in enumerate(order):
                if j >> step & 1:
                    if dim == "mod":
                        mod_mask ^= 1
                    else:
                        dp_mask ^= 1 << dim
            masks.append((dp_mask, mod_mask))
        masks = np.array(masks, np.int32)
        return self.dp_rank ^ masks[:, 0], self.mod_rank ^ masks[:, 1]

    def devices(self, order, chunks, core=0):
        dp, mod = self.ranks(order, chunks, core)
        return dp * self.mod + mod

    def local(self, order, chunks):
        dp, mod = self.ranks(order, chunks)
        return (dp >> 1) * self.mod + mod


class Gather:
    def __init__(self, net, shard):
        self.net, self.count = net, len(net.lead)
        self.third = shard.shape[1] // 3
        self.value, self.got, self.phase = shard, None, 0

    def start(self, *others):
        net, phase = self.net, self.phase
        if phase < self.count:
            self.value = after(self.value, *others) if others else self.value
            self.got = [net.swap(self.value, net.lead[phase])]
        else:
            if phase == self.count:
                kinds, _, width = self.value.shape
                whole = self.value.reshape(kinds, -1, 3, self.third, width)
                self.value = [whole[:, :, n].reshape(kinds, -1, width) for n in range(3)]
            if others:
                self.value = list(lax.optimization_barrier((*self.value, *others))[:3])
            step = phase - self.count
            self.got = [net.swap(self.value[n], net.turns[n][step]) for n in range(3)]
        self.phase += 1
        return self

    def finish(self):
        if self.phase <= self.count:
            self.value = jnp.concatenate([self.value, self.got[0]], axis=1)
        elif self.phase < self.count + 3:
            self.value = [jnp.concatenate(pair, axis=1) for pair in zip(self.value, self.got)]
        return self


class Scatter:
    def __init__(self, net):
        self.net = net
        self.own, self.got, self.step = [None] * 3, [None] * 3, [2] * 3
        self.whole = None

    def begin(self, n, own, other):
        self.own[n] = own
        self.got[n] = self.net.swap(other, self.net.turns[n][2])

    def arrived(self):
        return [got for got in self.got if got is not None]

    def hold(self, *others):
        self.own = [after(own, *others) for own in self.own]

    def advance(self, which=(0, 1, 2)):
        net = self.net
        if self.whole is None:
            for n in which:
                own, got = self.own[n], self.got[n]
                if got is None:
                    continue
                self.step[n] -= 1
                if self.step[n] >= 0:
                    half = own.shape[1] // 2
                    other = summed(own[:, half:], got[:, half:])
                    self.own[n] = summed(own[:, :half], got[:, :half])
                    self.got[n] = net.swap(other, net.turns[n][self.step[n]])
                else:
                    self.own[n], self.got[n] = summed(own, got), None
            if self.arrived():
                return self
            kinds, _, width = self.own[0].shape
            count = 1 << len(net.lead)
            whole = jnp.concatenate([own.reshape(kinds, count, -1, width) for own in self.own], axis=2)
            self.whole, self.left = whole.reshape(kinds, -1, width), len(net.lead)
        else:
            total = self.whole.astype(f32) + self.got[0].astype(f32)
            if self.left == 0:
                self.total, self.got = total, []
                return self
            self.whole = total.astype(bf16)
        half = self.whole.shape[1] // 2
        self.left -= 1
        self.got = [net.swap(self.whole[:, half:], net.lead[self.left])]
        self.whole = self.whole[:, :half]
        return self

    def rest(self):
        while self.got:
            self.advance()
        return self.total


any_spec = pl.BlockSpec(memory_space=pl.ANY)
vmem_spec = pl.BlockSpec(memory_space=pltpu.VMEM)
tiny = pl.CostEstimate(flops=1024, bytes_accessed=1024, transcendentals=0)


def run_copies(copies):
    for copy in copies:
        copy.start()
    for copy in copies:
        copy.wait()


def assemble_kernel(rows, each, index_ref, *refs):
    pieces, out_ref, hold, sems, last = refs[:-4], *refs[-4:]
    copies = []
    for n, piece in enumerate(pieces):
        for j in range(each):
            at = pl.multiple_of(index_ref[n * each + j] * rows, rows)
            copies.append(
                pltpu.make_async_copy(
                    piece.at[0, pl.ds(j * rows, rows)], hold.at[pl.ds(at, rows)], sems.at[n * each + j]
                )
            )
    run_copies(copies)
    run_copies([pltpu.make_async_copy(hold, out_ref, last)])


def assemble(pieces, index, rows):
    each, width = pieces[0].shape[1] // rows, pieces[0].shape[2]
    total = len(pieces) * each
    return pl.pallas_call(
        functools.partial(assemble_kernel, rows, each),
        grid_spec=pltpu.PrefetchScalarGridSpec(
            num_scalar_prefetch=1,
            grid=(1,),
            in_specs=[any_spec] * len(pieces),
            out_specs=any_spec,
            scratch_shapes=[
                pltpu.VMEM((total * rows, width), bf16),
                pltpu.SemaphoreType.DMA((total,)),
                pltpu.SemaphoreType.DMA,
            ],
        ),
        out_shape=jax.ShapeDtypeStruct((total * rows, width), bf16),
        compiler_params=pltpu.CompilerParams(vmem_limit_bytes=10 * MIB),
        name="assemble",
    )(index, *pieces)


def weight_grad_kernel(rows, each, index_ref, grad_ref, x_ref, mine_ref, other_ref, *refs):
    outs, hold, sems = refs[:-2], *refs[-2:]
    top = grad_ref.shape[0]
    step = top // 3
    for n in range(3):
        here = slice(n * step, (n + 1) * step)
        hold[here] = dot(grad_ref[here], x_ref[...], 1, 0).astype(bf16)
    hold[top:] = summed(mine_ref[...], other_ref[...])
    copies = []
    for n, out in enumerate(outs):
        for j in range(each):
            at = pl.multiple_of(index_ref[n * each + j] * rows, rows)
            copies.append(
                pltpu.make_async_copy(
                    hold.at[pl.ds(at, rows)], out.at[0, pl.ds(j * rows, rows)], sems.at[n * each + j]
                )
            )
    run_copies(copies)


def weight_grad(grad, x, mine, other, index, rows, count):
    total, width = grad.shape[0] + mine.shape[0], x.shape[1]
    each = total // rows // count
    return pl.pallas_call(
        functools.partial(weight_grad_kernel, rows, each),
        grid_spec=pltpu.PrefetchScalarGridSpec(
            num_scalar_prefetch=1,
            grid=(1,),
            in_specs=[vmem_spec] * 4,
            out_specs=[any_spec] * count,
            scratch_shapes=[pltpu.VMEM((total, width), bf16), pltpu.SemaphoreType.DMA((each * count,))],
        ),
        out_shape=[jax.ShapeDtypeStruct((1, each * rows, width), bf16)] * count,
        cost_estimate=tiny,
        compiler_params=pltpu.CompilerParams(vmem_limit_bytes=32 * MIB),
        name="weight_grad",
    )(index, grad, x, mine, other)


def by_core(core_ref, group, whole):
    if group is None:
        return [whole]
    picked = []
    for c in range(2):
        rows = []
        for at in range(0, whole.shape[0], 2 * group):
            first, second = whole[at : at + group], whole[at + group : at + 2 * group]
            rows.append(jnp.where(core_ref[0] == c, first, second))
        picked.append(jnp.concatenate(rows, axis=0))
    return picked


def token_block(pick, mods, n):
    width = mods.shape[1] // 6
    return dot(pick[...], mods[:, n * width : (n + 1) * width], 1, 0)


def middle_kernel(group, core_ref, *refs):
    back_a, back_b, mid, grad_out, pick, mods, weight, context = refs[:8]
    mid_ref, attn_ref, column_ref = refs[8:11]
    normed, inverse = layer_norm(mid[...])
    back = (back_a[...] + back_b[...]) * (1.0 + token_block(pick, mods, 4))
    grad_mid = grad_out[...].astype(f32) + norm_back(back, normed, inverse)
    mid_ref[...] = grad_mid
    grad_attn = (token_block(pick, mods, 2) * grad_mid).astype(bf16)
    attn_ref[...] = grad_attn
    column_ref[...] = jnp.sum(grad_attn.astype(f32), axis=0, keepdims=True)
    parts = by_core(core_ref, group, dot(weight[...], grad_attn, 0, 1))
    parts += by_core(core_ref, group, dot(grad_attn, context[...], 0, 1))
    for ref, value in zip(refs[11:], parts):
        ref[...] = value.astype(bf16)


def middle(core, group, *args):
    tokens, width = args[0].shape
    if group is None:
        sizes = [(width, tokens), (width, width)]
    else:
        sizes = [(width // 2, tokens)] * 2 + [(width // 2, width)] * 2
    return pl.pallas_call(
        functools.partial(middle_kernel, group),
        in_specs=[pl.BlockSpec(memory_space=pltpu.SMEM)] + [vmem_spec] * len(args),
        out_specs=[vmem_spec] * (3 + len(sizes)),
        out_shape=[
            jax.ShapeDtypeStruct((tokens, width), f32),
            jax.ShapeDtypeStruct((tokens, width), bf16),
            jax.ShapeDtypeStruct((1, width), f32),
        ]
        + [jax.ShapeDtypeStruct(size, bf16) for size in sizes],
        cost_estimate=tiny,
        compiler_params=pltpu.CompilerParams(vmem_limit_bytes=40 * MIB),
        name="middle",
    )(core.reshape(1), *args)


def slot_sums(pick, blocks, out_ref):
    for n, block in enumerate(blocks):
        high = block.astype(bf16)
        low = (block - high.astype(f32)).astype(bf16)
        total = dot(pick, high, 0, 0) + dot(pick, low, 0, 0)
        out_ref[:, n * block.shape[1] : (n + 1) * block.shape[1]] = total.astype(bf16)


def mlp_end_kernel(*refs):
    back_a, back_b, out_a, out_b, bias, grad_out, mid, pick, mods = refs[:9]
    result_ref, pair_ref = refs[9:]
    mlp_out = out_a[...] + out_b[...] + bias[...]
    result_ref[...] = (mid[...] + token_block(pick, mods, 5) * mlp_out).astype(bf16)
    back = back_a[...] + back_b[...]
    slot_sums(pick[...], (back, back * layer_norm(mid[...])[0], grad_out[...].astype(f32) * mlp_out), pair_ref)


def attn_end_kernel(*refs):
    back_a, back_b, resid, grad_mid, attn_out, pick, mods = refs[:7]
    tokens_ref, pair_ref = refs[7:]
    back = back_a[...] + back_b[...]
    normed, inverse = layer_norm(resid[...].astype(f32))
    slope = back * (1.0 + token_block(pick, mods, 1))
    tokens_ref[...] = grad_mid[...] + norm_back(slope, normed, inverse)
    slot_sums(pick[...], (back, back * normed, grad_mid[...] * attn_out[...]), pair_ref)


def end_call(kernel, dtype, slots, *args):
    tokens, width = args[0].shape
    return pl.pallas_call(
        kernel,
        in_specs=[vmem_spec] * len(args),
        out_specs=[vmem_spec] * 2,
        out_shape=[
            jax.ShapeDtypeStruct((tokens, width), dtype),
            jax.ShapeDtypeStruct((slots, 3 * width), bf16),
        ],
        cost_estimate=tiny,
        compiler_params=pltpu.CompilerParams(vmem_limit_bytes=32 * MIB),
        name=kernel.__name__,
    )(*args)


def rows_kernel(*refs):
    at = 0
    for ref in refs[:-1]:
        refs[-1][at : at + ref.shape[0]] = ref[...]
        at += ref.shape[0]


def stack_rows(*args):
    count = sum(a.shape[0] for a in args)
    return pl.pallas_call(
        rows_kernel,
        in_specs=[vmem_spec] * len(args),
        out_specs=vmem_spec,
        out_shape=jax.ShapeDtypeStruct((count, args[0].shape[1]), f32),
        cost_estimate=tiny,
        name="stack_rows",
    )(*args)


def softmax_t(key, query, same, scale):
    scores = jnp.where(same, dot(key, query, 0, 0) * scale, -1e30)
    weights = jnp.exp(scores - jnp.max(scores, axis=0, keepdims=True))
    return weights * (1.0 / jnp.sum(weights, axis=0, keepdims=True))


def heads_of(block, dim, cols):
    wide = block[:, cols].astype(f32)
    return [wide[n * dim : (n + 1) * dim].astype(bf16) for n in range(wide.shape[0] // dim)]


def attn_forward(dim, scale, row_ref, col_ref, q_ref, k_ref, v_ref, out_ref):
    length = col_ref.shape[0]
    for s in range(row_ref.shape[0]):
        cols = slice(s * length, (s + 1) * length)
        same = row_ref[s : s + 1] == col_ref[:, s : s + 1]
        outs = []
        for q, k, v in zip(*[heads_of(r[0, 0], dim, cols) for r in (q_ref, k_ref, v_ref)]):
            probs = softmax_t(k, q, same, scale).astype(bf16)
            outs.append(dot(v, probs, 1, 0))
        out_ref[0, :, cols] = jnp.concatenate(outs, axis=0).astype(bf16)


def attn_backward(dim, scale, row_ref, col_ref, q_ref, k_ref, v_ref, g_ref, out_ref):
    length = col_ref.shape[0]
    for s in range(row_ref.shape[0]):
        cols = slice(s * length, (s + 1) * length)
        same = row_ref[s : s + 1] == col_ref[:, s : s + 1]
        gq, gk, gv = [], [], []
        qs, ks, vs = [heads_of(r[0, 0], dim, cols) for r in (q_ref, k_ref, v_ref)]
        for q, k, v, g in zip(qs, ks, vs, heads_of(g_ref[0], dim, cols)):
            probs = softmax_t(k, q, same, scale)
            back = dot(v, g, 0, 0)
            back = probs * (back - jnp.sum(back * probs, axis=0, keepdims=True))
            back = back.astype(bf16)
            gq.append(dot(k, back, 1, 0) * scale)
            gk.append(dot(q, back, 1, 1) * scale)
            gv.append(dot(g, probs.astype(bf16), 1, 1))
        for n, parts in enumerate((gq, gk, gv)):
            out_ref[n, 0, :, cols] = jnp.concatenate(parts, axis=0).astype(bf16)


def attention(qkv, ids, dim, grad=None):
    _, groups, rows, tokens = qkv.shape
    scale = dim**-0.5
    ids_t = ids.T

    def one(n):
        return pl.BlockSpec((1, 1, rows, tokens), lambda i: (n, i, 0, 0))

    flat = pl.BlockSpec((1, rows, tokens), lambda i: (i, 0, 0))
    args = [ids, ids_t, qkv, qkv, qkv]
    specs = [pl.BlockSpec(a.shape, lambda i: (0, 0)) for a in (ids, ids_t)] + [one(0), one(1), one(2)]
    if grad is None:
        return pl.pallas_call(
            functools.partial(attn_forward, dim, scale),
            grid=(groups,),
            in_specs=specs,
            out_specs=flat,
            out_shape=jax.ShapeDtypeStruct((groups, rows, tokens), bf16),
            cost_estimate=tiny,
            compiler_params=pltpu.CompilerParams(vmem_limit_bytes=24 * MIB),
            name="attention",
        )(*args)
    return pl.pallas_call(
        functools.partial(attn_backward, dim, scale),
        grid=(groups,),
        in_specs=specs + [flat],
        out_specs=pl.BlockSpec((3, 1, rows, tokens), lambda i: (0, i, 0, 0)),
        out_shape=jax.ShapeDtypeStruct(qkv.shape, bf16),
        cost_estimate=tiny,
        compiler_params=pltpu.CompilerParams(vmem_limit_bytes=24 * MIB),
        name="attention_back",
    )(*args, grad)


def mlp_kernel(number, first, x_ref, g_ref, b_ref, *refs):
    if first:
        pieces, sums, before = refs[:2], refs[-4:], [None] * 4
    else:
        pieces, before, sums = refs[:2], refs[2:6], refs[-4:]
    grads, columns = refs[-7:-5], refs[-5]
    x, g = x_ref[...], g_ref[...]
    half = x.shape[0] // 2
    out_sum, back_sum = 0.0, 0.0
    root = 0.7978845608028654
    for n, piece in enumerate(pieces):
        w_in, w_out = piece[0], piece[1]
        hidden = dot(x, w_in, 1, 1) + b_ref[2 * number + n : 2 * number + n + 1]
        square = hidden * hidden
        tanh = jnp.tanh(root * hidden * (1.0 + 0.044715 * square))
        act = (0.5 * hidden * (1.0 + tanh)).astype(bf16)
        slope = 0.5 * (1.0 + tanh) + 0.5 * hidden * (1.0 - tanh * tanh) * (root * (1.0 + 0.134145 * square))
        back = dot(g, w_out, 1, 1) * slope
        back = back.astype(bf16)
        grads[n][1] = dot(act, g, 0, 0).astype(bf16)
        grads[n][0] = dot(back, x, 0, 0).astype(bf16)
        columns[n : n + 1] = jnp.sum(back.astype(f32), axis=0, keepdims=True)
        out_sum = out_sum + dot(act, w_out, 1, 0)
        back_sum = back_sum + dot(back, w_in, 1, 0)
    for ref, prior, value in zip(
        sums, before, (out_sum[:half], out_sum[half:], back_sum[:half], back_sum[half:])
    ):
        ref[...] = value if prior is None else value + prior[...]


def mlp_part(number, x, g, bias, own, other, before):
    tokens, width = x.shape
    units = own.shape[1]
    sums = [jax.ShapeDtypeStruct((tokens // 2, width), f32)] * 4
    outs = [jax.ShapeDtypeStruct(own.shape, bf16)] * 2 + [jax.ShapeDtypeStruct((2, units), f32)] + sums
    args = [x, g, bias, own, other, *before]
    return pl.pallas_call(
        functools.partial(mlp_kernel, number, not before),
        in_specs=[vmem_spec] * len(args),
        out_specs=[vmem_spec] * len(outs),
        out_shape=outs,
        cost_estimate=tiny,
        compiler_params=pltpu.CompilerParams(vmem_limit_bytes=48 * MIB),
        name="mlp_part",
    )(*args)


def on_device(
    tokens,
    cond,
    segment_ids,
    crop_slot,
    ada_weight,
    ada_bias,
    attn_weight,
    fc_in,
    fc_out,
    biases,
    out_grad,
):
    net = Net()
    tok_len, width = tokens.shape[1:]
    head_dim = width // HEADS
    mod_rank, core, chips = net.mod_rank, net.core, net.chips
    device_count = net.dp * net.mod
    crop_count = crop_slot.shape[1] // net.mod
    shard = attn_weight.shape[0]
    third = shard // 3
    chunks_of = [range(chips // 2), range(chips // 2, chips)]
    halves = [(n, side) for n in range(3) for side in range(2)]
    aligned = shard % (2 * head_dim) == 0 and third % 16 == 0 and width % (2 * net.mod * shard) == 0

    g_attn = Gather(net, attn_weight[None])
    g_fc = Gather(net, jnp.stack([fc_in, fc_out]))
    for n in range(g_attn.count):
        g_attn.start().finish()
    g_attn.start()
    first = g_attn.value
    for n in range(g_fc.count):
        g_fc.start(*first).finish()
    g_attn.finish().start()
    second = g_attn.value
    g_attn.finish().start()
    third_phase = g_attn.value
    g_fc.start(*g_attn.got)
    attn_pieces = [(g_attn.value, g_attn.got)[side][n] for n, side in halves]

    silu_cond = jax.nn.silu(after(cond, *first).astype(f32)).astype(bf16)
    mod_part = times(silu_cond, ada_weight) + ada_bias.reshape(-1).astype(f32)
    mod_own = mod_part.astype(bf16)
    mod_other = net.swap(mod_own, "mod")
    modulation = jnp.concatenate(
        [jnp.where(mod_rank == 0, mod_own, mod_other), jnp.where(mod_rank == 0, mod_other, mod_own)], axis=1
    )
    seg_ids = segment_ids[0]
    slots = lax.dynamic_slice_in_dim(crop_slot[0], mod_rank * crop_count, crop_count)
    crop_onehot = seg_ids[:, None] == jnp.arange(crop_count, dtype=jnp.int32)[None, :]
    token_slot = jnp.sum(jnp.where(crop_onehot, slots[None, :], 0), axis=1)
    slot_pick = token_slot[:, None] == jnp.arange(cond.shape[0], dtype=jnp.int32)[None, :]
    slot_pick = slot_pick.astype(bf16)
    mods = [modulation[:, n * width : (n + 1) * width] for n in range(6)]
    shift_a, scale_a, gate_a, shift_m, scale_m, gate_m = [times(slot_pick, block) for block in mods]

    slot_count, own_cols = cond.shape[0], width // net.dp
    to_dp = jnp.moveaxis(silu_cond.reshape(slot_count, net.dp, own_cols), 1, 0).reshape(net.dp, 1, -1)
    to_all = jnp.broadcast_to(to_dp, (net.dp, net.mod, slot_count * own_cols)).reshape(device_count, -1)
    to_all = after(to_all, *second)
    sent = jnp.concatenate([jnp.broadcast_to(biases[None], (device_count, biases.shape[0])), to_all], axis=1)
    met = lax.all_to_all(sent, ("dp", "mod"), split_axis=0, concat_axis=0, tiled=True)
    met = after(met, *third_phase)
    ada_order = list(range(1, net.bits)) + [0]
    dp_order = net.ranks(ada_order, range(net.dp))[0]
    dp_pick = (dp_order[:, None] == jnp.arange(net.dp)[None, :]).astype(bf16)
    cond_cols = times(dp_pick, met.reshape(net.dp, net.mod, -1)[:, 0, biases.shape[0] :]).astype(bf16)
    cond_cols = cond_cols.reshape(-1, own_cols)
    bias_all = met[:, : biases.shape[0]].reshape(-1, width)
    bias_query, bias_value, bias_proj, bias_out = [bias_all[n].astype(f32) for n in range(4)]
    bias_in = bias_all[4:].reshape(device_count, 3, third)
    picks = []
    for n, side in halves:
        devices = net.devices(net.orders[n], chunks_of[side])
        picks.append((devices[:, None] == jnp.arange(device_count)[None, :]).astype(bf16))
    picks = jnp.stack(picks).reshape(3, 2, chips // 2, device_count)
    bias_pieces = jnp.einsum("nsjd,dnr->nsjr", picks, bias_in, preferred_element_type=f32).reshape(6, -1)

    def join(own, other):
        own, other = [a.reshape(-1, 1, net.mod * shard, a.shape[-1]) for a in (own, other)]
        both = jnp.where(core == 0, jnp.concatenate([own, other], 1), jnp.concatenate([other, own], 1))
        return both.reshape(-1, both.shape[-1])

    def part(whole):
        whole = whole.reshape(-1, 2, net.mod * shard, whole.shape[-1])
        return [
            jnp.where(core == c, whole[:, 0], whole[:, 1]).reshape(-1, whole.shape[-1]) for c in range(2)
        ]

    resid = tokens[0].astype(f32)
    normed_a, _ = layer_norm(resid)
    attn_in = (normed_a * (1.0 + scale_a) + shift_a).astype(bf16)
    if aligned:
        index = jnp.concatenate([net.local(net.orders[n], chunks_of[side]) * 3 + n for n, side in halves])
        own_weight = assemble(attn_pieces, index, third)
        qkv_rows = own_weight.shape[0] * 3 // 4
        qkv_weight = own_weight[:qkv_rows]
        proj_own = own_weight[qkv_rows:]
        proj_weight = join(proj_own, net.swap(proj_own, 0))
        ids = jnp.stack([seg_ids, net.swap(seg_ids, 0)])
        attn_both = jnp.concatenate([attn_in, net.swap(attn_in, 0)], axis=0)
        own_query, own_value = part(bias_query[:, None])[0], part(bias_value[:, None])[0]
        qkv_bias = jnp.concatenate([own_query, jnp.zeros_like(own_query), own_value], axis=0)
        attn_both = after(attn_both, *g_fc.got)
        g_fc.finish().start()
        qkv = (times_rows(qkv_weight, attn_both) + qkv_bias).astype(bf16)
        qkv = qkv.reshape(3, -1, 2 * head_dim, 2 * tok_len)
        context_both = attention(qkv, ids, head_dim).reshape(-1, 2 * tok_len)
        context = join(context_both[:, :tok_len], net.swap(context_both[:, tok_len:], 0))
        attn_out = dot(context, proj_weight, 0, 1) + bias_proj
    else:
        arrays = attn_pieces + [net.swap(piece, 0) for piece in attn_pieces]
        places = jnp.concatenate(
            [net.devices(net.orders[n], chunks_of[side], c) * 3 + n for c in range(2) for n, side in halves]
        )
        spread = jnp.concatenate(arrays, axis=1)[0]

        def place(n, whole):
            block = lax.dynamic_slice_in_dim(spread, n * third, third)
            return lax.dynamic_update_slice_in_dim(whole, block, places[n] * third, 0)

        attn_w = lax.fori_loop(0, places.shape[0], place, jnp.zeros_like(spread))
        g_fc.finish().start()
        g_fc.finish().start()
        qkv_weight, proj_weight = attn_w[: 3 * width], attn_w[3 * width :]
        qkv_bias = jnp.concatenate([bias_query, jnp.zeros_like(bias_query), bias_value])
        qkv = (times_rows(qkv_weight, attn_in) + qkv_bias[:, None]).astype(bf16)
        qkv = qkv.reshape(3, -1, 2 * head_dim, tok_len)
        context = attention(qkv, seg_ids[None], head_dim).reshape(-1, tok_len)
        attn_out = dot(context, proj_weight, 0, 1) + bias_proj
    mid = resid + gate_a * attn_out
    normed_m, _ = layer_norm(mid)
    mlp_in = (normed_m * (1.0 + scale_m) + shift_m).astype(bf16)
    if aligned:
        mlp_in = after(mlp_in, *g_fc.got)
        g_fc.finish().start()
    grad_mlp = (gate_m * out_grad[0].astype(f32)).astype(bf16)

    mlp_both = jnp.concatenate([mlp_in, net.swap(mlp_in, 0)], axis=0)
    grad_both = jnp.concatenate([grad_mlp, net.swap(grad_mlp, 0)], axis=0)
    grad_bias_out = jnp.sum(grad_mlp.astype(f32), axis=0, keepdims=True)
    s_fc = Scatter(net)
    sums, columns = [], []
    for n in range(3):
        own, other, column, *sums = mlp_part(
            n, mlp_both, grad_both, bias_pieces, g_fc.value[n], g_fc.got[n], sums
        )
        s_fc.begin(n, own, other)
        columns.append(column)
    out_own, out_other, back_own, back_other = sums
    mlp_back_met = net.swap(back_other, 0)
    mlp_back_met = after(mlp_back_met, s_fc.got[0])
    s_fc.advance((0,))
    out_met = net.swap(after(out_other, mlp_back_met), 0)

    grad_mid, grad_attn, grad_bias_proj, *parts = middle(
        core,
        net.mod * shard if aligned else None,
        back_own,
        mlp_back_met,
        mid,
        out_grad[0],
        slot_pick,
        modulation,
        proj_weight,
        context,
    )
    s_attn = Scatter(net)
    if aligned:
        mine, other, proj_mine, proj_other = parts
        other_met = after(net.swap(other, 0), s_fc.got[1])
        s_fc.advance((1,))
        context_grads = jnp.concatenate([mine, other_met], axis=1)
        proj_met = net.swap(after(proj_other, context_grads), 0)
        grad_qkv = attention(qkv, ids, head_dim, context_grads.reshape(-1, 2 * head_dim, 2 * tok_len))
        grad_qkv = grad_qkv.reshape(-1, 2 * tok_len)
        pieces = weight_grad(grad_qkv, attn_both, proj_mine, proj_met, index, third, 6)
        grad_qkv, *pieces = lax.optimization_barrier((grad_qkv, *pieces))
        back_both = contract_rows(grad_qkv, qkv_weight)
        back_own, back_met = back_both[:tok_len], net.swap(back_both[tok_len:], 0)
        s_fc.hold(*pieces)
        back_met = after(back_met, *s_fc.got)
        s_fc.advance()
        out_met = after(out_met, *pieces)
        column = jnp.sum(grad_qkv.astype(f32), axis=1, keepdims=True).reshape(3, -1, 1)
        none = jnp.zeros_like(column[0])
        grad_bias_query, grad_bias_value = join(column[0], none)[:, 0], join(column[2], none)[:, 0]
    else:
        grad_context, grad_proj = parts
        grad_qkv = attention(
            qkv, seg_ids[None], head_dim, grad_context.reshape(-1, 2 * head_dim, tok_len)
        ).reshape(-1, tok_len)
        s_fc.advance()
        attn_grad = jnp.concatenate([times(grad_qkv, attn_in).astype(bf16), grad_proj], axis=0)

        def take(n, whole):
            block = lax.dynamic_slice_in_dim(attn_grad, places[n] * third, third)
            return lax.dynamic_update_slice_in_dim(whole, block, n * third, 0)

        grads = lax.fori_loop(0, places.shape[0], take, jnp.zeros_like(attn_grad))
        grads = jnp.split(grads[None], 12, axis=1)
        pieces = [summed(a, net.swap(b, 0)) for a, b in zip(grads[:6], grads[6:])]
        back_own = contract_rows(grad_qkv, qkv_weight)
        back_met = jnp.zeros_like(back_own)
        column = jnp.sum(grad_qkv.astype(f32), axis=1).reshape(3, -1)
        grad_bias_query, grad_bias_value = column[0], column[2]
    for n in range(3):
        s_attn.begin(n, pieces[2 * n], pieces[2 * n + 1])
    grad_tokens, pair_a = end_call(
        attn_end_kernel, f32, slot_count, back_own, back_met, tokens[0], grad_mid, attn_out, slot_pick, modulation
    )
    result, pair_m = end_call(
        mlp_end_kernel,
        bf16,
        slot_count,
        sums[2],
        mlp_back_met,
        out_own,
        out_met,
        bias_out[None],
        out_grad[0],
        mid,
        slot_pick,
        modulation,
    )
    if aligned:
        pair_a = after(pair_a, *s_attn.got)
        s_attn.advance()
    columns = jnp.concatenate(columns, axis=0).reshape(3, 2, chips // 2, third)
    grad_bias_in = jnp.einsum("nsjd,nsjr->dnr", picks.astype(f32), columns, precision=lax.Precision.HIGHEST)
    grad_bias = stack_rows(
        grad_bias_query[None],
        grad_bias_value[None],
        grad_bias_proj,
        grad_bias_out,
        grad_bias_in.reshape(-1, width),
    )
    bias_rows = lax.all_to_all(
        grad_bias.reshape(device_count, -1), ("dp", "mod"), split_axis=0, concat_axis=0, tiled=True
    )
    bias_sum = jnp.sum(bias_rows, axis=0)

    pair_own = jnp.where(mod_rank == 0, pair_a, pair_m)
    pair_send = jnp.where(mod_rank == 0, pair_m, pair_a)
    grad_mod = summed(pair_own, net.swap(pair_send, "mod"))
    grad_silu = times_rows(grad_mod, ada_weight)
    silu_own = jnp.where(mod_rank == 0, grad_silu[:crop_count], grad_silu[crop_count:])
    silu_send = jnp.where(mod_rank == 0, grad_silu[crop_count:], grad_silu[:crop_count])
    grad_silu = silu_own + net.swap(silu_send.astype(bf16), "mod").astype(f32)
    own_cond = lax.dynamic_slice_in_dim(cond, mod_rank * crop_count, crop_count, 0).astype(f32)
    silu_back = jax.vjp(jax.nn.silu, own_cond)[1]
    grad_cond = silu_back(grad_silu)[0]
    mod_rows = grad_mod
    for dim in ada_order:
        mod_rows = jnp.concatenate([mod_rows, net.swap(mod_rows, dim)], axis=0)
    ada_w_sum = contract_rows(cond_cols, mod_rows)
    ada_b_sum = jnp.sum(mod_rows.astype(f32), axis=0).reshape(ada_bias.shape[0], width)
    ada_b_sum = lax.dynamic_slice_in_dim(ada_b_sum, net.dp_rank * own_cols, own_cols, 1)

    fc_sum = s_fc.rest()
    attn_sum = s_attn.rest()[0]
    return (
        result[None],
        grad_tokens[None],
        grad_cond,
        ada_w_sum,
        ada_b_sum,
        attn_sum,
        fc_sum[0],
        fc_sum[1],
        bias_sum,
    )


def solution(mesh):
    placed = (
        P(("dp", "mod"), None, None),
        P("dp", None),
        P(("dp", "mod"), None),
        P("dp", None),
        P(None, "mod"),
        P("mod", None),
        P(("dp", "mod"), None),
        P(("dp", "mod"), None),
        P(("dp", "mod"), None),
        P(("dp", "mod")),
        P(("dp", "mod"), None, None),
    )
    return jax.shard_map(
        on_device,
        mesh=mesh,
        in_specs=placed,
        out_specs=(
            P(("dp", "mod"), None, None),
            P(("dp", "mod"), None, None),
            P(("dp", "mod"), None),
            P("dp", "mod"),
            P("mod", "dp"),
            P(("dp", "mod"), None),
            P(("dp", "mod"), None),
            P(("dp", "mod"), None),
            P(("dp", "mod")),
        ),
        check_vma=False,
    )
```

```python
import functools

import jax
import jax.numpy as jnp
import numpy as np
from jax import lax
from jax.experimental import pallas as pl
from jax.experimental.pallas import tpu as pltpu
from jax.sharding import PartitionSpec as P

HEADS = 16
norm_eps = 1e-06
bf16 = jnp.bfloat16
f32 = jnp.float32
MIB = 1024 * 1024


def layer_norm(values):
    center = values - jnp.mean(values, axis=-1, keepdims=True)
    inverse = lax.rsqrt(jnp.mean(center * center, axis=-1, keepdims=True) + norm_eps)
    return (center * inverse, inverse)


def norm_back(grad_in, normed, inverse):
    centered = grad_in - jnp.mean(grad_in, axis=-1, keepdims=True)
    return (centered - normed * jnp.mean(grad_in * normed, axis=-1, keepdims=True)) * inverse


def dot(left, right, left_dim, right_dim):
    return lax.dot_general(left, right, (((left_dim,), (right_dim,)), ((), ())), preferred_element_type=f32)


def times(left, right):
    return dot(left, right, 1, 0)


def times_rows(left, right):
    return dot(left, right, 1, 1)


def contract_rows(left, right):
    return dot(left, right, 0, 0)


def after(value, *others):
    return lax.optimization_barrier((value, *others))[0]


def summed(left, right):
    return (left.astype(f32) + right.astype(f32)).astype(bf16)


class Net:
    def __init__(self):
        self.dp = lax.axis_size("dp")
        self.mod = lax.axis_size("mod")
        self.bits = self.dp.bit_length() - 1
        self.dp_rank = lax.axis_index("dp")
        self.mod_rank = lax.axis_index("mod")
        self.core = self.dp_rank & 1
        self.chips = self.dp // 2 * self.mod
        self.lead = list(range(self.bits - 1, 2, -1))
        last = ["mod", 1, 2]
        self.turns = [last[n:] + last[:n] for n in range(3)]
        self.orders = [self.lead + turn for turn in self.turns]

    def swap(self, value, dim):
        if dim == "mod":
            return lax.ppermute(value, "mod", [(i, i ^ 1) for i in range(self.mod)])
        return lax.ppermute(value, "dp", [(i, i ^ (1 << dim)) for i in range(self.dp)])

    def ranks(self, order, chunks, core=0):
        masks = []
        for j in chunks:
            dp_mask, mod_mask = core, 0
            for step, dim in enumerate(order):
                if j >> step & 1:
                    if dim == "mod":
                        mod_mask ^= 1
                    else:
                        dp_mask ^= 1 << dim
            masks.append((dp_mask, mod_mask))
        masks = np.array(masks, np.int32)
        return self.dp_rank ^ masks[:, 0], self.mod_rank ^ masks[:, 1]

    def devices(self, order, chunks, core=0):
        dp, mod = self.ranks(order, chunks, core)
        return dp * self.mod + mod

    def local(self, order, chunks):
        dp, mod = self.ranks(order, chunks)
        return (dp >> 1) * self.mod + mod


class Gather:
    def __init__(self, net, shard):
        self.net, self.count = net, len(net.lead)
        self.third = shard.shape[1] // 3
        self.value, self.got, self.phase = shard, None, 0

    def start(self, *others):
        net, phase = self.net, self.phase
        if phase < self.count:
            self.value = after(self.value, *others) if others else self.value
            self.got = [net.swap(self.value, net.lead[phase])]
        else:
            if phase == self.count:
                kinds, _, width = self.value.shape
                whole = self.value.reshape(kinds, -1, 3, self.third, width)
                self.value = [whole[:, :, n].reshape(kinds, -1, width) for n in range(3)]
            if others:
                self.value = list(lax.optimization_barrier((*self.value, *others))[:3])
            step = phase - self.count
            self.got = [net.swap(self.value[n], net.turns[n][step]) for n in range(3)]
        self.phase += 1
        return self

    def finish(self):
        if self.phase <= self.count:
            self.value = jnp.concatenate([self.value, self.got[0]], axis=1)
        elif self.phase < self.count + 3:
            self.value = [jnp.concatenate(pair, axis=1) for pair in zip(self.value, self.got)]
        return self


class Scatter:
    def __init__(self, net):
        self.net = net
        self.own, self.got, self.step = [None] * 3, [None] * 3, [2] * 3
        self.whole = None

    def begin(self, n, own, other):
        self.own[n] = own
        self.got[n] = self.net.swap(other, self.net.turns[n][2])

    def arrived(self):
        return [got for got in self.got if got is not None]

    def hold(self, *others):
        self.own = [after(own, *others) for own in self.own]

    def advance(self, which=(0, 1, 2)):
        net = self.net
        if self.whole is None:
            for n in which:
                own, got = self.own[n], self.got[n]
                if got is None:
                    continue
                self.step[n] -= 1
                if self.step[n] >= 0:
                    half = own.shape[1] // 2
                    other = summed(own[:, half:], got[:, half:])
                    self.own[n] = summed(own[:, :half], got[:, :half])
                    self.got[n] = net.swap(other, net.turns[n][self.step[n]])
                else:
                    self.own[n], self.got[n] = summed(own, got), None
            if self.arrived():
                return self
            kinds, _, width = self.own[0].shape
            count = 1 << len(net.lead)
            whole = jnp.concatenate([own.reshape(kinds, count, -1, width) for own in self.own], axis=2)
            self.whole, self.left = whole.reshape(kinds, -1, width), len(net.lead)
        else:
            total = self.whole.astype(f32) + self.got[0].astype(f32)
            if self.left == 0:
                self.total, self.got = total, []
                return self
            self.whole = total.astype(bf16)
        half = self.whole.shape[1] // 2
        self.left -= 1
        self.got = [net.swap(self.whole[:, half:], net.lead[self.left])]
        self.whole = self.whole[:, :half]
        return self

    def rest(self):
        while self.got:
            self.advance()
        return self.total


any_spec = pl.BlockSpec(memory_space=pl.ANY)


def full(value):
    return pl.BlockSpec(value.shape, lambda *_: (0,) * len(value.shape))

tiny = pl.CostEstimate(flops=1024, bytes_accessed=1024, transcendentals=0)


def run_copies(copies):
    for copy in copies:
        copy.start()
    for copy in copies:
        copy.wait()


def assemble_kernel(rows, each, index_ref, *refs):
    pieces, out_ref, hold, sems, last = refs[:-4], *refs[-4:]
    copies = []
    for n, piece in enumerate(pieces):
        for j in range(each):
            at = pl.multiple_of(index_ref[n * each + j] * rows, rows)
            copies.append(
                pltpu.make_async_copy(
                    piece.at[0, pl.ds(j * rows, rows)], hold.at[pl.ds(at, rows)], sems.at[n * each + j]
                )
            )
    run_copies(copies)
    run_copies([pltpu.make_async_copy(hold, out_ref, last)])


def assemble(pieces, index, rows):
    each, width = pieces[0].shape[1] // rows, pieces[0].shape[2]
    total = len(pieces) * each
    return pl.pallas_call(
        functools.partial(assemble_kernel, rows, each),
        grid_spec=pltpu.PrefetchScalarGridSpec(
            num_scalar_prefetch=1,
            grid=(1,),
            in_specs=[any_spec] * len(pieces),
            out_specs=any_spec,
            scratch_shapes=[
                pltpu.VMEM((total * rows, width), bf16),
                pltpu.SemaphoreType.DMA((total,)),
                pltpu.SemaphoreType.DMA,
            ],
        ),
        out_shape=jax.ShapeDtypeStruct((total * rows, width), bf16),
        compiler_params=pltpu.CompilerParams(vmem_limit_bytes=10 * MIB),
        name="assemble",
    )(index, *pieces)


def weight_grad_kernel(rows, each, index_ref, grad_ref, x_ref, mine_ref, other_ref, *refs):
    outs, hold, sems = refs[:-2], *refs[-2:]
    top = grad_ref.shape[0]
    step = top // 3
    for n in range(3):
        here = slice(n * step, (n + 1) * step)
        hold[here] = dot(grad_ref[here], x_ref[...], 1, 0).astype(bf16)
    hold[top:] = summed(mine_ref[...], other_ref[...])
    copies = []
    for n, out in enumerate(outs):
        for j in range(each):
            at = pl.multiple_of(index_ref[n * each + j] * rows, rows)
            copies.append(
                pltpu.make_async_copy(
                    hold.at[pl.ds(at, rows)], out.at[0, pl.ds(j * rows, rows)], sems.at[n * each + j]
                )
            )
    run_copies(copies)


def weight_grad(grad, x, mine, other, index, rows, count):
    total, width = grad.shape[0] + mine.shape[0], x.shape[1]
    each = total // rows // count
    return pl.pallas_call(
        functools.partial(weight_grad_kernel, rows, each),
        grid_spec=pltpu.PrefetchScalarGridSpec(
            num_scalar_prefetch=1,
            grid=(1,),
            in_specs=[full(a) for a in (grad, x, mine, other)],
            out_specs=[any_spec] * count,
            scratch_shapes=[pltpu.VMEM((total, width), bf16), pltpu.SemaphoreType.DMA((each * count,))],
        ),
        out_shape=[jax.ShapeDtypeStruct((1, each * rows, width), bf16)] * count,
        cost_estimate=tiny,
        compiler_params=pltpu.CompilerParams(vmem_limit_bytes=32 * MIB),
        name="weight_grad",
    )(index, grad, x, mine, other)


def by_core(core_ref, group, whole):
    if group is None:
        return [whole]
    picked = []
    for c in range(2):
        rows = []
        for at in range(0, whole.shape[0], 2 * group):
            first, second = whole[at : at + group], whole[at + group : at + 2 * group]
            rows.append(jnp.where(core_ref[0] == c, first, second))
        picked.append(jnp.concatenate(rows, axis=0))
    return picked


def token_block(pick, mods, n):
    width = mods.shape[1] // 6
    return dot(pick[...], mods[:, n * width : (n + 1) * width], 1, 0)


def middle_kernel(group, core_ref, *refs):
    sums, met, mid, grad_out, pick, mods, weight, context = refs[:8]
    mid_ref, attn_ref, column_ref = refs[8:11]
    normed, inverse = layer_norm(mid[...])
    back = (sums[1] + met[1]) * (1.0 + token_block(pick, mods, 4))
    grad_mid = grad_out[...].astype(f32) + norm_back(back, normed, inverse)
    mid_ref[...] = grad_mid
    grad_attn = (token_block(pick, mods, 2) * grad_mid).astype(bf16)
    attn_ref[...] = grad_attn
    column_ref[...] = jnp.sum(grad_attn.astype(f32), axis=0, keepdims=True)
    parts = by_core(core_ref, group, dot(weight[...], grad_attn, 0, 1))
    parts += by_core(core_ref, group, dot(grad_attn, context[...], 0, 1))
    for ref, value in zip(refs[11:], parts):
        ref[...] = value.astype(bf16)


def middle(core, group, *args):
    _, tokens, width = args[0].shape
    if group is None:
        sizes = [(width, tokens), (width, width)]
    else:
        sizes = [(width // 2, tokens)] * 2 + [(width // 2, width)] * 2
    outs = [((tokens, width), f32), ((tokens, width), bf16), ((1, width), f32)] + [(s, bf16) for s in sizes]
    outs = [jax.ShapeDtypeStruct(*out) for out in outs]
    return pl.pallas_call(
        functools.partial(middle_kernel, group),
        grid=(1,),
        in_specs=[pl.BlockSpec(memory_space=pltpu.SMEM)] + [full(a) for a in args],
        out_specs=[full(a) for a in outs],
        out_shape=outs,
        cost_estimate=tiny,
        compiler_params=pltpu.CompilerParams(vmem_limit_bytes=40 * MIB),
        name="middle",
    )(core.reshape(1), *args)


def slot_sums(pick, blocks, out_ref):
    for n, block in enumerate(blocks):
        high = block.astype(bf16)
        low = (block - high.astype(f32)).astype(bf16)
        total = dot(pick, high, 0, 0) + dot(pick, low, 0, 0)
        out_ref[:, n * block.shape[1] : (n + 1) * block.shape[1]] = total.astype(bf16)


def mlp_end_kernel(*refs):
    mid, sums, met, bias, grad_out, pick, mods = refs[:7]
    result_ref, pair_ref = refs[7:]
    mlp_out = sums[0] + met[0] + bias[...]
    result_ref[...] = (mid[...] + token_block(pick, mods, 5) * mlp_out).astype(bf16)
    back = sums[1] + met[1]
    slot_sums(pick[...], (back, back * layer_norm(mid[...])[0], grad_out[...].astype(f32) * mlp_out), pair_ref)


def attn_end_kernel(*refs):
    back_a, back_b, resid, grad_mid, attn_out, pick, mods = refs[:7]
    tokens_ref, pair_ref = refs[7:]
    back = back_a[...] + back_b[...]
    normed, inverse = layer_norm(resid[...].astype(f32))
    slope = back * (1.0 + token_block(pick, mods, 1))
    tokens_ref[...] = grad_mid[...] + norm_back(slope, normed, inverse)
    slot_sums(pick[...], (back, back * normed, grad_mid[...] * attn_out[...]), pair_ref)


def end_call(kernel, dtype, slots, *args):
    tokens, width = args[0].shape
    outs = [jax.ShapeDtypeStruct((tokens, width), dtype), jax.ShapeDtypeStruct((slots, 3 * width), bf16)]
    return pl.pallas_call(
        kernel,
        grid=(1,),
        in_specs=[full(a) for a in args],
        out_specs=[full(a) for a in outs],
        out_shape=outs,
        cost_estimate=tiny,
        compiler_params=pltpu.CompilerParams(vmem_limit_bytes=32 * MIB),
        name=kernel.__name__,
    )(*args)


def rows_kernel(*refs):
    at = 0
    for ref in refs[:-1]:
        refs[-1][at : at + ref.shape[0]] = ref[...]
        at += ref.shape[0]


def stack_rows(*args):
    out = jax.ShapeDtypeStruct((sum(a.shape[0] for a in args), args[0].shape[1]), f32)
    return pl.pallas_call(
        rows_kernel,
        grid=(1,),
        in_specs=[full(a) for a in args],
        out_specs=full(out),
        out_shape=out,
        cost_estimate=tiny,
        name="stack_rows",
    )(*args)


def softmax_t(key, query, same, scale):
    scores = jnp.where(same, dot(key, query, 0, 0) * scale, -1e30)
    weights = jnp.exp(scores - jnp.max(scores, axis=0, keepdims=True))
    return weights * (1.0 / jnp.sum(weights, axis=0, keepdims=True))


def heads_of(block, dim, cols):
    wide = block[:, cols].astype(f32)
    return [wide[n * dim : (n + 1) * dim].astype(bf16) for n in range(wide.shape[0] // dim)]


def attn_forward(dim, scale, row_ref, col_ref, q_ref, k_ref, v_ref, out_ref):
    length = col_ref.shape[0]
    for s in range(row_ref.shape[0]):
        cols = slice(s * length, (s + 1) * length)
        same = row_ref[s : s + 1] == col_ref[:, s : s + 1]
        outs = []
        for q, k, v in zip(*[heads_of(r[0, 0], dim, cols) for r in (q_ref, k_ref, v_ref)]):
            probs = softmax_t(k, q, same, scale).astype(bf16)
            outs.append(dot(v, probs, 1, 0))
        out_ref[0, :, cols] = jnp.concatenate(outs, axis=0).astype(bf16)


def attn_backward(dim, scale, row_ref, col_ref, q_ref, k_ref, v_ref, g_ref, out_ref):
    length = col_ref.shape[0]
    for s in range(row_ref.shape[0]):
        cols = slice(s * length, (s + 1) * length)
        same = row_ref[s : s + 1] == col_ref[:, s : s + 1]
        gq, gk, gv = [], [], []
        qs, ks, vs = [heads_of(r[0, 0], dim, cols) for r in (q_ref, k_ref, v_ref)]
        for q, k, v, g in zip(qs, ks, vs, heads_of(g_ref[0], dim, cols)):
            probs = softmax_t(k, q, same, scale)
            back = dot(v, g, 0, 0)
            back = probs * (back - jnp.sum(back * probs, axis=0, keepdims=True))
            back = back.astype(bf16)
            gq.append(dot(k, back, 1, 0) * scale)
            gk.append(dot(q, back, 1, 1) * scale)
            gv.append(dot(g, probs.astype(bf16), 1, 1))
        for n, parts in enumerate((gq, gk, gv)):
            out_ref[n, 0, :, cols] = jnp.concatenate(parts, axis=0).astype(bf16)


def attention(qkv, ids, dim, grad=None):
    _, groups, rows, tokens = qkv.shape
    scale = dim**-0.5
    ids_t = ids.T

    def one(n):
        return pl.BlockSpec((1, 1, rows, tokens), lambda i: (n, i, 0, 0))

    flat = pl.BlockSpec((1, rows, tokens), lambda i: (i, 0, 0))
    args = [ids, ids_t, qkv, qkv, qkv]
    specs = [pl.BlockSpec(a.shape, lambda i: (0, 0)) for a in (ids, ids_t)] + [one(0), one(1), one(2)]
    if grad is None:
        return pl.pallas_call(
            functools.partial(attn_forward, dim, scale),
            grid=(groups,),
            in_specs=specs,
            out_specs=flat,
            out_shape=jax.ShapeDtypeStruct((groups, rows, tokens), bf16),
            cost_estimate=tiny,
            compiler_params=pltpu.CompilerParams(vmem_limit_bytes=24 * MIB),
            name="attention",
        )(*args)
    return pl.pallas_call(
        functools.partial(attn_backward, dim, scale),
        grid=(groups,),
        in_specs=specs + [flat],
        out_specs=pl.BlockSpec((3, 1, rows, tokens), lambda i: (0, i, 0, 0)),
        out_shape=jax.ShapeDtypeStruct(qkv.shape, bf16),
        cost_estimate=tiny,
        compiler_params=pltpu.CompilerParams(vmem_limit_bytes=24 * MIB),
        name="attention_back",
    )(*args, grad)


def mlp_kernel(number, first, *refs):
    own_ref, met_ref, b_ref, *pieces = refs[:5]
    before = () if first else refs[5:7]
    *grads, column_ref, own_sums, other_sums = refs[-13:-8]
    x, g, weights, products, prior, total, ins, outs = refs[-8:]
    half = own_ref.shape[1]
    low, high = pl.ds(0, half), pl.ds(half, half)
    copy = pltpu.make_async_copy
    loads = [
        copy(own_ref.at[0], x.at[low], ins.at[0]),
        copy(met_ref.at[0], x.at[high], ins.at[1]),
        copy(pieces[0], weights.at[0], ins.at[2]),
        copy(own_ref.at[1], g.at[low], ins.at[3]),
        copy(met_ref.at[1], g.at[high], ins.at[4]),
        copy(pieces[1], weights.at[1], ins.at[5]),
    ]
    loads += [copy(ref, prior.at[n], ins.at[6 + n]) for n, ref in enumerate(before)]
    for load in loads:
        load.start()
    stores = []
    root = 0.7978845608028654
    for n in range(2):
        for load in loads[:3] if n == 0 else loads[5:6]:
            load.wait()
        w_in, w_out = weights[n, 0], weights[n, 1]
        hidden = dot(x[...], w_in, 1, 1) + b_ref[2 * number + n : 2 * number + n + 1]
        square = hidden * hidden
        tanh = jnp.tanh(root * hidden * (1.0 + 0.044715 * square))
        act = (0.5 * hidden * (1.0 + tanh)).astype(bf16)
        slope = 0.5 * (1.0 + tanh) + 0.5 * hidden * (1.0 - tanh * tanh) * (root * (1.0 + 0.134145 * square))
        if n == 0:
            for load in loads[3:5]:
                load.wait()
        back = (dot(g[...], w_out, 1, 1) * slope).astype(bf16)
        products[n, 1] = dot(act, g[...], 0, 0).astype(bf16)
        products[n, 0] = dot(back, x[...], 0, 0).astype(bf16)
        stores.append(copy(products.at[n], grads[n], outs.at[n]))
        stores[-1].start()
        column_ref[n : n + 1] = jnp.sum(back.astype(f32), axis=0, keepdims=True)
        for m, value in enumerate((dot(act, w_out, 1, 0), dot(back, w_in, 1, 0))):
            for k in range(2):
                rows = value[k * half : (k + 1) * half]
                total[k, m] = rows if n == 0 else total[k, m] + rows
    for load in loads[6:]:
        load.wait()
    for k, ref in enumerate((own_sums, other_sums)):
        if before:
            total[k] = total[k] + prior[k]
        stores.append(copy(total.at[k], ref, outs.at[2 + k]))
        stores[-1].start()
    for store in stores:
        store.wait()


def mlp_part(number, own_in, met_in, bias, own, other, before):
    _, tokens, width = own_in.shape
    units = own.shape[1]
    column = jax.ShapeDtypeStruct((2, units), f32)
    sums = [jax.ShapeDtypeStruct((2, tokens, width), f32)] * 2
    dma = pltpu.SemaphoreType.DMA
    return pl.pallas_call(
        functools.partial(mlp_kernel, number, not before),
        grid=(1,),
        in_specs=[any_spec, any_spec, full(bias)] + [any_spec] * (2 + len(before)),
        out_specs=[any_spec, any_spec, full(column), any_spec, any_spec],
        out_shape=[jax.ShapeDtypeStruct(own.shape, bf16)] * 2 + [column] + sums,
        scratch_shapes=[
            pltpu.VMEM((2 * tokens, width), bf16),
            pltpu.VMEM((2 * tokens, width), bf16),
            pltpu.VMEM((2, *own.shape), bf16),
            pltpu.VMEM((2, *own.shape), bf16),
            pltpu.VMEM((2, 2, tokens, width), f32),
            pltpu.VMEM((2, 2, tokens, width), f32),
            dma((8,)),
            dma((4,)),
        ],
        cost_estimate=tiny,
        compiler_params=pltpu.CompilerParams(vmem_limit_bytes=44 * MIB),
        name="mlp_part",
    )(own_in, met_in, bias, own, other, *before)


def on_device(
    tokens,
    cond,
    segment_ids,
    crop_slot,
    ada_weight,
    ada_bias,
    attn_weight,
    fc_in,
    fc_out,
    biases,
    out_grad,
):
    net = Net()
    tok_len, width = tokens.shape[1:]
    head_dim = width // HEADS
    mod_rank, core, chips = net.mod_rank, net.core, net.chips
    device_count = net.dp * net.mod
    crop_count = crop_slot.shape[1] // net.mod
    shard = attn_weight.shape[0]
    third = shard // 3
    chunks_of = [range(chips // 2), range(chips // 2, chips)]
    halves = [(n, side) for n in range(3) for side in range(2)]
    aligned = shard % (2 * head_dim) == 0 and third % 16 == 0 and width % (2 * net.mod * shard) == 0

    g_attn = Gather(net, attn_weight[None])
    g_fc = Gather(net, jnp.stack([fc_in, fc_out]))
    for n in range(g_attn.count):
        g_attn.start().finish()
    g_attn.start()
    first = g_attn.value
    for n in range(g_fc.count):
        g_fc.start(*first).finish()
    g_attn.finish().start()
    g_attn.finish().start(g_fc.value)
    third_phase = g_attn.value
    g_fc.start(*g_attn.got)
    attn_pieces = [(g_attn.value, g_attn.got)[side][n] for n, side in halves]

    silu_cond = jax.nn.silu(after(cond, *first).astype(f32)).astype(bf16)
    mod_part = times(silu_cond, ada_weight) + ada_bias.reshape(-1).astype(f32)
    mod_own = mod_part.astype(bf16)
    mod_other = net.swap(mod_own, "mod")
    modulation = jnp.concatenate(
        [jnp.where(mod_rank == 0, mod_own, mod_other), jnp.where(mod_rank == 0, mod_other, mod_own)], axis=1
    )
    seg_ids = segment_ids[0]
    slots = lax.dynamic_slice_in_dim(crop_slot[0], mod_rank * crop_count, crop_count)
    crop_onehot = seg_ids[:, None] == jnp.arange(crop_count, dtype=jnp.int32)[None, :]
    token_slot = jnp.sum(jnp.where(crop_onehot, slots[None, :], 0), axis=1)
    slot_pick = token_slot[:, None] == jnp.arange(cond.shape[0], dtype=jnp.int32)[None, :]
    slot_pick = slot_pick.astype(bf16)
    modulation = lax.optimization_barrier(modulation)
    mods = [modulation[:, n * width : (n + 1) * width] for n in range(6)]
    shift_a, scale_a, gate_a, shift_m, scale_m, gate_m = [times(slot_pick, block) for block in mods]

    slot_count, own_cols = cond.shape[0], width // net.dp
    to_dp = jnp.moveaxis(silu_cond.reshape(slot_count, net.dp, own_cols), 1, 0).reshape(net.dp, 1, -1)
    to_all = jnp.broadcast_to(to_dp, (net.dp, net.mod, slot_count * own_cols)).reshape(device_count, -1)
    to_all = after(to_all, *third_phase)
    sent = jnp.concatenate([jnp.broadcast_to(biases[None], (device_count, biases.shape[0])), to_all], axis=1)
    met = lax.all_to_all(sent, ("dp", "mod"), split_axis=0, concat_axis=0, tiled=True)
    ada_order = list(range(1, net.bits)) + [0]
    dp_order = net.ranks(ada_order, range(net.dp))[0]
    dp_pick = (dp_order[:, None] == jnp.arange(net.dp)[None, :]).astype(bf16)
    cond_cols = times(dp_pick, met.reshape(net.dp, net.mod, -1)[:, 0, biases.shape[0] :]).astype(bf16)
    cond_cols = cond_cols.reshape(-1, own_cols)
    bias_all = met[:, : biases.shape[0]].reshape(-1, width)
    bias_query, bias_value, bias_proj, bias_out = [bias_all[n].astype(f32) for n in range(4)]
    bias_in = bias_all[4:].reshape(device_count, 3, third)
    picks = []
    for n, side in halves:
        devices = net.devices(net.orders[n], chunks_of[side])
        picks.append((devices[:, None] == jnp.arange(device_count)[None, :]).astype(bf16))
    picks = jnp.stack(picks).reshape(3, 2, chips // 2, device_count)
    bias_pieces = jnp.einsum("nsjd,dnr->nsjr", picks, bias_in, preferred_element_type=f32).reshape(6, -1)

    def join(own, other):
        own, other = [a.reshape(-1, 1, net.mod * shard, a.shape[-1]) for a in (own, other)]
        both = jnp.where(core == 0, jnp.concatenate([own, other], 1), jnp.concatenate([other, own], 1))
        return both.reshape(-1, both.shape[-1])

    def part(whole):
        whole = whole.reshape(-1, 2, net.mod * shard, whole.shape[-1])
        return [
            jnp.where(core == c, whole[:, 0], whole[:, 1]).reshape(-1, whole.shape[-1]) for c in range(2)
        ]

    resid = tokens[0].astype(f32)
    normed_a, _ = layer_norm(resid)
    attn_in = (normed_a * (1.0 + scale_a) + shift_a).astype(bf16)
    if aligned:
        index = jnp.concatenate([net.local(net.orders[n], chunks_of[side]) * 3 + n for n, side in halves])
        own_weight = assemble(attn_pieces, index, third)
        qkv_rows = own_weight.shape[0] * 3 // 4
        qkv_weight = own_weight[:qkv_rows]
        proj_own = own_weight[qkv_rows:]
        proj_weight = join(proj_own, net.swap(proj_own, 0))
        ids = jnp.stack([seg_ids, net.swap(seg_ids, 0)])
        attn_in = after(attn_in, *third_phase)
        attn_both = jnp.concatenate([attn_in, net.swap(attn_in, 0)], axis=0)
        own_query, own_value = part(bias_query[:, None])[0], part(bias_value[:, None])[0]
        qkv_bias = jnp.concatenate([own_query, jnp.zeros_like(own_query), own_value], axis=0)
        attn_both = after(attn_both, *g_fc.got)
        g_fc.finish().start()
        qkv = (times_rows(qkv_weight, attn_both) + qkv_bias).astype(bf16)
        qkv = qkv.reshape(3, -1, 2 * head_dim, 2 * tok_len)
        context_both = attention(qkv, ids, head_dim).reshape(-1, 2 * tok_len)
        context = join(context_both[:, :tok_len], net.swap(context_both[:, tok_len:], 0))
        attn_out = dot(context, proj_weight, 0, 1) + bias_proj
    else:
        arrays = attn_pieces + [net.swap(piece, 0) for piece in attn_pieces]
        places = jnp.concatenate(
            [net.devices(net.orders[n], chunks_of[side], c) * 3 + n for c in range(2) for n, side in halves]
        )
        spread = jnp.concatenate(arrays, axis=1)[0]

        def place(n, whole):
            block = lax.dynamic_slice_in_dim(spread, n * third, third)
            return lax.dynamic_update_slice_in_dim(whole, block, places[n] * third, 0)

        attn_w = lax.fori_loop(0, places.shape[0], place, jnp.zeros_like(spread))
        g_fc.finish().start()
        g_fc.finish().start()
        qkv_weight, proj_weight = attn_w[: 3 * width], attn_w[3 * width :]
        qkv_bias = jnp.concatenate([bias_query, jnp.zeros_like(bias_query), bias_value])
        qkv = (times_rows(qkv_weight, attn_in) + qkv_bias[:, None]).astype(bf16)
        qkv = qkv.reshape(3, -1, 2 * head_dim, tok_len)
        context = attention(qkv, seg_ids[None], head_dim).reshape(-1, tok_len)
        attn_out = dot(context, proj_weight, 0, 1) + bias_proj
    mid = resid + gate_a * attn_out
    normed_m, _ = layer_norm(mid)
    mlp_in = (normed_m * (1.0 + scale_m) + shift_m).astype(bf16)
    if aligned:
        mlp_in = after(mlp_in, *g_fc.got)
        g_fc.finish().start()
    grad_mlp = (gate_m * out_grad[0].astype(f32)).astype(bf16)

    mlp_own = jnp.stack([mlp_in, grad_mlp])
    mlp_met = net.swap(mlp_own, 0)
    grad_bias_out = jnp.sum(grad_mlp.astype(f32), axis=0, keepdims=True)
    s_fc = Scatter(net)
    sums, columns = [], []
    for n in range(3):
        own, other, column, *sums = mlp_part(n, mlp_own, mlp_met, bias_pieces, g_fc.value[n], g_fc.got[n], sums)
        s_fc.begin(n, own, other)
        columns.append(column)
    own_sums, other_sums = sums
    sums_met = net.swap(other_sums, 0)
    sums_met = after(sums_met, s_fc.got[0])
    s_fc.advance((0,))

    grad_mid, grad_attn, grad_bias_proj, *parts = middle(
        core,
        net.mod * shard if aligned else None,
        own_sums,
        sums_met,
        mid,
        out_grad[0],
        slot_pick,
        modulation,
        proj_weight,
        context,
    )
    s_attn = Scatter(net)
    if aligned:
        mine, other, proj_mine, proj_other = parts
        other_met = after(net.swap(other, 0), s_fc.got[1], s_fc.got[0])
        s_fc.advance((1, 0))
        context_grads = jnp.concatenate([mine, other_met], axis=1)
        proj_met = net.swap(after(proj_other, context_grads), 0)
        grad_qkv = attention(qkv, ids, head_dim, context_grads.reshape(-1, 2 * head_dim, 2 * tok_len))
        grad_qkv = after(grad_qkv.reshape(-1, 2 * tok_len), s_fc.got[2])
        s_fc.advance((2,))
        pieces = weight_grad(grad_qkv, attn_both, proj_mine, proj_met, index, third, 6)
        s_fc.hold(*pieces)
        *pieces, _ = lax.optimization_barrier((*pieces, s_fc.got[0]))
        s_fc.advance((0,))
        for n in range(3):
            s_attn.begin(n, pieces[2 * n], pieces[2 * n + 1])
        grad_qkv, *_ = lax.optimization_barrier((grad_qkv, *pieces))
        back_both = contract_rows(grad_qkv, qkv_weight)
        back_own, back_met = back_both[:tok_len], net.swap(back_both[tok_len:], 0)
        back_met = after(back_met, s_fc.got[1], *s_attn.got)
        s_fc.advance((1,))
        s_attn.advance()
        grad_qkv, *columns = lax.optimization_barrier((grad_qkv, *columns, back_met))[:-1]
        column = jnp.sum(grad_qkv.astype(f32), axis=1, keepdims=True).reshape(3, -1, 1)
        none = jnp.zeros_like(column[0])
        grad_bias_query, grad_bias_value = join(column[0], none)[:, 0], join(column[2], none)[:, 0]
    else:
        grad_context, grad_proj = parts
        grad_qkv = attention(
            qkv, seg_ids[None], head_dim, grad_context.reshape(-1, 2 * head_dim, tok_len)
        ).reshape(-1, tok_len)
        s_fc.advance()
        attn_grad = jnp.concatenate([times(grad_qkv, attn_in).astype(bf16), grad_proj], axis=0)

        def take(n, whole):
            block = lax.dynamic_slice_in_dim(attn_grad, places[n] * third, third)
            return lax.dynamic_update_slice_in_dim(whole, block, n * third, 0)

        grads = lax.fori_loop(0, places.shape[0], take, jnp.zeros_like(attn_grad))
        grads = jnp.split(grads[None], 12, axis=1)
        pieces = [summed(a, net.swap(b, 0)) for a, b in zip(grads[:6], grads[6:])]
        back_own = contract_rows(grad_qkv, qkv_weight)
        back_met = jnp.zeros_like(back_own)
        column = jnp.sum(grad_qkv.astype(f32), axis=1).reshape(3, -1)
        grad_bias_query, grad_bias_value = column[0], column[2]
    if not aligned:
        for n in range(3):
            s_attn.begin(n, pieces[2 * n], pieces[2 * n + 1])
    grad_tokens, pair_a = end_call(
        attn_end_kernel, f32, slot_count, back_own, back_met, tokens[0], grad_mid, attn_out, slot_pick, modulation
    )
    result, pair_m = end_call(
        mlp_end_kernel,
        bf16,
        slot_count,
        mid,
        own_sums,
        sums_met,
        bias_out[None],
        out_grad[0],
        slot_pick,
        modulation,
    )
    columns = jnp.concatenate(columns, axis=0).reshape(3, 2, chips // 2, third)
    grad_bias_in = jnp.einsum("nsjd,nsjr->dnr", picks.astype(f32), columns, precision=lax.Precision.HIGHEST)
    grad_bias = stack_rows(
        grad_bias_query[None],
        grad_bias_value[None],
        grad_bias_proj,
        grad_bias_out,
        grad_bias_in.reshape(-1, width),
    )
    bias_rows = lax.all_to_all(
        grad_bias.reshape(device_count, -1), ("dp", "mod"), split_axis=0, concat_axis=0, tiled=True
    )
    bias_sum = jnp.sum(bias_rows, axis=0)

    pair_own = jnp.where(mod_rank == 0, pair_a, pair_m)
    pair_send = jnp.where(mod_rank == 0, pair_m, pair_a)
    grad_mod = summed(pair_own, net.swap(pair_send, "mod"))
    grad_silu = times_rows(grad_mod, ada_weight)
    silu_own = jnp.where(mod_rank == 0, grad_silu[:crop_count], grad_silu[crop_count:])
    silu_send = jnp.where(mod_rank == 0, grad_silu[crop_count:], grad_silu[:crop_count])
    grad_silu = silu_own + net.swap(silu_send.astype(bf16), "mod").astype(f32)
    own_cond = lax.dynamic_slice_in_dim(cond, mod_rank * crop_count, crop_count, 0).astype(f32)
    silu_back = jax.vjp(jax.nn.silu, own_cond)[1]
    grad_cond = silu_back(grad_silu)[0]
    mod_rows = grad_mod
    for dim in ada_order:
        mod_rows = jnp.concatenate([mod_rows, net.swap(mod_rows, dim)], axis=0)
    ada_w_sum = contract_rows(cond_cols, mod_rows)
    ada_b_sum = jnp.sum(mod_rows.astype(f32), axis=0).reshape(ada_bias.shape[0], width)
    ada_b_sum = lax.dynamic_slice_in_dim(ada_b_sum, net.dp_rank * own_cols, own_cols, 1)

    fc_sum = s_fc.rest()
    attn_sum = s_attn.rest()[0]
    return (
        result[None],
        grad_tokens[None],
        grad_cond,
        ada_w_sum,
        ada_b_sum,
        attn_sum,
        fc_sum[0],
        fc_sum[1],
        bias_sum,
    )


def solution(mesh):
    placed = (
        P(("dp", "mod"), None, None),
        P("dp", None),
        P(("dp", "mod"), None),
        P("dp", None),
        P(None, "mod"),
        P("mod", None),
        P(("dp", "mod"), None),
        P(("dp", "mod"), None),
        P(("dp", "mod"), None),
        P(("dp", "mod")),
        P(("dp", "mod"), None, None),
    )
    return jax.shard_map(
        on_device,
        mesh=mesh,
        in_specs=placed,
        out_specs=(
            P(("dp", "mod"), None, None),
            P(("dp", "mod"), None, None),
            P(("dp", "mod"), None),
            P("dp", "mod"),
            P("mod", "dp"),
            P(("dp", "mod"), None),
            P(("dp", "mod"), None),
            P(("dp", "mod"), None),
            P(("dp", "mod")),
        ),
        check_vma=False,
    )
```

```python
import functools

import jax
import jax.numpy as jnp
import numpy as np
from jax import lax
from jax.experimental import pallas as pl
from jax.experimental.pallas import tpu as pltpu
from jax.sharding import PartitionSpec as P

HEADS = 16
norm_eps = 1e-06
bf16 = jnp.bfloat16
f32 = jnp.float32
MIB = 1024 * 1024


def layer_norm(values):
    center = values - jnp.mean(values, axis=-1, keepdims=True)
    inverse = lax.rsqrt(jnp.mean(center * center, axis=-1, keepdims=True) + norm_eps)
    return (center * inverse, inverse)


def norm_back(grad_in, normed, inverse):
    centered = grad_in - jnp.mean(grad_in, axis=-1, keepdims=True)
    return (centered - normed * jnp.mean(grad_in * normed, axis=-1, keepdims=True)) * inverse


def dot(left, right, left_dim, right_dim):
    return lax.dot_general(left, right, (((left_dim,), (right_dim,)), ((), ())), preferred_element_type=f32)


def times(left, right):
    return dot(left, right, 1, 0)


def times_rows(left, right):
    return dot(left, right, 1, 1)


def contract_rows(left, right):
    return dot(left, right, 0, 0)


def after(value, *others):
    return lax.optimization_barrier((value, *others))[0]


def summed(left, right):
    return (left.astype(f32) + right.astype(f32)).astype(bf16)


class Net:
    def __init__(self):
        self.dp = lax.axis_size("dp")
        self.mod = lax.axis_size("mod")
        self.bits = self.dp.bit_length() - 1
        self.dp_rank = lax.axis_index("dp")
        self.mod_rank = lax.axis_index("mod")
        self.core = self.dp_rank & 1
        self.chips = self.dp // 2 * self.mod
        self.lead = list(range(self.bits - 1, 2, -1))
        last = ["mod", 1, 2]
        self.turns = [last[n:] + last[:n] for n in range(3)]
        self.orders = [self.lead + turn for turn in self.turns]

    def swap(self, value, dim):
        if dim == "mod":
            return lax.ppermute(value, "mod", [(i, i ^ 1) for i in range(self.mod)])
        return lax.ppermute(value, "dp", [(i, i ^ (1 << dim)) for i in range(self.dp)])

    def ranks(self, order, chunks, core=0):
        masks = []
        for j in chunks:
            dp_mask, mod_mask = core, 0
            for step, dim in enumerate(order):
                if j >> step & 1:
                    if dim == "mod":
                        mod_mask ^= 1
                    else:
                        dp_mask ^= 1 << dim
            masks.append((dp_mask, mod_mask))
        masks = np.array(masks, np.int32)
        return self.dp_rank ^ masks[:, 0], self.mod_rank ^ masks[:, 1]

    def devices(self, order, chunks, core=0):
        dp, mod = self.ranks(order, chunks, core)
        return dp * self.mod + mod

    def local(self, order, chunks):
        dp, mod = self.ranks(order, chunks)
        return (dp >> 1) * self.mod + mod


class Gather:
    def __init__(self, net, shard):
        self.net, self.count = net, len(net.lead)
        self.third = shard.shape[1] // 3
        self.value, self.got, self.phase = shard, None, 0

    def start(self, *others):
        net, phase = self.net, self.phase
        if phase < self.count:
            self.value = after(self.value, *others) if others else self.value
            self.got = [net.swap(self.value, net.lead[phase])]
        else:
            if phase == self.count:
                kinds, _, width = self.value.shape
                whole = self.value.reshape(kinds, -1, 3, self.third, width)
                self.value = [whole[:, :, n].reshape(kinds, -1, width) for n in range(3)]
            if others:
                self.value = list(lax.optimization_barrier((*self.value, *others))[:3])
            step = phase - self.count
            self.got = [net.swap(self.value[n], net.turns[n][step]) for n in range(3)]
        self.phase += 1
        return self

    def finish(self):
        if self.phase <= self.count:
            self.value = jnp.concatenate([self.value, self.got[0]], axis=1)
        elif self.phase < self.count + 3:
            self.value = [jnp.concatenate(pair, axis=1) for pair in zip(self.value, self.got)]
        return self


def kept_and_sent(own, got):
    half = own.shape[1] // 2
    return summed(own[:, :half], got[:, :half]), summed(own[:, half:], got[:, half:])


class Scatter:
    def __init__(self, net, own, other):
        self.net = net
        self.own = list(own)
        self.got = [net.swap(other[n], net.turns[n][2]) for n in range(3)]

    def join(self, own, other):
        self.also = [own[(n + 2) % 3] for n in range(3)]
        self.also_send = [other[(n + 2) % 3] for n in range(3)]
        for n in range(3):
            self.own[n], send = kept_and_sent(self.own[n], self.got[n])
            self.send(n, send, 1)

    def send(self, n, send, step):
        kinds, rows, width = send.shape
        both = jnp.concatenate([send, self.also_send[n].reshape(-1, rows, width)], axis=0)
        self.got[n] = self.net.swap(both, self.net.turns[n][step])

    def take(self, n):
        kinds, _, width = self.own[n].shape
        return self.got[n][:kinds], self.got[n][kinds:].reshape(self.also[n].shape[0], -1, width)

    def second(self):
        for n in range(3):
            got, also_got = self.take(n)
            self.own[n], send = kept_and_sent(self.own[n], got)
            self.also[n], self.also_send[n] = kept_and_sent(self.also[n], also_got)
            self.send(n, send, 0)

    def third(self):
        net = self.net
        for n in range(3):
            got, also_got = self.take(n)
            self.own[n] = summed(self.own[n], got)
            self.also[n], send = kept_and_sent(self.also[n], also_got)
            self.got[n] = net.swap(send, net.turns[(n + 2) % 3][0])
        self.whole = self.together(self.own)
        first, self.whole = self.lead(self.whole, len(net.lead) - 1)
        also = [summed(self.also[n], self.got[n]) for n in (1, 2, 0)]
        whole = self.together(also)
        for step in range(len(net.lead) - 1, -1, -1):
            got, whole = self.lead(whole, step)
            whole = whole.astype(f32) + got.astype(f32)
            if step:
                whole = whole.astype(bf16)
        attn_total, got, whole = whole, first, self.whole
        for step in range(len(net.lead) - 1, -1, -1):
            if step < len(net.lead) - 1:
                got, whole = self.lead(whole, step)
            whole = whole.astype(f32) + got.astype(f32)
            if step:
                whole = whole.astype(bf16)
        return whole, attn_total

    def together(self, parts):
        kinds, _, width = parts[0].shape
        count = 1 << len(self.net.lead)
        return jnp.concatenate([p.reshape(kinds, count, -1, width) for p in parts], axis=2).reshape(kinds, -1, width)

    def lead(self, whole, step):
        half = whole.shape[1] // 2
        return self.net.swap(whole[:, half:], self.net.lead[step]), whole[:, :half]


any_spec = pl.BlockSpec(memory_space=pl.ANY)


def full(value):
    return pl.BlockSpec(value.shape, lambda *_: (0,) * len(value.shape))

tiny = pl.CostEstimate(flops=1024, bytes_accessed=1024, transcendentals=0)


def run_copies(copies):
    for copy in copies:
        copy.start()
    for copy in copies:
        copy.wait()


def assemble_kernel(rows, each, index_ref, *refs):
    pieces, out_ref, hold, sems, last = refs[:-4], *refs[-4:]
    copies = []
    for n, piece in enumerate(pieces):
        for j in range(each):
            at = pl.multiple_of(index_ref[n * each + j] * rows, rows)
            copies.append(
                pltpu.make_async_copy(
                    piece.at[0, pl.ds(j * rows, rows)], hold.at[pl.ds(at, rows)], sems.at[n * each + j]
                )
            )
    run_copies(copies)
    run_copies([pltpu.make_async_copy(hold, out_ref, last)])


def assemble(pieces, index, rows):
    each, width = pieces[0].shape[1] // rows, pieces[0].shape[2]
    total = len(pieces) * each
    return pl.pallas_call(
        functools.partial(assemble_kernel, rows, each),
        grid_spec=pltpu.PrefetchScalarGridSpec(
            num_scalar_prefetch=1,
            grid=(1,),
            in_specs=[any_spec] * len(pieces),
            out_specs=any_spec,
            scratch_shapes=[
                pltpu.VMEM((total * rows, width), bf16),
                pltpu.SemaphoreType.DMA((total,)),
                pltpu.SemaphoreType.DMA,
            ],
        ),
        out_shape=jax.ShapeDtypeStruct((total * rows, width), bf16),
        compiler_params=pltpu.CompilerParams(vmem_limit_bytes=10 * MIB),
        name="assemble",
    )(index, *pieces)


def weight_grad_kernel(rows, each, index_ref, grad_ref, x_ref, mine_ref, other_ref, *refs):
    outs, hold, sems = refs[:-2], *refs[-2:]
    top = grad_ref.shape[0]
    step = top // 3
    for n in range(3):
        here = slice(n * step, (n + 1) * step)
        hold[here] = dot(grad_ref[here], x_ref[...], 1, 0).astype(bf16)
    hold[top:] = summed(mine_ref[...], other_ref[...])
    copies = []
    for n, out in enumerate(outs):
        for j in range(each):
            at = pl.multiple_of(index_ref[n * each + j] * rows, rows)
            copies.append(
                pltpu.make_async_copy(
                    hold.at[pl.ds(at, rows)], out.at[0, pl.ds(j * rows, rows)], sems.at[n * each + j]
                )
            )
    run_copies(copies)


def weight_grad(grad, x, mine, other, index, rows, count):
    total, width = grad.shape[0] + mine.shape[0], x.shape[1]
    each = total // rows // count
    return pl.pallas_call(
        functools.partial(weight_grad_kernel, rows, each),
        grid_spec=pltpu.PrefetchScalarGridSpec(
            num_scalar_prefetch=1,
            grid=(1,),
            in_specs=[full(a) for a in (grad, x, mine, other)],
            out_specs=[any_spec] * count,
            scratch_shapes=[pltpu.VMEM((total, width), bf16), pltpu.SemaphoreType.DMA((each * count,))],
        ),
        out_shape=[jax.ShapeDtypeStruct((1, each * rows, width), bf16)] * count,
        cost_estimate=tiny,
        compiler_params=pltpu.CompilerParams(vmem_limit_bytes=32 * MIB),
        name="weight_grad",
    )(index, grad, x, mine, other)


def by_core(core_ref, group, whole):
    if group is None:
        return [whole]
    picked = []
    for c in range(2):
        rows = []
        for at in range(0, whole.shape[0], 2 * group):
            first, second = whole[at : at + group], whole[at + group : at + 2 * group]
            rows.append(jnp.where(core_ref[0] == c, first, second))
        picked.append(jnp.concatenate(rows, axis=0))
    return picked


def token_block(pick, mods, n):
    width = mods.shape[1] // 6
    return dot(pick[...], mods[:, n * width : (n + 1) * width], 1, 0)


def middle_kernel(group, core_ref, *refs):
    sums, met, mid, grad_out, pick, mods, weight, context = refs[:8]
    mid_ref, attn_ref, column_ref = refs[8:11]
    normed, inverse = layer_norm(mid[...])
    back = (sums[1] + met[1]) * (1.0 + token_block(pick, mods, 4))
    grad_mid = grad_out[...].astype(f32) + norm_back(back, normed, inverse)
    mid_ref[...] = grad_mid
    grad_attn = (token_block(pick, mods, 2) * grad_mid).astype(bf16)
    attn_ref[...] = grad_attn
    column_ref[...] = jnp.sum(grad_attn.astype(f32), axis=0, keepdims=True)
    parts = by_core(core_ref, group, dot(weight[...], grad_attn, 0, 1))
    parts += by_core(core_ref, group, dot(grad_attn, context[...], 0, 1))
    for ref, value in zip(refs[11:], parts):
        ref[...] = value.astype(bf16)


def middle(core, group, *args):
    _, tokens, width = args[0].shape
    if group is None:
        sizes = [(width, tokens), (width, width)]
    else:
        sizes = [(width // 2, tokens)] * 2 + [(width // 2, width)] * 2
    outs = [((tokens, width), f32), ((tokens, width), bf16), ((1, width), f32)] + [(s, bf16) for s in sizes]
    outs = [jax.ShapeDtypeStruct(*out) for out in outs]
    return pl.pallas_call(
        functools.partial(middle_kernel, group),
        grid=(1,),
        in_specs=[pl.BlockSpec(memory_space=pltpu.SMEM)] + [full(a) for a in args],
        out_specs=[full(a) for a in outs],
        out_shape=outs,
        cost_estimate=tiny,
        compiler_params=pltpu.CompilerParams(vmem_limit_bytes=40 * MIB),
        name="middle",
    )(core.reshape(1), *args)


def slot_sums(pick, blocks, out_ref):
    for n, block in enumerate(blocks):
        high = block.astype(bf16)
        low = (block - high.astype(f32)).astype(bf16)
        total = dot(pick, high, 0, 0) + dot(pick, low, 0, 0)
        out_ref[:, n * block.shape[1] : (n + 1) * block.shape[1]] = total.astype(bf16)


def mlp_end_kernel(*refs):
    mid, sums, met, bias, grad_out, pick, mods = refs[:7]
    result_ref, pair_ref = refs[7:]
    mlp_out = sums[0] + met[0] + bias[...]
    result_ref[...] = (mid[...] + token_block(pick, mods, 5) * mlp_out).astype(bf16)
    back = sums[1] + met[1]
    slot_sums(pick[...], (back, back * layer_norm(mid[...])[0], grad_out[...].astype(f32) * mlp_out), pair_ref)


def attn_end_kernel(*refs):
    back_a, back_b, resid, grad_mid, attn_out, pick, mods = refs[:7]
    tokens_ref, pair_ref = refs[7:]
    back = back_a[...] + back_b[...]
    normed, inverse = layer_norm(resid[...].astype(f32))
    slope = back * (1.0 + token_block(pick, mods, 1))
    tokens_ref[...] = grad_mid[...] + norm_back(slope, normed, inverse)
    slot_sums(pick[...], (back, back * normed, grad_mid[...] * attn_out[...]), pair_ref)


def end_call(kernel, dtype, slots, *args):
    tokens, width = args[0].shape
    outs = [jax.ShapeDtypeStruct((tokens, width), dtype), jax.ShapeDtypeStruct((slots, 3 * width), bf16)]
    return pl.pallas_call(
        kernel,
        grid=(1,),
        in_specs=[full(a) for a in args],
        out_specs=[full(a) for a in outs],
        out_shape=outs,
        cost_estimate=tiny,
        compiler_params=pltpu.CompilerParams(vmem_limit_bytes=32 * MIB),
        name=kernel.__name__,
    )(*args)


def rows_kernel(*refs):
    at = 0
    for ref in refs[:-1]:
        refs[-1][at : at + ref.shape[0]] = ref[...]
        at += ref.shape[0]


def stack_rows(*args):
    out = jax.ShapeDtypeStruct((sum(a.shape[0] for a in args), args[0].shape[1]), f32)
    return pl.pallas_call(
        rows_kernel,
        grid=(1,),
        in_specs=[full(a) for a in args],
        out_specs=full(out),
        out_shape=out,
        cost_estimate=tiny,
        name="stack_rows",
    )(*args)


def softmax_t(key, query, same, scale):
    scores = jnp.where(same, dot(key, query, 0, 0) * scale, -1e30)
    weights = jnp.exp(scores - jnp.max(scores, axis=0, keepdims=True))
    return weights * (1.0 / jnp.sum(weights, axis=0, keepdims=True))


def heads_of(block, dim, cols):
    wide = block[:, cols].astype(f32)
    return [wide[n * dim : (n + 1) * dim].astype(bf16) for n in range(wide.shape[0] // dim)]


def attn_forward(dim, scale, row_ref, col_ref, q_ref, k_ref, v_ref, out_ref):
    length = col_ref.shape[0]
    for s in range(row_ref.shape[0]):
        cols = slice(s * length, (s + 1) * length)
        same = row_ref[s : s + 1] == col_ref[:, s : s + 1]
        outs = []
        for q, k, v in zip(*[heads_of(r[0, 0], dim, cols) for r in (q_ref, k_ref, v_ref)]):
            probs = softmax_t(k, q, same, scale).astype(bf16)
            outs.append(dot(v, probs, 1, 0))
        out_ref[0, :, cols] = jnp.concatenate(outs, axis=0).astype(bf16)


def attn_backward(dim, scale, row_ref, col_ref, q_ref, k_ref, v_ref, g_ref, out_ref):
    length = col_ref.shape[0]
    for s in range(row_ref.shape[0]):
        cols = slice(s * length, (s + 1) * length)
        same = row_ref[s : s + 1] == col_ref[:, s : s + 1]
        gq, gk, gv = [], [], []
        qs, ks, vs = [heads_of(r[0, 0], dim, cols) for r in (q_ref, k_ref, v_ref)]
        for q, k, v, g in zip(qs, ks, vs, heads_of(g_ref[0], dim, cols)):
            probs = softmax_t(k, q, same, scale)
            back = dot(v, g, 0, 0)
            back = probs * (back - jnp.sum(back * probs, axis=0, keepdims=True))
            back = back.astype(bf16)
            gq.append(dot(k, back, 1, 0) * scale)
            gk.append(dot(q, back, 1, 1) * scale)
            gv.append(dot(g, probs.astype(bf16), 1, 1))
        for n, parts in enumerate((gq, gk, gv)):
            out_ref[n, 0, :, cols] = jnp.concatenate(parts, axis=0).astype(bf16)


def attention(qkv, ids, dim, grad=None):
    _, groups, rows, tokens = qkv.shape
    scale = dim**-0.5
    ids_t = ids.T

    def one(n):
        return pl.BlockSpec((1, 1, rows, tokens), lambda i: (n, i, 0, 0))

    flat = pl.BlockSpec((1, rows, tokens), lambda i: (i, 0, 0))
    args = [ids, ids_t, qkv, qkv, qkv]
    specs = [pl.BlockSpec(a.shape, lambda i: (0, 0)) for a in (ids, ids_t)] + [one(0), one(1), one(2)]
    if grad is None:
        return pl.pallas_call(
            functools.partial(attn_forward, dim, scale),
            grid=(groups,),
            in_specs=specs,
            out_specs=flat,
            out_shape=jax.ShapeDtypeStruct((groups, rows, tokens), bf16),
            cost_estimate=tiny,
            compiler_params=pltpu.CompilerParams(vmem_limit_bytes=24 * MIB),
            name="attention",
        )(*args)
    return pl.pallas_call(
        functools.partial(attn_backward, dim, scale),
        grid=(groups,),
        in_specs=specs + [flat],
        out_specs=pl.BlockSpec((3, 1, rows, tokens), lambda i: (0, i, 0, 0)),
        out_shape=jax.ShapeDtypeStruct(qkv.shape, bf16),
        cost_estimate=tiny,
        compiler_params=pltpu.CompilerParams(vmem_limit_bytes=24 * MIB),
        name="attention_back",
    )(*args, grad)


def mlp_kernel(parts, *refs):
    own_ref, met_ref, b_ref = refs[:3]
    pieces, grads = refs[3 : 3 + 2 * parts], refs[3 + 2 * parts : 3 + 4 * parts]
    column_ref, own_sums, other_sums, x, g, weights, products, total, ins, outs = refs[3 + 4 * parts :]
    half, units = own_ref.shape[1], pieces[0].shape[1]
    copy = pltpu.make_async_copy

    def load(n):
        slot, copies = n % 2, []
        for kind in range(2):
            for side in range(2):
                copies.append(
                    copy(
                        pieces[2 * n + side].at[kind],
                        weights.at[slot, kind, pl.ds(side * units, units)],
                        ins.at[4 + 4 * n + 2 * kind + side],
                    )
                )
        return copies

    low, high = pl.ds(0, half), pl.ds(half, half)
    inputs = [
        copy(own_ref.at[0], x.at[low], ins.at[0]),
        copy(met_ref.at[0], x.at[high], ins.at[1]),
        copy(own_ref.at[1], g.at[low], ins.at[2]),
        copy(met_ref.at[1], g.at[high], ins.at[3]),
    ]
    loads = [load(n) for n in range(parts)]
    for item in inputs[:2] + loads[0][:2] + inputs[2:] + loads[0][2:] + loads[1]:
        item.start()
    stores = []
    root = 0.7978845608028654
    for n in range(parts):
        slot = n % 2
        for item in (inputs[:2] if n == 0 else []) + loads[n][:2]:
            item.wait()
        hidden = dot(x[...], weights[slot, 0], 1, 1) + b_ref[n : n + 1]
        square = hidden * hidden
        tanh = jnp.tanh(root * hidden * (1.0 + 0.044715 * square))
        act = (0.5 * hidden * (1.0 + tanh)).astype(bf16)
        slope = 0.5 * (1.0 + tanh) + 0.5 * hidden * (1.0 - tanh * tanh) * (root * (1.0 + 0.134145 * square))
        for item in (inputs[2:] if n == 0 else []) + loads[n][2:]:
            item.wait()
        back = (dot(g[...], weights[slot, 1], 1, 1) * slope).astype(bf16)
        column_ref[n : n + 1] = jnp.sum(back.astype(f32), axis=0, keepdims=True)
        for m, value in enumerate((dot(act, weights[slot, 1], 1, 0), dot(back, weights[slot, 0], 1, 0))):
            for k in range(2):
                rows = value[k * half : (k + 1) * half]
                total[k, m] = rows if n == 0 else total[k, m] + rows
        if n + 2 < parts:
            for item in loads[n + 2]:
                item.start()
        if n == parts - 1:
            sums = [copy(total.at[k], ref, outs.at[2 * parts + k]) for k, ref in enumerate((own_sums, other_sums))]
            for item in sums:
                item.start()
        if n >= 2:
            for item in stores[n - 2]:
                item.wait()
        products[slot, 1] = dot(act, g[...], 0, 0).astype(bf16)
        products[slot, 0] = dot(back, x[...], 0, 0).astype(bf16)
        stores.append(
            [
                copy(products.at[slot, :, pl.ds(side * units, units)], grads[2 * n + side], outs.at[2 * n + side])
                for side in range(2)
            ]
        )
        for item in stores[n]:
            item.start()
    for item in stores[-2] + stores[-1] + sums:
        item.wait()


def feed_forward(own_in, met_in, bias, pieces):
    _, tokens, width = own_in.shape
    parts, units = len(pieces) // 2, pieces[0].shape[1]
    column = jax.ShapeDtypeStruct((parts, 2 * units), f32)
    sums = [jax.ShapeDtypeStruct((2, tokens, width), f32)] * 2
    dma = pltpu.SemaphoreType.DMA
    return pl.pallas_call(
        functools.partial(mlp_kernel, parts),
        grid=(1,),
        in_specs=[any_spec, any_spec, full(bias)] + [any_spec] * len(pieces),
        out_specs=[any_spec] * len(pieces) + [full(column), any_spec, any_spec],
        out_shape=[jax.ShapeDtypeStruct(p.shape, bf16) for p in pieces] + [column] + sums,
        scratch_shapes=[
            pltpu.VMEM((2 * tokens, width), bf16),
            pltpu.VMEM((2 * tokens, width), bf16),
            pltpu.VMEM((2, 2, 2 * units, width), bf16),
            pltpu.VMEM((2, 2, 2 * units, width), bf16),
            pltpu.VMEM((2, 2, tokens, width), f32),
            dma((4 + 4 * parts,)),
            dma((2 * parts + 2,)),
        ],
        cost_estimate=tiny,
        compiler_params=pltpu.CompilerParams(vmem_limit_bytes=56 * MIB),
        name="feed_forward",
    )(own_in, met_in, bias, *pieces)


def on_device(
    tokens,
    cond,
    segment_ids,
    crop_slot,
    ada_weight,
    ada_bias,
    attn_weight,
    fc_in,
    fc_out,
    biases,
    out_grad,
):
    net = Net()
    tok_len, width = tokens.shape[1:]
    head_dim = width // HEADS
    mod_rank, core, chips = net.mod_rank, net.core, net.chips
    device_count = net.dp * net.mod
    crop_count = crop_slot.shape[1] // net.mod
    shard = attn_weight.shape[0]
    third = shard // 3
    chunks_of = [range(chips // 2), range(chips // 2, chips)]
    halves = [(n, side) for n in range(3) for side in range(2)]
    aligned = shard % (2 * head_dim) == 0 and third % 16 == 0 and width % (2 * net.mod * shard) == 0

    g_attn = Gather(net, attn_weight[None])
    g_fc = Gather(net, jnp.stack([fc_in, fc_out]))
    for n in range(g_attn.count):
        g_attn.start().finish()
    g_attn.start()
    first = g_attn.value
    for n in range(g_fc.count):
        g_fc.start(*first).finish()
    g_attn.finish().start()
    second = g_attn.value
    g_attn.finish().start()
    third_phase = g_attn.value
    g_fc.start(*g_attn.got)
    attn_pieces = [(g_attn.value, g_attn.got)[side][n] for n, side in halves]

    silu_cond = jax.nn.silu(after(cond, *second).astype(f32)).astype(bf16)
    mod_part = times(silu_cond, ada_weight) + ada_bias.reshape(-1).astype(f32)
    mod_own = mod_part.astype(bf16)
    mod_other = net.swap(mod_own, "mod")
    modulation = jnp.concatenate(
        [jnp.where(mod_rank == 0, mod_own, mod_other), jnp.where(mod_rank == 0, mod_other, mod_own)], axis=1
    )
    seg_ids = segment_ids[0]
    slots = lax.dynamic_slice_in_dim(crop_slot[0], mod_rank * crop_count, crop_count)
    crop_onehot = seg_ids[:, None] == jnp.arange(crop_count, dtype=jnp.int32)[None, :]
    token_slot = jnp.sum(jnp.where(crop_onehot, slots[None, :], 0), axis=1)
    slot_pick = token_slot[:, None] == jnp.arange(cond.shape[0], dtype=jnp.int32)[None, :]
    slot_pick = slot_pick.astype(bf16)
    modulation = lax.optimization_barrier(modulation)
    mods = [modulation[:, n * width : (n + 1) * width] for n in range(6)]
    shift_a, scale_a, gate_a, shift_m, scale_m, gate_m = [times(slot_pick, block) for block in mods]

    slot_count, own_cols = cond.shape[0], width // net.dp
    to_dp = jnp.moveaxis(silu_cond.reshape(slot_count, net.dp, own_cols), 1, 0).reshape(net.dp, 1, -1)
    to_all = jnp.broadcast_to(to_dp, (net.dp, net.mod, slot_count * own_cols)).reshape(device_count, -1)
    to_all = after(to_all, *third_phase)
    sent = jnp.concatenate([jnp.broadcast_to(biases[None], (device_count, biases.shape[0])), to_all], axis=1)
    met = lax.all_to_all(sent, ("dp", "mod"), split_axis=0, concat_axis=0, tiled=True)
    ada_order = list(range(1, net.bits)) + [0]
    dp_order = net.ranks(ada_order, range(net.dp))[0]
    dp_pick = (dp_order[:, None] == jnp.arange(net.dp)[None, :]).astype(bf16)
    cond_cols = times(dp_pick, met.reshape(net.dp, net.mod, -1)[:, 0, biases.shape[0] :]).astype(bf16)
    cond_cols = cond_cols.reshape(-1, own_cols)
    bias_all = met[:, : biases.shape[0]].reshape(-1, width)
    bias_query, bias_value, bias_proj, bias_out = [bias_all[n].astype(f32) for n in range(4)]
    bias_in = bias_all[4:].reshape(device_count, 3, third)
    picks = []
    for n, side in halves:
        devices = net.devices(net.orders[n], chunks_of[side])
        picks.append((devices[:, None] == jnp.arange(device_count)[None, :]).astype(bf16))
    picks = jnp.stack(picks).reshape(3, 2, chips // 2, device_count)
    bias_pieces = jnp.einsum("nsjd,dnr->nsjr", picks, bias_in, preferred_element_type=f32).reshape(3, -1)

    def join(own, other):
        own, other = [a.reshape(-1, 1, net.mod * shard, a.shape[-1]) for a in (own, other)]
        both = jnp.where(core == 0, jnp.concatenate([own, other], 1), jnp.concatenate([other, own], 1))
        return both.reshape(-1, both.shape[-1])

    def part(whole):
        whole = whole.reshape(-1, 2, net.mod * shard, whole.shape[-1])
        return [
            jnp.where(core == c, whole[:, 0], whole[:, 1]).reshape(-1, whole.shape[-1]) for c in range(2)
        ]

    resid = tokens[0].astype(f32)
    normed_a, _ = layer_norm(resid)
    attn_in = (normed_a * (1.0 + scale_a) + shift_a).astype(bf16)
    if aligned:
        index = jnp.concatenate([net.local(net.orders[n], chunks_of[side]) * 3 + n for n, side in halves])
        own_weight = assemble(attn_pieces, index, third)
        qkv_rows = own_weight.shape[0] * 3 // 4
        qkv_weight = own_weight[:qkv_rows]
        proj_own = own_weight[qkv_rows:]
        proj_weight = join(proj_own, net.swap(proj_own, 0))
        ids = jnp.stack([seg_ids, net.swap(seg_ids, 0)])
        attn_in = after(attn_in, *third_phase)
        attn_both = jnp.concatenate([attn_in, net.swap(attn_in, 0)], axis=0)
        own_query, own_value = part(bias_query[:, None])[0], part(bias_value[:, None])[0]
        qkv_bias = jnp.concatenate([own_query, jnp.zeros_like(own_query), own_value], axis=0)
        attn_both = after(attn_both, *g_fc.got)
        g_fc.finish().start()
        qkv = (times_rows(qkv_weight, attn_both) + qkv_bias).astype(bf16)
        qkv = qkv.reshape(3, -1, 2 * head_dim, 2 * tok_len)
        context_both = attention(qkv, ids, head_dim).reshape(-1, 2 * tok_len)
        context = join(context_both[:, :tok_len], net.swap(context_both[:, tok_len:], 0))
        attn_out = dot(context, proj_weight, 0, 1) + bias_proj
    else:
        arrays = attn_pieces + [net.swap(piece, 0) for piece in attn_pieces]
        places = jnp.concatenate(
            [net.devices(net.orders[n], chunks_of[side], c) * 3 + n for c in range(2) for n, side in halves]
        )
        spread = jnp.concatenate(arrays, axis=1)[0]

        def place(n, whole):
            block = lax.dynamic_slice_in_dim(spread, n * third, third)
            return lax.dynamic_update_slice_in_dim(whole, block, places[n] * third, 0)

        attn_w = lax.fori_loop(0, places.shape[0], place, jnp.zeros_like(spread))
        g_fc.finish().start()
        g_fc.finish().start()
        qkv_weight, proj_weight = attn_w[: 3 * width], attn_w[3 * width :]
        qkv_bias = jnp.concatenate([bias_query, jnp.zeros_like(bias_query), bias_value])
        qkv = (times_rows(qkv_weight, attn_in) + qkv_bias[:, None]).astype(bf16)
        qkv = qkv.reshape(3, -1, 2 * head_dim, tok_len)
        context = attention(qkv, seg_ids[None], head_dim).reshape(-1, tok_len)
        attn_out = dot(context, proj_weight, 0, 1) + bias_proj
    mid = resid + gate_a * attn_out
    normed_m, _ = layer_norm(mid)
    mlp_in = (normed_m * (1.0 + scale_m) + shift_m).astype(bf16)
    if aligned:
        mlp_in = after(mlp_in, *g_fc.got)
        g_fc.finish().start()
    grad_mlp = (gate_m * out_grad[0].astype(f32)).astype(bf16)

    mlp_own = jnp.stack([mlp_in, grad_mlp])
    mlp_met = net.swap(mlp_own, 0)
    grad_bias_out = jnp.sum(grad_mlp.astype(f32), axis=0, keepdims=True)
    fc_pieces = [(g_fc.value, g_fc.got)[side][n] for n, side in halves]
    *fc_grads, columns, own_sums, other_sums = feed_forward(mlp_own, mlp_met, bias_pieces, fc_pieces)
    sums_met = net.swap(other_sums, 0)
    back_way = Scatter(net, fc_grads[0::2], fc_grads[1::2])

    grad_mid, grad_attn, grad_bias_proj, *parts = middle(
        core,
        net.mod * shard if aligned else None,
        own_sums,
        sums_met,
        mid,
        out_grad[0],
        slot_pick,
        modulation,
        proj_weight,
        context,
    )
    if aligned:
        mine, other, proj_mine, proj_other = parts
        context_grads = jnp.concatenate([mine, net.swap(other, 0)], axis=1)
        proj_met = net.swap(after(proj_other, context_grads), 0)
        grad_qkv = attention(qkv, ids, head_dim, context_grads.reshape(-1, 2 * head_dim, 2 * tok_len))
        grad_qkv = grad_qkv.reshape(-1, 2 * tok_len)
        pieces = weight_grad(grad_qkv, attn_both, proj_mine, proj_met, index, third, 6)
        grad_qkv, *pieces = lax.optimization_barrier((grad_qkv, *pieces))
        back_both = contract_rows(grad_qkv, qkv_weight)
        back_own, back_met = back_both[:tok_len], net.swap(back_both[tok_len:], 0)
        back_way.got = list(lax.optimization_barrier((*back_way.got, *pieces))[:3])
        column = jnp.sum(grad_qkv.astype(f32), axis=1, keepdims=True).reshape(3, -1, 1)
        none = jnp.zeros_like(column[0])
        grad_bias_query, grad_bias_value = join(column[0], none)[:, 0], join(column[2], none)[:, 0]
    else:
        grad_context, grad_proj = parts
        grad_qkv = attention(
            qkv, seg_ids[None], head_dim, grad_context.reshape(-1, 2 * head_dim, tok_len)
        ).reshape(-1, tok_len)
        attn_grad = jnp.concatenate([times(grad_qkv, attn_in).astype(bf16), grad_proj], axis=0)

        def take(n, whole):
            block = lax.dynamic_slice_in_dim(attn_grad, places[n] * third, third)
            return lax.dynamic_update_slice_in_dim(whole, block, n * third, 0)

        grads = lax.fori_loop(0, places.shape[0], take, jnp.zeros_like(attn_grad))
        grads = jnp.split(grads[None], 12, axis=1)
        pieces = [summed(a, net.swap(b, 0)) for a, b in zip(grads[:6], grads[6:])]
        back_own = contract_rows(grad_qkv, qkv_weight)
        back_met = jnp.zeros_like(back_own)
        column = jnp.sum(grad_qkv.astype(f32), axis=1).reshape(3, -1)
        grad_bias_query, grad_bias_value = column[0], column[2]
    back_way.join(pieces[0::2], pieces[1::2])
    grad_tokens, pair_a = end_call(
        attn_end_kernel, f32, slot_count, back_own, back_met, tokens[0], grad_mid, attn_out, slot_pick, modulation
    )
    result, pair_m = end_call(
        mlp_end_kernel,
        bf16,
        slot_count,
        mid,
        own_sums,
        sums_met,
        bias_out[None],
        out_grad[0],
        slot_pick,
        modulation,
    )
    columns = columns.reshape(3, 2, chips // 2, third)
    grad_bias_in = jnp.einsum("nsjd,nsjr->dnr", picks.astype(f32), columns, precision=lax.Precision.HIGHEST)
    grad_bias = stack_rows(
        grad_bias_query[None],
        grad_bias_value[None],
        grad_bias_proj,
        grad_bias_out,
        grad_bias_in.reshape(-1, width),
    )
    bias_rows = lax.all_to_all(
        grad_bias.reshape(device_count, -1), ("dp", "mod"), split_axis=0, concat_axis=0, tiled=True
    )
    bias_sum = jnp.sum(bias_rows, axis=0)

    pair_own = jnp.where(mod_rank == 0, pair_a, pair_m)
    pair_send = jnp.where(mod_rank == 0, pair_m, pair_a)
    grad_mod = summed(pair_own, net.swap(pair_send, "mod"))
    grad_silu = times_rows(grad_mod, ada_weight)
    silu_own = jnp.where(mod_rank == 0, grad_silu[:crop_count], grad_silu[crop_count:])
    silu_send = jnp.where(mod_rank == 0, grad_silu[crop_count:], grad_silu[:crop_count])
    grad_silu = silu_own + net.swap(silu_send.astype(bf16), "mod").astype(f32)
    own_cond = lax.dynamic_slice_in_dim(cond, mod_rank * crop_count, crop_count, 0).astype(f32)
    silu_back = jax.vjp(jax.nn.silu, own_cond)[1]
    grad_cond = silu_back(grad_silu)[0]
    mod_rows = grad_mod
    for step, dim in enumerate(ada_order):
        mod_rows = jnp.concatenate([mod_rows, net.swap(mod_rows, dim)], axis=0)
        if step == 0:
            back_way.got = list(lax.optimization_barrier((*back_way.got, mod_rows))[:3])
            back_way.second()
    ada_w_sum = contract_rows(cond_cols, mod_rows)
    ada_b_sum = jnp.sum(mod_rows.astype(f32), axis=0).reshape(ada_bias.shape[0], width)
    ada_b_sum = lax.dynamic_slice_in_dim(ada_b_sum, net.dp_rank * own_cols, own_cols, 1)
    fc_sum, attn_sum = back_way.third()
    return (
        result[None],
        grad_tokens[None],
        grad_cond,
        ada_w_sum,
        ada_b_sum,
        attn_sum[0],
        fc_sum[0],
        fc_sum[1],
        bias_sum,
    )


def solution(mesh):
    placed = (
        P(("dp", "mod"), None, None),
        P("dp", None),
        P(("dp", "mod"), None),
        P("dp", None),
        P(None, "mod"),
        P("mod", None),
        P(("dp", "mod"), None),
        P(("dp", "mod"), None),
        P(("dp", "mod"), None),
        P(("dp", "mod")),
        P(("dp", "mod"), None, None),
    )
    return jax.shard_map(
        on_device,
        mesh=mesh,
        in_specs=placed,
        out_specs=(
            P(("dp", "mod"), None, None),
            P(("dp", "mod"), None, None),
            P(("dp", "mod"), None),
            P("dp", "mod"),
            P("mod", "dp"),
            P(("dp", "mod"), None),
            P(("dp", "mod"), None),
            P(("dp", "mod"), None),
            P(("dp", "mod")),
        ),
        check_vma=False,
    )
```

```python
import functools

import jax
import jax.numpy as jnp
import numpy as np
from jax import lax
from jax.experimental import pallas as pl
from jax.experimental.pallas import tpu as pltpu
from jax.sharding import PartitionSpec as P

HEADS = 16
norm_eps = 1e-06
bf16 = jnp.bfloat16
f32 = jnp.float32
MIB = 1024 * 1024


def layer_norm(values):
    center = values - jnp.mean(values, axis=-1, keepdims=True)
    inverse = lax.rsqrt(jnp.mean(center * center, axis=-1, keepdims=True) + norm_eps)
    return (center * inverse, inverse)


def norm_back(grad_in, normed, inverse):
    centered = grad_in - jnp.mean(grad_in, axis=-1, keepdims=True)
    return (centered - normed * jnp.mean(grad_in * normed, axis=-1, keepdims=True)) * inverse


def dot(left, right, left_dim, right_dim):
    return lax.dot_general(left, right, (((left_dim,), (right_dim,)), ((), ())), preferred_element_type=f32)


def times(left, right):
    return dot(left, right, 1, 0)


def times_rows(left, right):
    return dot(left, right, 1, 1)


def contract_rows(left, right):
    return dot(left, right, 0, 0)


def after(value, *others):
    return lax.optimization_barrier((value, *others))[0]


def summed(left, right):
    return (left.astype(f32) + right.astype(f32)).astype(bf16)


class Net:
    def __init__(self):
        self.dp = lax.axis_size("dp")
        self.mod = lax.axis_size("mod")
        self.bits = self.dp.bit_length() - 1
        self.dp_rank = lax.axis_index("dp")
        self.mod_rank = lax.axis_index("mod")
        self.core = self.dp_rank & 1
        self.chips = self.dp // 2 * self.mod
        self.lead = list(range(self.bits - 1, 2, -1))
        last = ["mod", 1, 2]
        self.turns = [last[n:] + last[:n] for n in range(3)]
        self.orders = [self.lead + turn for turn in self.turns]

    def swap(self, value, dim):
        if dim == "mod":
            return lax.ppermute(value, "mod", [(i, i ^ 1) for i in range(self.mod)])
        return lax.ppermute(value, "dp", [(i, i ^ (1 << dim)) for i in range(self.dp)])

    def ranks(self, order, chunks, core=0):
        masks = []
        for j in chunks:
            dp_mask, mod_mask = core, 0
            for step, dim in enumerate(order):
                if j >> step & 1:
                    if dim == "mod":
                        mod_mask ^= 1
                    else:
                        dp_mask ^= 1 << dim
            masks.append((dp_mask, mod_mask))
        masks = np.array(masks, np.int32)
        return self.dp_rank ^ masks[:, 0], self.mod_rank ^ masks[:, 1]

    def devices(self, order, chunks, core=0):
        dp, mod = self.ranks(order, chunks, core)
        return dp * self.mod + mod

    def local(self, order, chunks):
        dp, mod = self.ranks(order, chunks)
        return (dp >> 1) * self.mod + mod


class Gather:
    def __init__(self, net, shard):
        self.net, self.count = net, len(net.lead)
        self.third = shard.shape[1] // 3
        self.value, self.got, self.phase = shard, None, 0

    def start(self, *others):
        net, phase = self.net, self.phase
        if phase < self.count:
            self.value = after(self.value, *others) if others else self.value
            self.got = [net.swap(self.value, net.lead[phase])]
        else:
            if phase == self.count:
                kinds, _, width = self.value.shape
                whole = self.value.reshape(kinds, -1, 3, self.third, width)
                self.value = [whole[:, :, n].reshape(kinds, -1, width) for n in range(3)]
            if others:
                self.value = list(lax.optimization_barrier((*self.value, *others))[:3])
            step = phase - self.count
            self.got = [net.swap(self.value[n], net.turns[n][step]) for n in range(3)]
        self.phase += 1
        return self

    def finish(self):
        if self.phase <= self.count:
            self.value = jnp.concatenate([self.value, self.got[0]], axis=1)
        elif self.phase < self.count + 3:
            self.value = [jnp.concatenate(pair, axis=1) for pair in zip(self.value, self.got)]
        return self


def kept_and_sent(own, got):
    half = own.shape[1] // 2
    return summed(own[:, :half], got[:, :half]), summed(own[:, half:], got[:, half:])


class Scatter:
    def __init__(self, net, own, other):
        self.net = net
        self.own = list(own)
        self.got = [net.swap(other[n], net.turns[n][2]) for n in range(3)]

    def join(self, own, other):
        self.also = [own[(n + 2) % 3] for n in range(3)]
        self.also_send = [other[(n + 2) % 3] for n in range(3)]
        for n in range(3):
            self.own[n], send = kept_and_sent(self.own[n], self.got[n])
            self.send(n, send, 1)

    def send(self, n, send, step):
        kinds, rows, width = send.shape
        both = jnp.concatenate([send, self.also_send[n].reshape(-1, rows, width)], axis=0)
        self.got[n] = self.net.swap(both, self.net.turns[n][step])

    def take(self, n):
        kinds, _, width = self.own[n].shape
        return self.got[n][:kinds], self.got[n][kinds:].reshape(self.also[n].shape[0], -1, width)

    def second(self):
        for n in range(3):
            got, also_got = self.take(n)
            self.own[n], send = kept_and_sent(self.own[n], got)
            self.also[n], self.also_send[n] = kept_and_sent(self.also[n], also_got)
            self.send(n, send, 0)

    def third(self):
        net = self.net
        for n in range(3):
            got, also_got = self.take(n)
            self.own[n] = summed(self.own[n], got)
            self.also[n], send = kept_and_sent(self.also[n], also_got)
            self.got[n] = net.swap(send, net.turns[(n + 2) % 3][0])
        self.whole = self.together(self.own)
        first, self.whole = self.lead(self.whole, len(net.lead) - 1)
        also = [summed(self.also[n], self.got[n]) for n in (1, 2, 0)]
        whole = self.together(also)
        for step in range(len(net.lead) - 1, -1, -1):
            got, whole = self.lead(whole, step)
            whole = whole.astype(f32) + got.astype(f32)
            if step:
                whole = whole.astype(bf16)
        attn_total, got, whole = whole, first, self.whole
        for step in range(len(net.lead) - 1, -1, -1):
            if step < len(net.lead) - 1:
                got, whole = self.lead(whole, step)
            whole = whole.astype(f32) + got.astype(f32)
            if step:
                whole = whole.astype(bf16)
        return whole, attn_total

    def together(self, parts):
        kinds, _, width = parts[0].shape
        count = 1 << len(self.net.lead)
        return jnp.concatenate([p.reshape(kinds, count, -1, width) for p in parts], axis=2).reshape(kinds, -1, width)

    def lead(self, whole, step):
        half = whole.shape[1] // 2
        return self.net.swap(whole[:, half:], self.net.lead[step]), whole[:, :half]


any_spec = pl.BlockSpec(memory_space=pl.ANY)


def full(value):
    return pl.BlockSpec(value.shape, lambda *_: (0,) * len(value.shape))

tiny = pl.CostEstimate(flops=1024, bytes_accessed=1024, transcendentals=0)


def run_copies(copies):
    for copy in copies:
        copy.start()
    for copy in copies:
        copy.wait()


def assemble_kernel(rows, each, index_ref, *refs):
    pieces, out_ref, hold, sems, last = refs[:-4], *refs[-4:]
    copies = []
    for n, piece in enumerate(pieces):
        for j in range(each):
            at = pl.multiple_of(index_ref[n * each + j] * rows, rows)
            copies.append(
                pltpu.make_async_copy(
                    piece.at[0, pl.ds(j * rows, rows)], hold.at[pl.ds(at, rows)], sems.at[n * each + j]
                )
            )
    run_copies(copies)
    run_copies([pltpu.make_async_copy(hold, out_ref, last)])


def assemble(pieces, index, rows):
    each, width = pieces[0].shape[1] // rows, pieces[0].shape[2]
    total = len(pieces) * each
    return pl.pallas_call(
        functools.partial(assemble_kernel, rows, each),
        grid_spec=pltpu.PrefetchScalarGridSpec(
            num_scalar_prefetch=1,
            grid=(1,),
            in_specs=[any_spec] * len(pieces),
            out_specs=any_spec,
            scratch_shapes=[
                pltpu.VMEM((total * rows, width), bf16),
                pltpu.SemaphoreType.DMA((total,)),
                pltpu.SemaphoreType.DMA,
            ],
        ),
        out_shape=jax.ShapeDtypeStruct((total * rows, width), bf16),
        compiler_params=pltpu.CompilerParams(vmem_limit_bytes=10 * MIB),
        name="assemble",
    )(index, *pieces)


def weight_grad_kernel(rows, place_ref, grad_ref, x_ref, mine_ref, other_ref, out_ref, hold, sems):
    top, copies = grad_ref.shape[0], []
    step = top // 3
    for n in (3, 0, 1, 2):
        start = n * step
        stop = min(start + step, hold.shape[0])
        if n == 3:
            hold[start:] = summed(mine_ref[...], other_ref[...])
        else:
            hold[start:stop] = dot(grad_ref[start:stop], x_ref[...], 1, 0).astype(bf16)
        for unit in range(start // rows, stop // rows):
            at = pl.multiple_of(place_ref[unit] * rows, rows)
            copies.append(
                pltpu.make_async_copy(
                    hold.at[pl.ds(unit * rows, rows)], out_ref.at[pl.ds(at, rows)], sems.at[unit]
                )
            )
            copies[-1].start()
    for copy in copies:
        copy.wait()


def weight_grad(grad, x, mine, other, places, rows):
    total, width = grad.shape[0] + mine.shape[0], x.shape[1]
    return pl.pallas_call(
        functools.partial(weight_grad_kernel, rows),
        grid_spec=pltpu.PrefetchScalarGridSpec(
            num_scalar_prefetch=1,
            grid=(1,),
            in_specs=[full(a) for a in (grad, x, mine, other)],
            out_specs=any_spec,
            scratch_shapes=[pltpu.VMEM((total, width), bf16), pltpu.SemaphoreType.DMA((total // rows,))],
        ),
        out_shape=jax.ShapeDtypeStruct((total, width), bf16),
        cost_estimate=tiny,
        compiler_params=pltpu.CompilerParams(vmem_limit_bytes=32 * MIB),
        name="weight_grad",
    )(places, grad, x, mine, other)


def by_core(core_ref, group, whole):
    if group is None:
        return [whole]
    picked = []
    for c in range(2):
        rows = []
        for at in range(0, whole.shape[0], 2 * group):
            first, second = whole[at : at + group], whole[at + group : at + 2 * group]
            rows.append(jnp.where(core_ref[0] == c, first, second))
        picked.append(jnp.concatenate(rows, axis=0))
    return picked


def token_block(pick, mods, n):
    width = mods.shape[1] // 6
    return dot(pick[...], mods[:, n * width : (n + 1) * width], 1, 0)


def middle_kernel(group, core_ref, *refs):
    sums, met, mid, grad_out, pick, mods, weight, context = refs[:8]
    mid_ref, attn_ref, column_ref = refs[8:11]
    normed, inverse = layer_norm(mid[...])
    back = (sums[1] + met[1]) * (1.0 + token_block(pick, mods, 4))
    grad_mid = grad_out[...].astype(f32) + norm_back(back, normed, inverse)
    mid_ref[...] = grad_mid
    grad_attn = (token_block(pick, mods, 2) * grad_mid).astype(bf16)
    attn_ref[...] = grad_attn
    column_ref[...] = jnp.sum(grad_attn.astype(f32), axis=0, keepdims=True)
    parts = by_core(core_ref, group, dot(weight[...], grad_attn, 0, 1))
    parts += by_core(core_ref, group, dot(grad_attn, context[...], 0, 1))
    for ref, value in zip(refs[11:], parts):
        ref[...] = value.astype(bf16)


def middle(core, group, *args):
    _, tokens, width = args[0].shape
    if group is None:
        sizes = [(width, tokens), (width, width)]
    else:
        sizes = [(width // 2, tokens)] * 2 + [(width // 2, width)] * 2
    outs = [((tokens, width), f32), ((tokens, width), bf16), ((1, width), f32)] + [(s, bf16) for s in sizes]
    outs = [jax.ShapeDtypeStruct(*out) for out in outs]
    return pl.pallas_call(
        functools.partial(middle_kernel, group),
        grid=(1,),
        in_specs=[pl.BlockSpec(memory_space=pltpu.SMEM)] + [full(a) for a in args],
        out_specs=[full(a) for a in outs],
        out_shape=outs,
        cost_estimate=tiny,
        compiler_params=pltpu.CompilerParams(vmem_limit_bytes=40 * MIB),
        name="middle",
    )(core.reshape(1), *args)


def slot_sums(pick, blocks, out_ref):
    for n, block in enumerate(blocks):
        high = block.astype(bf16)
        low = (block - high.astype(f32)).astype(bf16)
        total = dot(pick, high, 0, 0) + dot(pick, low, 0, 0)
        out_ref[:, n * block.shape[1] : (n + 1) * block.shape[1]] = total.astype(bf16)


def mlp_end_kernel(*refs):
    mid, sums, met, bias, grad_out, pick, mods = refs[:7]
    result_ref, pair_ref = refs[7:]
    mlp_out = sums[0] + met[0] + bias[...]
    result_ref[...] = (mid[...] + token_block(pick, mods, 5) * mlp_out).astype(bf16)
    back = sums[1] + met[1]
    slot_sums(pick[...], (back, back * layer_norm(mid[...])[0], grad_out[...].astype(f32) * mlp_out), pair_ref)


def attn_end_kernel(*refs):
    back_a, back_b, resid, grad_mid, attn_out, pick, mods = refs[:7]
    tokens_ref, pair_ref = refs[7:]
    back = back_a[...] + back_b[...]
    normed, inverse = layer_norm(resid[...].astype(f32))
    slope = back * (1.0 + token_block(pick, mods, 1))
    tokens_ref[...] = grad_mid[...] + norm_back(slope, normed, inverse)
    slot_sums(pick[...], (back, back * normed, grad_mid[...] * attn_out[...]), pair_ref)


def end_call(kernel, dtype, slots, *args):
    tokens, width = args[0].shape
    outs = [jax.ShapeDtypeStruct((tokens, width), dtype), jax.ShapeDtypeStruct((slots, 3 * width), bf16)]
    return pl.pallas_call(
        kernel,
        grid=(1,),
        in_specs=[full(a) for a in args],
        out_specs=[full(a) for a in outs],
        out_shape=outs,
        cost_estimate=tiny,
        compiler_params=pltpu.CompilerParams(vmem_limit_bytes=32 * MIB),
        name=kernel.__name__,
    )(*args)


def rows_kernel(*refs):
    at = 0
    for ref in refs[:-1]:
        refs[-1][at : at + ref.shape[0]] = ref[...]
        at += ref.shape[0]


def stack_rows(*args):
    out = jax.ShapeDtypeStruct((sum(a.shape[0] for a in args), args[0].shape[1]), f32)
    return pl.pallas_call(
        rows_kernel,
        grid=(1,),
        in_specs=[full(a) for a in args],
        out_specs=full(out),
        out_shape=out,
        cost_estimate=tiny,
        name="stack_rows",
    )(*args)


def softmax_t(key, query, same, scale):
    scores = jnp.where(same, dot(key, query, 0, 0) * scale, -1e30)
    weights = jnp.exp(scores - jnp.max(scores, axis=0, keepdims=True))
    return weights * (1.0 / jnp.sum(weights, axis=0, keepdims=True))


def heads_of(block, dim, cols):
    wide = block[:, cols].astype(f32)
    return [wide[n * dim : (n + 1) * dim].astype(bf16) for n in range(wide.shape[0] // dim)]


def attn_forward(dim, scale, row_ref, col_ref, q_ref, k_ref, v_ref, out_ref):
    length = col_ref.shape[0]
    for s in range(row_ref.shape[0]):
        cols = slice(s * length, (s + 1) * length)
        same = row_ref[s : s + 1] == col_ref[:, s : s + 1]
        outs = []
        for q, k, v in zip(*[heads_of(r[0, 0], dim, cols) for r in (q_ref, k_ref, v_ref)]):
            probs = softmax_t(k, q, same, scale).astype(bf16)
            outs.append(dot(v, probs, 1, 0))
        out_ref[0, :, cols] = jnp.concatenate(outs, axis=0).astype(bf16)


def attn_backward(dim, scale, row_ref, col_ref, q_ref, k_ref, v_ref, g_ref, out_ref):
    length = col_ref.shape[0]
    for s in range(row_ref.shape[0]):
        cols = slice(s * length, (s + 1) * length)
        same = row_ref[s : s + 1] == col_ref[:, s : s + 1]
        gq, gk, gv = [], [], []
        qs, ks, vs = [heads_of(r[0, 0], dim, cols) for r in (q_ref, k_ref, v_ref)]
        for q, k, v, g in zip(qs, ks, vs, heads_of(g_ref[0], dim, cols)):
            probs = softmax_t(k, q, same, scale)
            back = dot(v, g, 0, 0)
            back = probs * (back - jnp.sum(back * probs, axis=0, keepdims=True))
            back = back.astype(bf16)
            gq.append(dot(k, back, 1, 0) * scale)
            gk.append(dot(q, back, 1, 1) * scale)
            gv.append(dot(g, probs.astype(bf16), 1, 1))
        for n, parts in enumerate((gq, gk, gv)):
            out_ref[n, 0, :, cols] = jnp.concatenate(parts, axis=0).astype(bf16)


def attention(qkv, ids, dim, grad=None):
    _, groups, rows, tokens = qkv.shape
    scale = dim**-0.5
    ids_t = ids.T

    def one(n):
        return pl.BlockSpec((1, 1, rows, tokens), lambda i: (n, i, 0, 0))

    flat = pl.BlockSpec((1, rows, tokens), lambda i: (i, 0, 0))
    args = [ids, ids_t, qkv, qkv, qkv]
    specs = [pl.BlockSpec(a.shape, lambda i: (0, 0)) for a in (ids, ids_t)] + [one(0), one(1), one(2)]
    if grad is None:
        return pl.pallas_call(
            functools.partial(attn_forward, dim, scale),
            grid=(groups,),
            in_specs=specs,
            out_specs=flat,
            out_shape=jax.ShapeDtypeStruct((groups, rows, tokens), bf16),
            cost_estimate=tiny,
            compiler_params=pltpu.CompilerParams(vmem_limit_bytes=24 * MIB),
            name="attention",
        )(*args)
    return pl.pallas_call(
        functools.partial(attn_backward, dim, scale),
        grid=(groups,),
        in_specs=specs + [flat],
        out_specs=pl.BlockSpec((3, 1, rows, tokens), lambda i: (0, i, 0, 0)),
        out_shape=jax.ShapeDtypeStruct(qkv.shape, bf16),
        cost_estimate=tiny,
        compiler_params=pltpu.CompilerParams(vmem_limit_bytes=24 * MIB),
        name="attention_back",
    )(*args, grad)


def modulation_kernel(cond_ref, weight_ref, bias_ref, silu_ref, out_ref):
    cond = cond_ref[...].astype(f32)
    silu = (cond / (1.0 + jnp.exp(-cond))).astype(bf16)
    silu_ref[...] = silu
    out_ref[...] = (dot(silu, weight_ref[...], 1, 0) + bias_ref[...]).astype(bf16)


def modulate(cond, weight, bias):
    slots, width = cond.shape
    columns = weight.shape[1]
    tile = 384 if columns % 384 == 0 else columns
    return pl.pallas_call(
        modulation_kernel,
        grid=(columns // tile,),
        in_specs=[
            full(cond),
            pl.BlockSpec((width, tile), lambda i: (0, i)),
            pl.BlockSpec((1, tile), lambda i: (0, i)),
        ],
        out_specs=[full(cond), pl.BlockSpec((slots, tile), lambda i: (0, i))],
        out_shape=[
            jax.ShapeDtypeStruct((slots, width), bf16),
            jax.ShapeDtypeStruct((slots, columns), bf16),
        ],
        cost_estimate=tiny,
        compiler_params=pltpu.CompilerParams(vmem_limit_bytes=16 * MIB),
        name="modulate",
    )(cond, weight, bias)


def feed_forward_kernel(parts, *refs):
    own_ref, met_ref, b_ref = refs[:3]
    pieces = refs[3 : 3 + 2 * parts]
    act_ref, back_ref, column_ref, own_sums, other_sums = refs[3 + 2 * parts : 8 + 2 * parts]
    x, g, weights, acts, backs, total, ins, outs = refs[8 + 2 * parts :]
    half, units = own_ref.shape[1], pieces[0].shape[1]
    copy = pltpu.make_async_copy

    def load(n):
        slot, copies = n % 2, []
        for kind in range(2):
            for side in range(2):
                copies.append(
                    copy(
                        pieces[2 * n + side].at[kind],
                        weights.at[slot, kind, pl.ds(side * units, units)],
                        ins.at[4 + 4 * n + 2 * kind + side],
                    )
                )
        return copies

    low, high = pl.ds(0, half), pl.ds(half, half)
    inputs = [
        copy(own_ref.at[0], x.at[low], ins.at[0]),
        copy(met_ref.at[0], x.at[high], ins.at[1]),
        copy(own_ref.at[1], g.at[low], ins.at[2]),
        copy(met_ref.at[1], g.at[high], ins.at[3]),
    ]
    loads = [load(n) for n in range(parts)]
    for item in inputs[:2] + loads[0][:2] + inputs[2:] + loads[0][2:] + loads[1]:
        item.start()
    stores = []
    root = 0.7978845608028654
    for n in range(parts):
        slot = n % 2
        for item in (inputs[:2] if n == 0 else []) + loads[n][:2]:
            item.wait()
        hidden = dot(x[...], weights[slot, 0], 1, 1) + b_ref[n : n + 1]
        square = hidden * hidden
        tanh = jnp.tanh(root * hidden * (1.0 + 0.044715 * square))
        acts[n] = (0.5 * hidden * (1.0 + tanh)).astype(bf16)
        slope = 0.5 * (1.0 + tanh) + 0.5 * hidden * (1.0 - tanh * tanh) * (root * (1.0 + 0.134145 * square))
        stores.append(copy(acts.at[n], act_ref.at[n], outs.at[2 * n]))
        stores[-1].start()
        for item in (inputs[2:] if n == 0 else []) + loads[n][2:]:
            item.wait()
        back = (dot(g[...], weights[slot, 1], 1, 1) * slope).astype(bf16)
        backs[n] = back
        stores.append(copy(backs.at[n], back_ref.at[n], outs.at[2 * n + 1]))
        stores[-1].start()
        column_ref[n : n + 1] = jnp.sum(back.astype(f32), axis=0, keepdims=True)
        for m, value in enumerate((dot(acts[n], weights[slot, 1], 1, 0), dot(back, weights[slot, 0], 1, 0))):
            for k in range(2):
                rows = value[k * half : (k + 1) * half]
                total[k, m] = rows if n == 0 else total[k, m] + rows
        if n + 2 < parts:
            for item in loads[n + 2]:
                item.start()
    for k, ref in ((1, other_sums), (0, own_sums)):
        stores.append(copy(total.at[k], ref, outs.at[2 * parts + k]))
        stores[-1].start()
    for item in stores:
        item.wait()


def feed_forward(own_in, met_in, bias, pieces):
    _, tokens, width = own_in.shape
    parts, units = len(pieces) // 2, pieces[0].shape[1]
    column = jax.ShapeDtypeStruct((parts, 2 * units), f32)
    hidden = [jax.ShapeDtypeStruct((parts, 2 * tokens, 2 * units), bf16)] * 2
    sums = [jax.ShapeDtypeStruct((2, tokens, width), f32)] * 2
    dma = pltpu.SemaphoreType.DMA
    return pl.pallas_call(
        functools.partial(feed_forward_kernel, parts),
        grid=(1,),
        in_specs=[any_spec, any_spec, full(bias)] + [any_spec] * len(pieces),
        out_specs=[any_spec] * 2 + [full(column), any_spec, any_spec],
        out_shape=hidden + [column] + sums,
        scratch_shapes=[
            pltpu.VMEM((2 * tokens, width), bf16),
            pltpu.VMEM((2 * tokens, width), bf16),
            pltpu.VMEM((2, 2, 2 * units, width), bf16),
            pltpu.VMEM(hidden[0].shape, bf16),
            pltpu.VMEM(hidden[0].shape, bf16),
            pltpu.VMEM((2, 2, tokens, width), f32),
            dma((4 + 4 * parts,)),
            dma((2 * parts + 2,)),
        ],
        cost_estimate=tiny,
        compiler_params=pltpu.CompilerParams(vmem_limit_bytes=48 * MIB),
        name="feed_forward",
    )(own_in, met_in, bias, *pieces)


def fc_grad_kernel(parts, act_ref, back_ref, own_ref, met_ref, *refs):
    grads, (x, acts, backs, products, ins, outs) = refs[: 2 * parts], refs[2 * parts :]
    half, units = own_ref.shape[1], grads[0].shape[1]
    copy = pltpu.make_async_copy
    inputs = []
    for k, ref in enumerate((own_ref, met_ref)):
        for m in range(2):
            inputs.append(copy(ref.at[m], x.at[m, pl.ds(k * half, half)], ins.at[2 * k + m]))
    loads = [
        [
            copy(act_ref.at[n], acts.at[n], ins.at[4 + 2 * n]),
            copy(back_ref.at[n], backs.at[n], ins.at[5 + 2 * n]),
        ]
        for n in range(parts)
    ]
    for item in inputs + [item for pair in loads for item in pair]:
        item.start()
    stores = []
    for n in range(parts):
        for item in (inputs if n == 0 else []) + loads[n]:
            item.wait()
        if n >= 2:
            for item in stores[n - 2]:
                item.wait()
        stores.append([])
        for kind, left, right in ((0, backs, 0), (1, acts, 1)):
            products[n % 2, kind] = dot(left[n], x[right], 0, 0).astype(bf16)
            for side in range(2):
                stores[n].append(
                    copy(
                        products.at[n % 2, kind, pl.ds(side * units, units)],
                        grads[2 * n + side].at[kind],
                        outs.at[4 * n + 2 * kind + side],
                    )
                )
                stores[n][-1].start()
    for pair in stores[-2:]:
        for item in pair:
            item.wait()


def fc_grads_of(acts, backs, own_in, met_in):
    parts, tokens, columns = acts.shape
    width = own_in.shape[2]
    dma = pltpu.SemaphoreType.DMA
    return pl.pallas_call(
        functools.partial(fc_grad_kernel, parts),
        grid=(1,),
        in_specs=[any_spec] * 4,
        out_specs=[any_spec] * (2 * parts),
        out_shape=[jax.ShapeDtypeStruct((2, columns // 2, width), bf16)] * (2 * parts),
        scratch_shapes=[
            pltpu.VMEM((2, tokens, width), bf16),
            pltpu.VMEM(acts.shape, bf16),
            pltpu.VMEM(acts.shape, bf16),
            pltpu.VMEM((2, 2, columns, width), bf16),
            dma((4 + 2 * parts,)),
            dma((4 * parts,)),
        ],
        cost_estimate=tiny,
        compiler_params=pltpu.CompilerParams(vmem_limit_bytes=40 * MIB),
        name="fc_grads",
    )(acts, backs, own_in, met_in)


def on_device(
    tokens,
    cond,
    segment_ids,
    crop_slot,
    ada_weight,
    ada_bias,
    attn_weight,
    fc_in,
    fc_out,
    biases,
    out_grad,
):
    net = Net()
    tok_len, width = tokens.shape[1:]
    head_dim = width // HEADS
    mod_rank, core, chips = net.mod_rank, net.core, net.chips
    device_count = net.dp * net.mod
    crop_count = crop_slot.shape[1] // net.mod
    shard = attn_weight.shape[0]
    third = shard // 3
    chunks_of = [range(chips // 2), range(chips // 2, chips)]
    halves = [(n, side) for n in range(3) for side in range(2)]
    aligned = shard % (2 * head_dim) == 0 and third % 16 == 0 and width % (2 * net.mod * shard) == 0

    g_attn = Gather(net, attn_weight[None])
    g_fc = Gather(net, jnp.stack([fc_in, fc_out]))
    silu_cond, mod_own = modulate(cond, ada_weight, ada_bias.reshape(1, -1).astype(f32))
    for n in range(g_attn.count):
        g_attn.start()
        g_attn.got = [after(g_attn.got[0], mod_own)]
        g_attn.finish()
    g_attn.start()
    first = g_attn.value
    for n in range(g_fc.count):
        g_fc.start(*first).finish()
    g_attn.finish().start()
    g_attn.finish().start()
    third_phase = g_attn.value
    g_fc.start(*g_attn.got)
    attn_pieces = [(g_attn.value, g_attn.got)[side][n] for n, side in halves]

    mod_other = net.swap(after(mod_own, *first), "mod")
    modulation = jnp.concatenate(
        [jnp.where(mod_rank == 0, mod_own, mod_other), jnp.where(mod_rank == 0, mod_other, mod_own)], axis=1
    )
    seg_ids = segment_ids[0]
    slots = lax.dynamic_slice_in_dim(crop_slot[0], mod_rank * crop_count, crop_count)
    crop_onehot = seg_ids[:, None] == jnp.arange(crop_count, dtype=jnp.int32)[None, :]
    token_slot = jnp.sum(jnp.where(crop_onehot, slots[None, :], 0), axis=1)
    slot_pick = token_slot[:, None] == jnp.arange(cond.shape[0], dtype=jnp.int32)[None, :]
    slot_pick = slot_pick.astype(bf16)
    modulation = after(modulation, *third_phase)
    mods = [modulation[:, n * width : (n + 1) * width] for n in range(6)]
    shift_a, scale_a, gate_a, shift_m, scale_m, gate_m = [times(slot_pick, block) for block in mods]

    slot_count, own_cols = cond.shape[0], width // net.dp
    to_dp = jnp.moveaxis(silu_cond.reshape(slot_count, net.dp, own_cols), 1, 0).reshape(net.dp, 1, -1)
    to_all = jnp.broadcast_to(to_dp, (net.dp, net.mod, slot_count * own_cols)).reshape(device_count, -1)
    to_all = after(to_all, *third_phase)
    sent = jnp.concatenate([jnp.broadcast_to(biases[None], (device_count, biases.shape[0])), to_all], axis=1)
    met = lax.all_to_all(sent, ("dp", "mod"), split_axis=0, concat_axis=0, tiled=True)
    ada_order = list(range(2, net.bits)) + [1, 0]
    dp_order = net.ranks(ada_order, range(net.dp))[0]
    dp_pick = (dp_order[:, None] == jnp.arange(net.dp)[None, :]).astype(bf16)
    cond_cols = times(dp_pick, met.reshape(net.dp, net.mod, -1)[:, 0, biases.shape[0] :]).astype(bf16)
    cond_cols = cond_cols.reshape(-1, own_cols)
    bias_all = met[:, : biases.shape[0]].reshape(-1, width)
    bias_query, bias_value, bias_proj, bias_out = [bias_all[n].astype(f32) for n in range(4)]
    bias_in = bias_all[4:].reshape(device_count, 3, third)
    picks = []
    for n, side in halves:
        devices = net.devices(net.orders[n], chunks_of[side])
        picks.append((devices[:, None] == jnp.arange(device_count)[None, :]).astype(bf16))
    picks = jnp.stack(picks).reshape(3, 2, chips // 2, device_count)
    bias_pieces = jnp.einsum("nsjd,dnr->nsjr", picks, bias_in, preferred_element_type=f32).reshape(3, -1)

    def join(own, other):
        own, other = [a.reshape(-1, 1, net.mod * shard, a.shape[-1]) for a in (own, other)]
        both = jnp.where(core == 0, jnp.concatenate([own, other], 1), jnp.concatenate([other, own], 1))
        return both.reshape(-1, both.shape[-1])

    def part(whole):
        whole = whole.reshape(-1, 2, net.mod * shard, whole.shape[-1])
        return [
            jnp.where(core == c, whole[:, 0], whole[:, 1]).reshape(-1, whole.shape[-1]) for c in range(2)
        ]

    resid = tokens[0].astype(f32)
    normed_a, _ = layer_norm(resid)
    attn_in = (normed_a * (1.0 + scale_a) + shift_a).astype(bf16)
    if aligned:
        index = jnp.concatenate([net.local(net.orders[n], chunks_of[side]) * 3 + n for n, side in halves])
        own_weight = assemble(attn_pieces, index, third)
        qkv_rows = own_weight.shape[0] * 3 // 4
        qkv_weight = own_weight[:qkv_rows]
        proj_own = own_weight[qkv_rows:]
        proj_weight = join(proj_own, net.swap(proj_own, 0))
        ids = jnp.stack([seg_ids, net.swap(seg_ids, 0)])
        attn_in = after(attn_in, *third_phase)
        attn_both = jnp.concatenate([attn_in, net.swap(attn_in, 0)], axis=0)
        own_query, own_value = part(bias_query[:, None])[0], part(bias_value[:, None])[0]
        qkv_bias = jnp.concatenate([own_query, jnp.zeros_like(own_query), own_value], axis=0)
        attn_both = after(attn_both, *g_fc.got)
        g_fc.finish().start()
        qkv = (times_rows(qkv_weight, attn_both) + qkv_bias).astype(bf16)
        qkv = qkv.reshape(3, -1, 2 * head_dim, 2 * tok_len)
        context_both = attention(qkv, ids, head_dim).reshape(-1, 2 * tok_len)
        context = join(context_both[:, :tok_len], net.swap(context_both[:, tok_len:], 0))
        attn_out = dot(context, proj_weight, 0, 1) + bias_proj
    else:
        arrays = attn_pieces + [net.swap(piece, 0) for piece in attn_pieces]
        places = jnp.concatenate(
            [net.devices(net.orders[n], chunks_of[side], c) * 3 + n for c in range(2) for n, side in halves]
        )
        spread = jnp.concatenate(arrays, axis=1)[0]

        def place(n, whole):
            block = lax.dynamic_slice_in_dim(spread, n * third, third)
            return lax.dynamic_update_slice_in_dim(whole, block, places[n] * third, 0)

        attn_w = lax.fori_loop(0, places.shape[0], place, jnp.zeros_like(spread))
        g_fc.finish().start()
        g_fc.finish().start()
        qkv_weight, proj_weight = attn_w[: 3 * width], attn_w[3 * width :]
        qkv_bias = jnp.concatenate([bias_query, jnp.zeros_like(bias_query), bias_value])
        qkv = (times_rows(qkv_weight, attn_in) + qkv_bias[:, None]).astype(bf16)
        qkv = qkv.reshape(3, -1, 2 * head_dim, tok_len)
        context = attention(qkv, seg_ids[None], head_dim).reshape(-1, tok_len)
        attn_out = dot(context, proj_weight, 0, 1) + bias_proj
    mid = resid + gate_a * attn_out
    normed_m, _ = layer_norm(mid)
    mlp_in = (normed_m * (1.0 + scale_m) + shift_m).astype(bf16)
    if aligned:
        mlp_in = after(mlp_in, *g_fc.got)
        g_fc.finish().start()
    grad_mlp = (gate_m * out_grad[0].astype(f32)).astype(bf16)

    mlp_own = jnp.stack([mlp_in, grad_mlp])
    mlp_met = net.swap(mlp_own, 0)
    grad_bias_out = jnp.sum(grad_mlp.astype(f32), axis=0, keepdims=True)
    fc_pieces = [(g_fc.value, g_fc.got)[side][n] for n, side in halves]
    acts, backs, columns, own_sums, other_sums = feed_forward(mlp_own, mlp_met, bias_pieces, fc_pieces)
    sums_met = net.swap(other_sums, 0)
    fc_grads = fc_grads_of(acts, backs, mlp_own, mlp_met)
    sums_met = after(sums_met, *fc_grads)
    back_way = Scatter(net, fc_grads[0::2], fc_grads[1::2])

    grad_mid, grad_attn, grad_bias_proj, *parts = middle(
        core,
        net.mod * shard if aligned else None,
        own_sums,
        sums_met,
        mid,
        out_grad[0],
        slot_pick,
        modulation,
        proj_weight,
        context,
    )
    if aligned:
        mine, other, proj_mine, proj_other = parts
        context_grads = jnp.concatenate([mine, net.swap(other, 0)], axis=1)
        proj_met = net.swap(after(proj_other, context_grads), 0)
        grad_qkv = attention(qkv, ids, head_dim, context_grads.reshape(-1, 2 * head_dim, 2 * tok_len))
        grad_qkv = grad_qkv.reshape(-1, 2 * tok_len)
        back_both = contract_rows(grad_qkv, qkv_weight)
        back_own, back_met = back_both[:tok_len], net.swap(back_both[tok_len:], 0)
        grad_qkv, *back_way.got = lax.optimization_barrier((grad_qkv, *back_way.got, back_own))[:-1]
        places = jnp.sum(
            jnp.where(
                index[None, :] == jnp.arange(index.shape[0], dtype=index.dtype)[:, None],
                jnp.arange(index.shape[0], dtype=index.dtype)[None, :],
                0,
            ),
            axis=1,
        )
        pieces = weight_grad(grad_qkv, attn_both, proj_mine, proj_met, places, third)
        back_met, grad_qkv = lax.optimization_barrier((back_met, grad_qkv, pieces))[:2]
        rows_each = pieces.shape[0] // 6
        pieces = [pieces[None, n * rows_each : (n + 1) * rows_each] for n in range(6)]
        column = jnp.sum(grad_qkv.astype(f32), axis=1, keepdims=True).reshape(3, -1, 1)
        none = jnp.zeros_like(column[0])
        grad_bias_query, grad_bias_value = join(column[0], none)[:, 0], join(column[2], none)[:, 0]
    else:
        grad_context, grad_proj = parts
        grad_qkv = attention(
            qkv, seg_ids[None], head_dim, grad_context.reshape(-1, 2 * head_dim, tok_len)
        ).reshape(-1, tok_len)
        attn_grad = jnp.concatenate([times(grad_qkv, attn_in).astype(bf16), grad_proj], axis=0)

        def take(n, whole):
            block = lax.dynamic_slice_in_dim(attn_grad, places[n] * third, third)
            return lax.dynamic_update_slice_in_dim(whole, block, n * third, 0)

        grads = lax.fori_loop(0, places.shape[0], take, jnp.zeros_like(attn_grad))
        grads = jnp.split(grads[None], 12, axis=1)
        pieces = [summed(a, net.swap(b, 0)) for a, b in zip(grads[:6], grads[6:])]
        back_own = contract_rows(grad_qkv, qkv_weight)
        back_met = jnp.zeros_like(back_own)
        column = jnp.sum(grad_qkv.astype(f32), axis=1).reshape(3, -1)
        grad_bias_query, grad_bias_value = column[0], column[2]
    grad_tokens, pair_a = end_call(
        attn_end_kernel, f32, slot_count, back_own, back_met, tokens[0], grad_mid, attn_out, slot_pick, modulation
    )
    result, pair_m = end_call(
        mlp_end_kernel,
        bf16,
        slot_count,
        mid,
        own_sums,
        sums_met,
        bias_out[None],
        out_grad[0],
        slot_pick,
        modulation,
    )
    columns = columns.reshape(3, 2, chips // 2, third)
    grad_bias_in = jnp.einsum("nsjd,nsjr->dnr", picks.astype(f32), columns, precision=lax.Precision.HIGHEST)
    grad_bias = stack_rows(
        grad_bias_query[None],
        grad_bias_value[None],
        grad_bias_proj,
        grad_bias_out,
        grad_bias_in.reshape(-1, width),
    )
    bias_rows = lax.all_to_all(
        grad_bias.reshape(device_count, -1), ("dp", "mod"), split_axis=0, concat_axis=0, tiled=True
    )
    bias_sum = jnp.sum(bias_rows, axis=0)

    pair_own = jnp.where(mod_rank == 0, pair_a, pair_m)
    pair_send = jnp.where(mod_rank == 0, pair_m, pair_a)
    grad_mod = summed(pair_own, net.swap(pair_send, "mod"))
    back_way.got = list(lax.optimization_barrier((*back_way.got, grad_mod))[:3])
    back_way.join(pieces[0::2], pieces[1::2])
    grad_silu = times_rows(grad_mod, ada_weight)
    silu_own = jnp.where(mod_rank == 0, grad_silu[:crop_count], grad_silu[crop_count:])
    silu_send = jnp.where(mod_rank == 0, grad_silu[crop_count:], grad_silu[:crop_count])
    silu_send, mod_rows = lax.optimization_barrier((silu_send.astype(bf16), grad_mod, *back_way.got))[:2]
    silu_met = net.swap(silu_send, "mod")
    grad_silu = silu_own + silu_met.astype(f32)
    own_cond = lax.dynamic_slice_in_dim(cond, mod_rank * crop_count, crop_count, 0).astype(f32)
    silu_back = jax.vjp(jax.nn.silu, own_cond)[1]
    grad_cond = silu_back(grad_silu)[0]
    for step, dim in enumerate(ada_order):
        mod_rows = jnp.concatenate([mod_rows, net.swap(mod_rows, dim)], axis=0)
        if step == 0:
            back_way.got = list(lax.optimization_barrier((*back_way.got, mod_rows, silu_met))[:3])
            back_way.second()
            mod_rows = after(mod_rows, *back_way.got)
        if step == 1:
            back_way.got = list(lax.optimization_barrier((*back_way.got, mod_rows))[:3])
            fc_sum, attn_sum = back_way.third()
    ada_w_sum = contract_rows(cond_cols, mod_rows)
    ada_b_sum = jnp.sum(mod_rows.astype(f32), axis=0).reshape(ada_bias.shape[0], width)
    ada_b_sum = lax.dynamic_slice_in_dim(ada_b_sum, net.dp_rank * own_cols, own_cols, 1)
    return (
        result[None],
        grad_tokens[None],
        grad_cond,
        ada_w_sum,
        ada_b_sum,
        attn_sum[0],
        fc_sum[0],
        fc_sum[1],
        bias_sum,
    )


def solution(mesh):
    placed = (
        P(("dp", "mod"), None, None),
        P("dp", None),
        P(("dp", "mod"), None),
        P("dp", None),
        P(None, "mod"),
        P("mod", None),
        P(("dp", "mod"), None),
        P(("dp", "mod"), None),
        P(("dp", "mod"), None),
        P(("dp", "mod")),
        P(("dp", "mod"), None, None),
    )
    return jax.shard_map(
        on_device,
        mesh=mesh,
        in_specs=placed,
        out_specs=(
            P(("dp", "mod"), None, None),
            P(("dp", "mod"), None, None),
            P(("dp", "mod"), None),
            P("dp", "mod"),
            P("mod", "dp"),
            P(("dp", "mod"), None),
            P(("dp", "mod"), None),
            P(("dp", "mod"), None),
            P(("dp", "mod")),
        ),
        check_vma=False,
    )
```

```python
import functools

import jax
import jax.numpy as jnp
import numpy as np
from jax import lax
from jax.experimental import pallas as pl
from jax.experimental.pallas import tpu as pltpu
from jax.sharding import PartitionSpec as P

HEADS = 16
norm_eps = 1e-06
bf16 = jnp.bfloat16
f32 = jnp.float32
MIB = 1024 * 1024


def layer_norm(values):
    center = values - jnp.mean(values, axis=-1, keepdims=True)
    inverse = lax.rsqrt(jnp.mean(center * center, axis=-1, keepdims=True) + norm_eps)
    return (center * inverse, inverse)


def norm_back(grad_in, normed, inverse):
    centered = grad_in - jnp.mean(grad_in, axis=-1, keepdims=True)
    return (centered - normed * jnp.mean(grad_in * normed, axis=-1, keepdims=True)) * inverse


def dot(left, right, left_dim, right_dim):
    return lax.dot_general(left, right, (((left_dim,), (right_dim,)), ((), ())), preferred_element_type=f32)


def times(left, right):
    return dot(left, right, 1, 0)


def times_rows(left, right):
    return dot(left, right, 1, 1)


def contract_rows(left, right):
    return dot(left, right, 0, 0)


def after(value, *others):
    return lax.optimization_barrier((value, *others))[0]


def summed(left, right):
    return (left.astype(f32) + right.astype(f32)).astype(bf16)


class Net:
    def __init__(self):
        self.dp = lax.axis_size("dp")
        self.mod = lax.axis_size("mod")
        self.bits = self.dp.bit_length() - 1
        self.dp_rank = lax.axis_index("dp")
        self.mod_rank = lax.axis_index("mod")
        self.core = self.dp_rank & 1
        self.chips = self.dp // 2 * self.mod
        self.lead = list(range(self.bits - 1, 2, -1))
        last = ["mod", 1, 2]
        self.turns = [last[n:] + last[:n] for n in range(3)]
        self.orders = [self.lead + turn for turn in self.turns]

    def swap(self, value, dim):
        if dim == "mod":
            return lax.ppermute(value, "mod", [(i, i ^ 1) for i in range(self.mod)])
        return lax.ppermute(value, "dp", [(i, i ^ (1 << dim)) for i in range(self.dp)])

    def ranks(self, order, chunks, core=0):
        masks = []
        for j in chunks:
            dp_mask, mod_mask = core, 0
            for step, dim in enumerate(order):
                if j >> step & 1:
                    if dim == "mod":
                        mod_mask ^= 1
                    else:
                        dp_mask ^= 1 << dim
            masks.append((dp_mask, mod_mask))
        masks = np.array(masks, np.int32)
        return self.dp_rank ^ masks[:, 0], self.mod_rank ^ masks[:, 1]

    def devices(self, order, chunks, core=0):
        dp, mod = self.ranks(order, chunks, core)
        return dp * self.mod + mod

    def local(self, order, chunks):
        dp, mod = self.ranks(order, chunks)
        return (dp >> 1) * self.mod + mod


class Gather:
    def __init__(self, net, shard):
        self.net, self.count = net, len(net.lead)
        self.third = shard.shape[1] // 3
        self.value, self.got, self.phase = shard, None, 0

    def start(self, *others):
        net, phase = self.net, self.phase
        if phase < self.count:
            self.value = after(self.value, *others) if others else self.value
            self.got = [net.swap(self.value, net.lead[phase])]
        else:
            if phase == self.count:
                kinds, _, width = self.value.shape
                whole = self.value.reshape(kinds, -1, 3, self.third, width)
                self.value = [whole[:, :, n].reshape(kinds, -1, width) for n in range(3)]
            if others:
                self.value = list(lax.optimization_barrier((*self.value, *others))[:3])
            step = phase - self.count
            self.got = [net.swap(self.value[n], net.turns[n][step]) for n in range(3)]
        self.phase += 1
        return self

    def finish(self):
        if self.phase <= self.count:
            self.value = jnp.concatenate([self.value, self.got[0]], axis=1)
        elif self.phase < self.count + 3:
            self.value = [jnp.concatenate(pair, axis=1) for pair in zip(self.value, self.got)]
        return self


any_spec = pl.BlockSpec(memory_space=pl.ANY)


def full(value):
    return pl.BlockSpec(value.shape, lambda *_: (0,) * len(value.shape))

tiny = pl.CostEstimate(flops=1024, bytes_accessed=1024, transcendentals=0)


def run_copies(copies):
    for copy in copies:
        copy.start()
    for copy in copies:
        copy.wait()


def assemble_kernel(rows, each, index_ref, *refs):
    pieces, out_ref, hold, sems, last = refs[:-4], *refs[-4:]
    copies = []
    for n, piece in enumerate(pieces):
        for j in range(each):
            at = pl.multiple_of(index_ref[n * each + j] * rows, rows)
            copies.append(
                pltpu.make_async_copy(
                    piece.at[0, pl.ds(j * rows, rows)], hold.at[pl.ds(at, rows)], sems.at[n * each + j]
                )
            )
    run_copies(copies)
    run_copies([pltpu.make_async_copy(hold, out_ref, last)])


def assemble(pieces, index, rows):
    each, width = pieces[0].shape[1] // rows, pieces[0].shape[2]
    total = len(pieces) * each
    return pl.pallas_call(
        functools.partial(assemble_kernel, rows, each),
        grid_spec=pltpu.PrefetchScalarGridSpec(
            num_scalar_prefetch=1,
            grid=(1,),
            in_specs=[any_spec] * len(pieces),
            out_specs=any_spec,
            scratch_shapes=[
                pltpu.VMEM((total * rows, width), bf16),
                pltpu.SemaphoreType.DMA((total,)),
                pltpu.SemaphoreType.DMA,
            ],
        ),
        out_shape=jax.ShapeDtypeStruct((total * rows, width), bf16),
        compiler_params=pltpu.CompilerParams(vmem_limit_bytes=10 * MIB),
        name="assemble",
    )(index, *pieces)


def added(left, right):
    return (left.astype(f32) + right.astype(f32)).astype(bf16)


def sums_call(kernel, grid, in_specs, out_specs, outs, *args):
    return pl.pallas_call(
        kernel,
        grid=grid,
        in_specs=in_specs,
        out_specs=out_specs,
        out_shape=[jax.ShapeDtypeStruct(out, bf16) for out in outs],
        cost_estimate=tiny,
        compiler_params=pltpu.CompilerParams(vmem_limit_bytes=24 * MIB),
        name=kernel.__name__,
    )(*args)


def first_sums(own_low, own_high, got_low, got_high, also, keep, send):
    keep[...] = added(own_low[...], got_low[...])
    send[:2] = added(own_high[...], got_high[...])
    send[2:] = also[...]


def second_sums(own, got, also, keep, also_keep, send):
    half = keep.shape[1]
    keep[...] = added(own[:, :half], got[:2, :half])
    send[:2] = added(own[:, half:], got[:2, half:])
    also_keep[0] = added(also[0], got[2])
    other = added(also[1], got[3])
    send[2] = other[:half]
    send[3] = other[half:]


def third_sums(*refs):
    ins, outs = refs[:9], refs[9:]
    split = len(outs) == 8
    for n in range(3):
        own, got, also = ins[3 * n : 3 * n + 3]
        half = own.shape[1]
        total = added(own[...], got[:2])
        if split:
            rows = half // 2
            outs[0][:, n * rows : (n + 1) * rows] = total[:, :rows]
            outs[1][:, n * rows : (n + 1) * rows] = total[:, rows:]
        else:
            outs[n][...] = total
        outs[2 * n - 6][0] = added(also[0, :half], got[2])
        outs[2 * n - 5][0] = added(also[0, half:], got[3])


def fourth_sums(*refs):
    keep, send = refs[6:]
    rows = keep.shape[1] // 3
    for n in range(3):
        total = added(refs[n][0], refs[3 + n][0])
        keep[0, n * rows : (n + 1) * rows] = total[:rows]
        send[0, n * rows : (n + 1) * rows] = total[rows:]


class Scatter:
    def __init__(self, net, own, other):
        self.net = net
        self.own = list(own)
        self.got = [net.swap(other[n], net.turns[n][2]) for n in range(3)]
        self.aligned = len(net.lead) == 1 and own[0].shape[1] // 8 % 16 == 0

    def hold(self, n, *others):
        self.got[n] = after(self.got[n], *others)

    def join(self, n, pieces):
        _, rows, width = self.own[n].shape
        half = rows // 2
        step = half // 4
        also = 2 * ((n + 2) % 3)
        self.pieces = pieces.reshape(12, half, width)
        block = (2, step, width)
        low, high = pl.BlockSpec(block, lambda i: (0, i, 0)), pl.BlockSpec(block, lambda i: (0, i + 4, 0))
        self.own[n], send = sums_call(
            first_sums,
            (4,),
            [low, high, low, high, pl.BlockSpec(block, lambda i: (also + 1, i, 0))],
            [low, pl.BlockSpec((4, step, width), lambda i: (0, i, 0))],
            [(2, half, width), (4, half, width)],
            self.own[n],
            self.own[n],
            self.got[n],
            self.got[n],
            self.pieces,
        )
        self.got[n] = self.net.swap(send, self.net.turns[n][1])

    def second(self, n, also):
        _, rows, width = self.own[n].shape
        half = rows // 2
        piece = 2 * ((n + 2) % 3)
        outs = [(2, half, width), (1, rows, width), (4, half, width)]
        self.own[n], also[n], send = sums_call(
            second_sums,
            (1,),
            [full(self.own[n]), full(self.got[n]), pl.BlockSpec((2, rows, width), lambda i: (piece, 0, 0))],
            [full(jax.ShapeDtypeStruct(out, bf16)) for out in outs],
            outs,
            self.own[n],
            self.got[n],
            self.pieces,
        )
        self.got[n] = self.net.swap(send, self.net.turns[n][0])

    def third(self, also):
        net = self.net
        _, rows, width = self.own[0].shape
        args = [a for n in range(3) for a in (self.own[n], self.got[n], also[n])]
        if self.aligned:
            outs = [(2, rows // 2 * 3, width)] * 2
        else:
            outs = [(2, rows, width)] * 3
        count = len(outs)
        outs = outs + [(1, rows, width)] * 6
        results = sums_call(
            third_sums,
            (1,),
            [full(a) for a in args],
            [full(jax.ShapeDtypeStruct(out, bf16)) for out in outs],
            outs,
            *args,
        )
        also, send = results[count::2], results[count + 1 :: 2]
        self.also = also
        self.also_got = [net.swap(send[n], net.turns[(n + 2) % 3][0]) for n in range(3)]
        if self.aligned:
            self.fc = results[0], net.swap(results[1], net.lead[0])
        else:
            whole = self.together(results[:3])
            self.fc = self.lead(whole, len(net.lead) - 1)

    def last(self):
        net = self.net
        order = (1, 2, 0)
        keep, got = [self.also[n] for n in order], [self.also_got[n] for n in order]
        if self.aligned:
            _, rows, width = keep[0].shape
            outs = [(1, rows // 2 * 3, width)] * 2
            own, send = sums_call(
                fourth_sums,
                (1,),
                [full(a) for a in keep + got],
                [full(jax.ShapeDtypeStruct(out, bf16)) for out in outs],
                outs,
                *keep,
                *got,
            )
            attn = own, net.swap(send, net.lead[0])
        else:
            attn = self.lead(self.together([summed(a, b) for a, b in zip(keep, got)]), len(net.lead) - 1)
        sums = []
        for own, got in (self.fc, attn):
            for step in range(len(net.lead) - 1, -1, -1):
                total = own.astype(f32) + got.astype(f32)
                if step:
                    own, got = self.lead(total.astype(bf16), step - 1)
            sums.append(total)
        return sums

    def together(self, parts):
        kinds, _, width = parts[0].shape
        count = 1 << len(self.net.lead)
        return jnp.concatenate([p.reshape(kinds, count, -1, width) for p in parts], axis=2).reshape(kinds, -1, width)

    def lead(self, whole, step):
        half = whole.shape[1] // 2
        return whole[:, :half], self.net.swap(whole[:, half:], self.net.lead[step])


def attn_in_kernel(grad_ref, weight_ref, own_ref, other_ref):
    total = dot(grad_ref[...], weight_ref[...], 0, 0)
    half = own_ref.shape[0]
    own_ref[...] = total[:half]
    other_ref[...] = total[half:]


def attn_in_grads(grad, weight):
    rows, tokens = grad.shape
    width = weight.shape[1]
    out = jax.ShapeDtypeStruct((tokens // 2, width), f32)
    return pl.pallas_call(
        attn_in_kernel,
        grid=(1,),
        in_specs=[full(grad), pl.BlockSpec((rows, width), lambda i: (0, 0))],
        out_specs=[full(out)] * 2,
        out_shape=[out] * 2,
        cost_estimate=tiny,
        compiler_params=pltpu.CompilerParams(vmem_limit_bytes=40 * MIB),
        name="attn_in_grads",
    )(grad, weight)


def weight_grad_kernel(rows, place_ref, grad_ref, x_ref, mine_ref, other_ref, out_ref, hold, sems):
    top, copies = grad_ref.shape[0], []
    step = top // 3
    for n in (3, 0, 1, 2):
        start = n * step
        stop = min(start + step, hold.shape[0])
        if n == 3:
            hold[start:] = summed(mine_ref[...], other_ref[...])
        else:
            hold[start:stop] = dot(grad_ref[start:stop], x_ref[...], 1, 0).astype(bf16)
        for unit in range(start // rows, stop // rows):
            at = pl.multiple_of(place_ref[unit] * rows, rows)
            copies.append(
                pltpu.make_async_copy(
                    hold.at[pl.ds(unit * rows, rows)], out_ref.at[pl.ds(at, rows)], sems.at[unit]
                )
            )
            copies[-1].start()
    for copy in copies:
        copy.wait()


def weight_grad(grad, x, mine, other, places, rows):
    total, width = grad.shape[0] + mine.shape[0], x.shape[1]
    return pl.pallas_call(
        functools.partial(weight_grad_kernel, rows),
        grid_spec=pltpu.PrefetchScalarGridSpec(
            num_scalar_prefetch=1,
            grid=(1,),
            in_specs=[full(a) for a in (grad, x, mine, other)],
            out_specs=any_spec,
            scratch_shapes=[pltpu.VMEM((total, width), bf16), pltpu.SemaphoreType.DMA((total // rows,))],
        ),
        out_shape=jax.ShapeDtypeStruct((total, width), bf16),
        cost_estimate=tiny,
        compiler_params=pltpu.CompilerParams(vmem_limit_bytes=32 * MIB),
        name="weight_grad",
    )(places, grad, x, mine, other)


def by_core(core_ref, group, whole):
    if group is None:
        return [whole]
    picked = []
    for c in range(2):
        rows = []
        for at in range(0, whole.shape[0], 2 * group):
            first, second = whole[at : at + group], whole[at + group : at + 2 * group]
            rows.append(jnp.where(core_ref[0] == c, first, second))
        picked.append(jnp.concatenate(rows, axis=0))
    return picked


def token_block(pick, mods, n):
    width = mods.shape[1] // 6
    return dot(pick[...], mods[:, n * width : (n + 1) * width], 1, 0)


def middle_kernel(group, core_ref, *refs):
    sums, met, mid, grad_out, pick, mods, weight, context = refs[:8]
    mid_ref, attn_ref, column_ref = refs[8:11]
    normed, inverse = layer_norm(mid[...])
    back = (sums[1] + met[1]) * (1.0 + token_block(pick, mods, 4))
    grad_mid = grad_out[...].astype(f32) + norm_back(back, normed, inverse)
    mid_ref[...] = grad_mid
    grad_attn = (token_block(pick, mods, 2) * grad_mid).astype(bf16)
    attn_ref[...] = grad_attn
    column_ref[...] = jnp.sum(grad_attn.astype(f32), axis=0, keepdims=True)
    parts = by_core(core_ref, group, dot(weight[...], grad_attn, 0, 1))
    parts += by_core(core_ref, group, dot(grad_attn, context[...], 0, 1))
    for ref, value in zip(refs[11:], parts):
        ref[...] = value.astype(bf16)


def middle(core, group, *args):
    _, tokens, width = args[0].shape
    if group is None:
        sizes = [(width, tokens), (width, width)]
    else:
        sizes = [(width // 2, tokens)] * 2 + [(width // 2, width)] * 2
    outs = [((tokens, width), f32), ((tokens, width), bf16), ((1, width), f32)] + [(s, bf16) for s in sizes]
    outs = [jax.ShapeDtypeStruct(*out) for out in outs]
    return pl.pallas_call(
        functools.partial(middle_kernel, group),
        grid=(1,),
        in_specs=[pl.BlockSpec(memory_space=pltpu.SMEM)] + [full(a) for a in args],
        out_specs=[full(a) for a in outs],
        out_shape=outs,
        cost_estimate=tiny,
        compiler_params=pltpu.CompilerParams(vmem_limit_bytes=40 * MIB),
        name="middle",
    )(core.reshape(1), *args)


def slot_sums(pick, blocks, out_ref):
    for n, block in enumerate(blocks):
        high = block.astype(bf16)
        low = (block - high.astype(f32)).astype(bf16)
        total = dot(pick, high, 0, 0) + dot(pick, low, 0, 0)
        out_ref[:, n * block.shape[1] : (n + 1) * block.shape[1]] = total.astype(bf16)


def mlp_end_kernel(*refs):
    mid, sums, met, bias, grad_out, pick, mods = refs[:7]
    result_ref, pair_ref = refs[7:]
    mlp_out = sums[0] + met[0] + bias[...]
    result_ref[...] = (mid[...] + token_block(pick, mods, 5) * mlp_out).astype(bf16)
    back = sums[1] + met[1]
    slot_sums(pick[...], (back, back * layer_norm(mid[...])[0], grad_out[...].astype(f32) * mlp_out), pair_ref)


def attn_end_kernel(*refs):
    back_a, back_b, resid, grad_mid, attn_out, pick, mods = refs[:7]
    tokens_ref, pair_ref = refs[7:]
    back = back_a[...] + back_b[...]
    normed, inverse = layer_norm(resid[...].astype(f32))
    slope = back * (1.0 + token_block(pick, mods, 1))
    tokens_ref[...] = grad_mid[...] + norm_back(slope, normed, inverse)
    slot_sums(pick[...], (back, back * normed, grad_mid[...] * attn_out[...]), pair_ref)


def end_call(kernel, dtype, slots, *args):
    tokens, width = args[0].shape
    outs = [jax.ShapeDtypeStruct((tokens, width), dtype), jax.ShapeDtypeStruct((slots, 3 * width), bf16)]
    return pl.pallas_call(
        kernel,
        grid=(1,),
        in_specs=[full(a) for a in args],
        out_specs=[full(a) for a in outs],
        out_shape=outs,
        cost_estimate=tiny,
        compiler_params=pltpu.CompilerParams(vmem_limit_bytes=32 * MIB),
        name=kernel.__name__,
    )(*args)


def rows_kernel(*refs):
    at = 0
    for ref in refs[:-1]:
        refs[-1][at : at + ref.shape[0]] = ref[...]
        at += ref.shape[0]


def stack_rows(*args):
    out = jax.ShapeDtypeStruct((sum(a.shape[0] for a in args), args[0].shape[1]), f32)
    return pl.pallas_call(
        rows_kernel,
        grid=(1,),
        in_specs=[full(a) for a in args],
        out_specs=full(out),
        out_shape=out,
        cost_estimate=tiny,
        name="stack_rows",
    )(*args)


def softmax_t(key, query, same, scale):
    scores = jnp.where(same, dot(key, query, 0, 0) * scale, -1e30)
    weights = jnp.exp(scores - jnp.max(scores, axis=0, keepdims=True))
    return weights * (1.0 / jnp.sum(weights, axis=0, keepdims=True))


def heads_of(block, dim, cols):
    wide = block[:, cols].astype(f32)
    return [wide[n * dim : (n + 1) * dim].astype(bf16) for n in range(wide.shape[0] // dim)]


def attn_forward(dim, scale, row_ref, col_ref, q_ref, k_ref, v_ref, out_ref):
    length = col_ref.shape[0]
    for s in range(row_ref.shape[0]):
        cols = slice(s * length, (s + 1) * length)
        same = row_ref[s : s + 1] == col_ref[:, s : s + 1]
        outs = []
        for q, k, v in zip(*[heads_of(r[0, 0], dim, cols) for r in (q_ref, k_ref, v_ref)]):
            probs = softmax_t(k, q, same, scale).astype(bf16)
            outs.append(dot(v, probs, 1, 0))
        out_ref[0, :, cols] = jnp.concatenate(outs, axis=0).astype(bf16)


def attn_backward(dim, scale, row_ref, col_ref, q_ref, k_ref, v_ref, *refs):
    length, out_ref = col_ref.shape[0], refs[-1]
    for s in range(row_ref.shape[0]):
        cols = slice(s * length, (s + 1) * length)
        same = row_ref[s : s + 1] == col_ref[:, s : s + 1]
        gq, gk, gv = [], [], []
        qs, ks, vs = [heads_of(r[0, 0], dim, cols) for r in (q_ref, k_ref, v_ref)]
        for q, k, v, g in zip(qs, ks, vs, heads_of(refs[s][0], dim, slice(0, length))):
            probs = softmax_t(k, q, same, scale)
            back = dot(v, g, 0, 0)
            back = probs * (back - jnp.sum(back * probs, axis=0, keepdims=True))
            back = back.astype(bf16)
            gq.append(dot(k, back, 1, 0) * scale)
            gk.append(dot(q, back, 1, 1) * scale)
            gv.append(dot(g, probs.astype(bf16), 1, 1))
        for n, parts in enumerate((gq, gk, gv)):
            out_ref[n, 0, :, cols] = jnp.concatenate(parts, axis=0).astype(bf16)


def attention(qkv, ids, dim, grad=None):
    _, groups, rows, tokens = qkv.shape
    scale = dim**-0.5
    ids_t = ids.T

    def one(n):
        return pl.BlockSpec((1, 1, rows, tokens), lambda i: (n, i, 0, 0))

    flat = pl.BlockSpec((1, rows, tokens), lambda i: (i, 0, 0))
    short = pl.BlockSpec((1, rows, ids.shape[1]), lambda i: (i, 0, 0))
    args = [ids, ids_t, qkv, qkv, qkv]
    specs = [pl.BlockSpec(a.shape, lambda i: (0, 0)) for a in (ids, ids_t)] + [one(0), one(1), one(2)]
    if grad is None:
        return pl.pallas_call(
            functools.partial(attn_forward, dim, scale),
            grid=(groups,),
            in_specs=specs,
            out_specs=flat,
            out_shape=jax.ShapeDtypeStruct((groups, rows, tokens), bf16),
            cost_estimate=tiny,
            compiler_params=pltpu.CompilerParams(vmem_limit_bytes=24 * MIB),
            name="attention",
        )(*args)
    return pl.pallas_call(
        functools.partial(attn_backward, dim, scale),
        grid=(groups,),
        in_specs=specs + [short] * len(grad),
        out_specs=pl.BlockSpec((3, 1, rows, tokens), lambda i: (0, i, 0, 0)),
        out_shape=jax.ShapeDtypeStruct(qkv.shape, bf16),
        cost_estimate=tiny,
        compiler_params=pltpu.CompilerParams(vmem_limit_bytes=24 * MIB),
        name="attention_back",
    )(*args, *grad)


def modulation_kernel(cond_ref, weight_ref, bias_ref, silu_ref, out_ref):
    cond = cond_ref[...].astype(f32)
    silu = (cond / (1.0 + jnp.exp(-cond))).astype(bf16)
    silu_ref[...] = silu
    out_ref[...] = (dot(silu, weight_ref[...], 1, 0) + bias_ref[...]).astype(bf16)


def modulate(cond, weight, bias):
    slots, width = cond.shape
    columns = weight.shape[1]
    tile = 384 if columns % 384 == 0 else columns
    return pl.pallas_call(
        modulation_kernel,
        grid=(columns // tile,),
        in_specs=[
            full(cond),
            pl.BlockSpec((width, tile), lambda i: (0, i)),
            pl.BlockSpec((1, tile), lambda i: (0, i)),
        ],
        out_specs=[full(cond), pl.BlockSpec((slots, tile), lambda i: (0, i))],
        out_shape=[
            jax.ShapeDtypeStruct((slots, width), bf16),
            jax.ShapeDtypeStruct((slots, columns), bf16),
        ],
        cost_estimate=tiny,
        compiler_params=pltpu.CompilerParams(vmem_limit_bytes=16 * MIB),
        name="modulate",
    )(cond, weight, bias)


def feed_forward_kernel(parts, *refs):
    own_ref, met_ref, b_ref = refs[:3]
    pieces = refs[3 : 3 + 2 * parts]
    act_ref, back_ref, column_ref, own_sums, other_sums = refs[3 + 2 * parts : 8 + 2 * parts]
    x, g, weights, acts, backs, total, ins, outs = refs[8 + 2 * parts :]
    half, units = own_ref.shape[1], pieces[0].shape[1]
    copy = pltpu.make_async_copy

    def load(n):
        slot, copies = n % 2, []
        for kind in range(2):
            for side in range(2):
                copies.append(
                    copy(
                        pieces[2 * n + side].at[kind],
                        weights.at[slot, kind, pl.ds(side * units, units)],
                        ins.at[4 + 4 * n + 2 * kind + side],
                    )
                )
        return copies

    low, high = pl.ds(0, half), pl.ds(half, half)
    inputs = [
        copy(own_ref.at[0], x.at[low], ins.at[0]),
        copy(met_ref.at[0], x.at[high], ins.at[1]),
        copy(own_ref.at[1], g.at[low], ins.at[2]),
        copy(met_ref.at[1], g.at[high], ins.at[3]),
    ]
    loads = [load(n) for n in range(parts)]
    for item in inputs[:2] + loads[0][:2] + inputs[2:] + loads[0][2:] + loads[1]:
        item.start()
    stores = []
    root = 0.7978845608028654
    for n in range(parts):
        slot = n % 2
        for item in (inputs[:2] if n == 0 else []) + loads[n][:2]:
            item.wait()
        hidden = dot(x[...], weights[slot, 0], 1, 1) + b_ref[n : n + 1]
        square = hidden * hidden
        tanh = jnp.tanh(root * hidden * (1.0 + 0.044715 * square))
        acts[n] = (0.5 * hidden * (1.0 + tanh)).astype(bf16)
        slope = 0.5 * (1.0 + tanh) + 0.5 * hidden * (1.0 - tanh * tanh) * (root * (1.0 + 0.134145 * square))
        stores.append(copy(acts.at[n], act_ref.at[n], outs.at[2 * n]))
        stores[-1].start()
        for item in (inputs[2:] if n == 0 else []) + loads[n][2:]:
            item.wait()
        back = (dot(g[...], weights[slot, 1], 1, 1) * slope).astype(bf16)
        backs[n] = back
        stores.append(copy(backs.at[n], back_ref.at[n], outs.at[2 * n + 1]))
        stores[-1].start()
        column_ref[n : n + 1] = jnp.sum(back.astype(f32), axis=0, keepdims=True)
        for m, value in enumerate((dot(acts[n], weights[slot, 1], 1, 0), dot(back, weights[slot, 0], 1, 0))):
            for k in range(2):
                rows = value[k * half : (k + 1) * half]
                total[k, m] = rows if n == 0 else total[k, m] + rows
        if n + 2 < parts:
            for item in loads[n + 2]:
                item.start()
    for k, ref in ((1, other_sums), (0, own_sums)):
        stores.append(copy(total.at[k], ref, outs.at[2 * parts + k]))
        stores[-1].start()
    for item in stores:
        item.wait()


def feed_forward(own_in, met_in, bias, pieces):
    _, tokens, width = own_in.shape
    parts, units = len(pieces) // 2, pieces[0].shape[1]
    column = jax.ShapeDtypeStruct((parts, 2 * units), f32)
    hidden = [jax.ShapeDtypeStruct((parts, 2 * tokens, 2 * units), bf16)] * 2
    sums = [jax.ShapeDtypeStruct((2, tokens, width), f32)] * 2
    dma = pltpu.SemaphoreType.DMA
    return pl.pallas_call(
        functools.partial(feed_forward_kernel, parts),
        grid=(1,),
        in_specs=[any_spec, any_spec, full(bias)] + [any_spec] * len(pieces),
        out_specs=[any_spec] * 2 + [full(column), any_spec, any_spec],
        out_shape=hidden + [column] + sums,
        scratch_shapes=[
            pltpu.VMEM((2 * tokens, width), bf16),
            pltpu.VMEM((2 * tokens, width), bf16),
            pltpu.VMEM((2, 2, 2 * units, width), bf16),
            pltpu.VMEM(hidden[0].shape, bf16),
            pltpu.VMEM(hidden[0].shape, bf16),
            pltpu.VMEM((2, 2, tokens, width), f32),
            dma((4 + 4 * parts,)),
            dma((2 * parts + 2,)),
        ],
        cost_estimate=tiny,
        compiler_params=pltpu.CompilerParams(vmem_limit_bytes=48 * MIB),
        name="feed_forward",
    )(own_in, met_in, bias, *pieces)


def fc_grad_kernel(parts, act_ref, back_ref, own_ref, met_ref, *refs):
    grads, (x, acts, backs, products, ins, outs) = refs[: 2 * parts], refs[2 * parts :]
    half, units = own_ref.shape[1], grads[0].shape[1]
    copy = pltpu.make_async_copy
    inputs = []
    for k, ref in enumerate((own_ref, met_ref)):
        for m in range(2):
            inputs.append(copy(ref.at[m], x.at[m, pl.ds(k * half, half)], ins.at[2 * k + m]))
    loads = [
        [
            copy(act_ref.at[n], acts.at[n], ins.at[4 + 2 * n]),
            copy(back_ref.at[n], backs.at[n], ins.at[5 + 2 * n]),
        ]
        for n in range(parts)
    ]
    for item in inputs + [item for pair in loads for item in pair]:
        item.start()
    stores = []
    for n in range(parts):
        for item in (inputs if n == 0 else []) + loads[n]:
            item.wait()
        if n >= 2:
            for item in stores[n - 2]:
                item.wait()
        stores.append([])
        for kind, left, right in ((0, backs, 0), (1, acts, 1)):
            products[n % 2, kind] = dot(left[n], x[right], 0, 0).astype(bf16)
            for side in range(2):
                stores[n].append(
                    copy(
                        products.at[n % 2, kind, pl.ds(side * units, units)],
                        grads[2 * n + side].at[kind],
                        outs.at[4 * n + 2 * kind + side],
                    )
                )
                stores[n][-1].start()
    for pair in stores[-2:]:
        for item in pair:
            item.wait()


def fc_grads_of(acts, backs, own_in, met_in):
    parts, tokens, columns = acts.shape
    width = own_in.shape[2]
    dma = pltpu.SemaphoreType.DMA
    return pl.pallas_call(
        functools.partial(fc_grad_kernel, parts),
        grid=(1,),
        in_specs=[any_spec] * 4,
        out_specs=[any_spec] * (2 * parts),
        out_shape=[jax.ShapeDtypeStruct((2, columns // 2, width), bf16)] * (2 * parts),
        scratch_shapes=[
            pltpu.VMEM((2, tokens, width), bf16),
            pltpu.VMEM(acts.shape, bf16),
            pltpu.VMEM(acts.shape, bf16),
            pltpu.VMEM((2, 2, columns, width), bf16),
            dma((4 + 2 * parts,)),
            dma((4 * parts,)),
        ],
        cost_estimate=tiny,
        compiler_params=pltpu.CompilerParams(vmem_limit_bytes=40 * MIB),
        name="fc_grads",
    )(acts, backs, own_in, met_in)


def on_device(
    tokens,
    cond,
    segment_ids,
    crop_slot,
    ada_weight,
    ada_bias,
    attn_weight,
    fc_in,
    fc_out,
    biases,
    out_grad,
):
    net = Net()
    tok_len, width = tokens.shape[1:]
    head_dim = width // HEADS
    mod_rank, core, chips = net.mod_rank, net.core, net.chips
    device_count = net.dp * net.mod
    crop_count = crop_slot.shape[1] // net.mod
    shard = attn_weight.shape[0]
    third = shard // 3
    chunks_of = [range(chips // 2), range(chips // 2, chips)]
    halves = [(n, side) for n in range(3) for side in range(2)]
    aligned = shard % (2 * head_dim) == 0 and third % 16 == 0 and width % (2 * net.mod * shard) == 0

    g_attn = Gather(net, attn_weight[None])
    g_fc = Gather(net, jnp.stack([fc_in, fc_out]))
    silu_cond, mod_own = modulate(cond, ada_weight, ada_bias.reshape(1, -1).astype(f32))
    for n in range(g_attn.count):
        g_attn.start()
        g_attn.got = [after(g_attn.got[0], mod_own)]
        g_attn.finish()
    g_attn.start()
    first = g_attn.value
    for n in range(g_fc.count):
        g_fc.start(*first)
        if n < g_fc.count - 1:
            g_fc.finish()
    g_attn.finish().start()
    g_attn.finish().start()
    third_phase = g_attn.value
    g_fc.got = [after(g_fc.got[0], *third_phase)]
    g_fc.finish().start(*g_attn.got)
    attn_pieces = [(g_attn.value, g_attn.got)[side][n] for n, side in halves]

    mod_other = net.swap(after(mod_own, *first), "mod")
    modulation = jnp.concatenate(
        [jnp.where(mod_rank == 0, mod_own, mod_other), jnp.where(mod_rank == 0, mod_other, mod_own)], axis=1
    )
    seg_ids = segment_ids[0]
    slots = lax.dynamic_slice_in_dim(crop_slot[0], mod_rank * crop_count, crop_count)
    crop_onehot = seg_ids[:, None] == jnp.arange(crop_count, dtype=jnp.int32)[None, :]
    token_slot = jnp.sum(jnp.where(crop_onehot, slots[None, :], 0), axis=1)
    slot_pick = token_slot[:, None] == jnp.arange(cond.shape[0], dtype=jnp.int32)[None, :]
    slot_pick = slot_pick.astype(bf16)
    modulation = after(modulation, *third_phase)
    mods = [modulation[:, n * width : (n + 1) * width] for n in range(6)]
    shift_a, scale_a, gate_a, shift_m, scale_m, gate_m = [times(slot_pick, block) for block in mods]

    slot_count, own_cols = cond.shape[0], width // net.dp
    to_dp = jnp.moveaxis(silu_cond.reshape(slot_count, net.dp, own_cols), 1, 0).reshape(net.dp, 1, -1)
    to_all = jnp.broadcast_to(to_dp, (net.dp, net.mod, slot_count * own_cols)).reshape(device_count, -1)
    to_all = after(to_all, *third_phase)
    sent = jnp.concatenate([jnp.broadcast_to(biases[None], (device_count, biases.shape[0])), to_all], axis=1)
    met = lax.all_to_all(sent, ("dp", "mod"), split_axis=0, concat_axis=0, tiled=True)
    ada_order = list(range(net.bits - 1, -1, -1))
    dp_order = net.ranks(ada_order, range(net.dp))[0]
    dp_pick = (dp_order[:, None] == jnp.arange(net.dp)[None, :]).astype(bf16)
    cond_cols = times(dp_pick, met.reshape(net.dp, net.mod, -1)[:, 0, biases.shape[0] :]).astype(bf16)
    cond_cols = cond_cols.reshape(-1, own_cols)
    bias_all = met[:, : biases.shape[0]].reshape(-1, width)
    bias_query, bias_value, bias_proj, bias_out = [bias_all[n].astype(f32) for n in range(4)]
    bias_in = bias_all[4:].reshape(device_count, 3, third)
    picks = []
    for n, side in halves:
        devices = net.devices(net.orders[n], chunks_of[side])
        picks.append((devices[:, None] == jnp.arange(device_count)[None, :]).astype(bf16))
    picks = jnp.stack(picks).reshape(3, 2, chips // 2, device_count)
    bias_pieces = jnp.einsum("nsjd,dnr->nsjr", picks, bias_in, preferred_element_type=f32).reshape(3, -1)

    def join(own, other):
        own, other = [a.reshape(-1, 1, net.mod * shard, a.shape[-1]) for a in (own, other)]
        both = jnp.where(core == 0, jnp.concatenate([own, other], 1), jnp.concatenate([other, own], 1))
        return both.reshape(-1, both.shape[-1])

    def part(whole):
        whole = whole.reshape(-1, 2, net.mod * shard, whole.shape[-1])
        return [
            jnp.where(core == c, whole[:, 0], whole[:, 1]).reshape(-1, whole.shape[-1]) for c in range(2)
        ]

    resid = tokens[0].astype(f32)
    normed_a, _ = layer_norm(resid)
    attn_in = (normed_a * (1.0 + scale_a) + shift_a).astype(bf16)
    if aligned:
        index = jnp.concatenate([net.local(net.orders[n], chunks_of[side]) * 3 + n for n, side in halves])
        own_weight = assemble(attn_pieces, index, third)
        qkv_rows = own_weight.shape[0] * 3 // 4
        qkv_weight = own_weight[:qkv_rows]
        proj_own = own_weight[qkv_rows:]
        proj_weight = join(proj_own, net.swap(proj_own, 0))
        ids = jnp.stack([seg_ids, net.swap(seg_ids, 0)])
        attn_in = after(attn_in, *third_phase)
        attn_both = jnp.concatenate([attn_in, net.swap(attn_in, 0)], axis=0)
        own_query, own_value = part(bias_query[:, None])[0], part(bias_value[:, None])[0]
        qkv_bias = jnp.concatenate([own_query, jnp.zeros_like(own_query), own_value], axis=0)
        attn_both = after(attn_both, *g_fc.got)
        g_fc.finish().start()
        qkv = (times_rows(qkv_weight, attn_both) + qkv_bias).astype(bf16)
        qkv = qkv.reshape(3, -1, 2 * head_dim, 2 * tok_len)
        context_both = attention(qkv, ids, head_dim).reshape(-1, 2 * tok_len)
        context = join(context_both[:, :tok_len], net.swap(context_both[:, tok_len:], 0))
        attn_out = dot(context, proj_weight, 0, 1) + bias_proj
    else:
        arrays = attn_pieces + [net.swap(piece, 0) for piece in attn_pieces]
        places = jnp.concatenate(
            [net.devices(net.orders[n], chunks_of[side], c) * 3 + n for c in range(2) for n, side in halves]
        )
        spread = jnp.concatenate(arrays, axis=1)[0]

        def place(n, whole):
            block = lax.dynamic_slice_in_dim(spread, n * third, third)
            return lax.dynamic_update_slice_in_dim(whole, block, places[n] * third, 0)

        attn_w = lax.fori_loop(0, places.shape[0], place, jnp.zeros_like(spread))
        g_fc.finish().start()
        g_fc.finish().start()
        qkv_weight, proj_weight = attn_w[: 3 * width], attn_w[3 * width :]
        qkv_bias = jnp.concatenate([bias_query, jnp.zeros_like(bias_query), bias_value])
        qkv = (times_rows(qkv_weight, attn_in) + qkv_bias[:, None]).astype(bf16)
        qkv = qkv.reshape(3, -1, 2 * head_dim, tok_len)
        context = attention(qkv, seg_ids[None], head_dim).reshape(-1, tok_len)
        attn_out = dot(context, proj_weight, 0, 1) + bias_proj
    mid = resid + gate_a * attn_out
    normed_m, _ = layer_norm(mid)
    mlp_in = (normed_m * (1.0 + scale_m) + shift_m).astype(bf16)
    if aligned:
        mlp_in = after(mlp_in, *g_fc.got)
        g_fc.finish().start()
    grad_mlp = (gate_m * out_grad[0].astype(f32)).astype(bf16)

    mlp_own = jnp.stack([mlp_in, grad_mlp])
    mlp_met = net.swap(mlp_own, 0)
    grad_bias_out = jnp.sum(grad_mlp.astype(f32), axis=0, keepdims=True)
    fc_pieces = [(g_fc.value, g_fc.got)[side][n] for n, side in halves]
    acts, backs, columns, own_sums, other_sums = feed_forward(mlp_own, mlp_met, bias_pieces, fc_pieces)
    sums_met = net.swap(other_sums, 0)
    fc_grads = fc_grads_of(acts, backs, mlp_own, mlp_met)
    sums_met = after(sums_met, *fc_grads)
    back_way = Scatter(net, fc_grads[0::2], fc_grads[1::2])

    grad_mid, grad_attn, grad_bias_proj, *parts = middle(
        core,
        net.mod * shard if aligned else None,
        own_sums,
        sums_met,
        mid,
        out_grad[0],
        slot_pick,
        modulation,
        proj_weight,
        context,
    )
    if aligned:
        mine, other, proj_mine, proj_other = parts
        context_grads = [a.reshape(-1, 2 * head_dim, tok_len) for a in (mine, net.swap(other, 0))]
        proj_met = net.swap(after(proj_other, *context_grads), 0)
        grad_qkv = attention(qkv, ids, head_dim, context_grads)
        grad_qkv = grad_qkv.reshape(-1, 2 * tok_len)
        back_own, back_other = attn_in_grads(grad_qkv, own_weight)
        back_met = net.swap(back_other, 0)
        grad_qkv = after(grad_qkv, back_own)
        places = jnp.sum(
            jnp.where(
                index[None, :] == jnp.arange(index.shape[0], dtype=index.dtype)[:, None],
                jnp.arange(index.shape[0], dtype=index.dtype)[None, :],
                0,
            ),
            axis=1,
        )
        pieces = weight_grad(grad_qkv, attn_both, proj_mine, proj_met, places, third)
        back_met = after(back_met, pieces)
    else:
        grad_context, grad_proj = parts
        grad_qkv = attention(
            qkv, seg_ids[None], head_dim, [grad_context.reshape(-1, 2 * head_dim, tok_len)]
        ).reshape(-1, tok_len)
        attn_grad = jnp.concatenate([times(grad_qkv, attn_in).astype(bf16), grad_proj], axis=0)

        def take(n, whole):
            block = lax.dynamic_slice_in_dim(attn_grad, places[n] * third, third)
            return lax.dynamic_update_slice_in_dim(whole, block, n * third, 0)

        grads = lax.fori_loop(0, places.shape[0], take, jnp.zeros_like(attn_grad))
        grads = jnp.split(grads[None], 12, axis=1)
        pieces = jnp.concatenate([summed(a, net.swap(b, 0)) for a, b in zip(grads[:6], grads[6:])], axis=1)
        back_own = contract_rows(grad_qkv, qkv_weight)
        back_met = jnp.zeros_like(back_own)
    grad_tokens, pair_a = end_call(
        attn_end_kernel, f32, slot_count, back_own, back_met, tokens[0], grad_mid, attn_out, slot_pick, modulation
    )
    result, pair_m = end_call(
        mlp_end_kernel,
        bf16,
        slot_count,
        mid,
        own_sums,
        sums_met,
        bias_out[None],
        out_grad[0],
        slot_pick,
        modulation,
    )
    pair_a, *back_way.got = lax.optimization_barrier((pair_a, *back_way.got))
    pair_own = jnp.where(mod_rank == 0, pair_a, pair_m)
    pair_send = jnp.where(mod_rank == 0, pair_m, pair_a)
    grad_mod = summed(pair_own, net.swap(pair_send, "mod"))
    for n in range(3):
        back_way.hold(n, grad_mod)
    mod_rows = jnp.concatenate([grad_mod, net.swap(grad_mod, ada_order[0])], axis=0)
    back_way.join(0, pieces)
    back_way.join(1, pieces)
    back_way.hold(2, mod_rows)
    back_way.join(2, pieces)

    grad_silu = times_rows(grad_mod, ada_weight)
    silu_own = jnp.where(mod_rank == 0, grad_silu[:crop_count], grad_silu[crop_count:])
    silu_send = jnp.where(mod_rank == 0, grad_silu[crop_count:], grad_silu[:crop_count]).astype(bf16)

    mod_rows = after(mod_rows, *back_way.got)
    mod_rows = jnp.concatenate([mod_rows, net.swap(mod_rows, ada_order[1])], axis=0)
    also = [None] * 3
    for n in range(3):
        back_way.hold(n, silu_send)
    back_way.second(0, also)
    back_way.second(1, also)
    back_way.hold(2, mod_rows)
    back_way.second(2, also)
    silu_send, grad_qkv, columns, *_ = lax.optimization_barrier((silu_send, grad_qkv, columns, *also))
    back_way.third(also)
    silu_send = after(silu_send, *back_way.also)
    grad_silu = silu_own + net.swap(silu_send, "mod").astype(f32)
    own_cond = lax.dynamic_slice_in_dim(cond, mod_rank * crop_count, crop_count, 0).astype(f32)
    silu_back = jax.vjp(jax.nn.silu, own_cond)[1]
    grad_cond = silu_back(grad_silu)[0]

    mod_rows = after(mod_rows, *back_way.also_got)
    fc_sum, attn_sum = back_way.last()
    for dim in ada_order[2:]:
        mod_rows = jnp.concatenate([mod_rows, net.swap(mod_rows, dim)], axis=0)
    ada_w_sum = contract_rows(cond_cols, mod_rows)
    ada_b_sum = jnp.sum(mod_rows.astype(f32), axis=0).reshape(ada_bias.shape[0], width)
    ada_b_sum = lax.dynamic_slice_in_dim(ada_b_sum, net.dp_rank * own_cols, own_cols, 1)

    column = jnp.sum(grad_qkv.astype(f32), axis=1, keepdims=True).reshape(3, -1, 1)
    if aligned:
        none = jnp.zeros_like(column[0])
        column = [join(column[0], none), None, join(column[2], none)]
    columns = columns.reshape(3, 2, chips // 2, third)
    grad_bias_in = jnp.einsum("nsjd,nsjr->dnr", picks.astype(f32), columns, precision=lax.Precision.HIGHEST)
    grad_bias = stack_rows(
        column[0].reshape(1, -1),
        column[2].reshape(1, -1),
        grad_bias_proj,
        grad_bias_out,
        grad_bias_in.reshape(-1, width),
    )
    bias_rows = lax.all_to_all(
        grad_bias.reshape(device_count, -1), ("dp", "mod"), split_axis=0, concat_axis=0, tiled=True
    )
    bias_sum = jnp.sum(bias_rows, axis=0)
    return (
        result[None],
        grad_tokens[None],
        grad_cond,
        ada_w_sum,
        ada_b_sum,
        attn_sum[0],
        fc_sum[0],
        fc_sum[1],
        bias_sum,
    )


def solution(mesh):
    placed = (
        P(("dp", "mod"), None, None),
        P("dp", None),
        P(("dp", "mod"), None),
        P("dp", None),
        P(None, "mod"),
        P("mod", None),
        P(("dp", "mod"), None),
        P(("dp", "mod"), None),
        P(("dp", "mod"), None),
        P(("dp", "mod")),
        P(("dp", "mod"), None, None),
    )
    return jax.shard_map(
        on_device,
        mesh=mesh,
        in_specs=placed,
        out_specs=(
            P(("dp", "mod"), None, None),
            P(("dp", "mod"), None, None),
            P(("dp", "mod"), None),
            P("dp", "mod"),
            P("mod", "dp"),
            P(("dp", "mod"), None),
            P(("dp", "mod"), None),
            P(("dp", "mod"), None),
            P(("dp", "mod")),
        ),
        check_vma=False,
    )
```

```python
import functools

import jax
import jax.numpy as jnp
import numpy as np
from jax import lax
from jax.experimental import pallas as pl
from jax.experimental.pallas import tpu as pltpu
from jax.sharding import PartitionSpec as P

HEADS = 16
norm_eps = 1e-06
bf16 = jnp.bfloat16
f32 = jnp.float32
MIB = 1024 * 1024


def layer_norm(values):
    center = values - jnp.mean(values, axis=-1, keepdims=True)
    inverse = lax.rsqrt(jnp.mean(center * center, axis=-1, keepdims=True) + norm_eps)
    return (center * inverse, inverse)


def norm_back(grad_in, normed, inverse):
    centered = grad_in - jnp.mean(grad_in, axis=-1, keepdims=True)
    return (centered - normed * jnp.mean(grad_in * normed, axis=-1, keepdims=True)) * inverse


def dot(left, right, left_dim, right_dim):
    return lax.dot_general(left, right, (((left_dim,), (right_dim,)), ((), ())), preferred_element_type=f32)


def times(left, right):
    return dot(left, right, 1, 0)


def times_rows(left, right):
    return dot(left, right, 1, 1)


def contract_rows(left, right):
    return dot(left, right, 0, 0)


def after(value, *others):
    return lax.optimization_barrier((value, *others))[0]


def summed(left, right):
    return (left.astype(f32) + right.astype(f32)).astype(bf16)


class Net:
    def __init__(self):
        self.dp = lax.axis_size("dp")
        self.mod = lax.axis_size("mod")
        self.bits = self.dp.bit_length() - 1
        self.dp_rank = lax.axis_index("dp")
        self.mod_rank = lax.axis_index("mod")
        self.core = self.dp_rank & 1
        self.chips = self.dp // 2 * self.mod
        self.lead = list(range(self.bits - 1, 2, -1))
        last = ["mod", 1, 2]
        self.turns = [last[n:] + last[:n] for n in range(3)]
        self.orders = [self.lead + turn for turn in self.turns]

    def swap(self, value, dim):
        if dim == "mod":
            return lax.ppermute(value, "mod", [(i, i ^ 1) for i in range(self.mod)])
        return lax.ppermute(value, "dp", [(i, i ^ (1 << dim)) for i in range(self.dp)])

    def ranks(self, order, chunks, core=0):
        masks = []
        for j in chunks:
            dp_mask, mod_mask = core, 0
            for step, dim in enumerate(order):
                if j >> step & 1:
                    if dim == "mod":
                        mod_mask ^= 1
                    else:
                        dp_mask ^= 1 << dim
            masks.append((dp_mask, mod_mask))
        masks = np.array(masks, np.int32)
        return self.dp_rank ^ masks[:, 0], self.mod_rank ^ masks[:, 1]

    def devices(self, order, chunks, core=0):
        dp, mod = self.ranks(order, chunks, core)
        return dp * self.mod + mod

    def local(self, order, chunks):
        dp, mod = self.ranks(order, chunks)
        return (dp >> 1) * self.mod + mod


class Gather:
    def __init__(self, net, shard):
        self.net, self.count = net, len(net.lead)
        self.third = shard.shape[1] // 3
        self.value, self.got, self.phase = shard, None, 0

    def start(self, *others):
        net, phase = self.net, self.phase
        if phase < self.count:
            self.value = after(self.value, *others) if others else self.value
            self.got = [net.swap(self.value, net.lead[phase])]
        else:
            if phase == self.count:
                kinds, _, width = self.value.shape
                whole = self.value.reshape(kinds, -1, 3, self.third, width)
                self.value = [whole[:, :, n].reshape(kinds, -1, width) for n in range(3)]
            if others:
                self.value = list(lax.optimization_barrier((*self.value, *others))[:3])
            step = phase - self.count
            self.got = [net.swap(self.value[n], net.turns[n][step]) for n in range(3)]
        self.phase += 1
        return self

    def finish(self):
        if self.phase <= self.count:
            self.value = jnp.concatenate([self.value, self.got[0]], axis=1)
        elif self.phase < self.count + 3:
            self.value = [jnp.concatenate(pair, axis=1) for pair in zip(self.value, self.got)]
        return self


any_spec = pl.BlockSpec(memory_space=pl.ANY)


def full(value):
    return pl.BlockSpec(value.shape, lambda *_: (0,) * len(value.shape))

tiny = pl.CostEstimate(flops=1024, bytes_accessed=1024, transcendentals=0)


def run_copies(copies):
    for copy in copies:
        copy.start()
    for copy in copies:
        copy.wait()


def assemble_kernel(rows, each, index_ref, *refs):
    pieces, out_ref, hold, sems, last = refs[:-4], *refs[-4:]
    copies = []
    for n, piece in enumerate(pieces):
        for j in range(each):
            at = pl.multiple_of(index_ref[n * each + j] * rows, rows)
            copies.append(
                pltpu.make_async_copy(
                    piece.at[0, pl.ds(j * rows, rows)], hold.at[pl.ds(at, rows)], sems.at[n * each + j]
                )
            )
    run_copies(copies)
    run_copies([pltpu.make_async_copy(hold, out_ref, last)])


def assemble(pieces, index, rows):
    each, width = pieces[0].shape[1] // rows, pieces[0].shape[2]
    total = len(pieces) * each
    return pl.pallas_call(
        functools.partial(assemble_kernel, rows, each),
        grid_spec=pltpu.PrefetchScalarGridSpec(
            num_scalar_prefetch=1,
            grid=(1,),
            in_specs=[any_spec] * len(pieces),
            out_specs=any_spec,
            scratch_shapes=[
                pltpu.VMEM((total * rows, width), bf16),
                pltpu.SemaphoreType.DMA((total,)),
                pltpu.SemaphoreType.DMA,
            ],
        ),
        out_shape=jax.ShapeDtypeStruct((total * rows, width), bf16),
        compiler_params=pltpu.CompilerParams(vmem_limit_bytes=10 * MIB),
        name="assemble",
    )(index, *pieces)


def added(left, right):
    return (left.astype(f32) + right.astype(f32)).astype(bf16)


def sums_call(kernel, grid, in_specs, out_specs, outs, *args):
    return pl.pallas_call(
        kernel,
        grid=grid,
        in_specs=in_specs,
        out_specs=out_specs,
        out_shape=[pltpu.HBM(out, bf16) for out in outs],
        cost_estimate=tiny,
        compiler_params=pltpu.CompilerParams(vmem_limit_bytes=24 * MIB),
        name=kernel.__name__,
    )(*args)


def first_sums(own_low, own_high, got_low, got_high, also, keep, send):
    keep[...] = added(own_low[...], got_low[...])
    send[:2] = added(own_high[...], got_high[...])
    send[2:] = also[...]


def half_sums(own, got, keep, send):
    half = keep.shape[1]
    keep[...] = added(own[:, :half], got[:, :half])
    send[...] = added(own[:, half:], got[:, half:])


def block_sums(own, got, keep, send):
    keep[0] = added(own[0], got[0])
    send[0] = added(own[1], got[1])


def third_sums(*refs):
    outs = refs[6:]
    for n in range(3):
        total = added(refs[n][...], refs[3 + n][...])
        if len(outs) == 2:
            rows = total.shape[1] // 2
            outs[0][:, n * rows : (n + 1) * rows] = total[:, :rows]
            outs[1][:, n * rows : (n + 1) * rows] = total[:, rows:]
        else:
            outs[n][...] = total


def third_attn_sums(*refs):
    for n in range(3):
        half_sums(refs[n], refs[3 + n], refs[6 + 2 * n], refs[7 + 2 * n])


def fourth_sums(*refs):
    keep, send = refs[6:]
    rows = keep.shape[1] // 3
    for n in range(3):
        total = added(refs[n][0], refs[3 + n][0])
        keep[0, n * rows : (n + 1) * rows] = total[:rows]
        send[0, n * rows : (n + 1) * rows] = total[rows:]


class Scatter:
    def __init__(self, net, own, other):
        self.net = net
        self.own = list(own)
        self.got = [net.swap(other[n], net.turns[n][2]) for n in range(3)]
        self.aligned = len(net.lead) == 1 and own[0].shape[1] // 8 % 16 == 0

    def hold(self, n, *others):
        self.got[n] = after(self.got[n], *others)

    def join(self, n, pieces):
        _, rows, width = self.own[n].shape
        half = rows // 2
        step = half // 6
        also = 2 * ((n + 2) % 3)
        self.pieces = pieces.reshape(12, half, width)
        block = (2, step, width)
        low, high = pl.BlockSpec(block, lambda i: (0, i, 0)), pl.BlockSpec(block, lambda i: (0, i + 6, 0))
        self.own[n], send = sums_call(
            first_sums,
            (6,),
            [low, high, low, high, pl.BlockSpec(block, lambda i: (also + 1, i, 0))],
            [low, pl.BlockSpec((4, step, width), lambda i: (0, i, 0))],
            [(2, half, width), (4, half, width)],
            self.own[n],
            self.own[n],
            self.got[n],
            self.got[n],
            self.pieces,
        )
        self.got[n] = self.net.swap(send, self.net.turns[n][1])
        return send

    def second(self, n):
        _, rows, width = self.own[n].shape
        outs = [(2, rows // 2, width)] * 2
        self.both = getattr(self, "both", [None] * 3)
        self.both[n] = self.got[n]
        self.own[n], send = sums_call(
            half_sums,
            (1,),
            [full(self.own[n]), pl.BlockSpec((2, rows, width), lambda i: (0, 0, 0))],
            [full(jax.ShapeDtypeStruct(out, bf16)) for out in outs],
            outs,
            self.own[n],
            self.got[n],
        )
        self.got[n] = self.net.swap(send, self.net.turns[n][0])
        return send

    def second_attn(self, others):
        self.also, self.also_got = [None] * 3, [None] * 3
        both = list(lax.optimization_barrier((*self.both, *others))[:3])
        for n in range(3):
            _, rows, width = both[n].shape
            piece = 2 * ((n + 2) % 3)
            outs = [(1, rows, width)] * 2
            self.also[n], send = sums_call(
                block_sums,
                (1,),
                [
                    pl.BlockSpec((2, rows, width), lambda i: (piece, 0, 0)),
                    pl.BlockSpec((2, rows, width), lambda i: (1, 0, 0)),
                ],
                [full(jax.ShapeDtypeStruct(out, bf16)) for out in outs],
                outs,
                self.pieces,
                both[n],
            )
            self.also_got[n] = self.net.swap(send, self.net.turns[n][0])

    def third(self):
        net = self.net
        _, rows, width = self.own[0].shape
        outs = [(2, rows // 2 * 3, width)] * 2 if self.aligned else [(2, rows, width)] * 3
        args = self.own + self.got
        results = sums_call(
            third_sums,
            (1,),
            [full(a) for a in args],
            [full(jax.ShapeDtypeStruct(out, bf16)) for out in outs],
            outs,
            *args,
        )
        if self.aligned:
            self.fc = results[0], net.swap(results[1], net.lead[0])
        else:
            self.fc = self.lead(self.together(results), len(net.lead) - 1)
        self.also_got = list(lax.optimization_barrier((*self.also_got, results[1]))[:3])

    def third_attn(self):
        net = self.net
        _, rows, width = self.also[0].shape
        args, outs = self.also + self.also_got, [(1, rows // 2, width)] * 6
        results = sums_call(
            third_attn_sums,
            (1,),
            [full(a) for a in args],
            [full(jax.ShapeDtypeStruct(out, bf16)) for out in outs],
            outs,
            *args,
        )
        self.also = results[0::2]
        self.also_got = [net.swap(results[2 * n + 1], net.turns[(n + 2) % 3][0]) for n in range(3)]

    def last(self):
        net = self.net
        order = (1, 2, 0)
        keep, got = [self.also[n] for n in order], [self.also_got[n] for n in order]
        *got, fc_got = lax.optimization_barrier((*got, self.fc[1]))
        self.fc = self.fc[0], fc_got
        if self.aligned:
            _, rows, width = keep[0].shape
            outs = [(1, rows // 2 * 3, width)] * 2
            own, send = sums_call(
                fourth_sums,
                (1,),
                [full(a) for a in keep + got],
                [full(jax.ShapeDtypeStruct(out, bf16)) for out in outs],
                outs,
                *keep,
                *got,
            )
            attn = own, net.swap(send, net.lead[0])
        else:
            attn = self.lead(self.together([summed(a, b) for a, b in zip(keep, got)]), len(net.lead) - 1)
        sums = []
        for own, got in (self.fc, attn):
            for step in range(len(net.lead) - 1, -1, -1):
                total = own.astype(f32) + got.astype(f32)
                if step:
                    own, got = self.lead(total.astype(bf16), step - 1)
            sums.append(total)
        return sums

    def together(self, parts):
        kinds, _, width = parts[0].shape
        count = 1 << len(self.net.lead)
        return jnp.concatenate([p.reshape(kinds, count, -1, width) for p in parts], axis=2).reshape(kinds, -1, width)

    def lead(self, whole, step):
        half = whole.shape[1] // 2
        return whole[:, :half], self.net.swap(whole[:, half:], self.net.lead[step])


def attn_in_kernel(grad_ref, weight_ref, own_ref, other_ref):
    total = dot(grad_ref[...], weight_ref[...], 0, 0)
    half = own_ref.shape[0]
    own_ref[...] = total[:half]
    other_ref[...] = total[half:]


def attn_in_grads(grad, weight):
    rows, tokens = grad.shape
    width = weight.shape[1]
    out = jax.ShapeDtypeStruct((tokens // 2, width), f32)
    return pl.pallas_call(
        attn_in_kernel,
        grid=(1,),
        in_specs=[full(grad), pl.BlockSpec((rows, width), lambda i: (0, 0))],
        out_specs=[full(out)] * 2,
        out_shape=[out, pltpu.HBM(out.shape, f32)],
        cost_estimate=tiny,
        compiler_params=pltpu.CompilerParams(vmem_limit_bytes=40 * MIB),
        name="attn_in_grads",
    )(grad, weight)


def weight_grad_kernel(rows, place_ref, grad_ref, x_ref, mine_ref, other_ref, out_ref, hold, sems):
    top, copies = grad_ref.shape[0], []
    step = top // 3
    for n in (3, 0, 1, 2):
        start = n * step
        stop = min(start + step, hold.shape[0])
        if n == 3:
            hold[start:] = summed(mine_ref[...], other_ref[...])
        else:
            hold[start:stop] = dot(grad_ref[start:stop], x_ref[...], 1, 0).astype(bf16)
        for unit in range(start // rows, stop // rows):
            at = pl.multiple_of(place_ref[unit] * rows, rows)
            copies.append(
                pltpu.make_async_copy(
                    hold.at[pl.ds(unit * rows, rows)], out_ref.at[pl.ds(at, rows)], sems.at[unit]
                )
            )
            copies[-1].start()
    for copy in copies:
        copy.wait()


def weight_grad(grad, x, mine, other, places, rows):
    total, width = grad.shape[0] + mine.shape[0], x.shape[1]
    return pl.pallas_call(
        functools.partial(weight_grad_kernel, rows),
        grid_spec=pltpu.PrefetchScalarGridSpec(
            num_scalar_prefetch=1,
            grid=(1,),
            in_specs=[full(a) for a in (grad, x, mine, other)],
            out_specs=any_spec,
            scratch_shapes=[pltpu.VMEM((total, width), bf16), pltpu.SemaphoreType.DMA((total // rows,))],
        ),
        out_shape=jax.ShapeDtypeStruct((total, width), bf16),
        cost_estimate=tiny,
        compiler_params=pltpu.CompilerParams(vmem_limit_bytes=32 * MIB),
        name="weight_grad",
    )(places, grad, x, mine, other)


def by_core(core_ref, group, whole):
    if group is None:
        return [whole]
    picked = []
    for c in range(2):
        rows = []
        for at in range(0, whole.shape[0], 2 * group):
            first, second = whole[at : at + group], whole[at + group : at + 2 * group]
            rows.append(jnp.where(core_ref[0] == c, first, second))
        picked.append(jnp.concatenate(rows, axis=0))
    return picked


def token_block(pick, mods, n):
    width = mods.shape[1] // 6
    return dot(pick[...], mods[:, n * width : (n + 1) * width], 1, 0)


def middle_kernel(group, core_ref, *refs):
    sums, met, mid, grad_out, pick, mods, bias, weight, context = refs[:9]
    result_ref, pair_ref, mid_ref, attn_ref, column_ref = refs[9:14]
    normed, inverse = layer_norm(mid[...])
    back, outer = sums[1] + met[1], grad_out[...].astype(f32)
    mlp_out = sums[0] + met[0] + bias[...]
    result_ref[...] = (mid[...] + token_block(pick, mods, 5) * mlp_out).astype(bf16)
    slot_sums(pick[...], (back, back * normed, outer * mlp_out), pair_ref)
    grad_mid = outer + norm_back(back * (1.0 + token_block(pick, mods, 4)), normed, inverse)
    mid_ref[...] = grad_mid
    grad_attn = (token_block(pick, mods, 2) * grad_mid).astype(bf16)
    attn_ref[...] = grad_attn
    column_ref[...] = jnp.sum(grad_attn.astype(f32), axis=0, keepdims=True)
    parts = by_core(core_ref, group, dot(weight[...], grad_attn, 0, 1))
    parts += by_core(core_ref, group, dot(grad_attn, context[...], 0, 1))
    for ref, value in zip(refs[14:], parts):
        ref[...] = value.astype(bf16)


def middle(core, group, *args):
    _, tokens, width = args[0].shape
    if group is None:
        sizes = [(width, tokens), (width, width)]
    else:
        sizes = [(width // 2, tokens)] * 2 + [(width // 2, width)] * 2
    slots = args[4].shape[1]
    outs = [((tokens, width), bf16), ((slots, 3 * width), bf16)]
    outs += [((tokens, width), f32), ((tokens, width), bf16), ((1, width), f32)]
    outs = [jax.ShapeDtypeStruct(*out) for out in outs + [(s, bf16) for s in sizes]]
    return pl.pallas_call(
        functools.partial(middle_kernel, group),
        grid=(1,),
        in_specs=[pl.BlockSpec(memory_space=pltpu.SMEM)] + [full(a) for a in args],
        out_specs=[full(a) for a in outs],
        out_shape=outs[:5] + [pltpu.HBM(a.shape, bf16) for a in outs[5:]],
        cost_estimate=tiny,
        compiler_params=pltpu.CompilerParams(vmem_limit_bytes=48 * MIB),
        name="middle",
    )(core.reshape(1), *args)


def slot_sums(pick, blocks, out_ref):
    for n, block in enumerate(blocks):
        high = block.astype(bf16)
        low = (block - high.astype(f32)).astype(bf16)
        total = dot(pick, high, 0, 0) + dot(pick, low, 0, 0)
        out_ref[:, n * block.shape[1] : (n + 1) * block.shape[1]] = total.astype(bf16)


def attn_end_kernel(*refs):
    back_a, back_b, resid, grad_mid, attn_out, pick, mods = refs[:7]
    tokens_ref, pair_ref = refs[7:]
    back = back_a[...] + back_b[...]
    normed, inverse = layer_norm(resid[...].astype(f32))
    slope = back * (1.0 + token_block(pick, mods, 1))
    tokens_ref[...] = grad_mid[...] + norm_back(slope, normed, inverse)
    slot_sums(pick[...], (back, back * normed, grad_mid[...] * attn_out[...]), pair_ref)


def end_call(kernel, dtype, slots, *args):
    tokens, width = args[0].shape
    outs = [jax.ShapeDtypeStruct((tokens, width), dtype), jax.ShapeDtypeStruct((slots, 3 * width), bf16)]
    return pl.pallas_call(
        kernel,
        grid=(1,),
        in_specs=[full(a) for a in args],
        out_specs=[full(a) for a in outs],
        out_shape=outs,
        cost_estimate=tiny,
        compiler_params=pltpu.CompilerParams(vmem_limit_bytes=32 * MIB),
        name=kernel.__name__,
    )(*args)


def rows_kernel(*refs):
    at = 0
    for ref in refs[:-1]:
        refs[-1][at : at + ref.shape[0]] = ref[...]
        at += ref.shape[0]


def stack_rows(*args):
    out = jax.ShapeDtypeStruct((sum(a.shape[0] for a in args), args[0].shape[1]), f32)
    return pl.pallas_call(
        rows_kernel,
        grid=(1,),
        in_specs=[full(a) for a in args],
        out_specs=full(out),
        out_shape=out,
        cost_estimate=tiny,
        name="stack_rows",
    )(*args)


def softmax_t(key, query, same, scale):
    scores = jnp.where(same, dot(key, query, 0, 0) * scale, -1e30)
    weights = jnp.exp(scores - jnp.max(scores, axis=0, keepdims=True))
    return weights * (1.0 / jnp.sum(weights, axis=0, keepdims=True))


def heads_of(block, dim, cols):
    wide = block[:, cols].astype(f32)
    return [wide[n * dim : (n + 1) * dim].astype(bf16) for n in range(wide.shape[0] // dim)]


def attn_forward(dim, scale, row_ref, col_ref, q_ref, k_ref, v_ref, out_ref):
    length = col_ref.shape[0]
    for s in range(row_ref.shape[0]):
        cols = slice(s * length, (s + 1) * length)
        same = row_ref[s : s + 1] == col_ref[:, s : s + 1]
        outs = []
        for q, k, v in zip(*[heads_of(r[0, 0], dim, cols) for r in (q_ref, k_ref, v_ref)]):
            probs = softmax_t(k, q, same, scale).astype(bf16)
            outs.append(dot(v, probs, 1, 0))
        out_ref[0, :, cols] = jnp.concatenate(outs, axis=0).astype(bf16)


def attn_backward(dim, scale, row_ref, col_ref, q_ref, k_ref, v_ref, *refs):
    length, out_ref = col_ref.shape[0], refs[-1]
    for s in range(row_ref.shape[0]):
        cols = slice(s * length, (s + 1) * length)
        same = row_ref[s : s + 1] == col_ref[:, s : s + 1]
        gq, gk, gv = [], [], []
        qs, ks, vs = [heads_of(r[0, 0], dim, cols) for r in (q_ref, k_ref, v_ref)]
        for q, k, v, g in zip(qs, ks, vs, heads_of(refs[s][0], dim, slice(0, length))):
            probs = softmax_t(k, q, same, scale)
            back = dot(v, g, 0, 0)
            back = probs * (back - jnp.sum(back * probs, axis=0, keepdims=True))
            back = back.astype(bf16)
            gq.append(dot(k, back, 1, 0) * scale)
            gk.append(dot(q, back, 1, 1) * scale)
            gv.append(dot(g, probs.astype(bf16), 1, 1))
        for n, parts in enumerate((gq, gk, gv)):
            out_ref[n, 0, :, cols] = jnp.concatenate(parts, axis=0).astype(bf16)


def attention(qkv, ids, dim, grad=None):
    _, groups, rows, tokens = qkv.shape
    scale = dim**-0.5
    ids_t = ids.T

    def one(n):
        return pl.BlockSpec((1, 1, rows, tokens), lambda i: (n, i, 0, 0))

    flat = pl.BlockSpec((1, rows, tokens), lambda i: (i, 0, 0))
    short = pl.BlockSpec((1, rows, ids.shape[1]), lambda i: (i, 0, 0))
    args = [ids, ids_t, qkv, qkv, qkv]
    specs = [pl.BlockSpec(a.shape, lambda i: (0, 0)) for a in (ids, ids_t)] + [one(0), one(1), one(2)]
    if grad is None:
        return pl.pallas_call(
            functools.partial(attn_forward, dim, scale),
            grid=(groups,),
            in_specs=specs,
            out_specs=flat,
            out_shape=jax.ShapeDtypeStruct((groups, rows, tokens), bf16),
            cost_estimate=tiny,
            compiler_params=pltpu.CompilerParams(vmem_limit_bytes=24 * MIB),
            name="attention",
        )(*args)
    return pl.pallas_call(
        functools.partial(attn_backward, dim, scale),
        grid=(groups,),
        in_specs=specs + [short] * len(grad),
        out_specs=pl.BlockSpec((3, 1, rows, tokens), lambda i: (0, i, 0, 0)),
        out_shape=jax.ShapeDtypeStruct(qkv.shape, bf16),
        cost_estimate=tiny,
        compiler_params=pltpu.CompilerParams(vmem_limit_bytes=24 * MIB),
        name="attention_back",
    )(*args, *grad)


def modulation_kernel(cond_ref, weight_ref, bias_ref, silu_ref, out_ref):
    cond = cond_ref[...].astype(f32)
    silu = (cond / (1.0 + jnp.exp(-cond))).astype(bf16)
    silu_ref[...] = silu
    out_ref[...] = (dot(silu, weight_ref[...], 1, 0) + bias_ref[...]).astype(bf16)


def modulate(cond, weight, bias):
    slots, width = cond.shape
    columns = weight.shape[1]
    tile = 384 if columns % 384 == 0 else columns
    return pl.pallas_call(
        modulation_kernel,
        grid=(columns // tile,),
        in_specs=[
            full(cond),
            pl.BlockSpec((width, tile), lambda i: (0, i)),
            pl.BlockSpec((1, tile), lambda i: (0, i)),
        ],
        out_specs=[full(cond), pl.BlockSpec((slots, tile), lambda i: (0, i))],
        out_shape=[
            jax.ShapeDtypeStruct((slots, width), bf16),
            jax.ShapeDtypeStruct((slots, columns), bf16),
        ],
        cost_estimate=tiny,
        compiler_params=pltpu.CompilerParams(vmem_limit_bytes=16 * MIB),
        name="modulate",
    )(cond, weight, bias)


def feed_forward_kernel(parts, *refs):
    own_ref, met_ref, b_ref = refs[:3]
    pieces = refs[3 : 3 + 2 * parts]
    act_ref, back_ref, column_ref, own_sums, other_sums = refs[3 + 2 * parts : 8 + 2 * parts]
    x, g, weights, acts, backs, total, ins, outs = refs[8 + 2 * parts :]
    half, units = own_ref.shape[1], pieces[0].shape[1]
    copy = pltpu.make_async_copy

    def load(n):
        slot, copies = n % 2, []
        for kind in range(2):
            for side in range(2):
                copies.append(
                    copy(
                        pieces[2 * n + side].at[kind],
                        weights.at[slot, kind, pl.ds(side * units, units)],
                        ins.at[4 + 4 * n + 2 * kind + side],
                    )
                )
        return copies

    low, high = pl.ds(0, half), pl.ds(half, half)
    inputs = [
        copy(own_ref.at[0], x.at[low], ins.at[0]),
        copy(met_ref.at[0], x.at[high], ins.at[1]),
        copy(own_ref.at[1], g.at[low], ins.at[2]),
        copy(met_ref.at[1], g.at[high], ins.at[3]),
    ]
    loads = [load(n) for n in range(parts)]
    for item in inputs[:2] + loads[0][:2] + inputs[2:] + loads[0][2:] + loads[1]:
        item.start()
    stores = []
    root = 0.7978845608028654
    for n in range(parts):
        slot = n % 2
        for item in (inputs[:2] if n == 0 else []) + loads[n][:2]:
            item.wait()
        hidden = dot(x[...], weights[slot, 0], 1, 1) + b_ref[n : n + 1]
        square = hidden * hidden
        tanh = jnp.tanh(root * hidden * (1.0 + 0.044715 * square))
        acts[n] = (0.5 * hidden * (1.0 + tanh)).astype(bf16)
        slope = 0.5 * (1.0 + tanh) + 0.5 * hidden * (1.0 - tanh * tanh) * (root * (1.0 + 0.134145 * square))
        stores.append(copy(acts.at[n], act_ref.at[n], outs.at[2 * n]))
        stores[-1].start()
        for item in (inputs[2:] if n == 0 else []) + loads[n][2:]:
            item.wait()
        back = (dot(g[...], weights[slot, 1], 1, 1) * slope).astype(bf16)
        backs[n] = back
        stores.append(copy(backs.at[n], back_ref.at[n], outs.at[2 * n + 1]))
        stores[-1].start()
        column_ref[n : n + 1] = jnp.sum(back.astype(f32), axis=0, keepdims=True)
        for m, value in enumerate((dot(acts[n], weights[slot, 1], 1, 0), dot(back, weights[slot, 0], 1, 0))):
            for k in range(2):
                rows = value[k * half : (k + 1) * half]
                total[k, m] = rows if n == 0 else total[k, m] + rows
        if n + 2 < parts:
            for item in loads[n + 2]:
                item.start()
    for k, ref in ((1, other_sums), (0, own_sums)):
        stores.append(copy(total.at[k], ref, outs.at[2 * parts + k]))
        stores[-1].start()
    for item in stores:
        item.wait()


def feed_forward(own_in, met_in, bias, pieces):
    _, tokens, width = own_in.shape
    parts, units = len(pieces) // 2, pieces[0].shape[1]
    column = jax.ShapeDtypeStruct((parts, 2 * units), f32)
    hidden = [jax.ShapeDtypeStruct((parts, 2 * tokens, 2 * units), bf16)] * 2
    sums = [jax.ShapeDtypeStruct((2, tokens, width), f32)] * 2
    dma = pltpu.SemaphoreType.DMA
    return pl.pallas_call(
        functools.partial(feed_forward_kernel, parts),
        grid=(1,),
        in_specs=[any_spec, any_spec, full(bias)] + [any_spec] * len(pieces),
        out_specs=[any_spec] * 2 + [full(column), any_spec, any_spec],
        out_shape=hidden + [column] + [pltpu.HBM(a.shape, f32) for a in sums],
        scratch_shapes=[
            pltpu.VMEM((2 * tokens, width), bf16),
            pltpu.VMEM((2 * tokens, width), bf16),
            pltpu.VMEM((2, 2, 2 * units, width), bf16),
            pltpu.VMEM(hidden[0].shape, bf16),
            pltpu.VMEM(hidden[0].shape, bf16),
            pltpu.VMEM((2, 2, tokens, width), f32),
            dma((4 + 4 * parts,)),
            dma((2 * parts + 2,)),
        ],
        cost_estimate=tiny,
        compiler_params=pltpu.CompilerParams(vmem_limit_bytes=48 * MIB),
        name="feed_forward",
    )(own_in, met_in, bias, *pieces)


def fc_grad_kernel(parts, act_ref, back_ref, own_ref, met_ref, *refs):
    grads, (x, acts, backs, products, ins, outs) = refs[: 2 * parts], refs[2 * parts :]
    half, units = own_ref.shape[1], grads[0].shape[1]
    copy = pltpu.make_async_copy
    inputs = []
    for k, ref in enumerate((own_ref, met_ref)):
        for m in range(2):
            inputs.append(copy(ref.at[m], x.at[m, pl.ds(k * half, half)], ins.at[2 * k + m]))
    loads = [
        [
            copy(act_ref.at[n], acts.at[n], ins.at[4 + 2 * n]),
            copy(back_ref.at[n], backs.at[n], ins.at[5 + 2 * n]),
        ]
        for n in range(parts)
    ]
    for item in inputs + [item for pair in loads for item in pair]:
        item.start()
    stores = []
    for n in range(parts):
        for item in (inputs if n == 0 else []) + loads[n]:
            item.wait()
        if n >= 2:
            for item in stores[n - 2]:
                item.wait()
        stores.append([])
        for kind, left, right in ((0, backs, 0), (1, acts, 1)):
            products[n % 2, kind] = dot(left[n], x[right], 0, 0).astype(bf16)
            for side in range(2):
                stores[n].append(
                    copy(
                        products.at[n % 2, kind, pl.ds(side * units, units)],
                        grads[2 * n + side].at[kind],
                        outs.at[4 * n + 2 * kind + side],
                    )
                )
                stores[n][-1].start()
    for pair in stores[-2:]:
        for item in pair:
            item.wait()


def fc_grads_of(acts, backs, own_in, met_in):
    parts, tokens, columns = acts.shape
    width = own_in.shape[2]
    dma = pltpu.SemaphoreType.DMA
    return pl.pallas_call(
        functools.partial(fc_grad_kernel, parts),
        grid=(1,),
        in_specs=[any_spec] * 4,
        out_specs=[any_spec] * (2 * parts),
        out_shape=[pltpu.HBM((2, columns // 2, width), bf16)] * (2 * parts),
        scratch_shapes=[
            pltpu.VMEM((2, tokens, width), bf16),
            pltpu.VMEM(acts.shape, bf16),
            pltpu.VMEM(acts.shape, bf16),
            pltpu.VMEM((2, 2, columns, width), bf16),
            dma((4 + 2 * parts,)),
            dma((4 * parts,)),
        ],
        cost_estimate=tiny,
        compiler_params=pltpu.CompilerParams(vmem_limit_bytes=40 * MIB),
        name="fc_grads",
    )(acts, backs, own_in, met_in)


def on_device(
    tokens,
    cond,
    segment_ids,
    crop_slot,
    ada_weight,
    ada_bias,
    attn_weight,
    fc_in,
    fc_out,
    biases,
    out_grad,
):
    net = Net()
    tok_len, width = tokens.shape[1:]
    head_dim = width // HEADS
    mod_rank, core, chips = net.mod_rank, net.core, net.chips
    device_count = net.dp * net.mod
    crop_count = crop_slot.shape[1] // net.mod
    shard = attn_weight.shape[0]
    third = shard // 3
    chunks_of = [range(chips // 2), range(chips // 2, chips)]
    halves = [(n, side) for n in range(3) for side in range(2)]
    aligned = shard % (2 * head_dim) == 0 and third % 16 == 0 and width % (2 * net.mod * shard) == 0

    g_attn = Gather(net, attn_weight[None])
    g_fc = Gather(net, jnp.stack([fc_in, fc_out]))
    silu_cond, mod_own = modulate(cond, ada_weight, ada_bias.reshape(1, -1).astype(f32))
    for n in range(g_attn.count):
        g_attn.start()
        g_attn.got = [after(g_attn.got[0], mod_own)]
        g_attn.finish()
    g_attn.start()
    first = g_attn.value
    for n in range(g_fc.count):
        g_fc.start(*first)
        if n < g_fc.count - 1:
            g_fc.finish()
    g_attn.finish().start()
    g_attn.finish().start()
    third_phase = g_attn.value
    g_fc.got = [after(g_fc.got[0], *third_phase)]
    g_fc.finish().start(*g_attn.got)
    attn_pieces = [(g_attn.value, g_attn.got)[side][n] for n, side in halves]

    mod_other = net.swap(after(mod_own, *first), "mod")
    modulation = jnp.concatenate(
        [jnp.where(mod_rank == 0, mod_own, mod_other), jnp.where(mod_rank == 0, mod_other, mod_own)], axis=1
    )
    seg_ids = segment_ids[0]
    slots = lax.dynamic_slice_in_dim(crop_slot[0], mod_rank * crop_count, crop_count)
    crop_onehot = seg_ids[:, None] == jnp.arange(crop_count, dtype=jnp.int32)[None, :]
    token_slot = jnp.sum(jnp.where(crop_onehot, slots[None, :], 0), axis=1)
    slot_pick = token_slot[:, None] == jnp.arange(cond.shape[0], dtype=jnp.int32)[None, :]
    slot_pick = slot_pick.astype(bf16)
    modulation = after(modulation, *third_phase)
    mods = [modulation[:, n * width : (n + 1) * width] for n in range(6)]
    shift_a, scale_a, gate_a, shift_m, scale_m, gate_m = [times(slot_pick, block) for block in mods]

    slot_count, own_cols = cond.shape[0], width // net.dp
    to_dp = jnp.moveaxis(silu_cond.reshape(slot_count, net.dp, own_cols), 1, 0).reshape(net.dp, 1, -1)
    to_all = jnp.broadcast_to(to_dp, (net.dp, net.mod, slot_count * own_cols)).reshape(device_count, -1)
    to_all = after(to_all, *third_phase)
    sent = jnp.concatenate([jnp.broadcast_to(biases[None], (device_count, biases.shape[0])), to_all], axis=1)
    met = lax.all_to_all(sent, ("dp", "mod"), split_axis=0, concat_axis=0, tiled=True)
    ada_order = list(range(net.bits - 1, -1, -1))
    dp_order = net.ranks(ada_order, range(net.dp))[0]
    dp_pick = (dp_order[:, None] == jnp.arange(net.dp)[None, :]).astype(bf16)
    cond_cols = times(dp_pick, met.reshape(net.dp, net.mod, -1)[:, 0, biases.shape[0] :]).astype(bf16)
    cond_cols = cond_cols.reshape(-1, own_cols)
    bias_all = met[:, : biases.shape[0]].reshape(-1, width)
    bias_query, bias_value, bias_proj, bias_out = [bias_all[n].astype(f32) for n in range(4)]
    bias_in = bias_all[4:].reshape(device_count, 3, third)
    picks = []
    for n, side in halves:
        devices = net.devices(net.orders[n], chunks_of[side])
        picks.append((devices[:, None] == jnp.arange(device_count)[None, :]).astype(bf16))
    picks = jnp.stack(picks).reshape(3, 2, chips // 2, device_count)
    bias_pieces = jnp.einsum("nsjd,dnr->nsjr", picks, bias_in, preferred_element_type=f32).reshape(3, -1)

    def join(own, other):
        own, other = [a.reshape(-1, 1, net.mod * shard, a.shape[-1]) for a in (own, other)]
        both = jnp.where(core == 0, jnp.concatenate([own, other], 1), jnp.concatenate([other, own], 1))
        return both.reshape(-1, both.shape[-1])

    def part(whole):
        whole = whole.reshape(-1, 2, net.mod * shard, whole.shape[-1])
        return [
            jnp.where(core == c, whole[:, 0], whole[:, 1]).reshape(-1, whole.shape[-1]) for c in range(2)
        ]

    resid = tokens[0].astype(f32)
    normed_a, _ = layer_norm(resid)
    attn_in = (normed_a * (1.0 + scale_a) + shift_a).astype(bf16)
    if aligned:
        index = jnp.concatenate([net.local(net.orders[n], chunks_of[side]) * 3 + n for n, side in halves])
        own_weight = assemble(attn_pieces, index, third)
        qkv_rows = own_weight.shape[0] * 3 // 4
        qkv_weight = own_weight[:qkv_rows]
        proj_own = own_weight[qkv_rows:]
        proj_weight = join(proj_own, net.swap(proj_own, 0))
        ids = jnp.stack([seg_ids, net.swap(seg_ids, 0)])
        attn_in = after(attn_in, *third_phase)
        attn_both = jnp.concatenate([attn_in, net.swap(attn_in, 0)], axis=0)
        own_query, own_value = part(bias_query[:, None])[0], part(bias_value[:, None])[0]
        qkv_bias = jnp.concatenate([own_query, jnp.zeros_like(own_query), own_value], axis=0)
        attn_both = after(attn_both, *g_fc.got)
        g_fc.finish().start()
        qkv = (times_rows(qkv_weight, attn_both) + qkv_bias).astype(bf16)
        qkv = qkv.reshape(3, -1, 2 * head_dim, 2 * tok_len)
        context_both = attention(qkv, ids, head_dim).reshape(-1, 2 * tok_len)
        context = join(context_both[:, :tok_len], net.swap(context_both[:, tok_len:], 0))
        attn_out = dot(context, proj_weight, 0, 1) + bias_proj
    else:
        arrays = attn_pieces + [net.swap(piece, 0) for piece in attn_pieces]
        places = jnp.concatenate(
            [net.devices(net.orders[n], chunks_of[side], c) * 3 + n for c in range(2) for n, side in halves]
        )
        spread = jnp.concatenate(arrays, axis=1)[0]

        def place(n, whole):
            block = lax.dynamic_slice_in_dim(spread, n * third, third)
            return lax.dynamic_update_slice_in_dim(whole, block, places[n] * third, 0)

        attn_w = lax.fori_loop(0, places.shape[0], place, jnp.zeros_like(spread))
        g_fc.finish().start()
        g_fc.finish().start()
        qkv_weight, proj_weight = attn_w[: 3 * width], attn_w[3 * width :]
        qkv_bias = jnp.concatenate([bias_query, jnp.zeros_like(bias_query), bias_value])
        qkv = (times_rows(qkv_weight, attn_in) + qkv_bias[:, None]).astype(bf16)
        qkv = qkv.reshape(3, -1, 2 * head_dim, tok_len)
        context = attention(qkv, seg_ids[None], head_dim).reshape(-1, tok_len)
        attn_out = dot(context, proj_weight, 0, 1) + bias_proj
    mid = resid + gate_a * attn_out
    normed_m, _ = layer_norm(mid)
    mlp_in = (normed_m * (1.0 + scale_m) + shift_m).astype(bf16)
    if aligned:
        mlp_in = after(mlp_in, *g_fc.got)
        g_fc.finish().start()
    grad_mlp = (gate_m * out_grad[0].astype(f32)).astype(bf16)

    mlp_own = jnp.stack([mlp_in, grad_mlp])
    mlp_met = after(net.swap(mlp_own, 0), cond_cols, bias_pieces)
    grad_bias_out = jnp.sum(grad_mlp.astype(f32), axis=0, keepdims=True)
    fc_pieces = [(g_fc.value, g_fc.got)[side][n] for n, side in halves]
    acts, backs, columns, own_sums, other_sums = feed_forward(mlp_own, mlp_met, bias_pieces, fc_pieces)
    sums_met = net.swap(other_sums, 0)
    fc_grads = fc_grads_of(acts, backs, mlp_own, mlp_met)
    sums_met = after(sums_met, *fc_grads)
    back_way = Scatter(net, fc_grads[0::2], fc_grads[1::2])

    result, pair_m, grad_mid, grad_attn, grad_bias_proj, *parts = middle(
        core,
        net.mod * shard if aligned else None,
        own_sums,
        sums_met,
        mid,
        out_grad[0],
        slot_pick,
        modulation,
        bias_out[None],
        proj_weight,
        context,
    )
    if aligned:
        mine, other, proj_mine, proj_other = parts
        context_grads = [a.reshape(-1, 2 * head_dim, tok_len) for a in (mine, net.swap(other, 0))]
        proj_met = net.swap(after(proj_other, *context_grads), 0)
        grad_qkv = attention(qkv, ids, head_dim, context_grads)
        grad_qkv = grad_qkv.reshape(-1, 2 * tok_len)
        back_own, back_other = attn_in_grads(grad_qkv, own_weight)
        back_met = net.swap(back_other, 0)
        grad_qkv = after(grad_qkv, back_own)
        places = jnp.sum(
            jnp.where(
                index[None, :] == jnp.arange(index.shape[0], dtype=index.dtype)[:, None],
                jnp.arange(index.shape[0], dtype=index.dtype)[None, :],
                0,
            ),
            axis=1,
        )
        pieces = weight_grad(grad_qkv, attn_both, proj_mine, proj_met, places, third)
        back_met = after(back_met, pieces)
    else:
        grad_context, grad_proj = parts
        grad_qkv = attention(
            qkv, seg_ids[None], head_dim, [grad_context.reshape(-1, 2 * head_dim, tok_len)]
        ).reshape(-1, tok_len)
        attn_grad = jnp.concatenate([times(grad_qkv, attn_in).astype(bf16), grad_proj], axis=0)

        def take(n, whole):
            block = lax.dynamic_slice_in_dim(attn_grad, places[n] * third, third)
            return lax.dynamic_update_slice_in_dim(whole, block, n * third, 0)

        grads = lax.fori_loop(0, places.shape[0], take, jnp.zeros_like(attn_grad))
        grads = jnp.split(grads[None], 12, axis=1)
        pieces = jnp.concatenate([summed(a, net.swap(b, 0)) for a, b in zip(grads[:6], grads[6:])], axis=1)
        back_own = contract_rows(grad_qkv, qkv_weight)
        back_met = jnp.zeros_like(back_own)
    grad_tokens, pair_a = end_call(
        attn_end_kernel, f32, slot_count, back_own, back_met, tokens[0], grad_mid, attn_out, slot_pick, modulation
    )
    pair_a, *back_way.got = lax.optimization_barrier((pair_a, *back_way.got))
    pair_own = jnp.where(mod_rank == 0, pair_a, pair_m)
    pair_send = jnp.where(mod_rank == 0, pair_m, pair_a)
    grad_mod = summed(pair_own, net.swap(pair_send, "mod"))
    for n in range(3):
        back_way.hold(n, grad_mod)
    mod_rows = jnp.concatenate([grad_mod, net.swap(grad_mod, ada_order[0])], axis=0)
    sends = [back_way.join(0, pieces), back_way.join(1, pieces)]
    back_way.hold(2, mod_rows)
    sends.append(back_way.join(2, pieces))
    grad_qkv, columns = lax.optimization_barrier((grad_qkv, columns, *sends))[:2]

    grad_silu = times_rows(grad_mod, ada_weight)
    silu_own = jnp.where(mod_rank == 0, grad_silu[:crop_count], grad_silu[crop_count:])
    silu_send = jnp.where(mod_rank == 0, grad_silu[crop_count:], grad_silu[:crop_count]).astype(bf16)

    column = jnp.sum(grad_qkv.astype(f32), axis=1, keepdims=True).reshape(3, -1, 1)
    if aligned:
        none = jnp.zeros_like(column[0])
        column = [join(column[0], none), None, join(column[2], none)]
    columns = columns.reshape(3, 2, chips // 2, third)
    grad_bias_in = jnp.einsum("nsjd,nsjr->dnr", picks.astype(f32), columns, precision=lax.Precision.HIGHEST)
    grad_bias = stack_rows(
        column[0].reshape(1, -1),
        column[2].reshape(1, -1),
        grad_bias_proj,
        grad_bias_out,
        grad_bias_in.reshape(-1, width),
    )
    bias_rows = lax.all_to_all(
        grad_bias.reshape(device_count, -1), ("dp", "mod"), split_axis=0, concat_axis=0, tiled=True
    )
    bias_sum = jnp.sum(bias_rows, axis=0)
    mod_rows = after(mod_rows, *back_way.got)
    mod_rows = jnp.concatenate([mod_rows, net.swap(mod_rows, ada_order[1])], axis=0)
    for n in range(3):
        back_way.hold(n, silu_send, bias_sum)
    sends = [back_way.second(0), back_way.second(1)]
    back_way.hold(2, mod_rows)
    sends.append(back_way.second(2))
    back_way.second_attn(sends)
    back_way.third()
    back_way.third_attn()
    silu_send = after(silu_send, *back_way.also_got)
    grad_silu = silu_own + net.swap(silu_send, "mod").astype(f32)
    own_cond = lax.dynamic_slice_in_dim(cond, mod_rank * crop_count, crop_count, 0).astype(f32)
    silu_back = jax.vjp(jax.nn.silu, own_cond)[1]
    grad_cond = silu_back(grad_silu)[0]

    mod_rows = after(mod_rows, *back_way.also_got)
    fc_sum, attn_sum = back_way.last()
    for dim in ada_order[2:]:
        mod_rows = jnp.concatenate([mod_rows, net.swap(mod_rows, dim)], axis=0)
    ada_w_sum = contract_rows(cond_cols, mod_rows)
    ada_b_sum = jnp.sum(mod_rows.astype(f32), axis=0).reshape(ada_bias.shape[0], width)
    ada_b_sum = lax.dynamic_slice_in_dim(ada_b_sum, net.dp_rank * own_cols, own_cols, 1)

    return (
        result[None],
        grad_tokens[None],
        grad_cond,
        ada_w_sum,
        ada_b_sum,
        attn_sum[0],
        fc_sum[0],
        fc_sum[1],
        bias_sum,
    )


def solution(mesh):
    placed = (
        P(("dp", "mod"), None, None),
        P("dp", None),
        P(("dp", "mod"), None),
        P("dp", None),
        P(None, "mod"),
        P("mod", None),
        P(("dp", "mod"), None),
        P(("dp", "mod"), None),
        P(("dp", "mod"), None),
        P(("dp", "mod")),
        P(("dp", "mod"), None, None),
    )
    return jax.shard_map(
        on_device,
        mesh=mesh,
        in_specs=placed,
        out_specs=(
            P(("dp", "mod"), None, None),
            P(("dp", "mod"), None, None),
            P(("dp", "mod"), None),
            P("dp", "mod"),
            P("mod", "dp"),
            P(("dp", "mod"), None),
            P(("dp", "mod"), None),
            P(("dp", "mod"), None),
            P(("dp", "mod")),
        ),
        check_vma=False,
    )
```

```python
import functools

import jax
import jax.numpy as jnp
import numpy as np
from jax import lax
from jax.experimental import pallas as pl
from jax.experimental.pallas import tpu as pltpu
from jax.sharding import PartitionSpec as P

HEADS = 16
norm_eps = 1e-06
bf16 = jnp.bfloat16
f32 = jnp.float32
MIB = 1024 * 1024


def layer_norm(values):
    center = values - jnp.mean(values, axis=-1, keepdims=True)
    inverse = lax.rsqrt(jnp.mean(center * center, axis=-1, keepdims=True) + norm_eps)
    return (center * inverse, inverse)


def norm_back(grad_in, normed, inverse):
    centered = grad_in - jnp.mean(grad_in, axis=-1, keepdims=True)
    return (centered - normed * jnp.mean(grad_in * normed, axis=-1, keepdims=True)) * inverse


def dot(left, right, left_dim, right_dim):
    return lax.dot_general(left, right, (((left_dim,), (right_dim,)), ((), ())), preferred_element_type=f32)


def times(left, right):
    return dot(left, right, 1, 0)


def times_rows(left, right):
    return dot(left, right, 1, 1)


def contract_rows(left, right):
    return dot(left, right, 0, 0)


def after(value, *others):
    return lax.optimization_barrier((value, *others))[0]


def summed(left, right):
    return (left.astype(f32) + right.astype(f32)).astype(bf16)


class Net:
    def __init__(self):
        self.dp = lax.axis_size("dp")
        self.mod = lax.axis_size("mod")
        self.bits = self.dp.bit_length() - 1
        self.dp_rank = lax.axis_index("dp")
        self.mod_rank = lax.axis_index("mod")
        self.core = self.dp_rank & 1
        self.chips = self.dp // 2 * self.mod
        self.lead = list(range(self.bits - 1, 2, -1))
        last = ["mod", 1, 2]
        self.turns = [last[n:] + last[:n] for n in range(3)]
        self.orders = [self.lead + turn for turn in self.turns]

    def swap(self, value, dim):
        if dim == "mod":
            return lax.ppermute(value, "mod", [(i, i ^ 1) for i in range(self.mod)])
        return lax.ppermute(value, "dp", [(i, i ^ (1 << dim)) for i in range(self.dp)])

    def ranks(self, order, chunks, core=0):
        masks = []
        for j in chunks:
            dp_mask, mod_mask = core, 0
            for step, dim in enumerate(order):
                if j >> step & 1:
                    if dim == "mod":
                        mod_mask ^= 1
                    else:
                        dp_mask ^= 1 << dim
            masks.append((dp_mask, mod_mask))
        masks = np.array(masks, np.int32)
        return self.dp_rank ^ masks[:, 0], self.mod_rank ^ masks[:, 1]

    def devices(self, order, chunks, core=0):
        dp, mod = self.ranks(order, chunks, core)
        return dp * self.mod + mod

    def local(self, order, chunks):
        dp, mod = self.ranks(order, chunks)
        return (dp >> 1) * self.mod + mod


class Gather:
    def __init__(self, net, shard):
        self.net, self.count = net, len(net.lead)
        self.third = shard.shape[1] // 3
        self.value, self.got, self.phase = shard, None, 0

    def start(self, *others):
        net, phase = self.net, self.phase
        if phase < self.count:
            self.value = after(self.value, *others) if others else self.value
            self.got = [net.swap(self.value, net.lead[phase])]
        else:
            if phase == self.count:
                kinds, _, width = self.value.shape
                whole = self.value.reshape(kinds, -1, 3, self.third, width)
                self.value = [whole[:, :, n].reshape(kinds, -1, width) for n in range(3)]
            if others:
                self.value = list(lax.optimization_barrier((*self.value, *others))[:3])
            step = phase - self.count
            self.got = [net.swap(self.value[n], net.turns[n][step]) for n in range(3)]
        self.phase += 1
        return self

    def finish(self):
        if self.phase <= self.count:
            self.value = jnp.concatenate([self.value, self.got[0]], axis=1)
        elif self.phase < self.count + 3:
            self.value = [jnp.concatenate(pair, axis=1) for pair in zip(self.value, self.got)]
        return self


any_spec = pl.BlockSpec(memory_space=pl.ANY)


def full(value):
    return pl.BlockSpec(value.shape, lambda *_: (0,) * len(value.shape))

tiny = pl.CostEstimate(flops=1024, bytes_accessed=1024, transcendentals=0)


def run_copies(copies):
    for copy in copies:
        copy.start()
    for copy in copies:
        copy.wait()


def assemble_kernel(rows, each, index_ref, *refs):
    pieces, out_ref, hold, sems, last = refs[:-4], *refs[-4:]
    copies = []
    for n, piece in enumerate(pieces):
        for j in range(each):
            at = pl.multiple_of(index_ref[n * each + j] * rows, rows)
            copies.append(
                pltpu.make_async_copy(
                    piece.at[0, pl.ds(j * rows, rows)], hold.at[pl.ds(at, rows)], sems.at[n * each + j]
                )
            )
    run_copies(copies)
    run_copies([pltpu.make_async_copy(hold, out_ref, last)])


def assemble(pieces, index, rows):
    each, width = pieces[0].shape[1] // rows, pieces[0].shape[2]
    total = len(pieces) * each
    return pl.pallas_call(
        functools.partial(assemble_kernel, rows, each),
        grid_spec=pltpu.PrefetchScalarGridSpec(
            num_scalar_prefetch=1,
            grid=(1,),
            in_specs=[any_spec] * len(pieces),
            out_specs=any_spec,
            scratch_shapes=[
                pltpu.VMEM((total * rows, width), bf16),
                pltpu.SemaphoreType.DMA((total,)),
                pltpu.SemaphoreType.DMA,
            ],
        ),
        out_shape=jax.ShapeDtypeStruct((total * rows, width), bf16),
        compiler_params=pltpu.CompilerParams(vmem_limit_bytes=60 * MIB),
        name="assemble",
    )(index, *pieces)


def added(left, right):
    return (left.astype(f32) + right.astype(f32)).astype(bf16)


def sums_call(kernel, grid, in_specs, out_specs, outs, *args):
    return pl.pallas_call(
        kernel,
        grid=grid,
        in_specs=in_specs,
        out_specs=out_specs,
        out_shape=[pltpu.HBM(out, bf16) for out in outs],
        cost_estimate=tiny,
        compiler_params=pltpu.CompilerParams(vmem_limit_bytes=60 * MIB),
        name=kernel.__name__,
    )(*args)


def first_sums(own_low, own_high, got_low, got_high, also, keep, send):
    keep[...] = added(own_low[...], got_low[...])
    send[:2] = added(own_high[...], got_high[...])
    send[2:] = also[...]


def half_sums(own, got, keep, send):
    half = keep.shape[1]
    keep[...] = added(own[:, :half], got[:, :half])
    send[...] = added(own[:, half:], got[:, half:])


def block_sums(own, got, keep, send):
    keep[0] = added(own[0], got[0])
    send[0] = added(own[1], got[1])


def third_sums(*refs):
    outs = refs[6:]
    for n in range(3):
        total = added(refs[n][...], refs[3 + n][...])
        if len(outs) == 2:
            rows = total.shape[1] // 2
            outs[0][:, n * rows : (n + 1) * rows] = total[:, :rows]
            outs[1][:, n * rows : (n + 1) * rows] = total[:, rows:]
        else:
            outs[n][...] = total


def third_attn_sums(*refs):
    for n in range(3):
        half_sums(refs[n], refs[3 + n], refs[6 + 2 * n], refs[7 + 2 * n])


def fourth_sums(*refs):
    keep, send = refs[6:]
    rows = keep.shape[1] // 3
    for n in range(3):
        total = added(refs[n][0], refs[3 + n][0])
        keep[0, n * rows : (n + 1) * rows] = total[:rows]
        send[0, n * rows : (n + 1) * rows] = total[rows:]


class Scatter:
    def __init__(self, net, own, other):
        self.net = net
        self.own = list(own)
        self.got = [net.swap(other[n], net.turns[n][2]) for n in range(3)]
        self.aligned = len(net.lead) == 1 and own[0].shape[1] // 8 % 16 == 0

    def hold(self, n, *others):
        self.got[n] = after(self.got[n], *others)

    def join(self, n, pieces):
        _, rows, width = self.own[n].shape
        half = rows // 2
        step = half // 6
        also = 2 * ((n + 2) % 3)
        self.pieces = pieces.reshape(12, half, width)
        block = (2, step, width)
        low, high = pl.BlockSpec(block, lambda i: (0, i, 0)), pl.BlockSpec(block, lambda i: (0, i + 6, 0))
        self.own[n], send = sums_call(
            first_sums,
            (6,),
            [low, high, low, high, pl.BlockSpec(block, lambda i: (also + 1, i, 0))],
            [low, pl.BlockSpec((4, step, width), lambda i: (0, i, 0))],
            [(2, half, width), (4, half, width)],
            self.own[n],
            self.own[n],
            self.got[n],
            self.got[n],
            self.pieces,
        )
        self.got[n] = self.net.swap(send, self.net.turns[n][1])
        return send

    def second(self, n):
        _, rows, width = self.own[n].shape
        outs = [(2, rows // 2, width)] * 2
        self.both = getattr(self, "both", [None] * 3)
        self.both[n] = self.got[n]
        self.own[n], send = sums_call(
            half_sums,
            (1,),
            [full(self.own[n]), pl.BlockSpec((2, rows, width), lambda i: (0, 0, 0))],
            [full(jax.ShapeDtypeStruct(out, bf16)) for out in outs],
            outs,
            self.own[n],
            self.got[n],
        )
        self.got[n] = self.net.swap(send, self.net.turns[n][0])
        return send

    def second_attn(self, others):
        self.also, self.also_got = [None] * 3, [None] * 3
        both = list(lax.optimization_barrier((*self.both, *others))[:3])
        for n in range(3):
            _, rows, width = both[n].shape
            piece = 2 * ((n + 2) % 3)
            outs = [(1, rows, width)] * 2
            self.also[n], send = sums_call(
                block_sums,
                (1,),
                [
                    pl.BlockSpec((2, rows, width), lambda i: (piece, 0, 0)),
                    pl.BlockSpec((2, rows, width), lambda i: (1, 0, 0)),
                ],
                [full(jax.ShapeDtypeStruct(out, bf16)) for out in outs],
                outs,
                self.pieces,
                both[n],
            )
            self.also_got[n] = self.net.swap(send, self.net.turns[n][0])

    def third(self):
        net = self.net
        _, rows, width = self.own[0].shape
        outs = [(2, rows // 2 * 3, width)] * 2 if self.aligned else [(2, rows, width)] * 3
        args = self.own + self.got
        results = sums_call(
            third_sums,
            (1,),
            [full(a) for a in args],
            [full(jax.ShapeDtypeStruct(out, bf16)) for out in outs],
            outs,
            *args,
        )
        if self.aligned:
            self.fc = results[0], net.swap(results[1], net.lead[0])
        else:
            self.fc = self.lead(self.together(results), len(net.lead) - 1)
        self.also_got = list(lax.optimization_barrier((*self.also_got, results[1]))[:3])

    def third_attn(self):
        net = self.net
        _, rows, width = self.also[0].shape
        args, outs = self.also + self.also_got, [(1, rows // 2, width)] * 6
        results = sums_call(
            third_attn_sums,
            (1,),
            [full(a) for a in args],
            [full(jax.ShapeDtypeStruct(out, bf16)) for out in outs],
            outs,
            *args,
        )
        self.also = results[0::2]
        self.also_got = [net.swap(results[2 * n + 1], net.turns[(n + 2) % 3][0]) for n in range(3)]

    def last(self):
        net = self.net
        order = (1, 2, 0)
        keep, got = [self.also[n] for n in order], [self.also_got[n] for n in order]
        *got, fc_got = lax.optimization_barrier((*got, self.fc[1]))
        self.fc = self.fc[0], fc_got
        if self.aligned:
            _, rows, width = keep[0].shape
            outs = [(1, rows // 2 * 3, width)] * 2
            own, send = sums_call(
                fourth_sums,
                (1,),
                [full(a) for a in keep + got],
                [full(jax.ShapeDtypeStruct(out, bf16)) for out in outs],
                outs,
                *keep,
                *got,
            )
            attn = own, net.swap(send, net.lead[0])
        else:
            attn = self.lead(self.together([summed(a, b) for a, b in zip(keep, got)]), len(net.lead) - 1)
        sums = []
        for own, got in (self.fc, attn):
            for step in range(len(net.lead) - 1, -1, -1):
                total = own.astype(f32) + got.astype(f32)
                if step:
                    own, got = self.lead(total.astype(bf16), step - 1)
            sums.append(total)
        return sums

    def together(self, parts):
        kinds, _, width = parts[0].shape
        count = 1 << len(self.net.lead)
        return jnp.concatenate([p.reshape(kinds, count, -1, width) for p in parts], axis=2).reshape(kinds, -1, width)

    def lead(self, whole, step):
        half = whole.shape[1] // 2
        return whole[:, :half], self.net.swap(whole[:, half:], self.net.lead[step])


def attn_in_kernel(grad_ref, weight_ref, own_ref, other_ref):
    total = dot(grad_ref[...], weight_ref[...], 0, 0)
    half = own_ref.shape[0]
    own_ref[...] = total[:half]
    other_ref[...] = total[half:]


def attn_in_grads(grad, weight):
    rows, tokens = grad.shape
    width = weight.shape[1]
    out = jax.ShapeDtypeStruct((tokens // 2, width), f32)
    return pl.pallas_call(
        attn_in_kernel,
        grid=(1,),
        in_specs=[full(grad), pl.BlockSpec((rows, width), lambda i: (0, 0))],
        out_specs=[full(out)] * 2,
        out_shape=[out, pltpu.HBM(out.shape, f32)],
        cost_estimate=tiny,
        compiler_params=pltpu.CompilerParams(vmem_limit_bytes=60 * MIB),
        name="attn_in_grads",
    )(grad, weight)


def weight_grad_kernel(rows, place_ref, grad_ref, x_ref, mine_ref, other_ref, out_ref, hold, sems):
    top, copies = grad_ref.shape[0], []
    step = top // 3
    for n in (3, 0, 1, 2):
        start = n * step
        stop = min(start + step, hold.shape[0])
        if n == 3:
            hold[start:] = summed(mine_ref[...], other_ref[...])
        else:
            hold[start:stop] = dot(grad_ref[start:stop], x_ref[...], 1, 0).astype(bf16)
        for unit in range(start // rows, stop // rows):
            at = pl.multiple_of(place_ref[unit] * rows, rows)
            copies.append(
                pltpu.make_async_copy(
                    hold.at[pl.ds(unit * rows, rows)], out_ref.at[pl.ds(at, rows)], sems.at[unit]
                )
            )
            copies[-1].start()
    for copy in copies:
        copy.wait()


def weight_grad(grad, x, mine, other, places, rows):
    total, width = grad.shape[0] + mine.shape[0], x.shape[1]
    return pl.pallas_call(
        functools.partial(weight_grad_kernel, rows),
        grid_spec=pltpu.PrefetchScalarGridSpec(
            num_scalar_prefetch=1,
            grid=(1,),
            in_specs=[full(a) for a in (grad, x, mine, other)],
            out_specs=any_spec,
            scratch_shapes=[pltpu.VMEM((total, width), bf16), pltpu.SemaphoreType.DMA((total // rows,))],
        ),
        out_shape=jax.ShapeDtypeStruct((total, width), bf16),
        cost_estimate=tiny,
        compiler_params=pltpu.CompilerParams(vmem_limit_bytes=60 * MIB),
        name="weight_grad",
    )(places, grad, x, mine, other)


def by_core(core_ref, group, whole):
    if group is None:
        return [whole]
    picked = []
    for c in range(2):
        rows = []
        for at in range(0, whole.shape[0], 2 * group):
            first, second = whole[at : at + group], whole[at + group : at + 2 * group]
            rows.append(jnp.where(core_ref[0] == c, first, second))
        picked.append(jnp.concatenate(rows, axis=0))
    return picked


def token_block(pick, mods, n):
    width = mods.shape[1] // 6
    return dot(pick[...], mods[:, n * width : (n + 1) * width], 1, 0)


def middle_kernel(group, core_ref, *refs):
    sums, met, mid, grad_out, pick, mods, bias, weight, context = refs[:9]
    result_ref, pair_ref, mid_ref, attn_ref, column_ref = refs[9:14]
    normed, inverse = layer_norm(mid[...])
    back, outer = sums[1] + met[1], grad_out[...].astype(f32)
    mlp_out = sums[0] + met[0] + bias[...]
    result_ref[...] = (mid[...] + token_block(pick, mods, 5) * mlp_out).astype(bf16)
    slot_sums(pick[...], (back, back * normed, outer * mlp_out), pair_ref)
    grad_mid = outer + norm_back(back * (1.0 + token_block(pick, mods, 4)), normed, inverse)
    mid_ref[...] = grad_mid
    grad_attn = (token_block(pick, mods, 2) * grad_mid).astype(bf16)
    attn_ref[...] = grad_attn
    column_ref[...] = jnp.sum(grad_attn.astype(f32), axis=0, keepdims=True)
    parts = by_core(core_ref, group, dot(weight[...], grad_attn, 0, 1))
    parts += by_core(core_ref, group, dot(grad_attn, context[...], 0, 1))
    for ref, value in zip(refs[14:], parts):
        ref[...] = value.astype(bf16)


def middle(core, group, *args):
    _, tokens, width = args[0].shape
    if group is None:
        sizes = [(width, tokens), (width, width)]
    else:
        sizes = [(width // 2, tokens)] * 2 + [(width // 2, width)] * 2
    slots = args[4].shape[1]
    outs = [((tokens, width), bf16), ((slots, 3 * width), bf16)]
    outs += [((tokens, width), f32), ((tokens, width), bf16), ((1, width), f32)]
    outs = [jax.ShapeDtypeStruct(*out) for out in outs + [(s, bf16) for s in sizes]]
    return pl.pallas_call(
        functools.partial(middle_kernel, group),
        grid=(1,),
        in_specs=[pl.BlockSpec(memory_space=pltpu.SMEM)] + [full(a) for a in args],
        out_specs=[full(a) for a in outs],
        out_shape=outs[:5] + [pltpu.HBM(a.shape, bf16) for a in outs[5:]],
        cost_estimate=tiny,
        compiler_params=pltpu.CompilerParams(vmem_limit_bytes=60 * MIB),
        name="middle",
    )(core.reshape(1), *args)


def slot_sums(pick, blocks, out_ref):
    for n, block in enumerate(blocks):
        high = block.astype(bf16)
        low = (block - high.astype(f32)).astype(bf16)
        total = dot(pick, high, 0, 0) + dot(pick, low, 0, 0)
        out_ref[:, n * block.shape[1] : (n + 1) * block.shape[1]] = total.astype(bf16)


def attn_end_kernel(*refs):
    back_a, back_b, resid, grad_mid, attn_out, pick, mods = refs[:7]
    tokens_ref, pair_ref = refs[7:]
    back = back_a[...] + back_b[...]
    normed, inverse = layer_norm(resid[...].astype(f32))
    slope = back * (1.0 + token_block(pick, mods, 1))
    tokens_ref[...] = grad_mid[...] + norm_back(slope, normed, inverse)
    slot_sums(pick[...], (back, back * normed, grad_mid[...] * attn_out[...]), pair_ref)


def end_call(kernel, dtype, slots, *args):
    tokens, width = args[0].shape
    outs = [jax.ShapeDtypeStruct((tokens, width), dtype), jax.ShapeDtypeStruct((slots, 3 * width), bf16)]
    return pl.pallas_call(
        kernel,
        grid=(1,),
        in_specs=[full(a) for a in args],
        out_specs=[full(a) for a in outs],
        out_shape=outs,
        cost_estimate=tiny,
        compiler_params=pltpu.CompilerParams(vmem_limit_bytes=60 * MIB),
        name=kernel.__name__,
    )(*args)


def rows_kernel(*refs):
    at = 0
    for ref in refs[:-1]:
        refs[-1][at : at + ref.shape[0]] = ref[...]
        at += ref.shape[0]


def stack_rows(*args):
    out = jax.ShapeDtypeStruct((sum(a.shape[0] for a in args), args[0].shape[1]), f32)
    return pl.pallas_call(
        rows_kernel,
        grid=(1,),
        in_specs=[full(a) for a in args],
        out_specs=full(out),
        out_shape=out,
        cost_estimate=tiny,
        compiler_params=pltpu.CompilerParams(vmem_limit_bytes=60 * MIB),
        name="stack_rows",
    )(*args)


def softmax_t(key, query, same, scale):
    scores = jnp.where(same, dot(key, query, 0, 0) * scale, -1e30)
    weights = jnp.exp(scores - jnp.max(scores, axis=0, keepdims=True))
    return weights * (1.0 / jnp.sum(weights, axis=0, keepdims=True))


def heads_of(block, dim, cols):
    wide = block[:, cols].astype(f32)
    return [wide[n * dim : (n + 1) * dim].astype(bf16) for n in range(wide.shape[0] // dim)]


def attn_forward(dim, scale, row_ref, col_ref, q_ref, k_ref, v_ref, out_ref):
    length = col_ref.shape[0]
    for s in range(row_ref.shape[0]):
        cols = slice(s * length, (s + 1) * length)
        same = row_ref[s : s + 1] == col_ref[:, s : s + 1]
        outs = []
        for q, k, v in zip(*[heads_of(r[0, 0], dim, cols) for r in (q_ref, k_ref, v_ref)]):
            probs = softmax_t(k, q, same, scale).astype(bf16)
            outs.append(dot(v, probs, 1, 0))
        out_ref[0, :, cols] = jnp.concatenate(outs, axis=0).astype(bf16)


def attn_backward(dim, scale, row_ref, col_ref, q_ref, k_ref, v_ref, *refs):
    length, out_ref = col_ref.shape[0], refs[-1]
    for s in range(row_ref.shape[0]):
        cols = slice(s * length, (s + 1) * length)
        same = row_ref[s : s + 1] == col_ref[:, s : s + 1]
        gq, gk, gv = [], [], []
        qs, ks, vs = [heads_of(r[0, 0], dim, cols) for r in (q_ref, k_ref, v_ref)]
        for q, k, v, g in zip(qs, ks, vs, heads_of(refs[s][0], dim, slice(0, length))):
            probs = softmax_t(k, q, same, scale)
            back = dot(v, g, 0, 0)
            back = probs * (back - jnp.sum(back * probs, axis=0, keepdims=True))
            back = back.astype(bf16)
            gq.append(dot(k, back, 1, 0) * scale)
            gk.append(dot(q, back, 1, 1) * scale)
            gv.append(dot(g, probs.astype(bf16), 1, 1))
        for n, parts in enumerate((gq, gk, gv)):
            out_ref[n, 0, :, cols] = jnp.concatenate(parts, axis=0).astype(bf16)


def attention(qkv, ids, dim, grad=None):
    _, groups, rows, tokens = qkv.shape
    scale = dim**-0.5
    ids_t = ids.T

    def one(n):
        return pl.BlockSpec((1, 1, rows, tokens), lambda i: (n, i, 0, 0))

    flat = pl.BlockSpec((1, rows, tokens), lambda i: (i, 0, 0))
    short = pl.BlockSpec((1, rows, ids.shape[1]), lambda i: (i, 0, 0))
    args = [ids, ids_t, qkv, qkv, qkv]
    specs = [pl.BlockSpec(a.shape, lambda i: (0, 0)) for a in (ids, ids_t)] + [one(0), one(1), one(2)]
    if grad is None:
        return pl.pallas_call(
            functools.partial(attn_forward, dim, scale),
            grid=(groups,),
            in_specs=specs,
            out_specs=flat,
            out_shape=jax.ShapeDtypeStruct((groups, rows, tokens), bf16),
            cost_estimate=tiny,
            compiler_params=pltpu.CompilerParams(vmem_limit_bytes=60 * MIB),
            name="attention",
        )(*args)
    return pl.pallas_call(
        functools.partial(attn_backward, dim, scale),
        grid=(groups,),
        in_specs=specs + [short] * len(grad),
        out_specs=pl.BlockSpec((3, 1, rows, tokens), lambda i: (0, i, 0, 0)),
        out_shape=jax.ShapeDtypeStruct(qkv.shape, bf16),
        cost_estimate=tiny,
        compiler_params=pltpu.CompilerParams(vmem_limit_bytes=60 * MIB),
        name="attention_back",
    )(*args, *grad)


def modulation_kernel(cond_ref, weight_ref, bias_ref, silu_ref, out_ref):
    cond = cond_ref[...].astype(f32)
    silu = (cond / (1.0 + jnp.exp(-cond))).astype(bf16)
    silu_ref[...] = silu
    out_ref[...] = (dot(silu, weight_ref[...], 1, 0) + bias_ref[...]).astype(bf16)


def modulate(cond, weight, bias):
    slots, width = cond.shape
    columns = weight.shape[1]
    tile = 384 if columns % 384 == 0 else columns
    return pl.pallas_call(
        modulation_kernel,
        grid=(columns // tile,),
        in_specs=[
            full(cond),
            pl.BlockSpec((width, tile), lambda i: (0, i)),
            pl.BlockSpec((1, tile), lambda i: (0, i)),
        ],
        out_specs=[full(cond), pl.BlockSpec((slots, tile), lambda i: (0, i))],
        out_shape=[
            jax.ShapeDtypeStruct((slots, width), bf16),
            jax.ShapeDtypeStruct((slots, columns), bf16),
        ],
        cost_estimate=tiny,
        compiler_params=pltpu.CompilerParams(vmem_limit_bytes=60 * MIB),
        name="modulate",
    )(cond, weight, bias)


def feed_forward_kernel(parts, *refs):
    own_ref, met_ref, b_ref = refs[:3]
    pieces = refs[3 : 3 + 2 * parts]
    act_ref, back_ref, column_ref, own_sums, other_sums = refs[3 + 2 * parts : 8 + 2 * parts]
    x, g, weights, acts, backs, total, ins, outs = refs[8 + 2 * parts :]
    half, units = own_ref.shape[1], pieces[0].shape[1]
    copy = pltpu.make_async_copy

    def load(n):
        slot, copies = n % 2, []
        for kind in range(2):
            for side in range(2):
                copies.append(
                    copy(
                        pieces[2 * n + side].at[kind],
                        weights.at[slot, kind, pl.ds(side * units, units)],
                        ins.at[4 + 4 * n + 2 * kind + side],
                    )
                )
        return copies

    low, high = pl.ds(0, half), pl.ds(half, half)
    inputs = [
        copy(own_ref.at[0], x.at[low], ins.at[0]),
        copy(met_ref.at[0], x.at[high], ins.at[1]),
        copy(own_ref.at[1], g.at[low], ins.at[2]),
        copy(met_ref.at[1], g.at[high], ins.at[3]),
    ]
    loads = [load(n) for n in range(parts)]
    for item in inputs[:2] + loads[0][:2] + inputs[2:] + loads[0][2:] + loads[1]:
        item.start()
    stores = []
    root = 0.7978845608028654
    for n in range(parts):
        slot = n % 2
        for item in (inputs[:2] if n == 0 else []) + loads[n][:2]:
            item.wait()
        for item in (inputs[2:] if n == 0 else []) + loads[n][2:]:
            item.wait()
        col = 0.0
        for k in range(2):
            tok = slice(k * half, (k + 1) * half)
            hidden = dot(x[tok], weights[slot, 0], 1, 1) + b_ref[n : n + 1]
            square = hidden * hidden
            tanh = jnp.tanh(root * hidden * (1.0 + 0.044715 * square))
            act = (0.5 * hidden * (1.0 + tanh)).astype(bf16)
            acts[n, tok] = act
            slope = 0.5 * (1.0 + tanh) + 0.5 * hidden * (1.0 - tanh * tanh) * (root * (1.0 + 0.134145 * square))
            back = (dot(g[tok], weights[slot, 1], 1, 1) * slope).astype(bf16)
            backs[n, tok] = back
            col = col + jnp.sum(back.astype(f32), axis=0, keepdims=True)
            for m, value in enumerate((dot(act, weights[slot, 1], 1, 0), dot(back, weights[slot, 0], 1, 0))):
                total[k, m] = value if n == 0 else total[k, m] + value
        column_ref[n : n + 1] = col
        stores.append(copy(acts.at[n], act_ref.at[n], outs.at[2 * n]))
        stores[-1].start()
        stores.append(copy(backs.at[n], back_ref.at[n], outs.at[2 * n + 1]))
        stores[-1].start()
        if n + 2 < parts:
            for item in loads[n + 2]:
                item.start()
    for k, ref in ((1, other_sums), (0, own_sums)):
        stores.append(copy(total.at[k], ref, outs.at[2 * parts + k]))
        stores[-1].start()
    for item in stores:
        item.wait()


def feed_forward(own_in, met_in, bias, pieces):
    _, tokens, width = own_in.shape
    parts, units = len(pieces) // 2, pieces[0].shape[1]
    column = jax.ShapeDtypeStruct((parts, 2 * units), f32)
    hidden = [jax.ShapeDtypeStruct((parts, 2 * tokens, 2 * units), bf16)] * 2
    sums = [jax.ShapeDtypeStruct((2, tokens, width), f32)] * 2
    dma = pltpu.SemaphoreType.DMA
    return pl.pallas_call(
        functools.partial(feed_forward_kernel, parts),
        grid=(1,),
        in_specs=[any_spec, any_spec, full(bias)] + [any_spec] * len(pieces),
        out_specs=[any_spec] * 2 + [full(column), any_spec, any_spec],
        out_shape=hidden + [column] + sums,
        scratch_shapes=[
            pltpu.VMEM((2 * tokens, width), bf16),
            pltpu.VMEM((2 * tokens, width), bf16),
            pltpu.VMEM((2, 2, 2 * units, width), bf16),
            pltpu.VMEM(hidden[0].shape, bf16),
            pltpu.VMEM(hidden[0].shape, bf16),
            pltpu.VMEM((2, 2, tokens, width), f32),
            dma((4 + 4 * parts,)),
            dma((2 * parts + 2,)),
        ],
        cost_estimate=tiny,
        compiler_params=pltpu.CompilerParams(vmem_limit_bytes=60 * MIB),
        name="feed_forward",
    )(own_in, met_in, bias, *pieces)


def fc_grad_kernel(parts, act_ref, back_ref, own_ref, met_ref, *refs):
    grads, (x, acts, backs, products, ins, outs) = refs[: 2 * parts], refs[2 * parts :]
    half, units = own_ref.shape[1], grads[0].shape[1]
    copy = pltpu.make_async_copy
    inputs = []
    for k, ref in enumerate((own_ref, met_ref)):
        for m in range(2):
            inputs.append(copy(ref.at[m], x.at[m, pl.ds(k * half, half)], ins.at[2 * k + m]))
    loads = [
        [
            copy(act_ref.at[n], acts.at[n], ins.at[4 + 2 * n]),
            copy(back_ref.at[n], backs.at[n], ins.at[5 + 2 * n]),
        ]
        for n in range(parts)
    ]
    for item in inputs + [item for pair in loads for item in pair]:
        item.start()
    stores = []
    for n in range(parts):
        for item in (inputs if n == 0 else []) + loads[n]:
            item.wait()
        if n >= 2:
            for item in stores[n - 2]:
                item.wait()
        stores.append([])
        for kind, left, right in ((0, backs, 0), (1, acts, 1)):
            products[n % 2, kind] = dot(left[n], x[right], 0, 0).astype(bf16)
            for side in range(2):
                stores[n].append(
                    copy(
                        products.at[n % 2, kind, pl.ds(side * units, units)],
                        grads[2 * n + side].at[kind],
                        outs.at[4 * n + 2 * kind + side],
                    )
                )
                stores[n][-1].start()
    for pair in stores[-2:]:
        for item in pair:
            item.wait()


def fc_grads_of(acts, backs, own_in, met_in):
    parts, tokens, columns = acts.shape
    width = own_in.shape[2]
    dma = pltpu.SemaphoreType.DMA
    return pl.pallas_call(
        functools.partial(fc_grad_kernel, parts),
        grid=(1,),
        in_specs=[any_spec] * 4,
        out_specs=[any_spec] * (2 * parts),
        out_shape=[pltpu.HBM((2, columns // 2, width), bf16)] * (2 * parts),
        scratch_shapes=[
            pltpu.VMEM((2, tokens, width), bf16),
            pltpu.VMEM(acts.shape, bf16),
            pltpu.VMEM(acts.shape, bf16),
            pltpu.VMEM((2, 2, columns, width), bf16),
            dma((4 + 2 * parts,)),
            dma((4 * parts,)),
        ],
        cost_estimate=tiny,
        compiler_params=pltpu.CompilerParams(vmem_limit_bytes=60 * MIB),
        name="fc_grads",
    )(acts, backs, own_in, met_in)


def on_device(
    tokens,
    cond,
    segment_ids,
    crop_slot,
    ada_weight,
    ada_bias,
    attn_weight,
    fc_in,
    fc_out,
    biases,
    out_grad,
):
    net = Net()
    tok_len, width = tokens.shape[1:]
    head_dim = width // HEADS
    mod_rank, core, chips = net.mod_rank, net.core, net.chips
    device_count = net.dp * net.mod
    crop_count = crop_slot.shape[1] // net.mod
    shard = attn_weight.shape[0]
    third = shard // 3
    chunks_of = [range(chips // 2), range(chips // 2, chips)]
    halves = [(n, side) for n in range(3) for side in range(2)]
    aligned = shard % (2 * head_dim) == 0 and third % 16 == 0 and width % (2 * net.mod * shard) == 0

    g_attn = Gather(net, attn_weight[None])
    g_fc = Gather(net, jnp.stack([fc_in, fc_out]))
    silu_cond, mod_own = modulate(cond, ada_weight, ada_bias.reshape(1, -1).astype(f32))
    for n in range(g_attn.count):
        g_attn.start()
        g_attn.got = [after(g_attn.got[0], mod_own)]
        g_attn.finish()
    g_attn.start()
    first = g_attn.value
    for n in range(g_fc.count):
        g_fc.start(*first)
        if n < g_fc.count - 1:
            g_fc.finish()
    g_attn.finish().start()
    g_attn.finish().start()
    third_phase = g_attn.value
    g_fc.got = [after(g_fc.got[0], *third_phase)]
    g_fc.finish().start(*g_attn.got)
    attn_pieces = [(g_attn.value, g_attn.got)[side][n] for n, side in halves]

    mod_other = net.swap(after(mod_own, *first), "mod")
    modulation = jnp.concatenate(
        [jnp.where(mod_rank == 0, mod_own, mod_other), jnp.where(mod_rank == 0, mod_other, mod_own)], axis=1
    )
    seg_ids = segment_ids[0]
    slots = lax.dynamic_slice_in_dim(crop_slot[0], mod_rank * crop_count, crop_count)
    crop_onehot = seg_ids[:, None] == jnp.arange(crop_count, dtype=jnp.int32)[None, :]
    token_slot = jnp.sum(jnp.where(crop_onehot, slots[None, :], 0), axis=1)
    slot_pick = token_slot[:, None] == jnp.arange(cond.shape[0], dtype=jnp.int32)[None, :]
    slot_pick = slot_pick.astype(bf16)
    modulation = after(modulation, *third_phase)
    mods = [modulation[:, n * width : (n + 1) * width] for n in range(6)]
    shift_a, scale_a, gate_a, shift_m, scale_m, gate_m = [times(slot_pick, block) for block in mods]

    slot_count, own_cols = cond.shape[0], width // net.dp
    to_dp = jnp.moveaxis(silu_cond.reshape(slot_count, net.dp, own_cols), 1, 0).reshape(net.dp, 1, -1)
    to_all = jnp.broadcast_to(to_dp, (net.dp, net.mod, slot_count * own_cols)).reshape(device_count, -1)
    to_all = after(to_all, *third_phase)
    sent = jnp.concatenate([jnp.broadcast_to(biases[None], (device_count, biases.shape[0])), to_all], axis=1)
    met = lax.all_to_all(sent, ("dp", "mod"), split_axis=0, concat_axis=0, tiled=True)
    ada_order = list(range(net.bits - 1, -1, -1))
    dp_order = net.ranks(ada_order, range(net.dp))[0]
    dp_pick = (dp_order[:, None] == jnp.arange(net.dp)[None, :]).astype(bf16)
    cond_cols = times(dp_pick, met.reshape(net.dp, net.mod, -1)[:, 0, biases.shape[0] :]).astype(bf16)
    cond_cols = cond_cols.reshape(-1, own_cols)
    bias_all = met[:, : biases.shape[0]].reshape(-1, width)
    bias_query, bias_value, bias_proj, bias_out = [bias_all[n].astype(f32) for n in range(4)]
    bias_in = bias_all[4:].reshape(device_count, 3, third)
    picks = []
    for n, side in halves:
        devices = net.devices(net.orders[n], chunks_of[side])
        picks.append((devices[:, None] == jnp.arange(device_count)[None, :]).astype(bf16))
    picks = jnp.stack(picks).reshape(3, 2, chips // 2, device_count)
    bias_pieces = jnp.einsum("nsjd,dnr->nsjr", picks, bias_in, preferred_element_type=f32).reshape(3, -1)

    def join(own, other):
        own, other = [a.reshape(-1, 1, net.mod * shard, a.shape[-1]) for a in (own, other)]
        both = jnp.where(core == 0, jnp.concatenate([own, other], 1), jnp.concatenate([other, own], 1))
        return both.reshape(-1, both.shape[-1])

    def part(whole):
        whole = whole.reshape(-1, 2, net.mod * shard, whole.shape[-1])
        return [
            jnp.where(core == c, whole[:, 0], whole[:, 1]).reshape(-1, whole.shape[-1]) for c in range(2)
        ]

    resid = tokens[0].astype(f32)
    normed_a, _ = layer_norm(resid)
    attn_in = (normed_a * (1.0 + scale_a) + shift_a).astype(bf16)
    if aligned:
        index = jnp.concatenate([net.local(net.orders[n], chunks_of[side]) * 3 + n for n, side in halves])
        own_weight = assemble(attn_pieces, index, third)
        qkv_rows = own_weight.shape[0] * 3 // 4
        qkv_weight = own_weight[:qkv_rows]
        proj_own = own_weight[qkv_rows:]
        proj_weight = join(proj_own, net.swap(proj_own, 0))
        ids = jnp.stack([seg_ids, net.swap(seg_ids, 0)])
        attn_in = after(attn_in, *third_phase)
        attn_both = jnp.concatenate([attn_in, net.swap(attn_in, 0)], axis=0)
        own_query, own_value = part(bias_query[:, None])[0], part(bias_value[:, None])[0]
        qkv_bias = jnp.concatenate([own_query, jnp.zeros_like(own_query), own_value], axis=0)
        attn_both = after(attn_both, *g_fc.got)
        g_fc.finish().start()
        qkv = (times_rows(qkv_weight, attn_both) + qkv_bias).astype(bf16)
        qkv = qkv.reshape(3, -1, 2 * head_dim, 2 * tok_len)
        context_both = attention(qkv, ids, head_dim).reshape(-1, 2 * tok_len)
        context = join(context_both[:, :tok_len], net.swap(context_both[:, tok_len:], 0))
        attn_out = dot(context, proj_weight, 0, 1) + bias_proj
    else:
        arrays = attn_pieces + [net.swap(piece, 0) for piece in attn_pieces]
        places = jnp.concatenate(
            [net.devices(net.orders[n], chunks_of[side], c) * 3 + n for c in range(2) for n, side in halves]
        )
        spread = jnp.concatenate(arrays, axis=1)[0]

        def place(n, whole):
            block = lax.dynamic_slice_in_dim(spread, n * third, third)
            return lax.dynamic_update_slice_in_dim(whole, block, places[n] * third, 0)

        attn_w = lax.fori_loop(0, places.shape[0], place, jnp.zeros_like(spread))
        g_fc.finish().start()
        g_fc.finish().start()
        qkv_weight, proj_weight = attn_w[: 3 * width], attn_w[3 * width :]
        qkv_bias = jnp.concatenate([bias_query, jnp.zeros_like(bias_query), bias_value])
        qkv = (times_rows(qkv_weight, attn_in) + qkv_bias[:, None]).astype(bf16)
        qkv = qkv.reshape(3, -1, 2 * head_dim, tok_len)
        context = attention(qkv, seg_ids[None], head_dim).reshape(-1, tok_len)
        attn_out = dot(context, proj_weight, 0, 1) + bias_proj
    mid = resid + gate_a * attn_out
    normed_m, _ = layer_norm(mid)
    mlp_in = (normed_m * (1.0 + scale_m) + shift_m).astype(bf16)
    if aligned:
        mlp_in = after(mlp_in, *g_fc.got)
        g_fc.finish().start()
    grad_mlp = (gate_m * out_grad[0].astype(f32)).astype(bf16)

    mlp_own = jnp.stack([mlp_in, grad_mlp])
    mlp_met = after(net.swap(mlp_own, 0), cond_cols, bias_pieces)
    grad_bias_out = jnp.sum(grad_mlp.astype(f32), axis=0, keepdims=True)
    fc_pieces = [(g_fc.value, g_fc.got)[side][n] for n, side in halves]
    acts, backs, columns, own_sums, other_sums = feed_forward(mlp_own, mlp_met, bias_pieces, fc_pieces)
    sums_met = net.swap(other_sums, 0)
    fc_grads = fc_grads_of(acts, backs, mlp_own, mlp_met)
    sums_met = after(sums_met, *fc_grads)
    back_way = Scatter(net, fc_grads[0::2], fc_grads[1::2])

    result, pair_m, grad_mid, grad_attn, grad_bias_proj, *parts = middle(
        core,
        net.mod * shard if aligned else None,
        own_sums,
        sums_met,
        mid,
        out_grad[0],
        slot_pick,
        modulation,
        bias_out[None],
        proj_weight,
        context,
    )
    if aligned:
        mine, other, proj_mine, proj_other = parts
        context_grads = [a.reshape(-1, 2 * head_dim, tok_len) for a in (mine, net.swap(other, 0))]
        proj_met = net.swap(after(proj_other, *context_grads), 0)
        grad_qkv = attention(qkv, ids, head_dim, context_grads)
        grad_qkv = grad_qkv.reshape(-1, 2 * tok_len)
        back_own, back_other = attn_in_grads(grad_qkv, own_weight)
        back_met = net.swap(back_other, 0)
        grad_qkv = after(grad_qkv, back_own)
        places = jnp.sum(
            jnp.where(
                index[None, :] == jnp.arange(index.shape[0], dtype=index.dtype)[:, None],
                jnp.arange(index.shape[0], dtype=index.dtype)[None, :],
                0,
            ),
            axis=1,
        )
        pieces = weight_grad(grad_qkv, attn_both, proj_mine, proj_met, places, third)
        back_met = after(back_met, pieces)
    else:
        grad_context, grad_proj = parts
        grad_qkv = attention(
            qkv, seg_ids[None], head_dim, [grad_context.reshape(-1, 2 * head_dim, tok_len)]
        ).reshape(-1, tok_len)
        attn_grad = jnp.concatenate([times(grad_qkv, attn_in).astype(bf16), grad_proj], axis=0)

        def take(n, whole):
            block = lax.dynamic_slice_in_dim(attn_grad, places[n] * third, third)
            return lax.dynamic_update_slice_in_dim(whole, block, n * third, 0)

        grads = lax.fori_loop(0, places.shape[0], take, jnp.zeros_like(attn_grad))
        grads = jnp.split(grads[None], 12, axis=1)
        pieces = jnp.concatenate([summed(a, net.swap(b, 0)) for a, b in zip(grads[:6], grads[6:])], axis=1)
        back_own = contract_rows(grad_qkv, qkv_weight)
        back_met = jnp.zeros_like(back_own)
    grad_tokens, pair_a = end_call(
        attn_end_kernel, f32, slot_count, back_own, back_met, tokens[0], grad_mid, attn_out, slot_pick, modulation
    )
    pair_a, *back_way.got = lax.optimization_barrier((pair_a, *back_way.got))
    pair_own = jnp.where(mod_rank == 0, pair_a, pair_m)
    pair_send = jnp.where(mod_rank == 0, pair_m, pair_a)
    grad_mod = summed(pair_own, net.swap(pair_send, "mod"))
    for n in range(3):
        back_way.hold(n, grad_mod)
    mod_rows = jnp.concatenate([grad_mod, net.swap(grad_mod, ada_order[0])], axis=0)
    sends = [back_way.join(0, pieces), back_way.join(1, pieces)]
    back_way.hold(2, mod_rows)
    sends.append(back_way.join(2, pieces))
    grad_qkv, columns = lax.optimization_barrier((grad_qkv, columns, *sends))[:2]

    grad_silu = times_rows(grad_mod, ada_weight)
    silu_own = jnp.where(mod_rank == 0, grad_silu[:crop_count], grad_silu[crop_count:])
    silu_send = jnp.where(mod_rank == 0, grad_silu[crop_count:], grad_silu[:crop_count]).astype(bf16)

    column = jnp.sum(grad_qkv.astype(f32), axis=1, keepdims=True).reshape(3, -1, 1)
    if aligned:
        none = jnp.zeros_like(column[0])
        column = [join(column[0], none), None, join(column[2], none)]
    columns = columns.reshape(3, 2, chips // 2, third)
    grad_bias_in = jnp.einsum("nsjd,nsjr->dnr", picks.astype(f32), columns, precision=lax.Precision.HIGHEST)
    grad_bias = stack_rows(
        column[0].reshape(1, -1),
        column[2].reshape(1, -1),
        grad_bias_proj,
        grad_bias_out,
        grad_bias_in.reshape(-1, width),
    )
    bias_rows = lax.all_to_all(
        grad_bias.reshape(device_count, -1), ("dp", "mod"), split_axis=0, concat_axis=0, tiled=True
    )
    bias_sum = jnp.sum(bias_rows, axis=0)
    mod_rows = after(mod_rows, *back_way.got)
    mod_rows = jnp.concatenate([mod_rows, net.swap(mod_rows, ada_order[1])], axis=0)
    for n in range(3):
        back_way.hold(n, silu_send, bias_sum)
    sends = [back_way.second(0), back_way.second(1)]
    back_way.hold(2, mod_rows)
    sends.append(back_way.second(2))
    back_way.second_attn(sends)
    back_way.third()
    back_way.third_attn()
    silu_send = after(silu_send, *back_way.also_got)
    grad_silu = silu_own + net.swap(silu_send, "mod").astype(f32)
    own_cond = lax.dynamic_slice_in_dim(cond, mod_rank * crop_count, crop_count, 0).astype(f32)
    silu_back = jax.vjp(jax.nn.silu, own_cond)[1]
    grad_cond = silu_back(grad_silu)[0]

    mod_rows = after(mod_rows, *back_way.also_got)
    fc_sum, attn_sum = back_way.last()
    for dim in ada_order[2:]:
        mod_rows = jnp.concatenate([mod_rows, net.swap(mod_rows, dim)], axis=0)
    ada_w_sum = contract_rows(cond_cols, mod_rows)
    ada_b_sum = jnp.sum(mod_rows.astype(f32), axis=0).reshape(ada_bias.shape[0], width)
    ada_b_sum = lax.dynamic_slice_in_dim(ada_b_sum, net.dp_rank * own_cols, own_cols, 1)

    return (
        result[None],
        grad_tokens[None],
        grad_cond,
        ada_w_sum,
        ada_b_sum,
        attn_sum[0],
        fc_sum[0],
        fc_sum[1],
        bias_sum,
    )


def solution(mesh):
    placed = (
        P(("dp", "mod"), None, None),
        P("dp", None),
        P(("dp", "mod"), None),
        P("dp", None),
        P(None, "mod"),
        P("mod", None),
        P(("dp", "mod"), None),
        P(("dp", "mod"), None),
        P(("dp", "mod"), None),
        P(("dp", "mod")),
        P(("dp", "mod"), None, None),
    )
    return jax.shard_map(
        on_device,
        mesh=mesh,
        in_specs=placed,
        out_specs=(
            P(("dp", "mod"), None, None),
            P(("dp", "mod"), None, None),
            P(("dp", "mod"), None),
            P("dp", "mod"),
            P("mod", "dp"),
            P(("dp", "mod"), None),
            P(("dp", "mod"), None),
            P(("dp", "mod"), None),
            P(("dp", "mod")),
        ),
        check_vma=False,
    )
```

```python
import functools

import jax
import jax.numpy as jnp
import numpy as np
from jax import lax
from jax.experimental import pallas as pl
from jax.experimental.pallas import tpu as pltpu
from jax.sharding import PartitionSpec as P

HEADS = 16
norm_eps = 1e-06
bf16 = jnp.bfloat16
f32 = jnp.float32
MIB = 1024 * 1024


def layer_norm(values):
    center = values - jnp.mean(values, axis=-1, keepdims=True)
    inverse = lax.rsqrt(jnp.mean(center * center, axis=-1, keepdims=True) + norm_eps)
    return (center * inverse, inverse)


def norm_back(grad_in, normed, inverse):
    centered = grad_in - jnp.mean(grad_in, axis=-1, keepdims=True)
    return (centered - normed * jnp.mean(grad_in * normed, axis=-1, keepdims=True)) * inverse


def dot(left, right, left_dim, right_dim):
    return lax.dot_general(left, right, (((left_dim,), (right_dim,)), ((), ())), preferred_element_type=f32)


def times(left, right):
    return dot(left, right, 1, 0)


def times_rows(left, right):
    return dot(left, right, 1, 1)


def contract_rows(left, right):
    return dot(left, right, 0, 0)


def after(value, *others):
    return lax.optimization_barrier((value, *others))[0]


def summed(left, right):
    return (left.astype(f32) + right.astype(f32)).astype(bf16)


class Net:
    def __init__(self):
        self.dp = lax.axis_size("dp")
        self.mod = lax.axis_size("mod")
        self.bits = self.dp.bit_length() - 1
        self.dp_rank = lax.axis_index("dp")
        self.mod_rank = lax.axis_index("mod")
        self.core = self.dp_rank & 1
        self.chips = self.dp // 2 * self.mod
        self.lead = list(range(self.bits - 1, 2, -1))
        last = ["mod", 1, 2]
        self.turns = [last[n:] + last[:n] for n in range(3)]
        self.orders = [self.lead + turn for turn in self.turns]

    def swap(self, value, dim):
        if dim == "mod":
            return lax.ppermute(value, "mod", [(i, i ^ 1) for i in range(self.mod)])
        return lax.ppermute(value, "dp", [(i, i ^ (1 << dim)) for i in range(self.dp)])

    def ranks(self, order, chunks, core=0):
        masks = []
        for j in chunks:
            dp_mask, mod_mask = core, 0
            for step, dim in enumerate(order):
                if j >> step & 1:
                    if dim == "mod":
                        mod_mask ^= 1
                    else:
                        dp_mask ^= 1 << dim
            masks.append((dp_mask, mod_mask))
        masks = np.array(masks, np.int32)
        return self.dp_rank ^ masks[:, 0], self.mod_rank ^ masks[:, 1]

    def devices(self, order, chunks, core=0):
        dp, mod = self.ranks(order, chunks, core)
        return dp * self.mod + mod

    def local(self, order, chunks):
        dp, mod = self.ranks(order, chunks)
        return (dp >> 1) * self.mod + mod


class Gather:
    def __init__(self, net, shard):
        self.net, self.count = net, len(net.lead)
        self.third = shard.shape[1] // 3
        self.value, self.got, self.phase = shard, None, 0

    def start(self, *others):
        net, phase = self.net, self.phase
        if phase < self.count:
            self.value = after(self.value, *others) if others else self.value
            self.got = [net.swap(self.value, net.lead[phase])]
        else:
            if phase == self.count:
                kinds, _, width = self.value.shape
                whole = self.value.reshape(kinds, -1, 3, self.third, width)
                self.value = [whole[:, :, n].reshape(kinds, -1, width) for n in range(3)]
            if others:
                self.value = list(lax.optimization_barrier((*self.value, *others))[:3])
            step = phase - self.count
            self.got = [net.swap(self.value[n], net.turns[n][step]) for n in range(3)]
        self.phase += 1
        return self

    def finish(self):
        if self.phase <= self.count:
            self.value = jnp.concatenate([self.value, self.got[0]], axis=1)
        elif self.phase < self.count + 3:
            self.value = [jnp.concatenate(pair, axis=1) for pair in zip(self.value, self.got)]
        return self


any_spec = pl.BlockSpec(memory_space=pl.ANY)


def full(value):
    return pl.BlockSpec(value.shape, lambda *_: (0,) * len(value.shape))

tiny = pl.CostEstimate(flops=1024, bytes_accessed=1024, transcendentals=0)


def run_copies(copies):
    for copy in copies:
        copy.start()
    for copy in copies:
        copy.wait()


def assemble_kernel(rows, each, index_ref, *refs):
    pieces, out_ref, hold, sems, last = refs[:-4], *refs[-4:]
    copies = []
    for n, piece in enumerate(pieces):
        for j in range(each):
            at = pl.multiple_of(index_ref[n * each + j] * rows, rows)
            copies.append(
                pltpu.make_async_copy(
                    piece.at[0, pl.ds(j * rows, rows)], hold.at[pl.ds(at, rows)], sems.at[n * each + j]
                )
            )
    run_copies(copies)
    run_copies([pltpu.make_async_copy(hold, out_ref, last)])


def assemble(pieces, index, rows):
    each, width = pieces[0].shape[1] // rows, pieces[0].shape[2]
    total = len(pieces) * each
    return pl.pallas_call(
        functools.partial(assemble_kernel, rows, each),
        grid_spec=pltpu.PrefetchScalarGridSpec(
            num_scalar_prefetch=1,
            grid=(1,),
            in_specs=[any_spec] * len(pieces),
            out_specs=any_spec,
            scratch_shapes=[
                pltpu.VMEM((total * rows, width), bf16),
                pltpu.SemaphoreType.DMA((total,)),
                pltpu.SemaphoreType.DMA,
            ],
        ),
        out_shape=jax.ShapeDtypeStruct((total * rows, width), bf16),
        compiler_params=pltpu.CompilerParams(vmem_limit_bytes=10 * MIB),
        name="assemble",
    )(index, *pieces)


def added(left, right):
    return (left.astype(f32) + right.astype(f32)).astype(bf16)


def sums_call(kernel, grid, in_specs, out_specs, outs, *args, limit=24):
    return pl.pallas_call(
        kernel,
        grid=grid,
        in_specs=in_specs,
        out_specs=out_specs,
        out_shape=[pltpu.HBM(out, bf16) for out in outs],
        cost_estimate=tiny,
        compiler_params=pltpu.CompilerParams(vmem_limit_bytes=limit * MIB),
        name=kernel.__name__,
    )(*args)


def first_sums(own_low, own_high, got_low, got_high, also, keep, send):
    keep[...] = added(own_low[...], got_low[...])
    send[:2] = added(own_high[...], got_high[...])
    send[2:] = also[...]


def half_sums(own, got, keep, send):
    half = keep.shape[1]
    keep[...] = added(own[:, :half], got[:, :half])
    send[...] = added(own[:, half:], got[:, half:])


def block_sums(own, got, keep, send):
    keep[0] = added(own[0], got[0])
    send[0] = added(own[1], got[1])


def third_sums(*refs):
    outs = refs[6:]
    for n in range(3):
        total = added(refs[n][...], refs[3 + n][...])
        if len(outs) == 2:
            rows = total.shape[1] // 2
            outs[0][:, n * rows : (n + 1) * rows] = total[:, :rows]
            outs[1][:, n * rows : (n + 1) * rows] = total[:, rows:]
        else:
            outs[n][...] = total


def third_attn_sums(*refs):
    for n in range(3):
        half_sums(refs[n], refs[3 + n], refs[6 + 2 * n], refs[7 + 2 * n])


def fourth_sums(*refs):
    keep, send = refs[6:]
    rows = keep.shape[1] // 3
    for n in range(3):
        total = added(refs[n][0], refs[3 + n][0])
        keep[0, n * rows : (n + 1) * rows] = total[:rows]
        send[0, n * rows : (n + 1) * rows] = total[rows:]


class Scatter:
    def __init__(self, net, own, other):
        self.net = net
        self.own = list(own)
        self.got = [net.swap(other[n], net.turns[n][2]) for n in range(3)]
        self.aligned = len(net.lead) == 1 and own[0].shape[1] // 8 % 16 == 0

    def hold(self, n, *others):
        self.got[n] = after(self.got[n], *others)

    def join(self, n, pieces):
        _, rows, width = self.own[n].shape
        half = rows // 2
        step = half // 2
        also = 2 * ((n + 2) % 3)
        self.pieces = pieces.reshape(12, half, width)
        block = (2, step, width)
        low, high = pl.BlockSpec(block, lambda i: (0, i, 0)), pl.BlockSpec(block, lambda i: (0, i + 2, 0))
        self.own[n], send = sums_call(
            first_sums,
            (2,),
            [low, high, low, high, pl.BlockSpec(block, lambda i: (also + 1, i, 0))],
            [low, pl.BlockSpec((4, step, width), lambda i: (0, i, 0))],
            [(2, half, width), (4, half, width)],
            self.own[n],
            self.own[n],
            self.got[n],
            self.got[n],
            self.pieces,
            limit=60,
        )
        self.got[n] = self.net.swap(send, self.net.turns[n][1])
        return send

    def second(self, n):
        _, rows, width = self.own[n].shape
        outs = [(2, rows // 2, width)] * 2
        self.both = getattr(self, "both", [None] * 3)
        self.both[n] = self.got[n]
        self.own[n], send = sums_call(
            half_sums,
            (1,),
            [full(self.own[n]), pl.BlockSpec((2, rows, width), lambda i: (0, 0, 0))],
            [full(jax.ShapeDtypeStruct(out, bf16)) for out in outs],
            outs,
            self.own[n],
            self.got[n],
        )
        self.got[n] = self.net.swap(send, self.net.turns[n][0])
        return send

    def second_attn(self, others):
        self.also, self.also_got = [None] * 3, [None] * 3
        both = list(lax.optimization_barrier((*self.both, *others))[:3])
        for n in range(3):
            _, rows, width = both[n].shape
            piece = 2 * ((n + 2) % 3)
            outs = [(1, rows, width)] * 2
            self.also[n], send = sums_call(
                block_sums,
                (1,),
                [
                    pl.BlockSpec((2, rows, width), lambda i: (piece, 0, 0)),
                    pl.BlockSpec((2, rows, width), lambda i: (1, 0, 0)),
                ],
                [full(jax.ShapeDtypeStruct(out, bf16)) for out in outs],
                outs,
                self.pieces,
                both[n],
            )
            self.also_got[n] = self.net.swap(send, self.net.turns[n][0])

    def third(self):
        net = self.net
        _, rows, width = self.own[0].shape
        outs = [(2, rows // 2 * 3, width)] * 2 if self.aligned else [(2, rows, width)] * 3
        args = self.own + self.got
        results = sums_call(
            third_sums,
            (1,),
            [full(a) for a in args],
            [full(jax.ShapeDtypeStruct(out, bf16)) for out in outs],
            outs,
            *args,
        )
        if self.aligned:
            self.fc = results[0], net.swap(results[1], net.lead[0])
        else:
            self.fc = self.lead(self.together(results), len(net.lead) - 1)
        self.also_got = list(lax.optimization_barrier((*self.also_got, results[1]))[:3])

    def third_attn(self):
        net = self.net
        _, rows, width = self.also[0].shape
        args, outs = self.also + self.also_got, [(1, rows // 2, width)] * 6
        results = sums_call(
            third_attn_sums,
            (1,),
            [full(a) for a in args],
            [full(jax.ShapeDtypeStruct(out, bf16)) for out in outs],
            outs,
            *args,
        )
        self.also = results[0::2]
        self.also_got = [net.swap(results[2 * n + 1], net.turns[(n + 2) % 3][0]) for n in range(3)]

    def last(self):
        net = self.net
        order = (1, 2, 0)
        keep, got = [self.also[n] for n in order], [self.also_got[n] for n in order]
        *got, fc_got = lax.optimization_barrier((*got, self.fc[1]))
        self.fc = self.fc[0], fc_got
        if self.aligned:
            _, rows, width = keep[0].shape
            outs = [(1, rows // 2 * 3, width)] * 2
            own, send = sums_call(
                fourth_sums,
                (1,),
                [full(a) for a in keep + got],
                [full(jax.ShapeDtypeStruct(out, bf16)) for out in outs],
                outs,
                *keep,
                *got,
            )
            attn = own, net.swap(send, net.lead[0])
        else:
            attn = self.lead(self.together([summed(a, b) for a, b in zip(keep, got)]), len(net.lead) - 1)
        sums = []
        for own, got in (self.fc, attn):
            for step in range(len(net.lead) - 1, -1, -1):
                total = own.astype(f32) + got.astype(f32)
                if step:
                    own, got = self.lead(total.astype(bf16), step - 1)
            sums.append(total)
        return sums

    def together(self, parts):
        kinds, _, width = parts[0].shape
        count = 1 << len(self.net.lead)
        return jnp.concatenate([p.reshape(kinds, count, -1, width) for p in parts], axis=2).reshape(kinds, -1, width)

    def lead(self, whole, step):
        half = whole.shape[1] // 2
        return whole[:, :half], self.net.swap(whole[:, half:], self.net.lead[step])


def attn_in_kernel(grad_ref, weight_ref, own_ref, other_ref):
    total = dot(grad_ref[...], weight_ref[...], 0, 0)
    half = own_ref.shape[0]
    own_ref[...] = total[:half]
    other_ref[...] = total[half:]


def attn_in_grads(grad, weight):
    rows, tokens = grad.shape
    width = weight.shape[1]
    out = jax.ShapeDtypeStruct((tokens // 2, width), f32)
    return pl.pallas_call(
        attn_in_kernel,
        grid=(1,),
        in_specs=[full(grad), pl.BlockSpec((rows, width), lambda i: (0, 0))],
        out_specs=[full(out)] * 2,
        out_shape=[out, pltpu.HBM(out.shape, f32)],
        cost_estimate=tiny,
        compiler_params=pltpu.CompilerParams(vmem_limit_bytes=40 * MIB),
        name="attn_in_grads",
    )(grad, weight)


def weight_grad_kernel(rows, place_ref, grad_ref, x_ref, mine_ref, other_ref, out_ref, hold, sems):
    top, copies = grad_ref.shape[0], []
    step = top // 3
    for n in (3, 0, 1, 2):
        start = n * step
        stop = min(start + step, hold.shape[0])
        if n == 3:
            hold[start:] = summed(mine_ref[...], other_ref[...])
        else:
            hold[start:stop] = dot(grad_ref[start:stop], x_ref[...], 1, 0).astype(bf16)
        for unit in range(start // rows, stop // rows):
            at = pl.multiple_of(place_ref[unit] * rows, rows)
            copies.append(
                pltpu.make_async_copy(
                    hold.at[pl.ds(unit * rows, rows)], out_ref.at[pl.ds(at, rows)], sems.at[unit]
                )
            )
            copies[-1].start()
    for copy in copies:
        copy.wait()


def weight_grad(grad, x, mine, other, places, rows):
    total, width = grad.shape[0] + mine.shape[0], x.shape[1]
    return pl.pallas_call(
        functools.partial(weight_grad_kernel, rows),
        grid_spec=pltpu.PrefetchScalarGridSpec(
            num_scalar_prefetch=1,
            grid=(1,),
            in_specs=[full(a) for a in (grad, x, mine, other)],
            out_specs=any_spec,
            scratch_shapes=[pltpu.VMEM((total, width), bf16), pltpu.SemaphoreType.DMA((total // rows,))],
        ),
        out_shape=jax.ShapeDtypeStruct((total, width), bf16),
        cost_estimate=tiny,
        compiler_params=pltpu.CompilerParams(vmem_limit_bytes=60 * MIB),
        name="weight_grad",
    )(places, grad, x, mine, other)


def by_core(core_ref, group, whole):
    if group is None:
        return [whole]
    picked = []
    for c in range(2):
        rows = []
        for at in range(0, whole.shape[0], 2 * group):
            first, second = whole[at : at + group], whole[at + group : at + 2 * group]
            rows.append(jnp.where(core_ref[0] == c, first, second))
        picked.append(jnp.concatenate(rows, axis=0))
    return picked


def token_block(pick, mods, n):
    width = mods.shape[1] // 6
    return dot(pick[...], mods[:, n * width : (n + 1) * width], 1, 0)


def middle_kernel(group, core_ref, *refs):
    sums, met, mid, grad_out, pick, mods, bias, weight, context = refs[:9]
    result_ref, pair_ref, mid_ref, attn_ref, column_ref = refs[9:14]
    normed, inverse = layer_norm(mid[...])
    back, outer = sums[1] + met[1], grad_out[...].astype(f32)
    mlp_out = sums[0] + met[0] + bias[...]
    result_ref[...] = (mid[...] + token_block(pick, mods, 5) * mlp_out).astype(bf16)
    slot_sums(pick[...], (back, back * normed, outer * mlp_out), pair_ref)
    grad_mid = outer + norm_back(back * (1.0 + token_block(pick, mods, 4)), normed, inverse)
    mid_ref[...] = grad_mid
    grad_attn = (token_block(pick, mods, 2) * grad_mid).astype(bf16)
    attn_ref[...] = grad_attn
    column_ref[...] = jnp.sum(grad_attn.astype(f32), axis=0, keepdims=True)
    parts = by_core(core_ref, group, dot(weight[...], grad_attn, 0, 1))
    parts += by_core(core_ref, group, dot(grad_attn, context[...], 0, 1))
    for ref, value in zip(refs[14:], parts):
        ref[...] = value.astype(bf16)


def middle(core, group, *args):
    _, tokens, width = args[0].shape
    if group is None:
        sizes = [(width, tokens), (width, width)]
    else:
        sizes = [(width // 2, tokens)] * 2 + [(width // 2, width)] * 2
    slots = args[4].shape[1]
    outs = [((tokens, width), bf16), ((slots, 3 * width), bf16)]
    outs += [((tokens, width), f32), ((tokens, width), bf16), ((1, width), f32)]
    outs = [jax.ShapeDtypeStruct(*out) for out in outs + [(s, bf16) for s in sizes]]
    return pl.pallas_call(
        functools.partial(middle_kernel, group),
        grid=(1,),
        in_specs=[pl.BlockSpec(memory_space=pltpu.SMEM)] + [full(a) for a in args],
        out_specs=[full(a) for a in outs],
        out_shape=outs[:5] + [pltpu.HBM(a.shape, bf16) for a in outs[5:]],
        cost_estimate=tiny,
        compiler_params=pltpu.CompilerParams(vmem_limit_bytes=48 * MIB),
        name="middle",
    )(core.reshape(1), *args)


def slot_sums(pick, blocks, out_ref):
    for n, block in enumerate(blocks):
        high = block.astype(bf16)
        low = (block - high.astype(f32)).astype(bf16)
        total = dot(pick, high, 0, 0) + dot(pick, low, 0, 0)
        out_ref[:, n * block.shape[1] : (n + 1) * block.shape[1]] = total.astype(bf16)


def attn_end_kernel(*refs):
    back_a, back_b, resid, grad_mid, attn_out, pick, mods = refs[:7]
    tokens_ref, pair_ref = refs[7:]
    back = back_a[...] + back_b[...]
    normed, inverse = layer_norm(resid[...].astype(f32))
    slope = back * (1.0 + token_block(pick, mods, 1))
    tokens_ref[...] = grad_mid[...] + norm_back(slope, normed, inverse)
    slot_sums(pick[...], (back, back * normed, grad_mid[...] * attn_out[...]), pair_ref)


def end_call(kernel, dtype, slots, *args):
    tokens, width = args[0].shape
    outs = [jax.ShapeDtypeStruct((tokens, width), dtype), jax.ShapeDtypeStruct((slots, 3 * width), bf16)]
    return pl.pallas_call(
        kernel,
        grid=(1,),
        in_specs=[full(a) for a in args],
        out_specs=[full(a) for a in outs],
        out_shape=outs,
        cost_estimate=tiny,
        compiler_params=pltpu.CompilerParams(vmem_limit_bytes=32 * MIB),
        name=kernel.__name__,
    )(*args)


def rows_kernel(*refs):
    at = 0
    for ref in refs[:-1]:
        refs[-1][at : at + ref.shape[0]] = ref[...]
        at += ref.shape[0]


def stack_rows(*args):
    out = jax.ShapeDtypeStruct((sum(a.shape[0] for a in args), args[0].shape[1]), f32)
    return pl.pallas_call(
        rows_kernel,
        grid=(1,),
        in_specs=[full(a) for a in args],
        out_specs=full(out),
        out_shape=out,
        cost_estimate=tiny,
        compiler_params=pltpu.CompilerParams(vmem_limit_bytes=24 * MIB),
        name="stack_rows",
    )(*args)


def softmax_t(key, query, same, scale):
    scores = jnp.where(same, dot(key, query, 0, 0) * scale, -1e30)
    weights = jnp.exp(scores - jnp.max(scores, axis=0, keepdims=True))
    return weights * (1.0 / jnp.sum(weights, axis=0, keepdims=True))


def heads_of(block, dim, cols):
    wide = block[:, cols].astype(f32)
    return [wide[n * dim : (n + 1) * dim].astype(bf16) for n in range(wide.shape[0] // dim)]


def attn_forward(dim, scale, row_ref, col_ref, q_ref, k_ref, v_ref, out_ref):
    length = col_ref.shape[0]
    for s in range(row_ref.shape[0]):
        cols = slice(s * length, (s + 1) * length)
        same = row_ref[s : s + 1] == col_ref[:, s : s + 1]
        outs = []
        for q, k, v in zip(*[heads_of(r[0, 0], dim, cols) for r in (q_ref, k_ref, v_ref)]):
            probs = softmax_t(k, q, same, scale).astype(bf16)
            outs.append(dot(v, probs, 1, 0))
        out_ref[0, :, cols] = jnp.concatenate(outs, axis=0).astype(bf16)


def attn_backward(dim, scale, row_ref, col_ref, q_ref, k_ref, v_ref, *refs):
    length, out_ref = col_ref.shape[0], refs[-1]
    for s in range(row_ref.shape[0]):
        cols = slice(s * length, (s + 1) * length)
        same = row_ref[s : s + 1] == col_ref[:, s : s + 1]
        gq, gk, gv = [], [], []
        qs, ks, vs = [heads_of(r[0, 0], dim, cols) for r in (q_ref, k_ref, v_ref)]
        for q, k, v, g in zip(qs, ks, vs, heads_of(refs[s][0], dim, slice(0, length))):
            probs = softmax_t(k, q, same, scale)
            back = dot(v, g, 0, 0)
            back = probs * (back - jnp.sum(back * probs, axis=0, keepdims=True))
            back = back.astype(bf16)
            gq.append(dot(k, back, 1, 0) * scale)
            gk.append(dot(q, back, 1, 1) * scale)
            gv.append(dot(g, probs.astype(bf16), 1, 1))
        for n, parts in enumerate((gq, gk, gv)):
            out_ref[n, 0, :, cols] = jnp.concatenate(parts, axis=0).astype(bf16)


def attention(qkv, ids, dim, grad=None):
    _, groups, rows, tokens = qkv.shape
    scale = dim**-0.5
    ids_t = ids.T

    def one(n):
        return pl.BlockSpec((1, 1, rows, tokens), lambda i: (n, i, 0, 0))

    flat = pl.BlockSpec((1, rows, tokens), lambda i: (i, 0, 0))
    short = pl.BlockSpec((1, rows, ids.shape[1]), lambda i: (i, 0, 0))
    args = [ids, ids_t, qkv, qkv, qkv]
    specs = [pl.BlockSpec(a.shape, lambda i: (0, 0)) for a in (ids, ids_t)] + [one(0), one(1), one(2)]
    if grad is None:
        return pl.pallas_call(
            functools.partial(attn_forward, dim, scale),
            grid=(groups,),
            in_specs=specs,
            out_specs=flat,
            out_shape=jax.ShapeDtypeStruct((groups, rows, tokens), bf16),
            cost_estimate=tiny,
            compiler_params=pltpu.CompilerParams(vmem_limit_bytes=24 * MIB),
            name="attention",
        )(*args)
    return pl.pallas_call(
        functools.partial(attn_backward, dim, scale),
        grid=(groups,),
        in_specs=specs + [short] * len(grad),
        out_specs=pl.BlockSpec((3, 1, rows, tokens), lambda i: (0, i, 0, 0)),
        out_shape=jax.ShapeDtypeStruct(qkv.shape, bf16),
        cost_estimate=tiny,
        compiler_params=pltpu.CompilerParams(vmem_limit_bytes=24 * MIB),
        name="attention_back",
    )(*args, *grad)


def modulation_kernel(cond_ref, weight_ref, bias_ref, silu_ref, out_ref):
    cond = cond_ref[...].astype(f32)
    silu = (cond / (1.0 + jnp.exp(-cond))).astype(bf16)
    silu_ref[...] = silu
    out_ref[...] = (dot(silu, weight_ref[...], 1, 0) + bias_ref[...]).astype(bf16)


def modulate(cond, weight, bias):
    slots, width = cond.shape
    columns = weight.shape[1]
    tile = 384 if columns % 384 == 0 else columns
    return pl.pallas_call(
        modulation_kernel,
        grid=(columns // tile,),
        in_specs=[
            full(cond),
            pl.BlockSpec((width, tile), lambda i: (0, i)),
            pl.BlockSpec((1, tile), lambda i: (0, i)),
        ],
        out_specs=[full(cond), pl.BlockSpec((slots, tile), lambda i: (0, i))],
        out_shape=[
            jax.ShapeDtypeStruct((slots, width), bf16),
            jax.ShapeDtypeStruct((slots, columns), bf16),
        ],
        cost_estimate=tiny,
        compiler_params=pltpu.CompilerParams(vmem_limit_bytes=16 * MIB),
        name="modulate",
    )(cond, weight, bias)


def feed_forward_kernel(parts, *refs):
    own_ref, met_ref, b_ref = refs[:3]
    pieces = refs[3 : 3 + 2 * parts]
    act_ref, back_ref, column_ref, own_sums, other_sums = refs[3 + 2 * parts : 8 + 2 * parts]
    x, g, weights, acts, backs, total, ins, outs = refs[8 + 2 * parts :]
    half, units = own_ref.shape[1], pieces[0].shape[1]
    copy = pltpu.make_async_copy

    def load(n):
        slot, copies = n % 2, []
        for kind in range(2):
            for side in range(2):
                copies.append(
                    copy(
                        pieces[2 * n + side].at[kind],
                        weights.at[slot, kind, pl.ds(side * units, units)],
                        ins.at[4 + 4 * n + 2 * kind + side],
                    )
                )
        return copies

    low, high = pl.ds(0, half), pl.ds(half, half)
    inputs = [
        copy(own_ref.at[0], x.at[low], ins.at[0]),
        copy(met_ref.at[0], x.at[high], ins.at[1]),
        copy(own_ref.at[1], g.at[low], ins.at[2]),
        copy(met_ref.at[1], g.at[high], ins.at[3]),
    ]
    loads = [load(n) for n in range(parts)]
    for item in inputs[:2] + loads[0][:2] + inputs[2:] + loads[0][2:] + loads[1]:
        item.start()
    stores = []
    root = 0.7978845608028654
    for n in range(parts):
        slot = n % 2
        for item in (inputs[:2] if n == 0 else []) + loads[n][:2]:
            item.wait()
        for item in (inputs[2:] if n == 0 else []) + loads[n][2:]:
            item.wait()
        col = 0.0
        for k in range(2):
            tok = slice(k * half, (k + 1) * half)
            hidden = dot(x[tok], weights[slot, 0], 1, 1) + b_ref[n : n + 1]
            square = hidden * hidden
            tanh = jnp.tanh(root * hidden * (1.0 + 0.044715 * square))
            act = (0.5 * hidden * (1.0 + tanh)).astype(bf16)
            acts[n, tok] = act
            slope = 0.5 * (1.0 + tanh) + 0.5 * hidden * (1.0 - tanh * tanh) * (root * (1.0 + 0.134145 * square))
            back = (dot(g[tok], weights[slot, 1], 1, 1) * slope).astype(bf16)
            backs[n, tok] = back
            col = col + jnp.sum(back.astype(f32), axis=0, keepdims=True)
            for m, value in enumerate((dot(act, weights[slot, 1], 1, 0), dot(back, weights[slot, 0], 1, 0))):
                total[k, m] = value if n == 0 else total[k, m] + value
        column_ref[n : n + 1] = col
        stores.append(copy(acts.at[n], act_ref.at[n], outs.at[2 * n]))
        stores[-1].start()
        stores.append(copy(backs.at[n], back_ref.at[n], outs.at[2 * n + 1]))
        stores[-1].start()
        if n + 2 < parts:
            for item in loads[n + 2]:
                item.start()
    for k, ref in ((1, other_sums), (0, own_sums)):
        stores.append(copy(total.at[k], ref, outs.at[2 * parts + k]))
        stores[-1].start()
    for item in stores:
        item.wait()


def feed_forward(own_in, met_in, bias, pieces):
    _, tokens, width = own_in.shape
    parts, units = len(pieces) // 2, pieces[0].shape[1]
    column = jax.ShapeDtypeStruct((parts, 2 * units), f32)
    hidden = [jax.ShapeDtypeStruct((parts, 2 * tokens, 2 * units), bf16)] * 2
    sums = [jax.ShapeDtypeStruct((2, tokens, width), f32)] * 2
    dma = pltpu.SemaphoreType.DMA
    return pl.pallas_call(
        functools.partial(feed_forward_kernel, parts),
        grid=(1,),
        in_specs=[any_spec, any_spec, full(bias)] + [any_spec] * len(pieces),
        out_specs=[any_spec] * 2 + [full(column), any_spec, any_spec],
        out_shape=hidden + [column] + sums,
        scratch_shapes=[
            pltpu.VMEM((2 * tokens, width), bf16),
            pltpu.VMEM((2 * tokens, width), bf16),
            pltpu.VMEM((2, 2, 2 * units, width), bf16),
            pltpu.VMEM(hidden[0].shape, bf16),
            pltpu.VMEM(hidden[0].shape, bf16),
            pltpu.VMEM((2, 2, tokens, width), f32),
            dma((4 + 4 * parts,)),
            dma((2 * parts + 2,)),
        ],
        cost_estimate=tiny,
        compiler_params=pltpu.CompilerParams(vmem_limit_bytes=60 * MIB),
        name="feed_forward",
    )(own_in, met_in, bias, *pieces)


def fc_grad_kernel(parts, act_ref, back_ref, own_ref, met_ref, *refs):
    grads, (x, acts, backs, products, ins, outs) = refs[: 2 * parts], refs[2 * parts :]
    half, units = own_ref.shape[1], grads[0].shape[1]
    copy = pltpu.make_async_copy
    inputs = []
    for k, ref in enumerate((own_ref, met_ref)):
        for m in range(2):
            inputs.append(copy(ref.at[m], x.at[m, pl.ds(k * half, half)], ins.at[2 * k + m]))
    loads = [
        [
            copy(act_ref.at[n], acts.at[n], ins.at[4 + 2 * n]),
            copy(back_ref.at[n], backs.at[n], ins.at[5 + 2 * n]),
        ]
        for n in range(parts)
    ]
    for item in inputs + [item for pair in loads for item in pair]:
        item.start()
    stores = []
    for n in range(parts):
        for item in (inputs if n == 0 else []) + loads[n]:
            item.wait()
        if n >= 2:
            for item in stores[n - 2]:
                item.wait()
        stores.append([])
        for kind, left, right in ((0, backs, 0), (1, acts, 1)):
            products[n % 2, kind] = dot(left[n], x[right], 0, 0).astype(bf16)
            for side in range(2):
                stores[n].append(
                    copy(
                        products.at[n % 2, kind, pl.ds(side * units, units)],
                        grads[2 * n + side].at[kind],
                        outs.at[4 * n + 2 * kind + side],
                    )
                )
                stores[n][-1].start()
    for pair in stores[-2:]:
        for item in pair:
            item.wait()


def fc_grads_of(acts, backs, own_in, met_in):
    parts, tokens, columns = acts.shape
    width = own_in.shape[2]
    dma = pltpu.SemaphoreType.DMA
    return pl.pallas_call(
        functools.partial(fc_grad_kernel, parts),
        grid=(1,),
        in_specs=[any_spec] * 4,
        out_specs=[any_spec] * (2 * parts),
        out_shape=[pltpu.HBM((2, columns // 2, width), bf16)] * (2 * parts),
        scratch_shapes=[
            pltpu.VMEM((2, tokens, width), bf16),
            pltpu.VMEM(acts.shape, bf16),
            pltpu.VMEM(acts.shape, bf16),
            pltpu.VMEM((2, 2, columns, width), bf16),
            dma((4 + 2 * parts,)),
            dma((4 * parts,)),
        ],
        cost_estimate=tiny,
        compiler_params=pltpu.CompilerParams(vmem_limit_bytes=60 * MIB),
        name="fc_grads",
    )(acts, backs, own_in, met_in)


def on_device(
    tokens,
    cond,
    segment_ids,
    crop_slot,
    ada_weight,
    ada_bias,
    attn_weight,
    fc_in,
    fc_out,
    biases,
    out_grad,
):
    net = Net()
    tok_len, width = tokens.shape[1:]
    head_dim = width // HEADS
    mod_rank, core, chips = net.mod_rank, net.core, net.chips
    device_count = net.dp * net.mod
    crop_count = crop_slot.shape[1] // net.mod
    shard = attn_weight.shape[0]
    third = shard // 3
    chunks_of = [range(chips // 2), range(chips // 2, chips)]
    halves = [(n, side) for n in range(3) for side in range(2)]
    aligned = shard % (2 * head_dim) == 0 and third % 16 == 0 and width % (2 * net.mod * shard) == 0

    g_attn = Gather(net, attn_weight[None])
    g_fc = Gather(net, jnp.stack([fc_in, fc_out]))
    silu_cond, mod_own = modulate(cond, ada_weight, ada_bias.reshape(1, -1).astype(f32))
    for n in range(g_attn.count):
        g_attn.start()
        g_attn.got = [after(g_attn.got[0], mod_own)]
        g_attn.finish()
    g_attn.start()
    first = g_attn.value
    g_attn.finish().start()
    g_attn.finish().start()
    third_phase = g_attn.value
    for n in range(g_fc.count):
        g_fc.start(*third_phase)
        if n < g_fc.count - 1:
            g_fc.finish()
    g_fc.finish().start(*g_attn.got)
    attn_pieces = [(g_attn.value, g_attn.got)[side][n] for n, side in halves]

    mod_other = net.swap(after(mod_own, *first), "mod")
    modulation = jnp.concatenate(
        [jnp.where(mod_rank == 0, mod_own, mod_other), jnp.where(mod_rank == 0, mod_other, mod_own)], axis=1
    )
    seg_ids = segment_ids[0]
    slots = lax.dynamic_slice_in_dim(crop_slot[0], mod_rank * crop_count, crop_count)
    crop_onehot = seg_ids[:, None] == jnp.arange(crop_count, dtype=jnp.int32)[None, :]
    token_slot = jnp.sum(jnp.where(crop_onehot, slots[None, :], 0), axis=1)
    slot_pick = token_slot[:, None] == jnp.arange(cond.shape[0], dtype=jnp.int32)[None, :]
    slot_pick = slot_pick.astype(bf16)
    modulation = after(modulation, *third_phase)
    mods = [modulation[:, n * width : (n + 1) * width] for n in range(6)]
    shift_a, scale_a, gate_a, shift_m, scale_m, gate_m = [times(slot_pick, block) for block in mods]

    slot_count, own_cols = cond.shape[0], width // net.dp
    to_dp = jnp.moveaxis(silu_cond.reshape(slot_count, net.dp, own_cols), 1, 0).reshape(net.dp, 1, -1)
    to_all = jnp.broadcast_to(to_dp, (net.dp, net.mod, slot_count * own_cols)).reshape(device_count, -1)
    to_all = after(to_all, *third_phase)
    sent = jnp.concatenate([jnp.broadcast_to(biases[None], (device_count, biases.shape[0])), to_all], axis=1)
    met = lax.all_to_all(sent, ("dp", "mod"), split_axis=0, concat_axis=0, tiled=True)
    ada_order = list(range(net.bits - 1, -1, -1))
    dp_order = net.ranks(ada_order, range(net.dp))[0]
    dp_pick = (dp_order[:, None] == jnp.arange(net.dp)[None, :]).astype(bf16)
    cond_cols = times(dp_pick, met.reshape(net.dp, net.mod, -1)[:, 0, biases.shape[0] :]).astype(bf16)
    cond_cols = cond_cols.reshape(-1, own_cols)
    bias_all = met[:, : biases.shape[0]].reshape(-1, width)
    bias_query, bias_value, bias_proj, bias_out = [bias_all[n].astype(f32) for n in range(4)]
    bias_in = bias_all[4:].reshape(device_count, 3, third)
    picks = []
    for n, side in halves:
        devices = net.devices(net.orders[n], chunks_of[side])
        picks.append((devices[:, None] == jnp.arange(device_count)[None, :]).astype(bf16))
    picks = jnp.stack(picks).reshape(3, 2, chips // 2, device_count)
    bias_pieces = jnp.einsum("nsjd,dnr->nsjr", picks, bias_in, preferred_element_type=f32).reshape(3, -1)

    def join(own, other):
        own, other = [a.reshape(-1, 1, net.mod * shard, a.shape[-1]) for a in (own, other)]
        both = jnp.where(core == 0, jnp.concatenate([own, other], 1), jnp.concatenate([other, own], 1))
        return both.reshape(-1, both.shape[-1])

    def part(whole):
        whole = whole.reshape(-1, 2, net.mod * shard, whole.shape[-1])
        return [
            jnp.where(core == c, whole[:, 0], whole[:, 1]).reshape(-1, whole.shape[-1]) for c in range(2)
        ]

    resid = tokens[0].astype(f32)
    normed_a, _ = layer_norm(resid)
    attn_in = (normed_a * (1.0 + scale_a) + shift_a).astype(bf16)
    if aligned:
        index = jnp.concatenate([net.local(net.orders[n], chunks_of[side]) * 3 + n for n, side in halves])
        own_weight = assemble(attn_pieces, index, third)
        qkv_rows = own_weight.shape[0] * 3 // 4
        qkv_weight = own_weight[:qkv_rows]
        proj_own = own_weight[qkv_rows:]
        proj_weight = join(proj_own, net.swap(proj_own, 0))
        ids = jnp.stack([seg_ids, net.swap(seg_ids, 0)])
        attn_in = after(attn_in, *third_phase)
        attn_both = jnp.concatenate([attn_in, net.swap(attn_in, 0)], axis=0)
        own_query, own_value = part(bias_query[:, None])[0], part(bias_value[:, None])[0]
        qkv_bias = jnp.concatenate([own_query, jnp.zeros_like(own_query), own_value], axis=0)
        attn_both = after(attn_both, *g_fc.got)
        g_fc.finish().start()
        qkv = (times_rows(qkv_weight, attn_both) + qkv_bias).astype(bf16)
        qkv = qkv.reshape(3, -1, 2 * head_dim, 2 * tok_len)
        context_both = attention(qkv, ids, head_dim).reshape(-1, 2 * tok_len)
        context = join(context_both[:, :tok_len], net.swap(context_both[:, tok_len:], 0))
        attn_out = dot(context, proj_weight, 0, 1) + bias_proj
    else:
        arrays = attn_pieces + [net.swap(piece, 0) for piece in attn_pieces]
        places = jnp.concatenate(
            [net.devices(net.orders[n], chunks_of[side], c) * 3 + n for c in range(2) for n, side in halves]
        )
        spread = jnp.concatenate(arrays, axis=1)[0]

        def place(n, whole):
            block = lax.dynamic_slice_in_dim(spread, n * third, third)
            return lax.dynamic_update_slice_in_dim(whole, block, places[n] * third, 0)

        attn_w = lax.fori_loop(0, places.shape[0], place, jnp.zeros_like(spread))
        g_fc.finish().start()
        g_fc.finish().start()
        qkv_weight, proj_weight = attn_w[: 3 * width], attn_w[3 * width :]
        qkv_bias = jnp.concatenate([bias_query, jnp.zeros_like(bias_query), bias_value])
        qkv = (times_rows(qkv_weight, attn_in) + qkv_bias[:, None]).astype(bf16)
        qkv = qkv.reshape(3, -1, 2 * head_dim, tok_len)
        context = attention(qkv, seg_ids[None], head_dim).reshape(-1, tok_len)
        attn_out = dot(context, proj_weight, 0, 1) + bias_proj
    mid = resid + gate_a * attn_out
    normed_m, _ = layer_norm(mid)
    mlp_in = (normed_m * (1.0 + scale_m) + shift_m).astype(bf16)
    if aligned:
        mlp_in = after(mlp_in, *g_fc.got)
        g_fc.finish().start()
    grad_mlp = (gate_m * out_grad[0].astype(f32)).astype(bf16)

    mlp_own = jnp.stack([mlp_in, grad_mlp])
    mlp_met = after(net.swap(mlp_own, 0), cond_cols, bias_pieces)
    grad_bias_out = jnp.sum(grad_mlp.astype(f32), axis=0, keepdims=True)
    fc_pieces = [(g_fc.value, g_fc.got)[side][n] for n, side in halves]
    acts, backs, columns, own_sums, other_sums = feed_forward(mlp_own, mlp_met, bias_pieces, fc_pieces)
    sums_met = net.swap(other_sums, 0)
    fc_grads = fc_grads_of(acts, backs, mlp_own, mlp_met)
    sums_met = after(sums_met, *fc_grads)
    back_way = Scatter(net, fc_grads[0::2], fc_grads[1::2])

    result, pair_m, grad_mid, grad_attn, grad_bias_proj, *parts = middle(
        core,
        net.mod * shard if aligned else None,
        own_sums,
        sums_met,
        mid,
        out_grad[0],
        slot_pick,
        modulation,
        bias_out[None],
        proj_weight,
        context,
    )
    if aligned:
        mine, other, proj_mine, proj_other = parts
        context_grads = [a.reshape(-1, 2 * head_dim, tok_len) for a in (mine, net.swap(other, 0))]
        proj_met = net.swap(after(proj_other, *context_grads), 0)
        grad_qkv = attention(qkv, ids, head_dim, context_grads)
        grad_qkv = grad_qkv.reshape(-1, 2 * tok_len)
        back_own, back_other = attn_in_grads(grad_qkv, own_weight)
        back_met = net.swap(back_other, 0)
        grad_qkv = after(grad_qkv, back_own)
        places = jnp.sum(
            jnp.where(
                index[None, :] == jnp.arange(index.shape[0], dtype=index.dtype)[:, None],
                jnp.arange(index.shape[0], dtype=index.dtype)[None, :],
                0,
            ),
            axis=1,
        )
        pieces = weight_grad(grad_qkv, attn_both, proj_mine, proj_met, places, third)
        back_met = after(back_met, pieces)
    else:
        grad_context, grad_proj = parts
        grad_qkv = attention(
            qkv, seg_ids[None], head_dim, [grad_context.reshape(-1, 2 * head_dim, tok_len)]
        ).reshape(-1, tok_len)
        attn_grad = jnp.concatenate([times(grad_qkv, attn_in).astype(bf16), grad_proj], axis=0)

        def take(n, whole):
            block = lax.dynamic_slice_in_dim(attn_grad, places[n] * third, third)
            return lax.dynamic_update_slice_in_dim(whole, block, n * third, 0)

        grads = lax.fori_loop(0, places.shape[0], take, jnp.zeros_like(attn_grad))
        grads = jnp.split(grads[None], 12, axis=1)
        pieces = jnp.concatenate([summed(a, net.swap(b, 0)) for a, b in zip(grads[:6], grads[6:])], axis=1)
        back_own = contract_rows(grad_qkv, qkv_weight)
        back_met = jnp.zeros_like(back_own)
    grad_tokens, pair_a = end_call(
        attn_end_kernel, f32, slot_count, back_own, back_met, tokens[0], grad_mid, attn_out, slot_pick, modulation
    )
    pair_a, *back_way.got = lax.optimization_barrier((pair_a, *back_way.got))
    pair_own = jnp.where(mod_rank == 0, pair_a, pair_m)
    pair_send = jnp.where(mod_rank == 0, pair_m, pair_a)
    grad_mod = summed(pair_own, net.swap(pair_send, "mod"))
    for n in range(3):
        back_way.hold(n, grad_mod)
    mod_rows = jnp.concatenate([grad_mod, net.swap(grad_mod, ada_order[0])], axis=0)
    sends = [back_way.join(0, pieces), back_way.join(1, pieces)]
    back_way.hold(2, mod_rows)
    sends.append(back_way.join(2, pieces))
    grad_qkv, columns = lax.optimization_barrier((grad_qkv, columns, *sends))[:2]

    grad_silu = times_rows(grad_mod, ada_weight)
    silu_own = jnp.where(mod_rank == 0, grad_silu[:crop_count], grad_silu[crop_count:])
    silu_send = jnp.where(mod_rank == 0, grad_silu[crop_count:], grad_silu[:crop_count]).astype(bf16)

    column = jnp.sum(grad_qkv.astype(f32), axis=1, keepdims=True).reshape(3, -1, 1)
    if aligned:
        none = jnp.zeros_like(column[0])
        column = [join(column[0], none), None, join(column[2], none)]
    columns = columns.reshape(3, 2, chips // 2, third)
    grad_bias_in = jnp.einsum("nsjd,nsjr->dnr", picks.astype(f32), columns, precision=lax.Precision.HIGHEST)
    grad_bias = stack_rows(
        column[0].reshape(1, -1),
        column[2].reshape(1, -1),
        grad_bias_proj,
        grad_bias_out,
        grad_bias_in.reshape(-1, width),
    )
    bias_rows = lax.all_to_all(
        grad_bias.reshape(device_count, -1), ("dp", "mod"), split_axis=0, concat_axis=0, tiled=True
    )
    bias_sum = jnp.sum(bias_rows, axis=0)
    mod_rows = after(mod_rows, *back_way.got)
    mod_rows = jnp.concatenate([mod_rows, net.swap(mod_rows, ada_order[1])], axis=0)
    for n in range(3):
        back_way.hold(n, silu_send, bias_sum)
    sends = [back_way.second(0)]
    back_way.hold(1, mod_rows)
    sends += [back_way.second(1), back_way.second(2)]
    back_way.second_attn(sends)
    back_way.third()
    back_way.third_attn()
    silu_send = after(silu_send, *back_way.also_got)
    grad_silu = silu_own + net.swap(silu_send, "mod").astype(f32)
    own_cond = lax.dynamic_slice_in_dim(cond, mod_rank * crop_count, crop_count, 0).astype(f32)
    silu_back = jax.vjp(jax.nn.silu, own_cond)[1]
    grad_cond = silu_back(grad_silu)[0]

    mod_rows = after(mod_rows, *back_way.also_got)
    fc_sum, attn_sum = back_way.last()
    for dim in ada_order[2:]:
        mod_rows = jnp.concatenate([mod_rows, net.swap(mod_rows, dim)], axis=0)
    ada_w_sum = contract_rows(cond_cols, mod_rows)
    ada_b_sum = jnp.sum(mod_rows.astype(f32), axis=0).reshape(ada_bias.shape[0], width)
    ada_b_sum = lax.dynamic_slice_in_dim(ada_b_sum, net.dp_rank * own_cols, own_cols, 1)

    return (
        result[None],
        grad_tokens[None],
        grad_cond,
        ada_w_sum,
        ada_b_sum,
        attn_sum[0],
        fc_sum[0],
        fc_sum[1],
        bias_sum,
    )


def solution(mesh):
    placed = (
        P(("dp", "mod"), None, None),
        P("dp", None),
        P(("dp", "mod"), None),
        P("dp", None),
        P(None, "mod"),
        P("mod", None),
        P(("dp", "mod"), None),
        P(("dp", "mod"), None),
        P(("dp", "mod"), None),
        P(("dp", "mod")),
        P(("dp", "mod"), None, None),
    )
    return jax.shard_map(
        on_device,
        mesh=mesh,
        in_specs=placed,
        out_specs=(
            P(("dp", "mod"), None, None),
            P(("dp", "mod"), None, None),
            P(("dp", "mod"), None),
            P("dp", "mod"),
            P("mod", "dp"),
            P(("dp", "mod"), None),
            P(("dp", "mod"), None),
            P(("dp", "mod"), None),
            P(("dp", "mod")),
        ),
        check_vma=False,
    )
```

```python
import functools

import jax
import jax.numpy as jnp
import numpy as np
from jax import lax
from jax.experimental import pallas as pl
from jax.experimental.pallas import tpu as pltpu
from jax.sharding import PartitionSpec as P

HEADS = 16
norm_eps = 1e-06
bf16 = jnp.bfloat16
f32 = jnp.float32
MIB = 1024 * 1024


def layer_norm(values):
    center = values - jnp.mean(values, axis=-1, keepdims=True)
    inverse = lax.rsqrt(jnp.mean(center * center, axis=-1, keepdims=True) + norm_eps)
    return (center * inverse, inverse)


def norm_back(grad_in, normed, inverse):
    centered = grad_in - jnp.mean(grad_in, axis=-1, keepdims=True)
    return (centered - normed * jnp.mean(grad_in * normed, axis=-1, keepdims=True)) * inverse


def dot(left, right, left_dim, right_dim):
    return lax.dot_general(left, right, (((left_dim,), (right_dim,)), ((), ())), preferred_element_type=f32)


def times(left, right):
    return dot(left, right, 1, 0)


def times_rows(left, right):
    return dot(left, right, 1, 1)


def contract_rows(left, right):
    return dot(left, right, 0, 0)


def after(value, *others):
    return lax.optimization_barrier((value, *others))[0]


def summed(left, right):
    return (left.astype(f32) + right.astype(f32)).astype(bf16)


class Net:
    def __init__(self):
        self.dp = lax.axis_size("dp")
        self.mod = lax.axis_size("mod")
        self.bits = self.dp.bit_length() - 1
        self.dp_rank = lax.axis_index("dp")
        self.mod_rank = lax.axis_index("mod")
        self.core = self.dp_rank & 1
        self.chips = self.dp // 2 * self.mod
        self.lead = list(range(self.bits - 1, 2, -1))
        last = ["mod", 1, 2]
        self.turns = [last[n:] + last[:n] for n in range(3)]
        self.orders = [self.lead + turn for turn in self.turns]

    def swap(self, value, dim):
        if dim == "mod":
            return lax.ppermute(value, "mod", [(i, i ^ 1) for i in range(self.mod)])
        return lax.ppermute(value, "dp", [(i, i ^ (1 << dim)) for i in range(self.dp)])

    def ranks(self, order, chunks, core=0):
        masks = []
        for j in chunks:
            dp_mask, mod_mask = core, 0
            for step, dim in enumerate(order):
                if j >> step & 1:
                    if dim == "mod":
                        mod_mask ^= 1
                    else:
                        dp_mask ^= 1 << dim
            masks.append((dp_mask, mod_mask))
        masks = np.array(masks, np.int32)
        return self.dp_rank ^ masks[:, 0], self.mod_rank ^ masks[:, 1]

    def devices(self, order, chunks, core=0):
        dp, mod = self.ranks(order, chunks, core)
        return dp * self.mod + mod

    def local(self, order, chunks):
        dp, mod = self.ranks(order, chunks)
        return (dp >> 1) * self.mod + mod


class Gather:
    def __init__(self, net, shard):
        self.net, self.count = net, len(net.lead)
        self.third = shard.shape[1] // 3
        self.value, self.got, self.phase = shard, None, 0

    def start(self, *others):
        net, phase = self.net, self.phase
        if phase < self.count:
            self.value = after(self.value, *others) if others else self.value
            self.got = [net.swap(self.value, net.lead[phase])]
        else:
            if phase == self.count:
                kinds, _, width = self.value.shape
                whole = self.value.reshape(kinds, -1, 3, self.third, width)
                self.value = [whole[:, :, n].reshape(kinds, -1, width) for n in range(3)]
            if others:
                self.value = list(lax.optimization_barrier((*self.value, *others))[:3])
            step = phase - self.count
            self.got = [net.swap(self.value[n], net.turns[n][step]) for n in range(3)]
        self.phase += 1
        return self

    def finish(self):
        if self.phase <= self.count:
            self.value = jnp.concatenate([self.value, self.got[0]], axis=1)
        elif self.phase < self.count + 3:
            self.value = [jnp.concatenate(pair, axis=1) for pair in zip(self.value, self.got)]
        return self


any_spec = pl.BlockSpec(memory_space=pl.ANY)


def full(value):
    return pl.BlockSpec(value.shape, lambda *_: (0,) * len(value.shape))

tiny = pl.CostEstimate(flops=1024, bytes_accessed=1024, transcendentals=0)


def run_copies(copies):
    for copy in copies:
        copy.start()
    for copy in copies:
        copy.wait()


def assemble_kernel(rows, each, index_ref, *refs):
    pieces, out_ref, hold, sems, last = refs[:-4], *refs[-4:]
    copies = []
    for n, piece in enumerate(pieces):
        for j in range(each):
            at = pl.multiple_of(index_ref[n * each + j] * rows, rows)
            copies.append(
                pltpu.make_async_copy(
                    piece.at[0, pl.ds(j * rows, rows)], hold.at[pl.ds(at, rows)], sems.at[n * each + j]
                )
            )
    run_copies(copies)
    run_copies([pltpu.make_async_copy(hold, out_ref, last)])


def assemble(pieces, index, rows):
    each, width = pieces[0].shape[1] // rows, pieces[0].shape[2]
    total = len(pieces) * each
    return pl.pallas_call(
        functools.partial(assemble_kernel, rows, each),
        grid_spec=pltpu.PrefetchScalarGridSpec(
            num_scalar_prefetch=1,
            grid=(1,),
            in_specs=[any_spec] * len(pieces),
            out_specs=any_spec,
            scratch_shapes=[
                pltpu.VMEM((total * rows, width), bf16),
                pltpu.SemaphoreType.DMA((total,)),
                pltpu.SemaphoreType.DMA,
            ],
        ),
        out_shape=jax.ShapeDtypeStruct((total * rows, width), bf16),
        compiler_params=pltpu.CompilerParams(vmem_limit_bytes=10 * MIB),
        name="assemble",
    )(index, *pieces)


def added(left, right):
    return (left.astype(f32) + right.astype(f32)).astype(bf16)


def sums_call(kernel, grid, in_specs, out_specs, outs, *args, limit=24):
    return pl.pallas_call(
        kernel,
        grid=grid,
        in_specs=in_specs,
        out_specs=out_specs,
        out_shape=[pltpu.HBM(out, bf16) for out in outs],
        cost_estimate=tiny,
        compiler_params=pltpu.CompilerParams(vmem_limit_bytes=limit * MIB),
        name=kernel.__name__,
    )(*args)


def first_sums(own_low, own_high, got_low, got_high, also, keep, send):
    keep[...] = added(own_low[...], got_low[...])
    send[:2] = added(own_high[...], got_high[...])
    send[2:] = also[...]


def half_sums(own, got, keep, send):
    half = keep.shape[1]
    keep[...] = added(own[:, :half], got[:, :half])
    send[...] = added(own[:, half:], got[:, half:])


def block_sums(own, got, keep, send):
    keep[0] = added(own[0], got[0])
    send[0] = added(own[1], got[1])


def third_sums(*refs):
    outs = refs[6:]
    for n in range(3):
        total = added(refs[n][...], refs[3 + n][...])
        if len(outs) == 2:
            rows = total.shape[1] // 2
            outs[0][:, n * rows : (n + 1) * rows] = total[:, :rows]
            outs[1][:, n * rows : (n + 1) * rows] = total[:, rows:]
        else:
            outs[n][...] = total


def third_attn_sums(*refs):
    for n in range(3):
        half_sums(refs[n], refs[3 + n], refs[6 + 2 * n], refs[7 + 2 * n])


def fourth_sums(*refs):
    keep, send = refs[6:]
    rows = keep.shape[1] // 3
    for n in range(3):
        total = added(refs[n][0], refs[3 + n][0])
        keep[0, n * rows : (n + 1) * rows] = total[:rows]
        send[0, n * rows : (n + 1) * rows] = total[rows:]


class Scatter:
    def __init__(self, net, own, other):
        self.net = net
        self.own = list(own)
        self.got = [net.swap(other[n], net.turns[n][2]) for n in range(3)]
        self.aligned = len(net.lead) == 1 and own[0].shape[1] // 8 % 16 == 0

    def hold(self, n, *others):
        self.got[n] = after(self.got[n], *others)

    def join(self, n, pieces):
        _, rows, width = self.own[n].shape
        half = rows // 2
        step = half // 2
        also = 2 * ((n + 2) % 3)
        self.pieces = pieces.reshape(12, half, width)
        block = (2, step, width)
        low, high = pl.BlockSpec(block, lambda i: (0, i, 0)), pl.BlockSpec(block, lambda i: (0, i + 2, 0))
        self.own[n], send = sums_call(
            first_sums,
            (2,),
            [low, high, low, high, pl.BlockSpec(block, lambda i: (also + 1, i, 0))],
            [low, pl.BlockSpec((4, step, width), lambda i: (0, i, 0))],
            [(2, half, width), (4, half, width)],
            self.own[n],
            self.own[n],
            self.got[n],
            self.got[n],
            self.pieces,
            limit=60,
        )
        self.got[n] = self.net.swap(send, self.net.turns[n][1])
        return send

    def second(self, n):
        _, rows, width = self.own[n].shape
        outs = [(2, rows // 2, width)] * 2
        self.both = getattr(self, "both", [None] * 3)
        self.both[n] = self.got[n]
        self.own[n], send = sums_call(
            half_sums,
            (1,),
            [full(self.own[n]), pl.BlockSpec((2, rows, width), lambda i: (0, 0, 0))],
            [full(jax.ShapeDtypeStruct(out, bf16)) for out in outs],
            outs,
            self.own[n],
            self.got[n],
        )
        self.got[n] = self.net.swap(send, self.net.turns[n][0])
        return send

    def second_attn(self, others):
        self.also, self.also_got = [None] * 3, [None] * 3
        both = list(lax.optimization_barrier((*self.both, *others))[:3])
        for n in range(3):
            _, rows, width = both[n].shape
            piece = 2 * ((n + 2) % 3)
            outs = [(1, rows, width)] * 2
            self.also[n], send = sums_call(
                block_sums,
                (1,),
                [
                    pl.BlockSpec((2, rows, width), lambda i: (piece, 0, 0)),
                    pl.BlockSpec((2, rows, width), lambda i: (1, 0, 0)),
                ],
                [full(jax.ShapeDtypeStruct(out, bf16)) for out in outs],
                outs,
                self.pieces,
                both[n],
            )
            self.also_got[n] = self.net.swap(send, self.net.turns[n][0])

    def third(self):
        net = self.net
        _, rows, width = self.own[0].shape
        outs = [(2, rows // 2 * 3, width)] * 2 if self.aligned else [(2, rows, width)] * 3
        args = self.own + self.got
        results = sums_call(
            third_sums,
            (1,),
            [full(a) for a in args],
            [full(jax.ShapeDtypeStruct(out, bf16)) for out in outs],
            outs,
            *args,
        )
        if self.aligned:
            self.fc = results[0], net.swap(results[1], net.lead[0])
        else:
            self.fc = self.lead(self.together(results), len(net.lead) - 1)
        self.also_got = list(lax.optimization_barrier((*self.also_got, results[1]))[:3])

    def after_fc(self):
        *self.also_got, fc_got = lax.optimization_barrier((*self.also_got, self.fc[1]))
        self.fc = self.fc[0], fc_got

    def third_attn(self):
        net = self.net
        _, rows, width = self.also[0].shape
        args, outs = self.also + self.also_got, [(1, rows // 2, width)] * 6
        results = sums_call(
            third_attn_sums,
            (1,),
            [full(a) for a in args],
            [full(jax.ShapeDtypeStruct(out, bf16)) for out in outs],
            outs,
            *args,
        )
        self.also = results[0::2]
        self.also_got = [net.swap(results[2 * n + 1], net.turns[(n + 2) % 3][0]) for n in range(3)]

    def last(self):
        net = self.net
        order = (1, 2, 0)
        keep, got = [self.also[n] for n in order], [self.also_got[n] for n in order]
        if self.aligned:
            _, rows, width = keep[0].shape
            outs = [(1, rows // 2 * 3, width)] * 2
            own, send = sums_call(
                fourth_sums,
                (1,),
                [full(a) for a in keep + got],
                [full(jax.ShapeDtypeStruct(out, bf16)) for out in outs],
                outs,
                *keep,
                *got,
            )
            attn = own, net.swap(send, net.lead[0])
        else:
            attn = self.lead(self.together([summed(a, b) for a, b in zip(keep, got)]), len(net.lead) - 1)
        sums = []
        for own, got in (self.fc, attn):
            for step in range(len(net.lead) - 1, -1, -1):
                total = own.astype(f32) + got.astype(f32)
                if step:
                    own, got = self.lead(total.astype(bf16), step - 1)
            sums.append(total)
        return sums

    def together(self, parts):
        kinds, _, width = parts[0].shape
        count = 1 << len(self.net.lead)
        return jnp.concatenate([p.reshape(kinds, count, -1, width) for p in parts], axis=2).reshape(kinds, -1, width)

    def lead(self, whole, step):
        half = whole.shape[1] // 2
        return whole[:, :half], self.net.swap(whole[:, half:], self.net.lead[step])


def attn_in_kernel(grad_ref, weight_ref, own_ref, other_ref):
    total = dot(grad_ref[...], weight_ref[...], 0, 0)
    half = own_ref.shape[0]
    own_ref[...] = total[:half]
    other_ref[...] = total[half:]


def attn_in_grads(grad, weight):
    rows, tokens = grad.shape
    width = weight.shape[1]
    out = jax.ShapeDtypeStruct((tokens // 2, width), f32)
    return pl.pallas_call(
        attn_in_kernel,
        grid=(1,),
        in_specs=[full(grad), pl.BlockSpec((rows, width), lambda i: (0, 0))],
        out_specs=[full(out)] * 2,
        out_shape=[out, pltpu.HBM(out.shape, f32)],
        cost_estimate=tiny,
        compiler_params=pltpu.CompilerParams(vmem_limit_bytes=40 * MIB),
        name="attn_in_grads",
    )(grad, weight)


def weight_grad_kernel(rows, place_ref, grad_ref, x_ref, mine_ref, other_ref, out_ref, hold, sems):
    top, copies = grad_ref.shape[0], []
    step = top // 3
    for n in (3, 0, 1, 2):
        start = n * step
        stop = min(start + step, hold.shape[0])
        if n == 3:
            hold[start:] = summed(mine_ref[...], other_ref[...])
        else:
            hold[start:stop] = dot(grad_ref[start:stop], x_ref[...], 1, 0).astype(bf16)
        for unit in range(start // rows, stop // rows):
            at = pl.multiple_of(place_ref[unit] * rows, rows)
            copies.append(
                pltpu.make_async_copy(
                    hold.at[pl.ds(unit * rows, rows)], out_ref.at[pl.ds(at, rows)], sems.at[unit]
                )
            )
            copies[-1].start()
    for copy in copies:
        copy.wait()


def weight_grad(grad, x, mine, other, places, rows):
    total, width = grad.shape[0] + mine.shape[0], x.shape[1]
    return pl.pallas_call(
        functools.partial(weight_grad_kernel, rows),
        grid_spec=pltpu.PrefetchScalarGridSpec(
            num_scalar_prefetch=1,
            grid=(1,),
            in_specs=[full(a) for a in (grad, x, mine, other)],
            out_specs=any_spec,
            scratch_shapes=[pltpu.VMEM((total, width), bf16), pltpu.SemaphoreType.DMA((total // rows,))],
        ),
        out_shape=jax.ShapeDtypeStruct((total, width), bf16),
        cost_estimate=tiny,
        compiler_params=pltpu.CompilerParams(vmem_limit_bytes=60 * MIB),
        name="weight_grad",
    )(places, grad, x, mine, other)


def by_core(core_ref, group, whole):
    if group is None:
        return [whole]
    picked = []
    for c in range(2):
        rows = []
        for at in range(0, whole.shape[0], 2 * group):
            first, second = whole[at : at + group], whole[at + group : at + 2 * group]
            rows.append(jnp.where(core_ref[0] == c, first, second))
        picked.append(jnp.concatenate(rows, axis=0))
    return picked


def token_block(pick, mods, n):
    width = mods.shape[1] // 6
    return dot(pick[...], mods[:, n * width : (n + 1) * width], 1, 0)


def middle_kernel(group, core_ref, *refs):
    sums, met, mid, grad_out, pick, mods, bias, weight, context = refs[:9]
    result_ref, pair_ref, mid_ref, attn_ref, column_ref = refs[9:14]
    normed, inverse = layer_norm(mid[...])
    back, outer = sums[1] + met[1], grad_out[...].astype(f32)
    mlp_out = sums[0] + met[0] + bias[...]
    result_ref[...] = (mid[...] + token_block(pick, mods, 5) * mlp_out).astype(bf16)
    slot_sums(pick[...], (back, back * normed, outer * mlp_out), pair_ref)
    grad_mid = outer + norm_back(back * (1.0 + token_block(pick, mods, 4)), normed, inverse)
    mid_ref[...] = grad_mid
    grad_attn = (token_block(pick, mods, 2) * grad_mid).astype(bf16)
    attn_ref[...] = grad_attn
    column_ref[...] = jnp.sum(grad_attn.astype(f32), axis=0, keepdims=True)
    parts = by_core(core_ref, group, dot(weight[...], grad_attn, 0, 1))
    parts += by_core(core_ref, group, dot(grad_attn, context[...], 0, 1))
    for ref, value in zip(refs[14:], parts):
        ref[...] = value.astype(bf16)


def middle(core, group, *args):
    _, tokens, width = args[0].shape
    if group is None:
        sizes = [(width, tokens), (width, width)]
    else:
        sizes = [(width // 2, tokens)] * 2 + [(width // 2, width)] * 2
    slots = args[4].shape[1]
    outs = [((tokens, width), bf16), ((slots, 3 * width), bf16)]
    outs += [((tokens, width), f32), ((tokens, width), bf16), ((1, width), f32)]
    outs = [jax.ShapeDtypeStruct(*out) for out in outs + [(s, bf16) for s in sizes]]
    return pl.pallas_call(
        functools.partial(middle_kernel, group),
        grid=(1,),
        in_specs=[pl.BlockSpec(memory_space=pltpu.SMEM)] + [full(a) for a in args],
        out_specs=[full(a) for a in outs],
        out_shape=outs[:5] + [pltpu.HBM(a.shape, bf16) for a in outs[5:]],
        cost_estimate=tiny,
        compiler_params=pltpu.CompilerParams(vmem_limit_bytes=48 * MIB),
        name="middle",
    )(core.reshape(1), *args)


def slot_sums(pick, blocks, out_ref):
    for n, block in enumerate(blocks):
        high = block.astype(bf16)
        low = (block - high.astype(f32)).astype(bf16)
        total = dot(pick, high, 0, 0) + dot(pick, low, 0, 0)
        out_ref[:, n * block.shape[1] : (n + 1) * block.shape[1]] = total.astype(bf16)


def attn_end_kernel(*refs):
    back_a, back_b, resid, grad_mid, attn_out, pick, mods = refs[:7]
    tokens_ref, pair_ref = refs[7:]
    back = back_a[...] + back_b[...]
    normed, inverse = layer_norm(resid[...].astype(f32))
    slope = back * (1.0 + token_block(pick, mods, 1))
    tokens_ref[...] = grad_mid[...] + norm_back(slope, normed, inverse)
    slot_sums(pick[...], (back, back * normed, grad_mid[...] * attn_out[...]), pair_ref)


def end_call(kernel, dtype, slots, *args):
    tokens, width = args[0].shape
    outs = [jax.ShapeDtypeStruct((tokens, width), dtype), jax.ShapeDtypeStruct((slots, 3 * width), bf16)]
    return pl.pallas_call(
        kernel,
        grid=(1,),
        in_specs=[full(a) for a in args],
        out_specs=[full(a) for a in outs],
        out_shape=outs,
        cost_estimate=tiny,
        compiler_params=pltpu.CompilerParams(vmem_limit_bytes=32 * MIB),
        name=kernel.__name__,
    )(*args)


def rows_kernel(*refs):
    at = 0
    for ref in refs[:-1]:
        refs[-1][at : at + ref.shape[0]] = ref[...]
        at += ref.shape[0]


def stack_rows(*args):
    out = jax.ShapeDtypeStruct((sum(a.shape[0] for a in args), args[0].shape[1]), f32)
    return pl.pallas_call(
        rows_kernel,
        grid=(1,),
        in_specs=[full(a) for a in args],
        out_specs=full(out),
        out_shape=out,
        cost_estimate=tiny,
        compiler_params=pltpu.CompilerParams(vmem_limit_bytes=24 * MIB),
        name="stack_rows",
    )(*args)


def softmax_t(key, query, same, scale):
    scores = jnp.where(same, dot(key, query, 0, 0) * scale, -1e30)
    weights = jnp.exp(scores - jnp.max(scores, axis=0, keepdims=True))
    return weights * (1.0 / jnp.sum(weights, axis=0, keepdims=True))


def heads_of(block, dim, cols):
    wide = block[:, cols].astype(f32)
    return [wide[n * dim : (n + 1) * dim].astype(bf16) for n in range(wide.shape[0] // dim)]


def attn_forward(dim, scale, row_ref, col_ref, q_ref, k_ref, v_ref, out_ref):
    length = col_ref.shape[0]
    for s in range(row_ref.shape[0]):
        cols = slice(s * length, (s + 1) * length)
        same = row_ref[s : s + 1] == col_ref[:, s : s + 1]
        outs = []
        for q, k, v in zip(*[heads_of(r[0, 0], dim, cols) for r in (q_ref, k_ref, v_ref)]):
            probs = softmax_t(k, q, same, scale).astype(bf16)
            outs.append(dot(v, probs, 1, 0))
        out_ref[0, :, cols] = jnp.concatenate(outs, axis=0).astype(bf16)


def attn_backward(dim, scale, row_ref, col_ref, q_ref, k_ref, v_ref, *refs):
    length, out_ref = col_ref.shape[0], refs[-1]
    for s in range(row_ref.shape[0]):
        cols = slice(s * length, (s + 1) * length)
        same = row_ref[s : s + 1] == col_ref[:, s : s + 1]
        gq, gk, gv = [], [], []
        qs, ks, vs = [heads_of(r[0, 0], dim, cols) for r in (q_ref, k_ref, v_ref)]
        for q, k, v, g in zip(qs, ks, vs, heads_of(refs[s][0], dim, slice(0, length))):
            probs = softmax_t(k, q, same, scale)
            back = dot(v, g, 0, 0)
            back = probs * (back - jnp.sum(back * probs, axis=0, keepdims=True))
            back = back.astype(bf16)
            gq.append(dot(k, back, 1, 0) * scale)
            gk.append(dot(q, back, 1, 1) * scale)
            gv.append(dot(g, probs.astype(bf16), 1, 1))
        for n, parts in enumerate((gq, gk, gv)):
            out_ref[n, 0, :, cols] = jnp.concatenate(parts, axis=0).astype(bf16)


def attention(qkv, ids, dim, grad=None):
    _, groups, rows, tokens = qkv.shape
    scale = dim**-0.5
    ids_t = ids.T

    def one(n):
        return pl.BlockSpec((1, 1, rows, tokens), lambda i: (n, i, 0, 0))

    flat = pl.BlockSpec((1, rows, tokens), lambda i: (i, 0, 0))
    short = pl.BlockSpec((1, rows, ids.shape[1]), lambda i: (i, 0, 0))
    args = [ids, ids_t, qkv, qkv, qkv]
    specs = [pl.BlockSpec(a.shape, lambda i: (0, 0)) for a in (ids, ids_t)] + [one(0), one(1), one(2)]
    if grad is None:
        return pl.pallas_call(
            functools.partial(attn_forward, dim, scale),
            grid=(groups,),
            in_specs=specs,
            out_specs=flat,
            out_shape=jax.ShapeDtypeStruct((groups, rows, tokens), bf16),
            cost_estimate=tiny,
            compiler_params=pltpu.CompilerParams(vmem_limit_bytes=24 * MIB),
            name="attention",
        )(*args)
    return pl.pallas_call(
        functools.partial(attn_backward, dim, scale),
        grid=(groups,),
        in_specs=specs + [short] * len(grad),
        out_specs=pl.BlockSpec((3, 1, rows, tokens), lambda i: (0, i, 0, 0)),
        out_shape=jax.ShapeDtypeStruct(qkv.shape, bf16),
        cost_estimate=tiny,
        compiler_params=pltpu.CompilerParams(vmem_limit_bytes=24 * MIB),
        name="attention_back",
    )(*args, *grad)


def modulation_kernel(cond_ref, weight_ref, bias_ref, silu_ref, out_ref):
    cond = cond_ref[...].astype(f32)
    silu = (cond / (1.0 + jnp.exp(-cond))).astype(bf16)
    silu_ref[...] = silu
    out_ref[...] = (dot(silu, weight_ref[...], 1, 0) + bias_ref[...]).astype(bf16)


def modulate(cond, weight, bias):
    slots, width = cond.shape
    columns = weight.shape[1]
    tile = 384 if columns % 384 == 0 else columns
    return pl.pallas_call(
        modulation_kernel,
        grid=(columns // tile,),
        in_specs=[
            full(cond),
            pl.BlockSpec((width, tile), lambda i: (0, i)),
            pl.BlockSpec((1, tile), lambda i: (0, i)),
        ],
        out_specs=[full(cond), pl.BlockSpec((slots, tile), lambda i: (0, i))],
        out_shape=[
            jax.ShapeDtypeStruct((slots, width), bf16),
            jax.ShapeDtypeStruct((slots, columns), bf16),
        ],
        cost_estimate=tiny,
        compiler_params=pltpu.CompilerParams(vmem_limit_bytes=16 * MIB),
        name="modulate",
    )(cond, weight, bias)


def feed_forward_kernel(parts, *refs):
    own_ref, met_ref, b_ref = refs[:3]
    pieces = refs[3 : 3 + 2 * parts]
    act_ref, back_ref, column_ref, own_sums, other_sums = refs[3 + 2 * parts : 8 + 2 * parts]
    x, g, weights, acts, backs, total, ins, outs = refs[8 + 2 * parts :]
    half, units = own_ref.shape[1], pieces[0].shape[1]
    copy = pltpu.make_async_copy

    def load(n):
        slot, copies = n % 2, []
        for kind in range(2):
            for side in range(2):
                copies.append(
                    copy(
                        pieces[2 * n + side].at[kind],
                        weights.at[slot, kind, pl.ds(side * units, units)],
                        ins.at[4 + 4 * n + 2 * kind + side],
                    )
                )
        return copies

    low, high = pl.ds(0, half), pl.ds(half, half)
    inputs = [
        copy(own_ref.at[0], x.at[low], ins.at[0]),
        copy(met_ref.at[0], x.at[high], ins.at[1]),
        copy(own_ref.at[1], g.at[low], ins.at[2]),
        copy(met_ref.at[1], g.at[high], ins.at[3]),
    ]
    loads = [load(n) for n in range(parts)]
    for item in inputs[:2] + loads[0][:2] + inputs[2:] + loads[0][2:] + loads[1]:
        item.start()
    stores = []
    root = 0.7978845608028654
    for n in range(parts):
        slot = n % 2
        for item in (inputs[:2] if n == 0 else []) + loads[n][:2]:
            item.wait()
        for item in (inputs[2:] if n == 0 else []) + loads[n][2:]:
            item.wait()
        col = 0.0
        for k in range(2):
            tok = slice(k * half, (k + 1) * half)
            hidden = dot(x[tok], weights[slot, 0], 1, 1) + b_ref[n : n + 1]
            square = hidden * hidden
            tanh = jnp.tanh(root * hidden * (1.0 + 0.044715 * square))
            act = (0.5 * hidden * (1.0 + tanh)).astype(bf16)
            acts[n, tok] = act
            slope = 0.5 * (1.0 + tanh) + 0.5 * hidden * (1.0 - tanh * tanh) * (root * (1.0 + 0.134145 * square))
            back = (dot(g[tok], weights[slot, 1], 1, 1) * slope).astype(bf16)
            backs[n, tok] = back
            col = col + jnp.sum(back.astype(f32), axis=0, keepdims=True)
            for m, value in enumerate((dot(act, weights[slot, 1], 1, 0), dot(back, weights[slot, 0], 1, 0))):
                total[k, m] = value if n == 0 else total[k, m] + value
        column_ref[n : n + 1] = col
        stores.append(copy(acts.at[n], act_ref.at[n], outs.at[2 * n]))
        stores[-1].start()
        stores.append(copy(backs.at[n], back_ref.at[n], outs.at[2 * n + 1]))
        stores[-1].start()
        if n + 2 < parts:
            for item in loads[n + 2]:
                item.start()
    for k, ref in ((1, other_sums), (0, own_sums)):
        stores.append(copy(total.at[k], ref, outs.at[2 * parts + k]))
        stores[-1].start()
    for item in stores:
        item.wait()


def feed_forward(own_in, met_in, bias, pieces):
    _, tokens, width = own_in.shape
    parts, units = len(pieces) // 2, pieces[0].shape[1]
    column = jax.ShapeDtypeStruct((parts, 2 * units), f32)
    hidden = [jax.ShapeDtypeStruct((parts, 2 * tokens, 2 * units), bf16)] * 2
    sums = [jax.ShapeDtypeStruct((2, tokens, width), f32)] * 2
    dma = pltpu.SemaphoreType.DMA
    return pl.pallas_call(
        functools.partial(feed_forward_kernel, parts),
        grid=(1,),
        in_specs=[any_spec, any_spec, full(bias)] + [any_spec] * len(pieces),
        out_specs=[any_spec] * 2 + [full(column), any_spec, any_spec],
        out_shape=hidden + [column] + sums,
        scratch_shapes=[
            pltpu.VMEM((2 * tokens, width), bf16),
            pltpu.VMEM((2 * tokens, width), bf16),
            pltpu.VMEM((2, 2, 2 * units, width), bf16),
            pltpu.VMEM(hidden[0].shape, bf16),
            pltpu.VMEM(hidden[0].shape, bf16),
            pltpu.VMEM((2, 2, tokens, width), f32),
            dma((4 + 4 * parts,)),
            dma((2 * parts + 2,)),
        ],
        cost_estimate=tiny,
        compiler_params=pltpu.CompilerParams(vmem_limit_bytes=60 * MIB),
        name="feed_forward",
    )(own_in, met_in, bias, *pieces)


def fc_grad_kernel(parts, act_ref, back_ref, own_ref, met_ref, *refs):
    grads, (x, acts, backs, products, ins, outs) = refs[: 2 * parts], refs[2 * parts :]
    half, units = own_ref.shape[1], grads[0].shape[1]
    copy = pltpu.make_async_copy
    inputs = []
    for k, ref in enumerate((own_ref, met_ref)):
        for m in range(2):
            inputs.append(copy(ref.at[m], x.at[m, pl.ds(k * half, half)], ins.at[2 * k + m]))
    loads = [
        [
            copy(act_ref.at[n], acts.at[n], ins.at[4 + 2 * n]),
            copy(back_ref.at[n], backs.at[n], ins.at[5 + 2 * n]),
        ]
        for n in range(parts)
    ]
    for item in inputs + [item for pair in loads for item in pair]:
        item.start()
    stores = []
    for n in range(parts):
        for item in (inputs if n == 0 else []) + loads[n]:
            item.wait()
        if n >= 2:
            for item in stores[n - 2]:
                item.wait()
        stores.append([])
        for kind, left, right in ((0, backs, 0), (1, acts, 1)):
            products[n % 2, kind] = dot(left[n], x[right], 0, 0).astype(bf16)
            for side in range(2):
                stores[n].append(
                    copy(
                        products.at[n % 2, kind, pl.ds(side * units, units)],
                        grads[2 * n + side].at[kind],
                        outs.at[4 * n + 2 * kind + side],
                    )
                )
                stores[n][-1].start()
    for pair in stores[-2:]:
        for item in pair:
            item.wait()


def fc_grads_of(acts, backs, own_in, met_in):
    parts, tokens, columns = acts.shape
    width = own_in.shape[2]
    dma = pltpu.SemaphoreType.DMA
    return pl.pallas_call(
        functools.partial(fc_grad_kernel, parts),
        grid=(1,),
        in_specs=[any_spec] * 4,
        out_specs=[any_spec] * (2 * parts),
        out_shape=[pltpu.HBM((2, columns // 2, width), bf16)] * (2 * parts),
        scratch_shapes=[
            pltpu.VMEM((2, tokens, width), bf16),
            pltpu.VMEM(acts.shape, bf16),
            pltpu.VMEM(acts.shape, bf16),
            pltpu.VMEM((2, 2, columns, width), bf16),
            dma((4 + 2 * parts,)),
            dma((4 * parts,)),
        ],
        cost_estimate=tiny,
        compiler_params=pltpu.CompilerParams(vmem_limit_bytes=60 * MIB),
        name="fc_grads",
    )(acts, backs, own_in, met_in)


def on_device(
    tokens,
    cond,
    segment_ids,
    crop_slot,
    ada_weight,
    ada_bias,
    attn_weight,
    fc_in,
    fc_out,
    biases,
    out_grad,
):
    net = Net()
    tok_len, width = tokens.shape[1:]
    head_dim = width // HEADS
    mod_rank, core, chips = net.mod_rank, net.core, net.chips
    device_count = net.dp * net.mod
    crop_count = crop_slot.shape[1] // net.mod
    shard = attn_weight.shape[0]
    third = shard // 3
    chunks_of = [range(chips // 2), range(chips // 2, chips)]
    halves = [(n, side) for n in range(3) for side in range(2)]
    aligned = shard % (2 * head_dim) == 0 and third % 16 == 0 and width % (2 * net.mod * shard) == 0

    g_attn = Gather(net, attn_weight[None])
    g_fc = Gather(net, jnp.stack([fc_in, fc_out]))
    silu_cond, mod_own = modulate(cond, ada_weight, ada_bias.reshape(1, -1).astype(f32))
    for n in range(g_attn.count):
        g_attn.start()
        g_attn.got = [after(g_attn.got[0], mod_own)]
        g_attn.finish()
    g_attn.start()
    first = g_attn.value
    for n in range(g_fc.count):
        g_fc.start(*first)
        if n < g_fc.count - 1:
            g_fc.finish()
    g_attn.finish().start()
    g_attn.finish().start()
    third_phase = g_attn.value
    g_fc.got = [after(g_fc.got[0], *third_phase)]
    g_fc.finish().start(*g_attn.got)
    attn_pieces = [(g_attn.value, g_attn.got)[side][n] for n, side in halves]

    mod_other = net.swap(after(mod_own, *first), "mod")
    modulation = jnp.concatenate(
        [jnp.where(mod_rank == 0, mod_own, mod_other), jnp.where(mod_rank == 0, mod_other, mod_own)], axis=1
    )
    seg_ids = segment_ids[0]
    slots = lax.dynamic_slice_in_dim(crop_slot[0], mod_rank * crop_count, crop_count)
    crop_onehot = seg_ids[:, None] == jnp.arange(crop_count, dtype=jnp.int32)[None, :]
    token_slot = jnp.sum(jnp.where(crop_onehot, slots[None, :], 0), axis=1)
    slot_pick = token_slot[:, None] == jnp.arange(cond.shape[0], dtype=jnp.int32)[None, :]
    slot_pick = slot_pick.astype(bf16)
    modulation = after(modulation, *third_phase)
    mods = [modulation[:, n * width : (n + 1) * width] for n in range(6)]
    shift_a, scale_a, gate_a, shift_m, scale_m, gate_m = [times(slot_pick, block) for block in mods]

    slot_count, own_cols = cond.shape[0], width // net.dp
    to_dp = jnp.moveaxis(silu_cond.reshape(slot_count, net.dp, own_cols), 1, 0).reshape(net.dp, 1, -1)
    to_all = jnp.broadcast_to(to_dp, (net.dp, net.mod, slot_count * own_cols)).reshape(device_count, -1)
    to_all = after(to_all, *third_phase)
    sent = jnp.concatenate([jnp.broadcast_to(biases[None], (device_count, biases.shape[0])), to_all], axis=1)
    met = lax.all_to_all(sent, ("dp", "mod"), split_axis=0, concat_axis=0, tiled=True)
    ada_order = list(range(net.bits - 1, -1, -1))
    dp_order = net.ranks(ada_order, range(net.dp))[0]
    dp_pick = (dp_order[:, None] == jnp.arange(net.dp)[None, :]).astype(bf16)
    cond_cols = times(dp_pick, met.reshape(net.dp, net.mod, -1)[:, 0, biases.shape[0] :]).astype(bf16)
    cond_cols = cond_cols.reshape(-1, own_cols)
    bias_all = met[:, : biases.shape[0]].reshape(-1, width)
    bias_query, bias_value, bias_proj, bias_out = [bias_all[n].astype(f32) for n in range(4)]
    bias_in = bias_all[4:].reshape(device_count, 3, third)
    picks = []
    for n, side in halves:
        devices = net.devices(net.orders[n], chunks_of[side])
        picks.append((devices[:, None] == jnp.arange(device_count)[None, :]).astype(bf16))
    picks = jnp.stack(picks).reshape(3, 2, chips // 2, device_count)
    bias_pieces = jnp.einsum("nsjd,dnr->nsjr", picks, bias_in, preferred_element_type=f32).reshape(3, -1)

    def join(own, other):
        own, other = [a.reshape(-1, 1, net.mod * shard, a.shape[-1]) for a in (own, other)]
        both = jnp.where(core == 0, jnp.concatenate([own, other], 1), jnp.concatenate([other, own], 1))
        return both.reshape(-1, both.shape[-1])

    def part(whole):
        whole = whole.reshape(-1, 2, net.mod * shard, whole.shape[-1])
        return [
            jnp.where(core == c, whole[:, 0], whole[:, 1]).reshape(-1, whole.shape[-1]) for c in range(2)
        ]

    resid = tokens[0].astype(f32)
    normed_a, _ = layer_norm(resid)
    attn_in = (normed_a * (1.0 + scale_a) + shift_a).astype(bf16)
    if aligned:
        index = jnp.concatenate([net.local(net.orders[n], chunks_of[side]) * 3 + n for n, side in halves])
        own_weight = assemble(attn_pieces, index, third)
        qkv_rows = own_weight.shape[0] * 3 // 4
        qkv_weight = own_weight[:qkv_rows]
        proj_own = own_weight[qkv_rows:]
        proj_weight = join(proj_own, net.swap(proj_own, 0))
        ids = jnp.stack([seg_ids, net.swap(seg_ids, 0)])
        attn_in = after(attn_in, *third_phase)
        attn_both = jnp.concatenate([attn_in, net.swap(attn_in, 0)], axis=0)
        own_query, own_value = part(bias_query[:, None])[0], part(bias_value[:, None])[0]
        qkv_bias = jnp.concatenate([own_query, jnp.zeros_like(own_query), own_value], axis=0)
        attn_both = after(attn_both, *g_fc.got)
        g_fc.finish().start()
        qkv = (times_rows(qkv_weight, attn_both) + qkv_bias).astype(bf16)
        qkv = qkv.reshape(3, -1, 2 * head_dim, 2 * tok_len)
        context_both = attention(qkv, ids, head_dim).reshape(-1, 2 * tok_len)
        context = join(context_both[:, :tok_len], net.swap(context_both[:, tok_len:], 0))
        attn_out = dot(context, proj_weight, 0, 1) + bias_proj
    else:
        arrays = attn_pieces + [net.swap(piece, 0) for piece in attn_pieces]
        places = jnp.concatenate(
            [net.devices(net.orders[n], chunks_of[side], c) * 3 + n for c in range(2) for n, side in halves]
        )
        spread = jnp.concatenate(arrays, axis=1)[0]

        def place(n, whole):
            block = lax.dynamic_slice_in_dim(spread, n * third, third)
            return lax.dynamic_update_slice_in_dim(whole, block, places[n] * third, 0)

        attn_w = lax.fori_loop(0, places.shape[0], place, jnp.zeros_like(spread))
        g_fc.finish().start()
        g_fc.finish().start()
        qkv_weight, proj_weight = attn_w[: 3 * width], attn_w[3 * width :]
        qkv_bias = jnp.concatenate([bias_query, jnp.zeros_like(bias_query), bias_value])
        qkv = (times_rows(qkv_weight, attn_in) + qkv_bias[:, None]).astype(bf16)
        qkv = qkv.reshape(3, -1, 2 * head_dim, tok_len)
        context = attention(qkv, seg_ids[None], head_dim).reshape(-1, tok_len)
        attn_out = dot(context, proj_weight, 0, 1) + bias_proj
    mid = resid + gate_a * attn_out
    normed_m, _ = layer_norm(mid)
    mlp_in = (normed_m * (1.0 + scale_m) + shift_m).astype(bf16)
    if aligned:
        mlp_in = after(mlp_in, *g_fc.got)
        g_fc.finish().start()
    grad_mlp = (gate_m * out_grad[0].astype(f32)).astype(bf16)

    mlp_own = jnp.stack([mlp_in, grad_mlp])
    mlp_met = after(net.swap(mlp_own, 0), cond_cols, bias_pieces)
    grad_bias_out = jnp.sum(grad_mlp.astype(f32), axis=0, keepdims=True)
    fc_pieces = [(g_fc.value, g_fc.got)[side][n] for n, side in halves]
    acts, backs, columns, own_sums, other_sums = feed_forward(mlp_own, mlp_met, bias_pieces, fc_pieces)
    sums_met = net.swap(other_sums, 0)
    fc_grads = fc_grads_of(acts, backs, mlp_own, mlp_met)
    sums_met = after(sums_met, *fc_grads)
    back_way = Scatter(net, fc_grads[0::2], fc_grads[1::2])

    result, pair_m, grad_mid, grad_attn, grad_bias_proj, *parts = middle(
        core,
        net.mod * shard if aligned else None,
        own_sums,
        sums_met,
        mid,
        out_grad[0],
        slot_pick,
        modulation,
        bias_out[None],
        proj_weight,
        context,
    )
    if aligned:
        mine, other, proj_mine, proj_other = parts
        context_grads = [a.reshape(-1, 2 * head_dim, tok_len) for a in (mine, net.swap(other, 0))]
        proj_met = net.swap(after(proj_other, *context_grads), 0)
        grad_qkv = attention(qkv, ids, head_dim, context_grads)
        grad_qkv = grad_qkv.reshape(-1, 2 * tok_len)
        back_own, back_other = attn_in_grads(grad_qkv, own_weight)
        back_met = net.swap(back_other, 0)
        grad_qkv = after(grad_qkv, back_own)
        places = jnp.sum(
            jnp.where(
                index[None, :] == jnp.arange(index.shape[0], dtype=index.dtype)[:, None],
                jnp.arange(index.shape[0], dtype=index.dtype)[None, :],
                0,
            ),
            axis=1,
        )
        pieces = weight_grad(grad_qkv, attn_both, proj_mine, proj_met, places, third)
        back_met = after(back_met, pieces)
    else:
        grad_context, grad_proj = parts
        grad_qkv = attention(
            qkv, seg_ids[None], head_dim, [grad_context.reshape(-1, 2 * head_dim, tok_len)]
        ).reshape(-1, tok_len)
        attn_grad = jnp.concatenate([times(grad_qkv, attn_in).astype(bf16), grad_proj], axis=0)

        def take(n, whole):
            block = lax.dynamic_slice_in_dim(attn_grad, places[n] * third, third)
            return lax.dynamic_update_slice_in_dim(whole, block, n * third, 0)

        grads = lax.fori_loop(0, places.shape[0], take, jnp.zeros_like(attn_grad))
        grads = jnp.split(grads[None], 12, axis=1)
        pieces = jnp.concatenate([summed(a, net.swap(b, 0)) for a, b in zip(grads[:6], grads[6:])], axis=1)
        back_own = contract_rows(grad_qkv, qkv_weight)
        back_met = jnp.zeros_like(back_own)
    grad_tokens, pair_a = end_call(
        attn_end_kernel, f32, slot_count, back_own, back_met, tokens[0], grad_mid, attn_out, slot_pick, modulation
    )
    pair_a, *back_way.got = lax.optimization_barrier((pair_a, *back_way.got))
    pair_own = jnp.where(mod_rank == 0, pair_a, pair_m)
    pair_send = jnp.where(mod_rank == 0, pair_m, pair_a)
    grad_mod = summed(pair_own, net.swap(pair_send, "mod"))
    for n in range(3):
        back_way.hold(n, grad_mod)
    mod_rows = jnp.concatenate([grad_mod, net.swap(grad_mod, ada_order[0])], axis=0)
    sends = [back_way.join(0, pieces), back_way.join(1, pieces)]
    back_way.hold(2, mod_rows)
    sends.append(back_way.join(2, pieces))
    grad_qkv, columns = lax.optimization_barrier((grad_qkv, columns, *sends))[:2]

    grad_silu = times_rows(grad_mod, ada_weight)
    silu_own = jnp.where(mod_rank == 0, grad_silu[:crop_count], grad_silu[crop_count:])
    silu_send = jnp.where(mod_rank == 0, grad_silu[crop_count:], grad_silu[:crop_count]).astype(bf16)

    column = jnp.sum(grad_qkv.astype(f32), axis=1, keepdims=True).reshape(3, -1, 1)
    if aligned:
        none = jnp.zeros_like(column[0])
        column = [join(column[0], none), None, join(column[2], none)]
    columns = columns.reshape(3, 2, chips // 2, third)
    grad_bias_in = jnp.einsum("nsjd,nsjr->dnr", picks.astype(f32), columns, precision=lax.Precision.HIGHEST)
    grad_bias = stack_rows(
        column[0].reshape(1, -1),
        column[2].reshape(1, -1),
        grad_bias_proj,
        grad_bias_out,
        grad_bias_in.reshape(-1, width),
    )
    bias_rows = lax.all_to_all(
        grad_bias.reshape(device_count, -1), ("dp", "mod"), split_axis=0, concat_axis=0, tiled=True
    )
    bias_sum = jnp.sum(bias_rows, axis=0)
    mod_rows = after(mod_rows, *back_way.got)
    mod_rows = jnp.concatenate([mod_rows, net.swap(mod_rows, ada_order[1])], axis=0)
    for n in range(3):
        back_way.hold(n, silu_send, bias_sum)
    sends = [back_way.second(0)]
    back_way.hold(1, mod_rows)
    sends += [back_way.second(1), back_way.second(2)]
    back_way.second_attn(sends)
    back_way.third()
    silu_send, mod_rows = lax.optimization_barrier((silu_send, mod_rows, *back_way.also_got))[:2]
    grad_silu = silu_own + net.swap(silu_send, "mod").astype(f32)
    own_cond = lax.dynamic_slice_in_dim(cond, mod_rank * crop_count, crop_count, 0).astype(f32)
    silu_back = jax.vjp(jax.nn.silu, own_cond)[1]
    grad_cond = silu_back(grad_silu)[0]
    for dim in ada_order[2:]:
        mod_rows = jnp.concatenate([mod_rows, net.swap(mod_rows, dim)], axis=0)
    ada_w_sum = contract_rows(cond_cols, mod_rows)
    ada_b_sum = jnp.sum(mod_rows.astype(f32), axis=0).reshape(ada_bias.shape[0], width)
    ada_b_sum = lax.dynamic_slice_in_dim(ada_b_sum, net.dp_rank * own_cols, own_cols, 1)
    back_way.after_fc()
    back_way.third_attn()
    fc_sum, attn_sum = back_way.last()

    return (
        result[None],
        grad_tokens[None],
        grad_cond,
        ada_w_sum,
        ada_b_sum,
        attn_sum[0],
        fc_sum[0],
        fc_sum[1],
        bias_sum,
    )


def solution(mesh):
    placed = (
        P(("dp", "mod"), None, None),
        P("dp", None),
        P(("dp", "mod"), None),
        P("dp", None),
        P(None, "mod"),
        P("mod", None),
        P(("dp", "mod"), None),
        P(("dp", "mod"), None),
        P(("dp", "mod"), None),
        P(("dp", "mod")),
        P(("dp", "mod"), None, None),
    )
    return jax.shard_map(
        on_device,
        mesh=mesh,
        in_specs=placed,
        out_specs=(
            P(("dp", "mod"), None, None),
            P(("dp", "mod"), None, None),
            P(("dp", "mod"), None),
            P("dp", "mod"),
            P("mod", "dp"),
            P(("dp", "mod"), None),
            P(("dp", "mod"), None),
            P(("dp", "mod"), None),
            P(("dp", "mod")),
        ),
        check_vma=False,
    )
```

```python
import functools

import jax
import jax.numpy as jnp
import numpy as np
from jax import lax
from jax.experimental import pallas as pl
from jax.experimental.pallas import tpu as pltpu
from jax.sharding import PartitionSpec as P

HEADS = 16
norm_eps = 1e-06
bf16 = jnp.bfloat16
f32 = jnp.float32
MIB = 1024 * 1024


def layer_norm(values):
    center = values - jnp.mean(values, axis=-1, keepdims=True)
    inverse = lax.rsqrt(jnp.mean(center * center, axis=-1, keepdims=True) + norm_eps)
    return (center * inverse, inverse)


def norm_back(grad_in, normed, inverse):
    centered = grad_in - jnp.mean(grad_in, axis=-1, keepdims=True)
    return (centered - normed * jnp.mean(grad_in * normed, axis=-1, keepdims=True)) * inverse


def dot(left, right, left_dim, right_dim):
    return lax.dot_general(left, right, (((left_dim,), (right_dim,)), ((), ())), preferred_element_type=f32)


def times(left, right):
    return dot(left, right, 1, 0)


def times_rows(left, right):
    return dot(left, right, 1, 1)


def contract_rows(left, right):
    return dot(left, right, 0, 0)


def after(value, *others):
    return lax.optimization_barrier((value, *others))[0]


def summed(left, right):
    return (left.astype(f32) + right.astype(f32)).astype(bf16)


class Net:
    def __init__(self):
        self.dp = lax.axis_size("dp")
        self.mod = lax.axis_size("mod")
        self.bits = self.dp.bit_length() - 1
        self.dp_rank = lax.axis_index("dp")
        self.mod_rank = lax.axis_index("mod")
        self.core = self.dp_rank & 1
        self.chips = self.dp // 2 * self.mod
        self.lead = list(range(self.bits - 1, 2, -1))
        last = ["mod", 1, 2]
        self.turns = [last[n:] + last[:n] for n in range(3)]
        self.orders = [self.lead + turn for turn in self.turns]

    def swap(self, value, dim):
        if dim == "mod":
            return lax.ppermute(value, "mod", [(i, i ^ 1) for i in range(self.mod)])
        return lax.ppermute(value, "dp", [(i, i ^ (1 << dim)) for i in range(self.dp)])

    def ranks(self, order, chunks, core=0):
        masks = []
        for j in chunks:
            dp_mask, mod_mask = core, 0
            for step, dim in enumerate(order):
                if j >> step & 1:
                    if dim == "mod":
                        mod_mask ^= 1
                    else:
                        dp_mask ^= 1 << dim
            masks.append((dp_mask, mod_mask))
        masks = np.array(masks, np.int32)
        return self.dp_rank ^ masks[:, 0], self.mod_rank ^ masks[:, 1]

    def devices(self, order, chunks, core=0):
        dp, mod = self.ranks(order, chunks, core)
        return dp * self.mod + mod

    def local(self, order, chunks):
        dp, mod = self.ranks(order, chunks)
        return (dp >> 1) * self.mod + mod


class Gather:
    def __init__(self, net, shard):
        self.net, self.count = net, len(net.lead)
        self.third = shard.shape[1] // 3
        self.value, self.got, self.phase = shard, None, 0

    def start(self, *others):
        net, phase = self.net, self.phase
        if phase < self.count:
            self.value = after(self.value, *others) if others else self.value
            self.got = [net.swap(self.value, net.lead[phase])]
        else:
            if phase == self.count:
                kinds, _, width = self.value.shape
                whole = self.value.reshape(kinds, -1, 3, self.third, width)
                self.value = [whole[:, :, n].reshape(kinds, -1, width) for n in range(3)]
            if others:
                self.value = list(lax.optimization_barrier((*self.value, *others))[:3])
            step = phase - self.count
            self.got = [net.swap(self.value[n], net.turns[n][step]) for n in range(3)]
        self.phase += 1
        return self

    def finish(self):
        if self.phase <= self.count:
            self.value = jnp.concatenate([self.value, self.got[0]], axis=1)
        elif self.phase < self.count + 3:
            self.value = [jnp.concatenate(pair, axis=1) for pair in zip(self.value, self.got)]
        return self


any_spec = pl.BlockSpec(memory_space=pl.ANY)


def full(value):
    return pl.BlockSpec(value.shape, lambda *_: (0,) * len(value.shape))

tiny = pl.CostEstimate(flops=1024, bytes_accessed=1024, transcendentals=0)


def run_copies(copies):
    for copy in copies:
        copy.start()
    for copy in copies:
        copy.wait()


def assemble_kernel(rows, each, index_ref, *refs):
    pieces, out_ref, hold, sems, last = refs[:-4], *refs[-4:]
    copies = []
    for n, piece in enumerate(pieces):
        for j in range(each):
            at = pl.multiple_of(index_ref[n * each + j] * rows, rows)
            copies.append(
                pltpu.make_async_copy(
                    piece.at[0, pl.ds(j * rows, rows)], hold.at[pl.ds(at, rows)], sems.at[n * each + j]
                )
            )
    run_copies(copies)
    run_copies([pltpu.make_async_copy(hold, out_ref, last)])


def assemble(pieces, index, rows):
    each, width = pieces[0].shape[1] // rows, pieces[0].shape[2]
    total = len(pieces) * each
    return pl.pallas_call(
        functools.partial(assemble_kernel, rows, each),
        grid_spec=pltpu.PrefetchScalarGridSpec(
            num_scalar_prefetch=1,
            grid=(1,),
            in_specs=[any_spec] * len(pieces),
            out_specs=any_spec,
            scratch_shapes=[
                pltpu.VMEM((total * rows, width), bf16),
                pltpu.SemaphoreType.DMA((total,)),
                pltpu.SemaphoreType.DMA,
            ],
        ),
        out_shape=jax.ShapeDtypeStruct((total * rows, width), bf16),
        compiler_params=pltpu.CompilerParams(vmem_limit_bytes=10 * MIB),
        name="assemble",
    )(index, *pieces)


def added(left, right):
    return (left.astype(f32) + right.astype(f32)).astype(bf16)


def sums_call(kernel, grid, in_specs, out_specs, outs, *args, limit=24):
    return pl.pallas_call(
        kernel,
        grid=grid,
        in_specs=in_specs,
        out_specs=out_specs,
        out_shape=[pltpu.HBM(out, bf16) for out in outs],
        cost_estimate=tiny,
        compiler_params=pltpu.CompilerParams(vmem_limit_bytes=limit * MIB),
        name=kernel.__name__,
    )(*args)


def first_sums(own_low, own_high, got_low, got_high, also, keep, send):
    keep[...] = added(own_low[...], got_low[...])
    send[:2] = added(own_high[...], got_high[...])
    send[2:] = also[...]


def half_sums(own, got, keep, send):
    half = keep.shape[1]
    keep[...] = added(own[:, :half], got[:, :half])
    send[...] = added(own[:, half:], got[:, half:])


def block_sums(own, got, keep, send):
    keep[0] = added(own[0], got[0])
    send[0] = added(own[1], got[1])


def third_sums(*refs):
    outs = refs[6:]
    for n in range(3):
        total = added(refs[n][...], refs[3 + n][...])
        if len(outs) == 2:
            rows = total.shape[1] // 2
            outs[0][:, n * rows : (n + 1) * rows] = total[:, :rows]
            outs[1][:, n * rows : (n + 1) * rows] = total[:, rows:]
        else:
            outs[n][...] = total


def third_attn_sums(*refs):
    for n in range(3):
        half_sums(refs[n], refs[3 + n], refs[6 + 2 * n], refs[7 + 2 * n])


def fourth_sums(*refs):
    keep, send = refs[6:]
    rows = keep.shape[1] // 3
    for n in range(3):
        total = added(refs[n][0], refs[3 + n][0])
        keep[0, n * rows : (n + 1) * rows] = total[:rows]
        send[0, n * rows : (n + 1) * rows] = total[rows:]


class Scatter:
    def __init__(self, net, own, other):
        self.net = net
        self.own = list(own)
        self.got = [net.swap(other[n], net.turns[n][2]) for n in range(3)]
        self.aligned = len(net.lead) == 1 and own[0].shape[1] // 8 % 16 == 0

    def hold(self, n, *others):
        self.got[n] = after(self.got[n], *others)

    def join(self, n, pieces):
        _, rows, width = self.own[n].shape
        half = rows // 2
        step = half // 2
        also = 2 * ((n + 2) % 3)
        self.pieces = pieces.reshape(12, half, width)
        block = (2, step, width)
        low, high = pl.BlockSpec(block, lambda i: (0, i, 0)), pl.BlockSpec(block, lambda i: (0, i + 2, 0))
        self.own[n], send = sums_call(
            first_sums,
            (2,),
            [low, high, low, high, pl.BlockSpec(block, lambda i: (also + 1, i, 0))],
            [low, pl.BlockSpec((4, step, width), lambda i: (0, i, 0))],
            [(2, half, width), (4, half, width)],
            self.own[n],
            self.own[n],
            self.got[n],
            self.got[n],
            self.pieces,
            limit=60,
        )
        self.got[n] = self.net.swap(send, self.net.turns[n][1])
        return send

    def second(self, n):
        _, rows, width = self.own[n].shape
        outs = [(2, rows // 2, width)] * 2
        self.both = getattr(self, "both", [None] * 3)
        self.both[n] = self.got[n]
        self.own[n], send = sums_call(
            half_sums,
            (1,),
            [full(self.own[n]), pl.BlockSpec((2, rows, width), lambda i: (0, 0, 0))],
            [full(jax.ShapeDtypeStruct(out, bf16)) for out in outs],
            outs,
            self.own[n],
            self.got[n],
        )
        self.got[n] = self.net.swap(send, self.net.turns[n][0])
        return send

    def second_attn(self, others):
        self.also, self.also_got = [None] * 3, [None] * 3
        both = list(lax.optimization_barrier((*self.both, *others))[:3])
        for n in range(3):
            _, rows, width = both[n].shape
            piece = 2 * ((n + 2) % 3)
            outs = [(1, rows, width)] * 2
            self.also[n], send = sums_call(
                block_sums,
                (1,),
                [
                    pl.BlockSpec((2, rows, width), lambda i: (piece, 0, 0)),
                    pl.BlockSpec((2, rows, width), lambda i: (1, 0, 0)),
                ],
                [full(jax.ShapeDtypeStruct(out, bf16)) for out in outs],
                outs,
                self.pieces,
                both[n],
            )
            self.also_got[n] = self.net.swap(send, self.net.turns[n][0])

    def third(self):
        net = self.net
        _, rows, width = self.own[0].shape
        outs = [(2, rows // 2 * 3, width)] * 2 if self.aligned else [(2, rows, width)] * 3
        args = self.own + self.got
        results = sums_call(
            third_sums,
            (1,),
            [full(a) for a in args],
            [full(jax.ShapeDtypeStruct(out, bf16)) for out in outs],
            outs,
            *args,
        )
        if self.aligned:
            self.fc = results[0], net.swap(results[1], net.lead[0])
        else:
            self.fc = self.lead(self.together(results), len(net.lead) - 1)
        self.fc_sent = results[1]
        self.also_got = list(lax.optimization_barrier((*self.also_got, results[1]))[:3])

    def after_fc(self):
        *self.also_got, fc_got = lax.optimization_barrier((*self.also_got, self.fc[1]))
        self.fc = self.fc[0], fc_got

    def third_attn(self):
        net = self.net
        _, rows, width = self.also[0].shape
        args, outs = self.also + self.also_got, [(1, rows // 2, width)] * 6
        results = sums_call(
            third_attn_sums,
            (1,),
            [full(a) for a in args],
            [full(jax.ShapeDtypeStruct(out, bf16)) for out in outs],
            outs,
            *args,
        )
        self.also = results[0::2]
        self.also_got = [net.swap(results[2 * n + 1], net.turns[(n + 2) % 3][0]) for n in range(3)]

    def last(self):
        net = self.net
        order = (1, 2, 0)
        keep, got = [self.also[n] for n in order], [self.also_got[n] for n in order]
        if self.aligned:
            _, rows, width = keep[0].shape
            outs = [(1, rows // 2 * 3, width)] * 2
            own, send = sums_call(
                fourth_sums,
                (1,),
                [full(a) for a in keep + got],
                [full(jax.ShapeDtypeStruct(out, bf16)) for out in outs],
                outs,
                *keep,
                *got,
            )
            attn = own, net.swap(send, net.lead[0])
        else:
            attn = self.lead(self.together([summed(a, b) for a, b in zip(keep, got)]), len(net.lead) - 1)
        sums = []
        for own, got in (self.fc, attn):
            for step in range(len(net.lead) - 1, -1, -1):
                total = own.astype(f32) + got.astype(f32)
                if step:
                    own, got = self.lead(total.astype(bf16), step - 1)
            sums.append(total)
        return sums

    def together(self, parts):
        kinds, _, width = parts[0].shape
        count = 1 << len(self.net.lead)
        return jnp.concatenate([p.reshape(kinds, count, -1, width) for p in parts], axis=2).reshape(kinds, -1, width)

    def lead(self, whole, step):
        half = whole.shape[1] // 2
        return whole[:, :half], self.net.swap(whole[:, half:], self.net.lead[step])


def attn_in_kernel(grad_ref, weight_ref, own_ref, other_ref):
    total = dot(grad_ref[...], weight_ref[...], 0, 0)
    half = own_ref.shape[0]
    own_ref[...] = total[:half]
    other_ref[...] = total[half:]


def attn_in_grads(grad, weight):
    rows, tokens = grad.shape
    width = weight.shape[1]
    out = jax.ShapeDtypeStruct((tokens // 2, width), f32)
    return pl.pallas_call(
        attn_in_kernel,
        grid=(1,),
        in_specs=[full(grad), pl.BlockSpec((rows, width), lambda i: (0, 0))],
        out_specs=[full(out)] * 2,
        out_shape=[out, pltpu.HBM(out.shape, f32)],
        cost_estimate=tiny,
        compiler_params=pltpu.CompilerParams(vmem_limit_bytes=40 * MIB),
        name="attn_in_grads",
    )(grad, weight)


def weight_grad_kernel(rows, place_ref, grad_ref, x_ref, mine_ref, other_ref, out_ref, hold, sems):
    top, copies = grad_ref.shape[0], []
    step = top // 3
    for n in (3, 0, 1, 2):
        start = n * step
        stop = min(start + step, hold.shape[0])
        if n == 3:
            hold[start:] = summed(mine_ref[...], other_ref[...])
        else:
            hold[start:stop] = dot(grad_ref[start:stop], x_ref[...], 1, 0).astype(bf16)
        for unit in range(start // rows, stop // rows):
            at = pl.multiple_of(place_ref[unit] * rows, rows)
            copies.append(
                pltpu.make_async_copy(
                    hold.at[pl.ds(unit * rows, rows)], out_ref.at[pl.ds(at, rows)], sems.at[unit]
                )
            )
            copies[-1].start()
    for copy in copies:
        copy.wait()


def weight_grad(grad, x, mine, other, places, rows):
    total, width = grad.shape[0] + mine.shape[0], x.shape[1]
    return pl.pallas_call(
        functools.partial(weight_grad_kernel, rows),
        grid_spec=pltpu.PrefetchScalarGridSpec(
            num_scalar_prefetch=1,
            grid=(1,),
            in_specs=[full(a) for a in (grad, x, mine, other)],
            out_specs=any_spec,
            scratch_shapes=[pltpu.VMEM((total, width), bf16), pltpu.SemaphoreType.DMA((total // rows,))],
        ),
        out_shape=jax.ShapeDtypeStruct((total, width), bf16),
        cost_estimate=tiny,
        compiler_params=pltpu.CompilerParams(vmem_limit_bytes=60 * MIB),
        name="weight_grad",
    )(places, grad, x, mine, other)


def by_core(core_ref, group, whole):
    if group is None:
        return [whole]
    picked = []
    for c in range(2):
        rows = []
        for at in range(0, whole.shape[0], 2 * group):
            first, second = whole[at : at + group], whole[at + group : at + 2 * group]
            rows.append(jnp.where(core_ref[0] == c, first, second))
        picked.append(jnp.concatenate(rows, axis=0))
    return picked


def token_block(pick, mods, n):
    width = mods.shape[1] // 6
    return dot(pick[...], mods[:, n * width : (n + 1) * width], 1, 0)


def middle_kernel(group, core_ref, *refs):
    sums, met, mid, grad_out, pick, mods, bias, weight, context = refs[:9]
    result_ref, pair_ref, mid_ref, attn_ref, column_ref = refs[9:14]
    normed, inverse = layer_norm(mid[...])
    back, outer = sums[1] + met[1], grad_out[...].astype(f32)
    mlp_out = sums[0] + met[0] + bias[...]
    result_ref[...] = (mid[...] + token_block(pick, mods, 5) * mlp_out).astype(bf16)
    slot_sums(pick[...], (back, back * normed, outer * mlp_out), pair_ref)
    grad_mid = outer + norm_back(back * (1.0 + token_block(pick, mods, 4)), normed, inverse)
    mid_ref[...] = grad_mid
    grad_attn = (token_block(pick, mods, 2) * grad_mid).astype(bf16)
    attn_ref[...] = grad_attn
    column_ref[...] = jnp.sum(grad_attn.astype(f32), axis=0, keepdims=True)
    parts = by_core(core_ref, group, dot(weight[...], grad_attn, 0, 1))
    parts += by_core(core_ref, group, dot(grad_attn, context[...], 0, 1))
    for ref, value in zip(refs[14:], parts):
        ref[...] = value.astype(bf16)


def middle(core, group, *args):
    _, tokens, width = args[0].shape
    if group is None:
        sizes = [(width, tokens), (width, width)]
    else:
        sizes = [(width // 2, tokens)] * 2 + [(width // 2, width)] * 2
    slots = args[4].shape[1]
    outs = [((tokens, width), bf16), ((slots, 3 * width), bf16)]
    outs += [((tokens, width), f32), ((tokens, width), bf16), ((1, width), f32)]
    outs = [jax.ShapeDtypeStruct(*out) for out in outs + [(s, bf16) for s in sizes]]
    return pl.pallas_call(
        functools.partial(middle_kernel, group),
        grid=(1,),
        in_specs=[pl.BlockSpec(memory_space=pltpu.SMEM)] + [full(a) for a in args],
        out_specs=[full(a) for a in outs],
        out_shape=outs[:5] + [pltpu.HBM(a.shape, bf16) for a in outs[5:]],
        cost_estimate=tiny,
        compiler_params=pltpu.CompilerParams(vmem_limit_bytes=48 * MIB),
        name="middle",
    )(core.reshape(1), *args)


def slot_sums(pick, blocks, out_ref):
    for n, block in enumerate(blocks):
        high = block.astype(bf16)
        low = (block - high.astype(f32)).astype(bf16)
        total = dot(pick, high, 0, 0) + dot(pick, low, 0, 0)
        out_ref[:, n * block.shape[1] : (n + 1) * block.shape[1]] = total.astype(bf16)


def attn_end_kernel(*refs):
    back_a, back_b, resid, grad_mid, attn_out, pick, mods = refs[:7]
    tokens_ref, pair_ref = refs[7:]
    back = back_a[...] + back_b[...]
    normed, inverse = layer_norm(resid[...].astype(f32))
    slope = back * (1.0 + token_block(pick, mods, 1))
    tokens_ref[...] = grad_mid[...] + norm_back(slope, normed, inverse)
    slot_sums(pick[...], (back, back * normed, grad_mid[...] * attn_out[...]), pair_ref)


def end_call(kernel, dtype, slots, *args):
    tokens, width = args[0].shape
    outs = [jax.ShapeDtypeStruct((tokens, width), dtype), jax.ShapeDtypeStruct((slots, 3 * width), bf16)]
    return pl.pallas_call(
        kernel,
        grid=(1,),
        in_specs=[full(a) for a in args],
        out_specs=[full(a) for a in outs],
        out_shape=outs,
        cost_estimate=tiny,
        compiler_params=pltpu.CompilerParams(vmem_limit_bytes=32 * MIB),
        name=kernel.__name__,
    )(*args)


def rows_kernel(*refs):
    at = 0
    for ref in refs[:-1]:
        refs[-1][at : at + ref.shape[0]] = ref[...]
        at += ref.shape[0]


def stack_rows(*args):
    out = jax.ShapeDtypeStruct((sum(a.shape[0] for a in args), args[0].shape[1]), f32)
    return pl.pallas_call(
        rows_kernel,
        grid=(1,),
        in_specs=[full(a) for a in args],
        out_specs=full(out),
        out_shape=out,
        cost_estimate=tiny,
        compiler_params=pltpu.CompilerParams(vmem_limit_bytes=24 * MIB),
        name="stack_rows",
    )(*args)


def softmax_t(key, query, same, scale):
    scores = jnp.where(same, dot(key, query, 0, 0) * scale, -1e30)
    weights = jnp.exp(scores - jnp.max(scores, axis=0, keepdims=True))
    return weights * (1.0 / jnp.sum(weights, axis=0, keepdims=True))


def heads_of(block, dim, cols):
    wide = block[:, cols].astype(f32)
    return [wide[n * dim : (n + 1) * dim].astype(bf16) for n in range(wide.shape[0] // dim)]


def attn_forward(dim, scale, row_ref, col_ref, q_ref, k_ref, v_ref, out_ref):
    length = col_ref.shape[0]
    for s in range(row_ref.shape[0]):
        cols = slice(s * length, (s + 1) * length)
        same = row_ref[s : s + 1] == col_ref[:, s : s + 1]
        outs = []
        for q, k, v in zip(*[heads_of(r[0, 0], dim, cols) for r in (q_ref, k_ref, v_ref)]):
            probs = softmax_t(k, q, same, scale).astype(bf16)
            outs.append(dot(v, probs, 1, 0))
        out_ref[0, :, cols] = jnp.concatenate(outs, axis=0).astype(bf16)


def attn_backward(dim, scale, row_ref, col_ref, q_ref, k_ref, v_ref, *refs):
    length, out_ref = col_ref.shape[0], refs[-1]
    for s in range(row_ref.shape[0]):
        cols = slice(s * length, (s + 1) * length)
        same = row_ref[s : s + 1] == col_ref[:, s : s + 1]
        gq, gk, gv = [], [], []
        qs, ks, vs = [heads_of(r[0, 0], dim, cols) for r in (q_ref, k_ref, v_ref)]
        for q, k, v, g in zip(qs, ks, vs, heads_of(refs[s][0], dim, slice(0, length))):
            probs = softmax_t(k, q, same, scale)
            back = dot(v, g, 0, 0)
            back = probs * (back - jnp.sum(back * probs, axis=0, keepdims=True))
            back = back.astype(bf16)
            gq.append(dot(k, back, 1, 0) * scale)
            gk.append(dot(q, back, 1, 1) * scale)
            gv.append(dot(g, probs.astype(bf16), 1, 1))
        for n, parts in enumerate((gq, gk, gv)):
            out_ref[n, 0, :, cols] = jnp.concatenate(parts, axis=0).astype(bf16)


def attention(qkv, ids, dim, grad=None):
    _, groups, rows, tokens = qkv.shape
    scale = dim**-0.5
    ids_t = ids.T

    def one(n):
        return pl.BlockSpec((1, 1, rows, tokens), lambda i: (n, i, 0, 0))

    flat = pl.BlockSpec((1, rows, tokens), lambda i: (i, 0, 0))
    short = pl.BlockSpec((1, rows, ids.shape[1]), lambda i: (i, 0, 0))
    args = [ids, ids_t, qkv, qkv, qkv]
    specs = [pl.BlockSpec(a.shape, lambda i: (0, 0)) for a in (ids, ids_t)] + [one(0), one(1), one(2)]
    if grad is None:
        return pl.pallas_call(
            functools.partial(attn_forward, dim, scale),
            grid=(groups,),
            in_specs=specs,
            out_specs=flat,
            out_shape=jax.ShapeDtypeStruct((groups, rows, tokens), bf16),
            cost_estimate=tiny,
            compiler_params=pltpu.CompilerParams(vmem_limit_bytes=24 * MIB),
            name="attention",
        )(*args)
    return pl.pallas_call(
        functools.partial(attn_backward, dim, scale),
        grid=(groups,),
        in_specs=specs + [short] * len(grad),
        out_specs=pl.BlockSpec((3, 1, rows, tokens), lambda i: (0, i, 0, 0)),
        out_shape=jax.ShapeDtypeStruct(qkv.shape, bf16),
        cost_estimate=tiny,
        compiler_params=pltpu.CompilerParams(vmem_limit_bytes=24 * MIB),
        name="attention_back",
    )(*args, *grad)


def modulation_kernel(cond_ref, weight_ref, bias_ref, silu_ref, out_ref):
    cond = cond_ref[...].astype(f32)
    silu = (cond / (1.0 + jnp.exp(-cond))).astype(bf16)
    silu_ref[...] = silu
    out_ref[...] = (dot(silu, weight_ref[...], 1, 0) + bias_ref[...]).astype(bf16)


def modulate(cond, weight, bias):
    slots, width = cond.shape
    columns = weight.shape[1]
    tile = 384 if columns % 384 == 0 else columns
    return pl.pallas_call(
        modulation_kernel,
        grid=(columns // tile,),
        in_specs=[
            full(cond),
            pl.BlockSpec((width, tile), lambda i: (0, i)),
            pl.BlockSpec((1, tile), lambda i: (0, i)),
        ],
        out_specs=[full(cond), pl.BlockSpec((slots, tile), lambda i: (0, i))],
        out_shape=[
            jax.ShapeDtypeStruct((slots, width), bf16),
            jax.ShapeDtypeStruct((slots, columns), bf16),
        ],
        cost_estimate=tiny,
        compiler_params=pltpu.CompilerParams(vmem_limit_bytes=16 * MIB),
        name="modulate",
    )(cond, weight, bias)


def feed_forward_kernel(parts, *refs):
    own_ref, met_ref, b_ref = refs[:3]
    pieces = refs[3 : 3 + 2 * parts]
    act_ref, back_ref, column_ref, own_sums, other_sums = refs[3 + 2 * parts : 8 + 2 * parts]
    x, g, weights, acts, backs, total, ins, outs = refs[8 + 2 * parts :]
    half, units = own_ref.shape[1], pieces[0].shape[1]
    copy = pltpu.make_async_copy

    def load(n):
        slot, copies = n % 2, []
        for kind in range(2):
            for side in range(2):
                copies.append(
                    copy(
                        pieces[2 * n + side].at[kind],
                        weights.at[slot, kind, pl.ds(side * units, units)],
                        ins.at[4 + 4 * n + 2 * kind + side],
                    )
                )
        return copies

    low, high = pl.ds(0, half), pl.ds(half, half)
    inputs = [
        copy(own_ref.at[0], x.at[low], ins.at[0]),
        copy(met_ref.at[0], x.at[high], ins.at[1]),
        copy(own_ref.at[1], g.at[low], ins.at[2]),
        copy(met_ref.at[1], g.at[high], ins.at[3]),
    ]
    loads = [load(n) for n in range(parts)]
    for item in inputs[:2] + loads[0][:2] + inputs[2:] + loads[0][2:] + loads[1]:
        item.start()
    stores = []
    root = 0.7978845608028654
    for n in range(parts):
        slot = n % 2
        for item in (inputs[:2] if n == 0 else []) + loads[n][:2]:
            item.wait()
        for item in (inputs[2:] if n == 0 else []) + loads[n][2:]:
            item.wait()
        col = 0.0
        for k in range(2):
            tok = slice(k * half, (k + 1) * half)
            hidden = dot(x[tok], weights[slot, 0], 1, 1) + b_ref[n : n + 1]
            square = hidden * hidden
            tanh = jnp.tanh(root * hidden * (1.0 + 0.044715 * square))
            act = (0.5 * hidden * (1.0 + tanh)).astype(bf16)
            acts[n, tok] = act
            slope = 0.5 * (1.0 + tanh) + 0.5 * hidden * (1.0 - tanh * tanh) * (root * (1.0 + 0.134145 * square))
            back = (dot(g[tok], weights[slot, 1], 1, 1) * slope).astype(bf16)
            backs[n, tok] = back
            col = col + jnp.sum(back.astype(f32), axis=0, keepdims=True)
            for m, value in enumerate((dot(act, weights[slot, 1], 1, 0), dot(back, weights[slot, 0], 1, 0))):
                total[k, m] = value if n == 0 else total[k, m] + value
        column_ref[n : n + 1] = col
        stores.append(copy(acts.at[n], act_ref.at[n], outs.at[2 * n]))
        stores[-1].start()
        stores.append(copy(backs.at[n], back_ref.at[n], outs.at[2 * n + 1]))
        stores[-1].start()
        if n + 2 < parts:
            for item in loads[n + 2]:
                item.start()
    for k, ref in ((1, other_sums), (0, own_sums)):
        stores.append(copy(total.at[k], ref, outs.at[2 * parts + k]))
        stores[-1].start()
    for item in stores:
        item.wait()


def feed_forward(own_in, met_in, bias, pieces):
    _, tokens, width = own_in.shape
    parts, units = len(pieces) // 2, pieces[0].shape[1]
    column = jax.ShapeDtypeStruct((parts, 2 * units), f32)
    hidden = [jax.ShapeDtypeStruct((parts, 2 * tokens, 2 * units), bf16)] * 2
    sums = [jax.ShapeDtypeStruct((2, tokens, width), f32)] * 2
    dma = pltpu.SemaphoreType.DMA
    return pl.pallas_call(
        functools.partial(feed_forward_kernel, parts),
        grid=(1,),
        in_specs=[any_spec, any_spec, full(bias)] + [any_spec] * len(pieces),
        out_specs=[any_spec] * 2 + [full(column), any_spec, any_spec],
        out_shape=hidden + [column] + sums,
        scratch_shapes=[
            pltpu.VMEM((2 * tokens, width), bf16),
            pltpu.VMEM((2 * tokens, width), bf16),
            pltpu.VMEM((2, 2, 2 * units, width), bf16),
            pltpu.VMEM(hidden[0].shape, bf16),
            pltpu.VMEM(hidden[0].shape, bf16),
            pltpu.VMEM((2, 2, tokens, width), f32),
            dma((4 + 4 * parts,)),
            dma((2 * parts + 2,)),
        ],
        cost_estimate=tiny,
        compiler_params=pltpu.CompilerParams(vmem_limit_bytes=60 * MIB),
        name="feed_forward",
    )(own_in, met_in, bias, *pieces)


def fc_grad_kernel(parts, act_ref, back_ref, own_ref, met_ref, *refs):
    grads, (x, acts, backs, products, ins, outs) = refs[: 2 * parts], refs[2 * parts :]
    half, units = own_ref.shape[1], grads[0].shape[1]
    copy = pltpu.make_async_copy
    inputs = []
    for k, ref in enumerate((own_ref, met_ref)):
        for m in range(2):
            inputs.append(copy(ref.at[m], x.at[m, pl.ds(k * half, half)], ins.at[2 * k + m]))
    loads = [
        [
            copy(act_ref.at[n], acts.at[n], ins.at[4 + 2 * n]),
            copy(back_ref.at[n], backs.at[n], ins.at[5 + 2 * n]),
        ]
        for n in range(parts)
    ]
    for item in inputs + [item for pair in loads for item in pair]:
        item.start()
    stores = []
    for n in range(parts):
        for item in (inputs if n == 0 else []) + loads[n]:
            item.wait()
        if n >= 2:
            for item in stores[n - 2]:
                item.wait()
        stores.append([])
        for kind, left, right in ((0, backs, 0), (1, acts, 1)):
            products[n % 2, kind] = dot(left[n], x[right], 0, 0).astype(bf16)
            for side in range(2):
                stores[n].append(
                    copy(
                        products.at[n % 2, kind, pl.ds(side * units, units)],
                        grads[2 * n + side].at[kind],
                        outs.at[4 * n + 2 * kind + side],
                    )
                )
                stores[n][-1].start()
    for pair in stores[-2:]:
        for item in pair:
            item.wait()


def fc_grads_of(acts, backs, own_in, met_in):
    parts, tokens, columns = acts.shape
    width = own_in.shape[2]
    dma = pltpu.SemaphoreType.DMA
    return pl.pallas_call(
        functools.partial(fc_grad_kernel, parts),
        grid=(1,),
        in_specs=[any_spec] * 4,
        out_specs=[any_spec] * (2 * parts),
        out_shape=[pltpu.HBM((2, columns // 2, width), bf16)] * (2 * parts),
        scratch_shapes=[
            pltpu.VMEM((2, tokens, width), bf16),
            pltpu.VMEM(acts.shape, bf16),
            pltpu.VMEM(acts.shape, bf16),
            pltpu.VMEM((2, 2, columns, width), bf16),
            dma((4 + 2 * parts,)),
            dma((4 * parts,)),
        ],
        cost_estimate=tiny,
        compiler_params=pltpu.CompilerParams(vmem_limit_bytes=60 * MIB),
        name="fc_grads",
    )(acts, backs, own_in, met_in)


def on_device(
    tokens,
    cond,
    segment_ids,
    crop_slot,
    ada_weight,
    ada_bias,
    attn_weight,
    fc_in,
    fc_out,
    biases,
    out_grad,
):
    net = Net()
    tok_len, width = tokens.shape[1:]
    head_dim = width // HEADS
    mod_rank, core, chips = net.mod_rank, net.core, net.chips
    device_count = net.dp * net.mod
    crop_count = crop_slot.shape[1] // net.mod
    shard = attn_weight.shape[0]
    third = shard // 3
    chunks_of = [range(chips // 2), range(chips // 2, chips)]
    halves = [(n, side) for n in range(3) for side in range(2)]
    aligned = shard % (2 * head_dim) == 0 and third % 16 == 0 and width % (2 * net.mod * shard) == 0

    g_attn = Gather(net, attn_weight[None])
    g_fc = Gather(net, jnp.stack([fc_in, fc_out]))
    silu_cond, mod_own = modulate(cond, ada_weight, ada_bias.reshape(1, -1).astype(f32))
    slot_count, own_cols = cond.shape[0], width // net.dp
    to_dp = jnp.moveaxis(silu_cond.reshape(slot_count, net.dp, own_cols), 1, 0).reshape(net.dp, 1, -1)
    to_all = jnp.broadcast_to(to_dp, (net.dp, net.mod, slot_count * own_cols)).reshape(device_count, -1)
    sent = jnp.concatenate([jnp.broadcast_to(biases[None], (device_count, biases.shape[0])), to_all], axis=1)
    for n in range(g_attn.count):
        g_attn.start()
        g_attn.got = [after(g_attn.got[0], mod_own, sent)]
        g_attn.finish()
    g_attn.start()
    first = g_attn.value
    for n in range(g_fc.count):
        g_fc.start(*first)
        if n < g_fc.count - 1:
            g_fc.finish()
    g_attn.finish().start()
    g_attn.finish().start()
    third_phase = g_attn.value
    g_fc.got = [after(g_fc.got[0], *third_phase)]
    g_fc.finish().start(*g_attn.got)
    attn_pieces = [(g_attn.value, g_attn.got)[side][n] for n, side in halves]

    mod_other = net.swap(after(mod_own, *first), "mod")
    modulation = jnp.concatenate(
        [jnp.where(mod_rank == 0, mod_own, mod_other), jnp.where(mod_rank == 0, mod_other, mod_own)], axis=1
    )
    seg_ids = segment_ids[0]
    slots = lax.dynamic_slice_in_dim(crop_slot[0], mod_rank * crop_count, crop_count)
    crop_onehot = seg_ids[:, None] == jnp.arange(crop_count, dtype=jnp.int32)[None, :]
    token_slot = jnp.sum(jnp.where(crop_onehot, slots[None, :], 0), axis=1)
    slot_pick = token_slot[:, None] == jnp.arange(cond.shape[0], dtype=jnp.int32)[None, :]
    slot_pick = slot_pick.astype(bf16)
    modulation = after(modulation, *third_phase)
    mods = [modulation[:, n * width : (n + 1) * width] for n in range(6)]
    shift_a, scale_a, gate_a, shift_m, scale_m, gate_m = [times(slot_pick, block) for block in mods]

    sent = after(sent, *third_phase)
    met = lax.all_to_all(sent, ("dp", "mod"), split_axis=0, concat_axis=0, tiled=True)
    met = after(met, *g_fc.value)
    ada_order = list(range(net.bits - 1, -1, -1))
    dp_order = net.ranks(ada_order, range(net.dp))[0]
    dp_pick = (dp_order[:, None] == jnp.arange(net.dp)[None, :]).astype(bf16)
    cond_cols = times(dp_pick, met.reshape(net.dp, net.mod, -1)[:, 0, biases.shape[0] :]).astype(bf16)
    cond_cols = cond_cols.reshape(-1, own_cols)
    bias_all = met[:, : biases.shape[0]].reshape(-1, width)
    bias_query, bias_value, bias_proj, bias_out = [bias_all[n].astype(f32) for n in range(4)]
    bias_in = bias_all[4:].reshape(device_count, 3, third)
    picks = []
    for n, side in halves:
        devices = net.devices(net.orders[n], chunks_of[side])
        picks.append((devices[:, None] == jnp.arange(device_count)[None, :]).astype(bf16))
    picks = jnp.stack(picks).reshape(3, 2, chips // 2, device_count)
    bias_pieces = jnp.einsum("nsjd,dnr->nsjr", picks, bias_in, preferred_element_type=f32).reshape(3, -1)

    def join(own, other):
        own, other = [a.reshape(-1, 1, net.mod * shard, a.shape[-1]) for a in (own, other)]
        both = jnp.where(core == 0, jnp.concatenate([own, other], 1), jnp.concatenate([other, own], 1))
        return both.reshape(-1, both.shape[-1])

    def part(whole):
        whole = whole.reshape(-1, 2, net.mod * shard, whole.shape[-1])
        return [
            jnp.where(core == c, whole[:, 0], whole[:, 1]).reshape(-1, whole.shape[-1]) for c in range(2)
        ]

    resid = tokens[0].astype(f32)
    normed_a, _ = layer_norm(resid)
    attn_in = (normed_a * (1.0 + scale_a) + shift_a).astype(bf16)
    if aligned:
        index = jnp.concatenate([net.local(net.orders[n], chunks_of[side]) * 3 + n for n, side in halves])
        own_weight = assemble(attn_pieces, index, third)
        qkv_rows = own_weight.shape[0] * 3 // 4
        qkv_weight = own_weight[:qkv_rows]
        proj_own = own_weight[qkv_rows:]
        proj_weight = join(proj_own, net.swap(proj_own, 0))
        ids = jnp.stack([seg_ids, net.swap(seg_ids, 0)])
        attn_in = after(attn_in, *third_phase)
        attn_both = jnp.concatenate([attn_in, net.swap(attn_in, 0)], axis=0)
        own_query, own_value = part(bias_query[:, None])[0], part(bias_value[:, None])[0]
        qkv_bias = jnp.concatenate([own_query, jnp.zeros_like(own_query), own_value], axis=0)
        attn_both = after(attn_both, *g_fc.got)
        g_fc.finish().start()
        qkv = (times_rows(qkv_weight, attn_both) + qkv_bias).astype(bf16)
        qkv = qkv.reshape(3, -1, 2 * head_dim, 2 * tok_len)
        context_both = attention(qkv, ids, head_dim).reshape(-1, 2 * tok_len)
        context = join(context_both[:, :tok_len], net.swap(context_both[:, tok_len:], 0))
        attn_out = dot(context, proj_weight, 0, 1) + bias_proj
    else:
        arrays = attn_pieces + [net.swap(piece, 0) for piece in attn_pieces]
        places = jnp.concatenate(
            [net.devices(net.orders[n], chunks_of[side], c) * 3 + n for c in range(2) for n, side in halves]
        )
        spread = jnp.concatenate(arrays, axis=1)[0]

        def place(n, whole):
            block = lax.dynamic_slice_in_dim(spread, n * third, third)
            return lax.dynamic_update_slice_in_dim(whole, block, places[n] * third, 0)

        attn_w = lax.fori_loop(0, places.shape[0], place, jnp.zeros_like(spread))
        g_fc.finish().start()
        g_fc.finish().start()
        qkv_weight, proj_weight = attn_w[: 3 * width], attn_w[3 * width :]
        qkv_bias = jnp.concatenate([bias_query, jnp.zeros_like(bias_query), bias_value])
        qkv = (times_rows(qkv_weight, attn_in) + qkv_bias[:, None]).astype(bf16)
        qkv = qkv.reshape(3, -1, 2 * head_dim, tok_len)
        context = attention(qkv, seg_ids[None], head_dim).reshape(-1, tok_len)
        attn_out = dot(context, proj_weight, 0, 1) + bias_proj
    mid = resid + gate_a * attn_out
    normed_m, _ = layer_norm(mid)
    mlp_in = (normed_m * (1.0 + scale_m) + shift_m).astype(bf16)
    if aligned:
        mlp_in = after(mlp_in, *g_fc.got)
        g_fc.finish().start()
    grad_mlp = (gate_m * out_grad[0].astype(f32)).astype(bf16)

    mlp_own = jnp.stack([mlp_in, grad_mlp])
    mlp_met = after(net.swap(mlp_own, 0), cond_cols, bias_pieces)
    grad_bias_out = jnp.sum(grad_mlp.astype(f32), axis=0, keepdims=True)
    fc_pieces = [(g_fc.value, g_fc.got)[side][n] for n, side in halves]
    acts, backs, columns, own_sums, other_sums = feed_forward(mlp_own, mlp_met, bias_pieces, fc_pieces)
    sums_met = net.swap(other_sums, 0)
    fc_grads = fc_grads_of(acts, backs, mlp_own, mlp_met)
    sums_met = after(sums_met, *fc_grads)
    back_way = Scatter(net, fc_grads[0::2], fc_grads[1::2])

    result, pair_m, grad_mid, grad_attn, grad_bias_proj, *parts = middle(
        core,
        net.mod * shard if aligned else None,
        own_sums,
        sums_met,
        mid,
        out_grad[0],
        slot_pick,
        modulation,
        bias_out[None],
        proj_weight,
        context,
    )
    if aligned:
        mine, other, proj_mine, proj_other = parts
        context_grads = [a.reshape(-1, 2 * head_dim, tok_len) for a in (mine, net.swap(other, 0))]
        proj_met = net.swap(after(proj_other, *context_grads), 0)
        grad_qkv = attention(qkv, ids, head_dim, context_grads)
        grad_qkv = grad_qkv.reshape(-1, 2 * tok_len)
        back_own, back_other = attn_in_grads(grad_qkv, own_weight)
        back_met = net.swap(back_other, 0)
        grad_qkv = after(grad_qkv, back_own)
        places = jnp.sum(
            jnp.where(
                index[None, :] == jnp.arange(index.shape[0], dtype=index.dtype)[:, None],
                jnp.arange(index.shape[0], dtype=index.dtype)[None, :],
                0,
            ),
            axis=1,
        )
        pieces = weight_grad(grad_qkv, attn_both, proj_mine, proj_met, places, third)
        back_met = after(back_met, pieces)
    else:
        grad_context, grad_proj = parts
        grad_qkv = attention(
            qkv, seg_ids[None], head_dim, [grad_context.reshape(-1, 2 * head_dim, tok_len)]
        ).reshape(-1, tok_len)
        attn_grad = jnp.concatenate([times(grad_qkv, attn_in).astype(bf16), grad_proj], axis=0)

        def take(n, whole):
            block = lax.dynamic_slice_in_dim(attn_grad, places[n] * third, third)
            return lax.dynamic_update_slice_in_dim(whole, block, n * third, 0)

        grads = lax.fori_loop(0, places.shape[0], take, jnp.zeros_like(attn_grad))
        grads = jnp.split(grads[None], 12, axis=1)
        pieces = jnp.concatenate([summed(a, net.swap(b, 0)) for a, b in zip(grads[:6], grads[6:])], axis=1)
        back_own = contract_rows(grad_qkv, qkv_weight)
        back_met = jnp.zeros_like(back_own)
    grad_tokens, pair_a = end_call(
        attn_end_kernel, f32, slot_count, back_own, back_met, tokens[0], grad_mid, attn_out, slot_pick, modulation
    )
    pair_a, *back_way.got = lax.optimization_barrier((pair_a, *back_way.got))
    pair_own = jnp.where(mod_rank == 0, pair_a, pair_m)
    pair_send = jnp.where(mod_rank == 0, pair_m, pair_a)
    grad_mod = summed(pair_own, net.swap(pair_send, "mod"))
    for n in range(3):
        back_way.hold(n, grad_mod)
    mod_rows = jnp.concatenate([grad_mod, net.swap(grad_mod, ada_order[0])], axis=0)
    sends = [back_way.join(0, pieces), back_way.join(1, pieces)]
    back_way.hold(2, mod_rows)
    sends.append(back_way.join(2, pieces))
    grad_qkv, columns = lax.optimization_barrier((grad_qkv, columns, *sends))[:2]

    grad_silu = times_rows(grad_mod, ada_weight)
    silu_own = jnp.where(mod_rank == 0, grad_silu[:crop_count], grad_silu[crop_count:])
    silu_send = jnp.where(mod_rank == 0, grad_silu[crop_count:], grad_silu[:crop_count]).astype(bf16)

    column = jnp.sum(grad_qkv.astype(f32), axis=1, keepdims=True).reshape(3, -1, 1)
    if aligned:
        none = jnp.zeros_like(column[0])
        column = [join(column[0], none), None, join(column[2], none)]
    columns = columns.reshape(3, 2, chips // 2, third)
    grad_bias_in = jnp.einsum("nsjd,nsjr->dnr", picks.astype(f32), columns, precision=lax.Precision.HIGHEST)
    grad_bias = stack_rows(
        column[0].reshape(1, -1),
        column[2].reshape(1, -1),
        grad_bias_proj,
        grad_bias_out,
        grad_bias_in.reshape(-1, width),
    )
    bias_rows = lax.all_to_all(
        grad_bias.reshape(device_count, -1), ("dp", "mod"), split_axis=0, concat_axis=0, tiled=True
    )
    bias_sum = jnp.sum(bias_rows, axis=0)
    for n in range(3):
        back_way.hold(n, silu_send, bias_sum)
    sends = [back_way.second(n) for n in range(3)]
    back_way.second_attn(sends)
    back_way.third()
    silu_send, mod_rows = lax.optimization_barrier((silu_send, mod_rows, back_way.fc_sent))[:2]
    grad_silu = silu_own + net.swap(silu_send, "mod").astype(f32)
    own_cond = lax.dynamic_slice_in_dim(cond, mod_rank * crop_count, crop_count, 0).astype(f32)
    silu_back = jax.vjp(jax.nn.silu, own_cond)[1]
    grad_cond = silu_back(grad_silu)[0]
    for dim in ada_order[1:]:
        mod_rows = jnp.concatenate([mod_rows, net.swap(mod_rows, dim)], axis=0)
    ada_w_sum = contract_rows(cond_cols, mod_rows)
    ada_b_sum = jnp.sum(mod_rows.astype(f32), axis=0).reshape(ada_bias.shape[0], width)
    ada_b_sum = lax.dynamic_slice_in_dim(ada_b_sum, net.dp_rank * own_cols, own_cols, 1)
    back_way.after_fc()
    back_way.third_attn()
    fc_sum, attn_sum = back_way.last()

    return (
        result[None],
        grad_tokens[None],
        grad_cond,
        ada_w_sum,
        ada_b_sum,
        attn_sum[0],
        fc_sum[0],
        fc_sum[1],
        bias_sum,
    )


def solution(mesh):
    placed = (
        P(("dp", "mod"), None, None),
        P("dp", None),
        P(("dp", "mod"), None),
        P("dp", None),
        P(None, "mod"),
        P("mod", None),
        P(("dp", "mod"), None),
        P(("dp", "mod"), None),
        P(("dp", "mod"), None),
        P(("dp", "mod")),
        P(("dp", "mod"), None, None),
    )
    return jax.shard_map(
        on_device,
        mesh=mesh,
        in_specs=placed,
        out_specs=(
            P(("dp", "mod"), None, None),
            P(("dp", "mod"), None, None),
            P(("dp", "mod"), None),
            P("dp", "mod"),
            P("mod", "dp"),
            P(("dp", "mod"), None),
            P(("dp", "mod"), None),
            P(("dp", "mod"), None),
            P(("dp", "mod")),
        ),
        check_vma=False,
    )
```

```python
import functools

import jax
import jax.numpy as jnp
import numpy as np
from jax import lax
from jax.experimental import pallas as pl
from jax.experimental.pallas import tpu as pltpu
from jax.sharding import PartitionSpec as P

HEADS = 16
norm_eps = 1e-06
bf16 = jnp.bfloat16
f32 = jnp.float32
MIB = 1024 * 1024


def layer_norm(values):
    center = values - jnp.mean(values, axis=-1, keepdims=True)
    inverse = lax.rsqrt(jnp.mean(center * center, axis=-1, keepdims=True) + norm_eps)
    return (center * inverse, inverse)


def norm_back(grad_in, normed, inverse):
    centered = grad_in - jnp.mean(grad_in, axis=-1, keepdims=True)
    return (centered - normed * jnp.mean(grad_in * normed, axis=-1, keepdims=True)) * inverse


def dot(left, right, left_dim, right_dim):
    return lax.dot_general(left, right, (((left_dim,), (right_dim,)), ((), ())), preferred_element_type=f32)


def times(left, right):
    return dot(left, right, 1, 0)


def times_rows(left, right):
    return dot(left, right, 1, 1)


def contract_rows(left, right):
    return dot(left, right, 0, 0)


def after(value, *others):
    return lax.optimization_barrier((value, *others))[0]


def summed(left, right):
    return (left.astype(f32) + right.astype(f32)).astype(bf16)


class Net:
    def __init__(self):
        self.dp = lax.axis_size("dp")
        self.mod = lax.axis_size("mod")
        self.bits = self.dp.bit_length() - 1
        self.dp_rank = lax.axis_index("dp")
        self.mod_rank = lax.axis_index("mod")
        self.core = self.dp_rank & 1
        self.chips = self.dp // 2 * self.mod
        self.lead = list(range(self.bits - 1, 2, -1))
        last = ["mod", 1, 2]
        self.turns = [last[n:] + last[:n] for n in range(3)]
        self.orders = [self.lead + turn for turn in self.turns]

    def swap(self, value, dim):
        if dim == "mod":
            return lax.ppermute(value, "mod", [(i, i ^ 1) for i in range(self.mod)])
        return lax.ppermute(value, "dp", [(i, i ^ (1 << dim)) for i in range(self.dp)])

    def ranks(self, order, chunks, core=0):
        masks = []
        for j in chunks:
            dp_mask, mod_mask = core, 0
            for step, dim in enumerate(order):
                if j >> step & 1:
                    if dim == "mod":
                        mod_mask ^= 1
                    else:
                        dp_mask ^= 1 << dim
            masks.append((dp_mask, mod_mask))
        masks = np.array(masks, np.int32)
        return self.dp_rank ^ masks[:, 0], self.mod_rank ^ masks[:, 1]

    def devices(self, order, chunks, core=0):
        dp, mod = self.ranks(order, chunks, core)
        return dp * self.mod + mod

    def local(self, order, chunks):
        dp, mod = self.ranks(order, chunks)
        return (dp >> 1) * self.mod + mod


class Gather:
    def __init__(self, net, shard):
        self.net, self.count = net, len(net.lead)
        self.third = shard.shape[1] // 3
        self.value, self.got, self.phase = shard, None, 0

    def start(self, *others):
        net, phase = self.net, self.phase
        if phase < self.count:
            self.value = after(self.value, *others) if others else self.value
            self.got = [net.swap(self.value, net.lead[phase])]
        else:
            if phase == self.count:
                kinds, _, width = self.value.shape
                whole = self.value.reshape(kinds, -1, 3, self.third, width)
                self.value = [whole[:, :, n].reshape(kinds, -1, width) for n in range(3)]
            if others:
                self.value = list(lax.optimization_barrier((*self.value, *others))[:3])
            step = phase - self.count
            self.got = [net.swap(self.value[n], net.turns[n][step]) for n in range(3)]
        self.phase += 1
        return self

    def finish(self):
        if self.phase <= self.count:
            self.value = jnp.concatenate([self.value, self.got[0]], axis=1)
        elif self.phase < self.count + 3:
            self.value = [jnp.concatenate(pair, axis=1) for pair in zip(self.value, self.got)]
        return self


any_spec = pl.BlockSpec(memory_space=pl.ANY)


def full(value):
    return pl.BlockSpec(value.shape, lambda *_: (0,) * len(value.shape))

tiny = pl.CostEstimate(flops=1024, bytes_accessed=1024, transcendentals=0)


def run_copies(copies):
    for copy in copies:
        copy.start()
    for copy in copies:
        copy.wait()


def assemble_kernel(rows, each, index_ref, *refs):
    pieces, out_ref, hold, sems, last = refs[:-4], *refs[-4:]
    copies = []
    for n, piece in enumerate(pieces):
        for j in range(each):
            at = pl.multiple_of(index_ref[n * each + j] * rows, rows)
            copies.append(
                pltpu.make_async_copy(
                    piece.at[0, pl.ds(j * rows, rows)], hold.at[pl.ds(at, rows)], sems.at[n * each + j]
                )
            )
    run_copies(copies)
    run_copies([pltpu.make_async_copy(hold, out_ref, last)])


def assemble(pieces, index, rows):
    each, width = pieces[0].shape[1] // rows, pieces[0].shape[2]
    total = len(pieces) * each
    return pl.pallas_call(
        functools.partial(assemble_kernel, rows, each),
        grid_spec=pltpu.PrefetchScalarGridSpec(
            num_scalar_prefetch=1,
            grid=(1,),
            in_specs=[any_spec] * len(pieces),
            out_specs=any_spec,
            scratch_shapes=[
                pltpu.VMEM((total * rows, width), bf16),
                pltpu.SemaphoreType.DMA((total,)),
                pltpu.SemaphoreType.DMA,
            ],
        ),
        out_shape=jax.ShapeDtypeStruct((total * rows, width), bf16),
        compiler_params=pltpu.CompilerParams(vmem_limit_bytes=10 * MIB),
        name="assemble",
    )(index, *pieces)


def added(left, right):
    return (left.astype(f32) + right.astype(f32)).astype(bf16)


def sums_call(kernel, grid, in_specs, out_specs, outs, *args, limit=24):
    return pl.pallas_call(
        kernel,
        grid=grid,
        in_specs=in_specs,
        out_specs=out_specs,
        out_shape=[pltpu.HBM(out, bf16) for out in outs],
        cost_estimate=tiny,
        compiler_params=pltpu.CompilerParams(vmem_limit_bytes=limit * MIB),
        name=kernel.__name__,
    )(*args)


def first_sums(own_low, own_high, got_low, got_high, also, keep, send):
    keep[...] = added(own_low[...], got_low[...])
    send[:2] = added(own_high[...], got_high[...])
    send[2:] = also[...]


def half_sums(own, got, keep, send):
    half = keep.shape[1]
    keep[...] = added(own[:, :half], got[:, :half])
    send[...] = added(own[:, half:], got[:, half:])


def block_sums(own, got, keep, send):
    keep[0] = added(own[0], got[0])
    send[0] = added(own[1], got[1])


def third_sums(*refs):
    outs = refs[6:]
    for n in range(3):
        total = added(refs[n][...], refs[3 + n][...])
        if len(outs) == 2:
            rows = total.shape[1] // 2
            outs[0][:, n * rows : (n + 1) * rows] = total[:, :rows]
            outs[1][:, n * rows : (n + 1) * rows] = total[:, rows:]
        else:
            outs[n][...] = total


def third_attn_sums(*refs):
    for n in range(3):
        half_sums(refs[n], refs[3 + n], refs[6 + 2 * n], refs[7 + 2 * n])


def fourth_sums(*refs):
    keep, send = refs[6:]
    rows = keep.shape[1] // 3
    for n in range(3):
        total = added(refs[n][0], refs[3 + n][0])
        keep[0, n * rows : (n + 1) * rows] = total[:rows]
        send[0, n * rows : (n + 1) * rows] = total[rows:]


class Scatter:
    def __init__(self, net, own, other):
        self.net = net
        self.own = list(own)
        self.got = [net.swap(other[n], net.turns[n][2]) for n in range(3)]
        self.aligned = len(net.lead) == 1 and own[0].shape[1] // 8 % 16 == 0

    def hold(self, n, *others):
        self.got[n] = after(self.got[n], *others)

    def join(self, n, pieces):
        _, rows, width = self.own[n].shape
        half = rows // 2
        step = half // 2
        also = 2 * ((n + 2) % 3)
        self.pieces = pieces.reshape(12, half, width)
        block = (2, step, width)
        low, high = pl.BlockSpec(block, lambda i: (0, i, 0)), pl.BlockSpec(block, lambda i: (0, i + 2, 0))
        self.own[n], send = sums_call(
            first_sums,
            (2,),
            [low, high, low, high, pl.BlockSpec(block, lambda i: (also + 1, i, 0))],
            [low, pl.BlockSpec((4, step, width), lambda i: (0, i, 0))],
            [(2, half, width), (4, half, width)],
            self.own[n],
            self.own[n],
            self.got[n],
            self.got[n],
            self.pieces,
            limit=60,
        )
        self.got[n] = self.net.swap(send, self.net.turns[n][1])
        return send

    def second(self, n):
        _, rows, width = self.own[n].shape
        outs = [(2, rows // 2, width)] * 2
        self.both = getattr(self, "both", [None] * 3)
        self.both[n] = self.got[n]
        self.own[n], send = sums_call(
            half_sums,
            (1,),
            [full(self.own[n]), pl.BlockSpec((2, rows, width), lambda i: (0, 0, 0))],
            [full(jax.ShapeDtypeStruct(out, bf16)) for out in outs],
            outs,
            self.own[n],
            self.got[n],
        )
        self.got[n] = self.net.swap(send, self.net.turns[n][0])
        return send

    def second_attn(self, others):
        self.also, self.also_got = [None] * 3, [None] * 3
        both = list(lax.optimization_barrier((*self.both, *others))[:3])
        for n in range(3):
            _, rows, width = both[n].shape
            piece = 2 * ((n + 2) % 3)
            outs = [(1, rows, width)] * 2
            self.also[n], send = sums_call(
                block_sums,
                (1,),
                [
                    pl.BlockSpec((2, rows, width), lambda i: (piece, 0, 0)),
                    pl.BlockSpec((2, rows, width), lambda i: (1, 0, 0)),
                ],
                [full(jax.ShapeDtypeStruct(out, bf16)) for out in outs],
                outs,
                self.pieces,
                both[n],
            )
            self.also_got[n] = self.net.swap(send, self.net.turns[n][0])

    def third(self):
        net = self.net
        _, rows, width = self.own[0].shape
        outs = [(2, rows // 2 * 3, width)] * 2 if self.aligned else [(2, rows, width)] * 3
        args = self.own + self.got
        results = sums_call(
            third_sums,
            (1,),
            [full(a) for a in args],
            [full(jax.ShapeDtypeStruct(out, bf16)) for out in outs],
            outs,
            *args,
        )
        if self.aligned:
            self.fc = results[0], net.swap(results[1], net.lead[0])
        else:
            self.fc = self.lead(self.together(results), len(net.lead) - 1)
        self.fc_sent = results[1]
        self.also_got = list(lax.optimization_barrier((*self.also_got, results[1]))[:3])

    def after_fc(self):
        *self.also_got, fc_got = lax.optimization_barrier((*self.also_got, self.fc[1]))
        self.fc = self.fc[0], fc_got

    def third_attn(self):
        net = self.net
        _, rows, width = self.also[0].shape
        args, outs = self.also + self.also_got, [(1, rows // 2, width)] * 6
        results = sums_call(
            third_attn_sums,
            (1,),
            [full(a) for a in args],
            [full(jax.ShapeDtypeStruct(out, bf16)) for out in outs],
            outs,
            *args,
        )
        self.also = results[0::2]
        self.also_got = [net.swap(results[2 * n + 1], net.turns[(n + 2) % 3][0]) for n in range(3)]

    def last(self):
        net = self.net
        order = (1, 2, 0)
        keep, got = [self.also[n] for n in order], [self.also_got[n] for n in order]
        if self.aligned:
            _, rows, width = keep[0].shape
            outs = [(1, rows // 2 * 3, width)] * 2
            own, send = sums_call(
                fourth_sums,
                (1,),
                [full(a) for a in keep + got],
                [full(jax.ShapeDtypeStruct(out, bf16)) for out in outs],
                outs,
                *keep,
                *got,
            )
            attn = own, net.swap(send, net.lead[0])
        else:
            attn = self.lead(self.together([summed(a, b) for a, b in zip(keep, got)]), len(net.lead) - 1)
        sums = []
        for own, got in (self.fc, attn):
            for step in range(len(net.lead) - 1, -1, -1):
                total = own.astype(f32) + got.astype(f32)
                if step:
                    own, got = self.lead(total.astype(bf16), step - 1)
            sums.append(total)
        return sums

    def together(self, parts):
        kinds, _, width = parts[0].shape
        count = 1 << len(self.net.lead)
        return jnp.concatenate([p.reshape(kinds, count, -1, width) for p in parts], axis=2).reshape(kinds, -1, width)

    def lead(self, whole, step):
        half = whole.shape[1] // 2
        return whole[:, :half], self.net.swap(whole[:, half:], self.net.lead[step])


def attn_in_kernel(grad_ref, weight_ref, own_ref, other_ref):
    total = dot(grad_ref[...], weight_ref[...], 0, 0)
    half = own_ref.shape[0]
    own_ref[...] = total[:half]
    other_ref[...] = total[half:]


def attn_in_grads(grad, weight):
    rows, tokens = grad.shape
    width = weight.shape[1]
    out = jax.ShapeDtypeStruct((tokens // 2, width), f32)
    return pl.pallas_call(
        attn_in_kernel,
        grid=(1,),
        in_specs=[full(grad), pl.BlockSpec((rows, width), lambda i: (0, 0))],
        out_specs=[full(out)] * 2,
        out_shape=[out, pltpu.HBM(out.shape, f32)],
        cost_estimate=tiny,
        compiler_params=pltpu.CompilerParams(vmem_limit_bytes=40 * MIB),
        name="attn_in_grads",
    )(grad, weight)


def weight_grad_kernel(rows, place_ref, grad_ref, x_ref, mine_ref, other_ref, out_ref, hold, sems):
    top, copies = grad_ref.shape[0], []
    step = top // 3
    for n in (3, 0, 1, 2):
        start = n * step
        stop = min(start + step, hold.shape[0])
        if n == 3:
            hold[start:] = summed(mine_ref[...], other_ref[...])
        else:
            hold[start:stop] = dot(grad_ref[start:stop], x_ref[...], 1, 0).astype(bf16)
        for unit in range(start // rows, stop // rows):
            at = pl.multiple_of(place_ref[unit] * rows, rows)
            copies.append(
                pltpu.make_async_copy(
                    hold.at[pl.ds(unit * rows, rows)], out_ref.at[pl.ds(at, rows)], sems.at[unit]
                )
            )
            copies[-1].start()
    for copy in copies:
        copy.wait()


def weight_grad(grad, x, mine, other, places, rows):
    total, width = grad.shape[0] + mine.shape[0], x.shape[1]
    return pl.pallas_call(
        functools.partial(weight_grad_kernel, rows),
        grid_spec=pltpu.PrefetchScalarGridSpec(
            num_scalar_prefetch=1,
            grid=(1,),
            in_specs=[full(a) for a in (grad, x, mine, other)],
            out_specs=any_spec,
            scratch_shapes=[pltpu.VMEM((total, width), bf16), pltpu.SemaphoreType.DMA((total // rows,))],
        ),
        out_shape=jax.ShapeDtypeStruct((total, width), bf16),
        cost_estimate=tiny,
        compiler_params=pltpu.CompilerParams(vmem_limit_bytes=60 * MIB),
        name="weight_grad",
    )(places, grad, x, mine, other)


def by_core(core_ref, group, whole):
    if group is None:
        return [whole]
    picked = []
    for c in range(2):
        rows = []
        for at in range(0, whole.shape[0], 2 * group):
            first, second = whole[at : at + group], whole[at + group : at + 2 * group]
            rows.append(jnp.where(core_ref[0] == c, first, second))
        picked.append(jnp.concatenate(rows, axis=0))
    return picked


def token_block(pick, mods, n):
    width = mods.shape[1] // 6
    return dot(pick[...], mods[:, n * width : (n + 1) * width], 1, 0)


def middle_kernel(group, core_ref, *refs):
    sums, met, mid, grad_out, pick, mods, bias, weight, context = refs[:9]
    result_ref, pair_ref, mid_ref, attn_ref, column_ref = refs[9:14]
    normed, inverse = layer_norm(mid[...])
    back, outer = sums[1] + met[1], grad_out[...].astype(f32)
    mlp_out = sums[0] + met[0] + bias[...]
    result_ref[...] = (mid[...] + token_block(pick, mods, 5) * mlp_out).astype(bf16)
    slot_sums(pick[...], (back, back * normed, outer * mlp_out), pair_ref)
    grad_mid = outer + norm_back(back * (1.0 + token_block(pick, mods, 4)), normed, inverse)
    mid_ref[...] = grad_mid
    grad_attn = (token_block(pick, mods, 2) * grad_mid).astype(bf16)
    attn_ref[...] = grad_attn
    column_ref[...] = jnp.sum(grad_attn.astype(f32), axis=0, keepdims=True)
    parts = by_core(core_ref, group, dot(weight[...], grad_attn, 0, 1))
    parts += by_core(core_ref, group, dot(grad_attn, context[...], 0, 1))
    for ref, value in zip(refs[14:], parts):
        ref[...] = value.astype(bf16)


def middle(core, group, *args):
    _, tokens, width = args[0].shape
    if group is None:
        sizes = [(width, tokens), (width, width)]
    else:
        sizes = [(width // 2, tokens)] * 2 + [(width // 2, width)] * 2
    slots = args[4].shape[1]
    outs = [((tokens, width), bf16), ((slots, 3 * width), bf16)]
    outs += [((tokens, width), f32), ((tokens, width), bf16), ((1, width), f32)]
    outs = [jax.ShapeDtypeStruct(*out) for out in outs + [(s, bf16) for s in sizes]]
    return pl.pallas_call(
        functools.partial(middle_kernel, group),
        grid=(1,),
        in_specs=[pl.BlockSpec(memory_space=pltpu.SMEM)] + [full(a) for a in args],
        out_specs=[full(a) for a in outs],
        out_shape=outs[:5] + [pltpu.HBM(a.shape, bf16) for a in outs[5:]],
        cost_estimate=tiny,
        compiler_params=pltpu.CompilerParams(vmem_limit_bytes=48 * MIB),
        name="middle",
    )(core.reshape(1), *args)


def slot_sums(pick, blocks, out_ref):
    for n, block in enumerate(blocks):
        high = block.astype(bf16)
        low = (block - high.astype(f32)).astype(bf16)
        total = dot(pick, high, 0, 0) + dot(pick, low, 0, 0)
        out_ref[:, n * block.shape[1] : (n + 1) * block.shape[1]] = total.astype(bf16)


def attn_end_kernel(*refs):
    back_a, back_b, resid, grad_mid, attn_out, pick, mods = refs[:7]
    tokens_ref, pair_ref = refs[7:]
    back = back_a[...] + back_b[...]
    normed, inverse = layer_norm(resid[...].astype(f32))
    slope = back * (1.0 + token_block(pick, mods, 1))
    tokens_ref[...] = grad_mid[...] + norm_back(slope, normed, inverse)
    slot_sums(pick[...], (back, back * normed, grad_mid[...] * attn_out[...]), pair_ref)


def end_call(kernel, dtype, slots, *args):
    tokens, width = args[0].shape
    outs = [jax.ShapeDtypeStruct((tokens, width), dtype), jax.ShapeDtypeStruct((slots, 3 * width), bf16)]
    return pl.pallas_call(
        kernel,
        grid=(1,),
        in_specs=[full(a) for a in args],
        out_specs=[full(a) for a in outs],
        out_shape=outs,
        cost_estimate=tiny,
        compiler_params=pltpu.CompilerParams(vmem_limit_bytes=32 * MIB),
        name=kernel.__name__,
    )(*args)


def rows_kernel(*refs):
    at = 0
    for ref in refs[:-1]:
        refs[-1][at : at + ref.shape[0]] = ref[...]
        at += ref.shape[0]


def stack_rows(*args):
    out = jax.ShapeDtypeStruct((sum(a.shape[0] for a in args), args[0].shape[1]), f32)
    return pl.pallas_call(
        rows_kernel,
        grid=(1,),
        in_specs=[full(a) for a in args],
        out_specs=full(out),
        out_shape=out,
        cost_estimate=tiny,
        compiler_params=pltpu.CompilerParams(vmem_limit_bytes=24 * MIB),
        name="stack_rows",
    )(*args)


def softmax_t(key, query, same, scale):
    scores = jnp.where(same, dot(key, query, 0, 0) * scale, -1e30)
    weights = jnp.exp(scores - jnp.max(scores, axis=0, keepdims=True))
    return weights * (1.0 / jnp.sum(weights, axis=0, keepdims=True))


def heads_of(block, dim, cols):
    wide = block[:, cols].astype(f32)
    return [wide[n * dim : (n + 1) * dim].astype(bf16) for n in range(wide.shape[0] // dim)]


def attn_forward(dim, scale, row_ref, col_ref, q_ref, k_ref, v_ref, out_ref):
    length = col_ref.shape[0]
    for s in range(row_ref.shape[0]):
        cols = slice(s * length, (s + 1) * length)
        same = row_ref[s : s + 1] == col_ref[:, s : s + 1]
        outs = []
        for q, k, v in zip(*[heads_of(r[0, 0], dim, cols) for r in (q_ref, k_ref, v_ref)]):
            probs = softmax_t(k, q, same, scale).astype(bf16)
            outs.append(dot(v, probs, 1, 0))
        out_ref[0, :, cols] = jnp.concatenate(outs, axis=0).astype(bf16)


def attn_backward(dim, scale, row_ref, col_ref, q_ref, k_ref, v_ref, *refs):
    length, out_ref = col_ref.shape[0], refs[-1]
    for s in range(row_ref.shape[0]):
        cols = slice(s * length, (s + 1) * length)
        same = row_ref[s : s + 1] == col_ref[:, s : s + 1]
        gq, gk, gv = [], [], []
        qs, ks, vs = [heads_of(r[0, 0], dim, cols) for r in (q_ref, k_ref, v_ref)]
        for q, k, v, g in zip(qs, ks, vs, heads_of(refs[s][0], dim, slice(0, length))):
            probs = softmax_t(k, q, same, scale)
            back = dot(v, g, 0, 0)
            back = probs * (back - jnp.sum(back * probs, axis=0, keepdims=True))
            back = back.astype(bf16)
            gq.append(dot(k, back, 1, 0) * scale)
            gk.append(dot(q, back, 1, 1) * scale)
            gv.append(dot(g, probs.astype(bf16), 1, 1))
        for n, parts in enumerate((gq, gk, gv)):
            out_ref[n, 0, :, cols] = jnp.concatenate(parts, axis=0).astype(bf16)


def attention(qkv, ids, dim, grad=None):
    _, groups, rows, tokens = qkv.shape
    scale = dim**-0.5
    ids_t = ids.T

    def one(n):
        return pl.BlockSpec((1, 1, rows, tokens), lambda i: (n, i, 0, 0))

    flat = pl.BlockSpec((1, rows, tokens), lambda i: (i, 0, 0))
    short = pl.BlockSpec((1, rows, ids.shape[1]), lambda i: (i, 0, 0))
    args = [ids, ids_t, qkv, qkv, qkv]
    specs = [pl.BlockSpec(a.shape, lambda i: (0, 0)) for a in (ids, ids_t)] + [one(0), one(1), one(2)]
    if grad is None:
        return pl.pallas_call(
            functools.partial(attn_forward, dim, scale),
            grid=(groups,),
            in_specs=specs,
            out_specs=flat,
            out_shape=jax.ShapeDtypeStruct((groups, rows, tokens), bf16),
            cost_estimate=tiny,
            compiler_params=pltpu.CompilerParams(vmem_limit_bytes=24 * MIB),
            name="attention",
        )(*args)
    return pl.pallas_call(
        functools.partial(attn_backward, dim, scale),
        grid=(groups,),
        in_specs=specs + [short] * len(grad),
        out_specs=pl.BlockSpec((3, 1, rows, tokens), lambda i: (0, i, 0, 0)),
        out_shape=jax.ShapeDtypeStruct(qkv.shape, bf16),
        cost_estimate=tiny,
        compiler_params=pltpu.CompilerParams(vmem_limit_bytes=24 * MIB),
        name="attention_back",
    )(*args, *grad)


def modulation_kernel(cond_ref, weight_ref, bias_ref, silu_ref, out_ref):
    cond = cond_ref[...].astype(f32)
    silu = (cond / (1.0 + jnp.exp(-cond))).astype(bf16)
    silu_ref[...] = silu
    out_ref[...] = (dot(silu, weight_ref[...], 1, 0) + bias_ref[...]).astype(bf16)


def modulate(cond, weight, bias):
    slots, width = cond.shape
    columns = weight.shape[1]
    tile = 384 if columns % 384 == 0 else columns
    return pl.pallas_call(
        modulation_kernel,
        grid=(columns // tile,),
        in_specs=[
            full(cond),
            pl.BlockSpec((width, tile), lambda i: (0, i)),
            pl.BlockSpec((1, tile), lambda i: (0, i)),
        ],
        out_specs=[full(cond), pl.BlockSpec((slots, tile), lambda i: (0, i))],
        out_shape=[
            jax.ShapeDtypeStruct((slots, width), bf16),
            jax.ShapeDtypeStruct((slots, columns), bf16),
        ],
        cost_estimate=tiny,
        compiler_params=pltpu.CompilerParams(vmem_limit_bytes=16 * MIB),
        name="modulate",
    )(cond, weight, bias)


def feed_forward_kernel(parts, *refs):
    own_ref, met_ref, b_ref = refs[:3]
    pieces = refs[3 : 3 + 2 * parts]
    act_ref, back_ref, column_ref, own_sums, other_sums = refs[3 + 2 * parts : 8 + 2 * parts]
    x, g, weights, acts, backs, total, ins, outs = refs[8 + 2 * parts :]
    half, units = own_ref.shape[1], pieces[0].shape[1]
    copy = pltpu.make_async_copy

    def load(n):
        slot, copies = n % 2, []
        for kind in range(2):
            for side in range(2):
                copies.append(
                    copy(
                        pieces[2 * n + side].at[kind],
                        weights.at[slot, kind, pl.ds(side * units, units)],
                        ins.at[4 + 4 * n + 2 * kind + side],
                    )
                )
        return copies

    low, high = pl.ds(0, half), pl.ds(half, half)
    inputs = [
        copy(own_ref.at[0], x.at[low], ins.at[0]),
        copy(met_ref.at[0], x.at[high], ins.at[1]),
        copy(own_ref.at[1], g.at[low], ins.at[2]),
        copy(met_ref.at[1], g.at[high], ins.at[3]),
    ]
    loads = [load(n) for n in range(parts)]
    for item in inputs[:2] + loads[0][:2] + inputs[2:] + loads[0][2:] + loads[1]:
        item.start()
    stores = []
    root = 0.7978845608028654
    for n in range(parts):
        slot = n % 2
        for item in (inputs[:2] if n == 0 else []) + loads[n][:2]:
            item.wait()
        for item in (inputs[2:] if n == 0 else []) + loads[n][2:]:
            item.wait()
        col = 0.0
        for k in range(2):
            tok = slice(k * half, (k + 1) * half)
            hidden = dot(x[tok], weights[slot, 0], 1, 1) + b_ref[n : n + 1]
            square = hidden * hidden
            tanh = jnp.tanh(root * hidden * (1.0 + 0.044715 * square))
            act = (0.5 * hidden * (1.0 + tanh)).astype(bf16)
            acts[n, tok] = act
            slope = 0.5 * (1.0 + tanh) + 0.5 * hidden * (1.0 - tanh * tanh) * (root * (1.0 + 0.134145 * square))
            back = (dot(g[tok], weights[slot, 1], 1, 1) * slope).astype(bf16)
            backs[n, tok] = back
            col = col + jnp.sum(back.astype(f32), axis=0, keepdims=True)
            for m, value in enumerate((dot(act, weights[slot, 1], 1, 0), dot(back, weights[slot, 0], 1, 0))):
                total[k, m] = value if n == 0 else total[k, m] + value
        column_ref[n : n + 1] = col
        stores.append(copy(acts.at[n], act_ref.at[n], outs.at[2 * n]))
        stores[-1].start()
        stores.append(copy(backs.at[n], back_ref.at[n], outs.at[2 * n + 1]))
        stores[-1].start()
        if n + 2 < parts:
            for item in loads[n + 2]:
                item.start()
    for k, ref in ((1, other_sums), (0, own_sums)):
        stores.append(copy(total.at[k], ref, outs.at[2 * parts + k]))
        stores[-1].start()
    for item in stores:
        item.wait()


def feed_forward(own_in, met_in, bias, pieces):
    _, tokens, width = own_in.shape
    parts, units = len(pieces) // 2, pieces[0].shape[1]
    column = jax.ShapeDtypeStruct((parts, 2 * units), f32)
    hidden = [jax.ShapeDtypeStruct((parts, 2 * tokens, 2 * units), bf16)] * 2
    sums = [jax.ShapeDtypeStruct((2, tokens, width), f32)] * 2
    dma = pltpu.SemaphoreType.DMA
    return pl.pallas_call(
        functools.partial(feed_forward_kernel, parts),
        grid=(1,),
        in_specs=[any_spec, any_spec, full(bias)] + [any_spec] * len(pieces),
        out_specs=[any_spec] * 2 + [full(column), any_spec, any_spec],
        out_shape=hidden + [column] + sums,
        scratch_shapes=[
            pltpu.VMEM((2 * tokens, width), bf16),
            pltpu.VMEM((2 * tokens, width), bf16),
            pltpu.VMEM((2, 2, 2 * units, width), bf16),
            pltpu.VMEM(hidden[0].shape, bf16),
            pltpu.VMEM(hidden[0].shape, bf16),
            pltpu.VMEM((2, 2, tokens, width), f32),
            dma((4 + 4 * parts,)),
            dma((2 * parts + 2,)),
        ],
        cost_estimate=tiny,
        compiler_params=pltpu.CompilerParams(vmem_limit_bytes=60 * MIB),
        name="feed_forward",
    )(own_in, met_in, bias, *pieces)


def fc_grad_kernel(parts, act_ref, back_ref, own_ref, met_ref, *refs):
    grads, (x, acts, backs, products, ins, outs) = refs[: 2 * parts], refs[2 * parts :]
    half, units = own_ref.shape[1], grads[0].shape[1]
    copy = pltpu.make_async_copy
    inputs = []
    for k, ref in enumerate((own_ref, met_ref)):
        for m in range(2):
            inputs.append(copy(ref.at[m], x.at[m, pl.ds(k * half, half)], ins.at[2 * k + m]))
    loads = [
        [
            copy(act_ref.at[n], acts.at[n], ins.at[4 + 2 * n]),
            copy(back_ref.at[n], backs.at[n], ins.at[5 + 2 * n]),
        ]
        for n in range(parts)
    ]
    for item in inputs + [item for pair in loads for item in pair]:
        item.start()
    stores = []
    for n in range(parts):
        for item in (inputs if n == 0 else []) + loads[n]:
            item.wait()
        if n >= 2:
            for item in stores[n - 2]:
                item.wait()
        stores.append([])
        for kind, left, right in ((0, backs, 0), (1, acts, 1)):
            products[n % 2, kind] = dot(left[n], x[right], 0, 0).astype(bf16)
            for side in range(2):
                stores[n].append(
                    copy(
                        products.at[n % 2, kind, pl.ds(side * units, units)],
                        grads[2 * n + side].at[kind],
                        outs.at[4 * n + 2 * kind + side],
                    )
                )
                stores[n][-1].start()
    for pair in stores[-2:]:
        for item in pair:
            item.wait()


def fc_grads_of(acts, backs, own_in, met_in):
    parts, tokens, columns = acts.shape
    width = own_in.shape[2]
    dma = pltpu.SemaphoreType.DMA
    return pl.pallas_call(
        functools.partial(fc_grad_kernel, parts),
        grid=(1,),
        in_specs=[any_spec] * 4,
        out_specs=[any_spec] * (2 * parts),
        out_shape=[pltpu.HBM((2, columns // 2, width), bf16)] * (2 * parts),
        scratch_shapes=[
            pltpu.VMEM((2, tokens, width), bf16),
            pltpu.VMEM(acts.shape, bf16),
            pltpu.VMEM(acts.shape, bf16),
            pltpu.VMEM((2, 2, columns, width), bf16),
            dma((4 + 2 * parts,)),
            dma((4 * parts,)),
        ],
        cost_estimate=tiny,
        compiler_params=pltpu.CompilerParams(vmem_limit_bytes=60 * MIB),
        name="fc_grads",
    )(acts, backs, own_in, met_in)


def on_device(
    tokens,
    cond,
    segment_ids,
    crop_slot,
    ada_weight,
    ada_bias,
    attn_weight,
    fc_in,
    fc_out,
    biases,
    out_grad,
):
    net = Net()
    tok_len, width = tokens.shape[1:]
    head_dim = width // HEADS
    mod_rank, core, chips = net.mod_rank, net.core, net.chips
    device_count = net.dp * net.mod
    crop_count = crop_slot.shape[1] // net.mod
    shard = attn_weight.shape[0]
    third = shard // 3
    chunks_of = [range(chips // 2), range(chips // 2, chips)]
    halves = [(n, side) for n in range(3) for side in range(2)]
    aligned = shard % (2 * head_dim) == 0 and third % 16 == 0 and width % (2 * net.mod * shard) == 0

    g_attn = Gather(net, attn_weight[None])
    g_fc = Gather(net, jnp.stack([fc_in, fc_out]))
    silu_cond, mod_own = modulate(cond, ada_weight, ada_bias.reshape(1, -1).astype(f32))
    slot_count, own_cols = cond.shape[0], width // net.dp
    to_dp = jnp.moveaxis(silu_cond.reshape(slot_count, net.dp, own_cols), 1, 0).reshape(net.dp, 1, -1)
    to_all = jnp.broadcast_to(to_dp, (net.dp, net.mod, slot_count * own_cols)).reshape(device_count, -1)
    sent = jnp.concatenate([jnp.broadcast_to(biases[None], (device_count, biases.shape[0])), to_all], axis=1)
    for n in range(g_attn.count):
        g_attn.start()
        g_attn.got = [after(g_attn.got[0], mod_own, sent)]
        g_attn.finish()
    g_attn.start()
    first = g_attn.value
    for n in range(g_fc.count):
        g_fc.start(*first)
        if n < g_fc.count - 1:
            g_fc.finish()
    g_attn.finish().start()
    second = g_attn.value
    g_attn.finish().start()
    third_phase = g_attn.value
    g_fc.got = [after(g_fc.got[0], *third_phase)]
    g_fc.finish().start(*g_attn.got)
    attn_pieces = [(g_attn.value, g_attn.got)[side][n] for n, side in halves]

    mod_other = net.swap(after(mod_own, *first), "mod")
    modulation = jnp.concatenate(
        [jnp.where(mod_rank == 0, mod_own, mod_other), jnp.where(mod_rank == 0, mod_other, mod_own)], axis=1
    )
    seg_ids = segment_ids[0]
    slots = lax.dynamic_slice_in_dim(crop_slot[0], mod_rank * crop_count, crop_count)
    crop_onehot = seg_ids[:, None] == jnp.arange(crop_count, dtype=jnp.int32)[None, :]
    token_slot = jnp.sum(jnp.where(crop_onehot, slots[None, :], 0), axis=1)
    slot_pick = token_slot[:, None] == jnp.arange(cond.shape[0], dtype=jnp.int32)[None, :]
    slot_pick = slot_pick.astype(bf16)
    modulation = after(modulation, *third_phase)
    mods = [modulation[:, n * width : (n + 1) * width] for n in range(6)]
    shift_a, scale_a, gate_a, shift_m, scale_m, gate_m = [times(slot_pick, block) for block in mods]

    sent = after(sent, *second)
    met = lax.all_to_all(sent, ("dp", "mod"), split_axis=0, concat_axis=0, tiled=True)
    met = after(met, *third_phase)
    ada_order = list(range(net.bits - 1, -1, -1))
    dp_order = net.ranks(ada_order, range(net.dp))[0]
    dp_pick = (dp_order[:, None] == jnp.arange(net.dp)[None, :]).astype(bf16)
    cond_cols = times(dp_pick, met.reshape(net.dp, net.mod, -1)[:, 0, biases.shape[0] :]).astype(bf16)
    cond_cols = cond_cols.reshape(-1, own_cols)
    bias_all = met[:, : biases.shape[0]].reshape(-1, width)
    bias_query, bias_value, bias_proj, bias_out = [bias_all[n].astype(f32) for n in range(4)]
    bias_in = bias_all[4:].reshape(device_count, 3, third)
    picks = []
    for n, side in halves:
        devices = net.devices(net.orders[n], chunks_of[side])
        picks.append((devices[:, None] == jnp.arange(device_count)[None, :]).astype(bf16))
    picks = jnp.stack(picks).reshape(3, 2, chips // 2, device_count)
    bias_pieces = jnp.einsum("nsjd,dnr->nsjr", picks, bias_in, preferred_element_type=f32).reshape(3, -1)

    def join(own, other):
        own, other = [a.reshape(-1, 1, net.mod * shard, a.shape[-1]) for a in (own, other)]
        both = jnp.where(core == 0, jnp.concatenate([own, other], 1), jnp.concatenate([other, own], 1))
        return both.reshape(-1, both.shape[-1])

    def part(whole):
        whole = whole.reshape(-1, 2, net.mod * shard, whole.shape[-1])
        return [
            jnp.where(core == c, whole[:, 0], whole[:, 1]).reshape(-1, whole.shape[-1]) for c in range(2)
        ]

    resid = tokens[0].astype(f32)
    normed_a, _ = layer_norm(resid)
    attn_in = (normed_a * (1.0 + scale_a) + shift_a).astype(bf16)
    if aligned:
        index = jnp.concatenate([net.local(net.orders[n], chunks_of[side]) * 3 + n for n, side in halves])
        own_weight = assemble(attn_pieces, index, third)
        qkv_rows = own_weight.shape[0] * 3 // 4
        qkv_weight = own_weight[:qkv_rows]
        proj_own = own_weight[qkv_rows:]
        proj_weight = join(proj_own, net.swap(proj_own, 0))
        ids = jnp.stack([seg_ids, net.swap(seg_ids, 0)])
        attn_in = after(attn_in, *third_phase)
        attn_both = jnp.concatenate([attn_in, net.swap(attn_in, 0)], axis=0)
        own_query, own_value = part(bias_query[:, None])[0], part(bias_value[:, None])[0]
        qkv_bias = jnp.concatenate([own_query, jnp.zeros_like(own_query), own_value], axis=0)
        attn_both = after(attn_both, *g_fc.got)
        g_fc.finish().start()
        qkv = (times_rows(qkv_weight, attn_both) + qkv_bias).astype(bf16)
        qkv = qkv.reshape(3, -1, 2 * head_dim, 2 * tok_len)
        context_both = attention(qkv, ids, head_dim).reshape(-1, 2 * tok_len)
        context = join(context_both[:, :tok_len], net.swap(context_both[:, tok_len:], 0))
        attn_out = dot(context, proj_weight, 0, 1) + bias_proj
    else:
        arrays = attn_pieces + [net.swap(piece, 0) for piece in attn_pieces]
        places = jnp.concatenate(
            [net.devices(net.orders[n], chunks_of[side], c) * 3 + n for c in range(2) for n, side in halves]
        )
        spread = jnp.concatenate(arrays, axis=1)[0]

        def place(n, whole):
            block = lax.dynamic_slice_in_dim(spread, n * third, third)
            return lax.dynamic_update_slice_in_dim(whole, block, places[n] * third, 0)

        attn_w = lax.fori_loop(0, places.shape[0], place, jnp.zeros_like(spread))
        g_fc.finish().start()
        g_fc.finish().start()
        qkv_weight, proj_weight = attn_w[: 3 * width], attn_w[3 * width :]
        qkv_bias = jnp.concatenate([bias_query, jnp.zeros_like(bias_query), bias_value])
        qkv = (times_rows(qkv_weight, attn_in) + qkv_bias[:, None]).astype(bf16)
        qkv = qkv.reshape(3, -1, 2 * head_dim, tok_len)
        context = attention(qkv, seg_ids[None], head_dim).reshape(-1, tok_len)
        attn_out = dot(context, proj_weight, 0, 1) + bias_proj
    mid = resid + gate_a * attn_out
    normed_m, _ = layer_norm(mid)
    mlp_in = (normed_m * (1.0 + scale_m) + shift_m).astype(bf16)
    if aligned:
        mlp_in = after(mlp_in, *g_fc.got)
        g_fc.finish().start()
    grad_mlp = (gate_m * out_grad[0].astype(f32)).astype(bf16)

    mlp_own = jnp.stack([mlp_in, grad_mlp])
    mlp_met = after(net.swap(mlp_own, 0), cond_cols, bias_pieces)
    grad_bias_out = jnp.sum(grad_mlp.astype(f32), axis=0, keepdims=True)
    fc_pieces = [(g_fc.value, g_fc.got)[side][n] for n, side in halves]
    acts, backs, columns, own_sums, other_sums = feed_forward(mlp_own, mlp_met, bias_pieces, fc_pieces)
    sums_met = net.swap(other_sums, 0)
    fc_grads = fc_grads_of(acts, backs, mlp_own, mlp_met)
    sums_met = after(sums_met, *fc_grads)
    back_way = Scatter(net, fc_grads[0::2], fc_grads[1::2])

    result, pair_m, grad_mid, grad_attn, grad_bias_proj, *parts = middle(
        core,
        net.mod * shard if aligned else None,
        own_sums,
        sums_met,
        mid,
        out_grad[0],
        slot_pick,
        modulation,
        bias_out[None],
        proj_weight,
        context,
    )
    if aligned:
        mine, other, proj_mine, proj_other = parts
        context_grads = [a.reshape(-1, 2 * head_dim, tok_len) for a in (mine, net.swap(other, 0))]
        proj_met = net.swap(after(proj_other, *context_grads), 0)
        grad_qkv = attention(qkv, ids, head_dim, context_grads)
        grad_qkv = grad_qkv.reshape(-1, 2 * tok_len)
        back_own, back_other = attn_in_grads(grad_qkv, own_weight)
        back_met = net.swap(back_other, 0)
        grad_qkv = after(grad_qkv, back_own)
        places = jnp.sum(
            jnp.where(
                index[None, :] == jnp.arange(index.shape[0], dtype=index.dtype)[:, None],
                jnp.arange(index.shape[0], dtype=index.dtype)[None, :],
                0,
            ),
            axis=1,
        )
        pieces = weight_grad(grad_qkv, attn_both, proj_mine, proj_met, places, third)
        back_met = after(back_met, pieces)
    else:
        grad_context, grad_proj = parts
        grad_qkv = attention(
            qkv, seg_ids[None], head_dim, [grad_context.reshape(-1, 2 * head_dim, tok_len)]
        ).reshape(-1, tok_len)
        attn_grad = jnp.concatenate([times(grad_qkv, attn_in).astype(bf16), grad_proj], axis=0)

        def take(n, whole):
            block = lax.dynamic_slice_in_dim(attn_grad, places[n] * third, third)
            return lax.dynamic_update_slice_in_dim(whole, block, n * third, 0)

        grads = lax.fori_loop(0, places.shape[0], take, jnp.zeros_like(attn_grad))
        grads = jnp.split(grads[None], 12, axis=1)
        pieces = jnp.concatenate([summed(a, net.swap(b, 0)) for a, b in zip(grads[:6], grads[6:])], axis=1)
        back_own = contract_rows(grad_qkv, qkv_weight)
        back_met = jnp.zeros_like(back_own)
    grad_tokens, pair_a = end_call(
        attn_end_kernel, f32, slot_count, back_own, back_met, tokens[0], grad_mid, attn_out, slot_pick, modulation
    )
    pair_a, *back_way.got = lax.optimization_barrier((pair_a, *back_way.got))
    pair_own = jnp.where(mod_rank == 0, pair_a, pair_m)
    pair_send = jnp.where(mod_rank == 0, pair_m, pair_a)
    grad_mod = summed(pair_own, net.swap(pair_send, "mod"))
    for n in range(3):
        back_way.hold(n, grad_mod)
    mod_rows = jnp.concatenate([grad_mod, net.swap(grad_mod, ada_order[0])], axis=0)
    sends = [back_way.join(0, pieces), back_way.join(1, pieces)]
    back_way.hold(2, mod_rows)
    sends.append(back_way.join(2, pieces))
    grad_qkv, columns = lax.optimization_barrier((grad_qkv, columns, *sends))[:2]

    grad_silu = times_rows(grad_mod, ada_weight)
    silu_own = jnp.where(mod_rank == 0, grad_silu[:crop_count], grad_silu[crop_count:])
    silu_send = jnp.where(mod_rank == 0, grad_silu[crop_count:], grad_silu[:crop_count]).astype(bf16)

    column = jnp.sum(grad_qkv.astype(f32), axis=1, keepdims=True).reshape(3, -1, 1)
    if aligned:
        none = jnp.zeros_like(column[0])
        column = [join(column[0], none), None, join(column[2], none)]
    columns = columns.reshape(3, 2, chips // 2, third)
    grad_bias_in = jnp.einsum("nsjd,nsjr->dnr", picks.astype(f32), columns, precision=lax.Precision.HIGHEST)
    grad_bias = stack_rows(
        column[0].reshape(1, -1),
        column[2].reshape(1, -1),
        grad_bias_proj,
        grad_bias_out,
        grad_bias_in.reshape(-1, width),
    )
    bias_rows = lax.all_to_all(
        grad_bias.reshape(device_count, -1), ("dp", "mod"), split_axis=0, concat_axis=0, tiled=True
    )
    bias_sum = jnp.sum(bias_rows, axis=0)
    for n in range(3):
        back_way.hold(n, silu_send, bias_sum)
    sends = [back_way.second(n) for n in range(3)]
    back_way.second_attn(sends)
    back_way.third()
    silu_send, mod_rows = lax.optimization_barrier((silu_send, mod_rows, back_way.fc_sent))[:2]
    grad_silu = silu_own + net.swap(silu_send, "mod").astype(f32)
    own_cond = lax.dynamic_slice_in_dim(cond, mod_rank * crop_count, crop_count, 0).astype(f32)
    silu_back = jax.vjp(jax.nn.silu, own_cond)[1]
    grad_cond = silu_back(grad_silu)[0]
    for dim in ada_order[1:]:
        mod_rows = jnp.concatenate([mod_rows, net.swap(mod_rows, dim)], axis=0)
    ada_w_sum = contract_rows(cond_cols, mod_rows)
    ada_b_sum = jnp.sum(mod_rows.astype(f32), axis=0).reshape(ada_bias.shape[0], width)
    ada_b_sum = lax.dynamic_slice_in_dim(ada_b_sum, net.dp_rank * own_cols, own_cols, 1)
    back_way.after_fc()
    back_way.third_attn()
    fc_sum, attn_sum = back_way.last()

    return (
        result[None],
        grad_tokens[None],
        grad_cond,
        ada_w_sum,
        ada_b_sum,
        attn_sum[0],
        fc_sum[0],
        fc_sum[1],
        bias_sum,
    )


def solution(mesh):
    placed = (
        P(("dp", "mod"), None, None),
        P("dp", None),
        P(("dp", "mod"), None),
        P("dp", None),
        P(None, "mod"),
        P("mod", None),
        P(("dp", "mod"), None),
        P(("dp", "mod"), None),
        P(("dp", "mod"), None),
        P(("dp", "mod")),
        P(("dp", "mod"), None, None),
    )
    return jax.shard_map(
        on_device,
        mesh=mesh,
        in_specs=placed,
        out_specs=(
            P(("dp", "mod"), None, None),
            P(("dp", "mod"), None, None),
            P(("dp", "mod"), None),
            P("dp", "mod"),
            P("mod", "dp"),
            P(("dp", "mod"), None),
            P(("dp", "mod"), None),
            P(("dp", "mod"), None),
            P(("dp", "mod")),
        ),
        check_vma=False,
    )
```

```python
import functools

import jax
import jax.numpy as jnp
import numpy as np
from jax import lax
from jax.experimental import pallas as pl
from jax.experimental.pallas import tpu as pltpu
from jax.sharding import PartitionSpec as P

HEADS = 16
norm_eps = 1e-06
bf16 = jnp.bfloat16
f32 = jnp.float32
MIB = 1024 * 1024


def layer_norm(values):
    center = values - jnp.mean(values, axis=-1, keepdims=True)
    inverse = lax.rsqrt(jnp.mean(center * center, axis=-1, keepdims=True) + norm_eps)
    return (center * inverse, inverse)


def norm_back(grad_in, normed, inverse):
    centered = grad_in - jnp.mean(grad_in, axis=-1, keepdims=True)
    return (centered - normed * jnp.mean(grad_in * normed, axis=-1, keepdims=True)) * inverse


def dot(left, right, left_dim, right_dim):
    return lax.dot_general(left, right, (((left_dim,), (right_dim,)), ((), ())), preferred_element_type=f32)


def times(left, right):
    return dot(left, right, 1, 0)


def times_rows(left, right):
    return dot(left, right, 1, 1)


def contract_rows(left, right):
    return dot(left, right, 0, 0)


def after(value, *others):
    return lax.optimization_barrier((value, *others))[0]


def summed(left, right):
    return (left.astype(f32) + right.astype(f32)).astype(bf16)


class Net:
    def __init__(self):
        self.dp = lax.axis_size("dp")
        self.mod = lax.axis_size("mod")
        self.bits = self.dp.bit_length() - 1
        self.dp_rank = lax.axis_index("dp")
        self.mod_rank = lax.axis_index("mod")
        self.core = self.dp_rank & 1
        self.chips = self.dp // 2 * self.mod
        self.lead = list(range(self.bits - 1, 2, -1))
        last = ["mod", 1, 2]
        self.turns = [last[n:] + last[:n] for n in range(3)]
        self.orders = [self.lead + turn for turn in self.turns]

    def swap(self, value, dim):
        if dim == "mod":
            return lax.ppermute(value, "mod", [(i, i ^ 1) for i in range(self.mod)])
        return lax.ppermute(value, "dp", [(i, i ^ (1 << dim)) for i in range(self.dp)])

    def ranks(self, order, chunks, core=0):
        masks = []
        for j in chunks:
            dp_mask, mod_mask = core, 0
            for step, dim in enumerate(order):
                if j >> step & 1:
                    if dim == "mod":
                        mod_mask ^= 1
                    else:
                        dp_mask ^= 1 << dim
            masks.append((dp_mask, mod_mask))
        masks = np.array(masks, np.int32)
        return self.dp_rank ^ masks[:, 0], self.mod_rank ^ masks[:, 1]

    def devices(self, order, chunks, core=0):
        dp, mod = self.ranks(order, chunks, core)
        return dp * self.mod + mod

    def local(self, order, chunks):
        dp, mod = self.ranks(order, chunks)
        return (dp >> 1) * self.mod + mod


class Gather:
    def __init__(self, net, shard):
        self.net, self.count = net, len(net.lead)
        self.third = shard.shape[1] // 3
        self.value, self.got, self.phase = shard, None, 0

    def start(self, *others):
        net, phase = self.net, self.phase
        if phase < self.count:
            self.value = after(self.value, *others) if others else self.value
            self.got = [net.swap(self.value, net.lead[phase])]
        else:
            if phase == self.count:
                kinds, _, width = self.value.shape
                whole = self.value.reshape(kinds, -1, 3, self.third, width)
                self.value = [whole[:, :, n].reshape(kinds, -1, width) for n in range(3)]
            if others:
                self.value = list(lax.optimization_barrier((*self.value, *others))[:3])
            step = phase - self.count
            self.got = [net.swap(self.value[n], net.turns[n][step]) for n in range(3)]
        self.phase += 1
        return self

    def finish(self):
        if self.phase <= self.count:
            self.value = jnp.concatenate([self.value, self.got[0]], axis=1)
        elif self.phase < self.count + 3:
            self.value = [jnp.concatenate(pair, axis=1) for pair in zip(self.value, self.got)]
        return self


any_spec = pl.BlockSpec(memory_space=pl.ANY)


def full(value):
    return pl.BlockSpec(value.shape, lambda *_: (0,) * len(value.shape))

tiny = pl.CostEstimate(flops=1024, bytes_accessed=1024, transcendentals=0)


def run_copies(copies):
    for copy in copies:
        copy.start()
    for copy in copies:
        copy.wait()


def assemble_kernel(rows, each, index_ref, *refs):
    pieces, out_ref, hold, sems, last = refs[:-4], *refs[-4:]
    copies = []
    for n, piece in enumerate(pieces):
        for j in range(each):
            at = pl.multiple_of(index_ref[n * each + j] * rows, rows)
            copies.append(
                pltpu.make_async_copy(
                    piece.at[0, pl.ds(j * rows, rows)], hold.at[pl.ds(at, rows)], sems.at[n * each + j]
                )
            )
    run_copies(copies)
    run_copies([pltpu.make_async_copy(hold, out_ref, last)])


def assemble(pieces, index, rows):
    each, width = pieces[0].shape[1] // rows, pieces[0].shape[2]
    total = len(pieces) * each
    return pl.pallas_call(
        functools.partial(assemble_kernel, rows, each),
        grid_spec=pltpu.PrefetchScalarGridSpec(
            num_scalar_prefetch=1,
            grid=(1,),
            in_specs=[any_spec] * len(pieces),
            out_specs=any_spec,
            scratch_shapes=[
                pltpu.VMEM((total * rows, width), bf16),
                pltpu.SemaphoreType.DMA((total,)),
                pltpu.SemaphoreType.DMA,
            ],
        ),
        out_shape=jax.ShapeDtypeStruct((total * rows, width), bf16),
        compiler_params=pltpu.CompilerParams(vmem_limit_bytes=10 * MIB),
        name="assemble",
    )(index, *pieces)


def added(left, right):
    return (left.astype(f32) + right.astype(f32)).astype(bf16)


def sums_call(kernel, grid, in_specs, out_specs, outs, *args, limit=24):
    return pl.pallas_call(
        kernel,
        grid=grid,
        in_specs=in_specs,
        out_specs=out_specs,
        out_shape=[pltpu.HBM(out, bf16) for out in outs],
        cost_estimate=tiny,
        compiler_params=pltpu.CompilerParams(vmem_limit_bytes=limit * MIB),
        name=kernel.__name__,
    )(*args)


def first_sums(own_low, own_high, got_low, got_high, also, keep, send):
    keep[...] = added(own_low[...], got_low[...])
    send[:2] = added(own_high[...], got_high[...])
    send[2:] = also[...]


def half_sums(own, got, keep, send):
    half = keep.shape[1]
    keep[...] = added(own[:, :half], got[:, :half])
    send[...] = added(own[:, half:], got[:, half:])


def block_sums(own, got, keep, send):
    keep[0] = added(own[0], got[0])
    send[0] = added(own[1], got[1])


def third_sums(*refs):
    outs = refs[6:]
    for n in range(3):
        total = added(refs[n][...], refs[3 + n][...])
        if len(outs) == 2:
            rows = total.shape[1] // 2
            outs[0][:, n * rows : (n + 1) * rows] = total[:, :rows]
            outs[1][:, n * rows : (n + 1) * rows] = total[:, rows:]
        else:
            outs[n][...] = total


def third_attn_sums(*refs):
    for n in range(3):
        half_sums(refs[n], refs[3 + n], refs[6 + 2 * n], refs[7 + 2 * n])


def fourth_sums(*refs):
    keep, send = refs[6:]
    rows = keep.shape[1] // 3
    for n in range(3):
        total = added(refs[n][0], refs[3 + n][0])
        keep[0, n * rows : (n + 1) * rows] = total[:rows]
        send[0, n * rows : (n + 1) * rows] = total[rows:]


class Scatter:
    def __init__(self, net, own, other):
        self.net = net
        self.own = list(own)
        self.got = [net.swap(other[n], net.turns[n][2]) for n in range(3)]
        self.aligned = len(net.lead) == 1 and own[0].shape[1] // 8 % 16 == 0

    def hold(self, n, *others):
        self.got[n] = after(self.got[n], *others)

    def join(self, n, pieces):
        _, rows, width = self.own[n].shape
        half = rows // 2
        step = half // 2
        also = 2 * ((n + 2) % 3)
        self.pieces = pieces.reshape(12, half, width)
        block = (2, step, width)
        low, high = pl.BlockSpec(block, lambda i: (0, i, 0)), pl.BlockSpec(block, lambda i: (0, i + 2, 0))
        self.own[n], send = sums_call(
            first_sums,
            (2,),
            [low, high, low, high, pl.BlockSpec(block, lambda i: (also + 1, i, 0))],
            [low, pl.BlockSpec((4, step, width), lambda i: (0, i, 0))],
            [(2, half, width), (4, half, width)],
            self.own[n],
            self.own[n],
            self.got[n],
            self.got[n],
            self.pieces,
            limit=60,
        )
        self.got[n] = self.net.swap(send, self.net.turns[n][1])
        return send

    def second(self, n):
        _, rows, width = self.own[n].shape
        outs = [(2, rows // 2, width)] * 2
        self.both = getattr(self, "both", [None] * 3)
        self.both[n] = self.got[n]
        self.own[n], send = sums_call(
            half_sums,
            (1,),
            [full(self.own[n]), pl.BlockSpec((2, rows, width), lambda i: (0, 0, 0))],
            [full(jax.ShapeDtypeStruct(out, bf16)) for out in outs],
            outs,
            self.own[n],
            self.got[n],
        )
        self.got[n] = self.net.swap(send, self.net.turns[n][0])
        return send

    def second_attn(self, others):
        self.also, self.also_got = [None] * 3, [None] * 3
        both = list(lax.optimization_barrier((*self.both, *others))[:3])
        for n in range(3):
            _, rows, width = both[n].shape
            piece = 2 * ((n + 2) % 3)
            outs = [(1, rows, width)] * 2
            self.also[n], send = sums_call(
                block_sums,
                (1,),
                [
                    pl.BlockSpec((2, rows, width), lambda i: (piece, 0, 0)),
                    pl.BlockSpec((2, rows, width), lambda i: (1, 0, 0)),
                ],
                [full(jax.ShapeDtypeStruct(out, bf16)) for out in outs],
                outs,
                self.pieces,
                both[n],
            )
            self.also_got[n] = self.net.swap(send, self.net.turns[n][0])

    def third(self):
        net = self.net
        _, rows, width = self.own[0].shape
        outs = [(2, rows // 2 * 3, width)] * 2 if self.aligned else [(2, rows, width)] * 3
        args = self.own + self.got
        results = sums_call(
            third_sums,
            (1,),
            [full(a) for a in args],
            [full(jax.ShapeDtypeStruct(out, bf16)) for out in outs],
            outs,
            *args,
        )
        if self.aligned:
            self.fc = results[0], net.swap(results[1], net.lead[0])
        else:
            self.fc = self.lead(self.together(results), len(net.lead) - 1)
        self.fc_sent = results[1]
        self.also_got = list(lax.optimization_barrier((*self.also_got, results[1]))[:3])

    def after_fc(self):
        *self.also_got, fc_got = lax.optimization_barrier((*self.also_got, self.fc[1]))
        self.fc = self.fc[0], fc_got

    def third_attn(self):
        net = self.net
        _, rows, width = self.also[0].shape
        args, outs = self.also + self.also_got, [(1, rows // 2, width)] * 6
        results = sums_call(
            third_attn_sums,
            (1,),
            [full(a) for a in args],
            [full(jax.ShapeDtypeStruct(out, bf16)) for out in outs],
            outs,
            *args,
        )
        self.also = results[0::2]
        self.also_got = [net.swap(results[2 * n + 1], net.turns[(n + 2) % 3][0]) for n in range(3)]

    def last(self):
        net = self.net
        order = (1, 2, 0)
        keep, got = [self.also[n] for n in order], [self.also_got[n] for n in order]
        if self.aligned:
            _, rows, width = keep[0].shape
            outs = [(1, rows // 2 * 3, width)] * 2
            own, send = sums_call(
                fourth_sums,
                (1,),
                [full(a) for a in keep + got],
                [full(jax.ShapeDtypeStruct(out, bf16)) for out in outs],
                outs,
                *keep,
                *got,
            )
            attn = own, net.swap(send, net.lead[0])
        else:
            attn = self.lead(self.together([summed(a, b) for a, b in zip(keep, got)]), len(net.lead) - 1)
        sums = []
        for own, got in (self.fc, attn):
            for step in range(len(net.lead) - 1, -1, -1):
                total = own.astype(f32) + got.astype(f32)
                if step:
                    own, got = self.lead(total.astype(bf16), step - 1)
            sums.append(total)
        return sums

    def together(self, parts):
        kinds, _, width = parts[0].shape
        count = 1 << len(self.net.lead)
        return jnp.concatenate([p.reshape(kinds, count, -1, width) for p in parts], axis=2).reshape(kinds, -1, width)

    def lead(self, whole, step):
        half = whole.shape[1] // 2
        return whole[:, :half], self.net.swap(whole[:, half:], self.net.lead[step])


def attn_in_kernel(grad_ref, weight_ref, own_ref, other_ref):
    total = dot(grad_ref[...], weight_ref[...], 0, 0)
    half = own_ref.shape[0]
    own_ref[...] = total[:half]
    other_ref[...] = total[half:]


def attn_in_grads(grad, weight):
    rows, tokens = grad.shape
    width = weight.shape[1]
    out = jax.ShapeDtypeStruct((tokens // 2, width), f32)
    return pl.pallas_call(
        attn_in_kernel,
        grid=(1,),
        in_specs=[full(grad), pl.BlockSpec((rows, width), lambda i: (0, 0))],
        out_specs=[full(out)] * 2,
        out_shape=[out, pltpu.HBM(out.shape, f32)],
        cost_estimate=tiny,
        compiler_params=pltpu.CompilerParams(vmem_limit_bytes=40 * MIB),
        name="attn_in_grads",
    )(grad, weight)


def weight_grad_kernel(rows, place_ref, grad_ref, x_ref, mine_ref, other_ref, out_ref, hold, sems):
    top, copies = grad_ref.shape[0], []
    step = top // 3
    for n in (3, 0, 1, 2):
        start = n * step
        stop = min(start + step, hold.shape[0])
        if n == 3:
            hold[start:] = summed(mine_ref[...], other_ref[...])
        else:
            hold[start:stop] = dot(grad_ref[start:stop], x_ref[...], 1, 0).astype(bf16)
        for unit in range(start // rows, stop // rows):
            at = pl.multiple_of(place_ref[unit] * rows, rows)
            copies.append(
                pltpu.make_async_copy(
                    hold.at[pl.ds(unit * rows, rows)], out_ref.at[pl.ds(at, rows)], sems.at[unit]
                )
            )
            copies[-1].start()
    for copy in copies:
        copy.wait()


def weight_grad(grad, x, mine, other, places, rows):
    total, width = grad.shape[0] + mine.shape[0], x.shape[1]
    return pl.pallas_call(
        functools.partial(weight_grad_kernel, rows),
        grid_spec=pltpu.PrefetchScalarGridSpec(
            num_scalar_prefetch=1,
            grid=(1,),
            in_specs=[full(a) for a in (grad, x, mine, other)],
            out_specs=any_spec,
            scratch_shapes=[pltpu.VMEM((total, width), bf16), pltpu.SemaphoreType.DMA((total // rows,))],
        ),
        out_shape=jax.ShapeDtypeStruct((total, width), bf16),
        cost_estimate=tiny,
        compiler_params=pltpu.CompilerParams(vmem_limit_bytes=60 * MIB),
        name="weight_grad",
    )(places, grad, x, mine, other)


def by_core(core_ref, group, whole):
    if group is None:
        return [whole]
    picked = []
    for c in range(2):
        rows = []
        for at in range(0, whole.shape[0], 2 * group):
            first, second = whole[at : at + group], whole[at + group : at + 2 * group]
            rows.append(jnp.where(core_ref[0] == c, first, second))
        picked.append(jnp.concatenate(rows, axis=0))
    return picked


def token_block(pick, mods, n):
    width = mods.shape[1] // 6
    return dot(pick[...], mods[:, n * width : (n + 1) * width], 1, 0)


def middle_kernel(group, core_ref, *refs):
    sums, met, mid, grad_out, pick, mods, bias, weight, context = refs[:9]
    result_ref, pair_ref, mid_ref, attn_ref, column_ref = refs[9:14]
    normed, inverse = layer_norm(mid[...])
    back, outer = sums[1] + met[1], grad_out[...].astype(f32)
    mlp_out = sums[0] + met[0] + bias[...]
    result_ref[...] = (mid[...] + token_block(pick, mods, 5) * mlp_out).astype(bf16)
    slot_sums(pick[...], (back, back * normed, outer * mlp_out), pair_ref)
    grad_mid = outer + norm_back(back * (1.0 + token_block(pick, mods, 4)), normed, inverse)
    mid_ref[...] = grad_mid
    grad_attn = (token_block(pick, mods, 2) * grad_mid).astype(bf16)
    attn_ref[...] = grad_attn
    column_ref[...] = jnp.sum(grad_attn.astype(f32), axis=0, keepdims=True)
    parts = by_core(core_ref, group, dot(weight[...], grad_attn, 0, 1))
    parts += by_core(core_ref, group, dot(grad_attn, context[...], 0, 1))
    for ref, value in zip(refs[14:], parts):
        ref[...] = value.astype(bf16)


def middle(core, group, *args):
    _, tokens, width = args[0].shape
    if group is None:
        sizes = [(width, tokens), (width, width)]
    else:
        sizes = [(width // 2, tokens)] * 2 + [(width // 2, width)] * 2
    slots = args[4].shape[1]
    outs = [((tokens, width), bf16), ((slots, 3 * width), bf16)]
    outs += [((tokens, width), f32), ((tokens, width), bf16), ((1, width), f32)]
    outs = [jax.ShapeDtypeStruct(*out) for out in outs + [(s, bf16) for s in sizes]]
    return pl.pallas_call(
        functools.partial(middle_kernel, group),
        grid=(1,),
        in_specs=[pl.BlockSpec(memory_space=pltpu.SMEM)] + [full(a) for a in args],
        out_specs=[full(a) for a in outs],
        out_shape=outs[:5] + [pltpu.HBM(a.shape, bf16) for a in outs[5:]],
        cost_estimate=tiny,
        compiler_params=pltpu.CompilerParams(vmem_limit_bytes=48 * MIB),
        name="middle",
    )(core.reshape(1), *args)


def slot_sums(pick, blocks, out_ref):
    for n, block in enumerate(blocks):
        high = block.astype(bf16)
        low = (block - high.astype(f32)).astype(bf16)
        total = dot(pick, high, 0, 0) + dot(pick, low, 0, 0)
        out_ref[:, n * block.shape[1] : (n + 1) * block.shape[1]] = total.astype(bf16)


def attn_end_kernel(*refs):
    back_a, back_b, resid, grad_mid, attn_out, pick, mods = refs[:7]
    tokens_ref, pair_ref = refs[7:]
    back = back_a[...] + back_b[...]
    normed, inverse = layer_norm(resid[...].astype(f32))
    slope = back * (1.0 + token_block(pick, mods, 1))
    tokens_ref[...] = grad_mid[...] + norm_back(slope, normed, inverse)
    slot_sums(pick[...], (back, back * normed, grad_mid[...] * attn_out[...]), pair_ref)


def end_call(kernel, dtype, slots, *args):
    tokens, width = args[0].shape
    outs = [jax.ShapeDtypeStruct((tokens, width), dtype), jax.ShapeDtypeStruct((slots, 3 * width), bf16)]
    return pl.pallas_call(
        kernel,
        grid=(1,),
        in_specs=[full(a) for a in args],
        out_specs=[full(a) for a in outs],
        out_shape=outs,
        cost_estimate=tiny,
        compiler_params=pltpu.CompilerParams(vmem_limit_bytes=32 * MIB),
        name=kernel.__name__,
    )(*args)


def rows_kernel(*refs):
    at = 0
    for ref in refs[:-1]:
        refs[-1][at : at + ref.shape[0]] = ref[...]
        at += ref.shape[0]


def stack_rows(*args):
    out = jax.ShapeDtypeStruct((sum(a.shape[0] for a in args), args[0].shape[1]), f32)
    return pl.pallas_call(
        rows_kernel,
        grid=(1,),
        in_specs=[full(a) for a in args],
        out_specs=full(out),
        out_shape=out,
        cost_estimate=tiny,
        compiler_params=pltpu.CompilerParams(vmem_limit_bytes=24 * MIB),
        name="stack_rows",
    )(*args)


def softmax_t(key, query, same, scale):
    scores = jnp.where(same, dot(key, query, 0, 0) * scale, -1e30)
    weights = jnp.exp(scores - jnp.max(scores, axis=0, keepdims=True))
    return weights * (1.0 / jnp.sum(weights, axis=0, keepdims=True))


def heads_of(block, dim, cols):
    wide = block[:, cols].astype(f32)
    return [wide[n * dim : (n + 1) * dim].astype(bf16) for n in range(wide.shape[0] // dim)]


def attn_forward(dim, scale, row_ref, col_ref, q_ref, k_ref, v_ref, out_ref):
    length = col_ref.shape[0]
    for s in range(row_ref.shape[0]):
        cols = slice(s * length, (s + 1) * length)
        same = row_ref[s : s + 1] == col_ref[:, s : s + 1]
        outs = []
        for q, k, v in zip(*[heads_of(r[0, 0], dim, cols) for r in (q_ref, k_ref, v_ref)]):
            probs = softmax_t(k, q, same, scale).astype(bf16)
            outs.append(dot(v, probs, 1, 0))
        out_ref[0, :, cols] = jnp.concatenate(outs, axis=0).astype(bf16)


def attn_backward(dim, scale, row_ref, col_ref, q_ref, k_ref, v_ref, *refs):
    length, out_ref = col_ref.shape[0], refs[-1]
    for s in range(row_ref.shape[0]):
        cols = slice(s * length, (s + 1) * length)
        same = row_ref[s : s + 1] == col_ref[:, s : s + 1]
        gq, gk, gv = [], [], []
        qs, ks, vs = [heads_of(r[0, 0], dim, cols) for r in (q_ref, k_ref, v_ref)]
        for q, k, v, g in zip(qs, ks, vs, heads_of(refs[s][0], dim, slice(0, length))):
            probs = softmax_t(k, q, same, scale)
            back = dot(v, g, 0, 0)
            back = probs * (back - jnp.sum(back * probs, axis=0, keepdims=True))
            back = back.astype(bf16)
            gq.append(dot(k, back, 1, 0) * scale)
            gk.append(dot(q, back, 1, 1) * scale)
            gv.append(dot(g, probs.astype(bf16), 1, 1))
        for n, parts in enumerate((gq, gk, gv)):
            out_ref[n, 0, :, cols] = jnp.concatenate(parts, axis=0).astype(bf16)


def attention(qkv, ids, dim, grad=None):
    _, groups, rows, tokens = qkv.shape
    scale = dim**-0.5
    ids_t = ids.T

    def one(n):
        return pl.BlockSpec((1, 1, rows, tokens), lambda i: (n, i, 0, 0))

    flat = pl.BlockSpec((1, rows, tokens), lambda i: (i, 0, 0))
    short = pl.BlockSpec((1, rows, ids.shape[1]), lambda i: (i, 0, 0))
    args = [ids, ids_t, qkv, qkv, qkv]
    specs = [pl.BlockSpec(a.shape, lambda i: (0, 0)) for a in (ids, ids_t)] + [one(0), one(1), one(2)]
    if grad is None:
        return pl.pallas_call(
            functools.partial(attn_forward, dim, scale),
            grid=(groups,),
            in_specs=specs,
            out_specs=flat,
            out_shape=jax.ShapeDtypeStruct((groups, rows, tokens), bf16),
            cost_estimate=tiny,
            compiler_params=pltpu.CompilerParams(vmem_limit_bytes=24 * MIB),
            name="attention",
        )(*args)
    return pl.pallas_call(
        functools.partial(attn_backward, dim, scale),
        grid=(groups,),
        in_specs=specs + [short] * len(grad),
        out_specs=pl.BlockSpec((3, 1, rows, tokens), lambda i: (0, i, 0, 0)),
        out_shape=jax.ShapeDtypeStruct(qkv.shape, bf16),
        cost_estimate=tiny,
        compiler_params=pltpu.CompilerParams(vmem_limit_bytes=24 * MIB),
        name="attention_back",
    )(*args, *grad)


def modulation_kernel(cond_ref, weight_ref, bias_ref, silu_ref, out_ref):
    cond = cond_ref[...].astype(f32)
    silu = (cond / (1.0 + jnp.exp(-cond))).astype(bf16)
    silu_ref[...] = silu
    out_ref[...] = (dot(silu, weight_ref[...], 1, 0) + bias_ref[...]).astype(bf16)


def modulate(cond, weight, bias):
    slots, width = cond.shape
    columns = weight.shape[1]
    tile = 384 if columns % 384 == 0 else columns
    return pl.pallas_call(
        modulation_kernel,
        grid=(columns // tile,),
        in_specs=[
            full(cond),
            pl.BlockSpec((width, tile), lambda i: (0, i)),
            pl.BlockSpec((1, tile), lambda i: (0, i)),
        ],
        out_specs=[full(cond), pl.BlockSpec((slots, tile), lambda i: (0, i))],
        out_shape=[
            jax.ShapeDtypeStruct((slots, width), bf16),
            jax.ShapeDtypeStruct((slots, columns), bf16),
        ],
        cost_estimate=tiny,
        compiler_params=pltpu.CompilerParams(vmem_limit_bytes=16 * MIB),
        name="modulate",
    )(cond, weight, bias)


def feed_forward_kernel(parts, *refs):
    own_ref, met_ref, b_ref = refs[:3]
    pieces = refs[3 : 3 + 2 * parts]
    act_ref, back_ref, column_ref, own_sums, other_sums = refs[3 + 2 * parts : 8 + 2 * parts]
    x, g, weights, acts, backs, total, ins, outs = refs[8 + 2 * parts :]
    half, units = own_ref.shape[1], pieces[0].shape[1]
    copy = pltpu.make_async_copy

    def load(n):
        slot, copies = n % 2, []
        for kind in range(2):
            for side in range(2):
                copies.append(
                    copy(
                        pieces[2 * n + side].at[kind],
                        weights.at[slot, kind, pl.ds(side * units, units)],
                        ins.at[4 + 4 * n + 2 * kind + side],
                    )
                )
        return copies

    low, high = pl.ds(0, half), pl.ds(half, half)
    inputs = [
        copy(own_ref.at[0], x.at[low], ins.at[0]),
        copy(met_ref.at[0], x.at[high], ins.at[1]),
        copy(own_ref.at[1], g.at[low], ins.at[2]),
        copy(met_ref.at[1], g.at[high], ins.at[3]),
    ]
    loads = [load(n) for n in range(parts)]
    for item in inputs[:2] + loads[0][:2] + inputs[2:] + loads[0][2:] + loads[1]:
        item.start()
    stores = []
    root = 0.7978845608028654
    for n in range(parts):
        slot = n % 2
        for item in (inputs[:2] if n == 0 else []) + loads[n][:2]:
            item.wait()
        for item in (inputs[2:] if n == 0 else []) + loads[n][2:]:
            item.wait()
        col = 0.0
        for k in range(2):
            tok = slice(k * half, (k + 1) * half)
            hidden = dot(x[tok], weights[slot, 0], 1, 1) + b_ref[n : n + 1]
            square = hidden * hidden
            tanh = jnp.tanh(root * hidden * (1.0 + 0.044715 * square))
            act = (0.5 * hidden * (1.0 + tanh)).astype(bf16)
            acts[n, tok] = act
            slope = 0.5 * (1.0 + tanh) + 0.5 * hidden * (1.0 - tanh * tanh) * (root * (1.0 + 0.134145 * square))
            back = (dot(g[tok], weights[slot, 1], 1, 1) * slope).astype(bf16)
            backs[n, tok] = back
            col = col + jnp.sum(back.astype(f32), axis=0, keepdims=True)
            for m, value in enumerate((dot(act, weights[slot, 1], 1, 0), dot(back, weights[slot, 0], 1, 0))):
                total[k, m] = value if n == 0 else total[k, m] + value
        column_ref[n : n + 1] = col
        stores.append(copy(acts.at[n], act_ref.at[n], outs.at[2 * n]))
        stores[-1].start()
        stores.append(copy(backs.at[n], back_ref.at[n], outs.at[2 * n + 1]))
        stores[-1].start()
        if n + 2 < parts:
            for item in loads[n + 2]:
                item.start()
    for k, ref in ((1, other_sums), (0, own_sums)):
        stores.append(copy(total.at[k], ref, outs.at[2 * parts + k]))
        stores[-1].start()
    for item in stores:
        item.wait()


def feed_forward(own_in, met_in, bias, pieces):
    _, tokens, width = own_in.shape
    parts, units = len(pieces) // 2, pieces[0].shape[1]
    column = jax.ShapeDtypeStruct((parts, 2 * units), f32)
    hidden = [jax.ShapeDtypeStruct((parts, 2 * tokens, 2 * units), bf16)] * 2
    sums = [jax.ShapeDtypeStruct((2, tokens, width), f32)] * 2
    dma = pltpu.SemaphoreType.DMA
    return pl.pallas_call(
        functools.partial(feed_forward_kernel, parts),
        grid=(1,),
        in_specs=[any_spec, any_spec, full(bias)] + [any_spec] * len(pieces),
        out_specs=[any_spec] * 2 + [full(column), any_spec, any_spec],
        out_shape=hidden + [column] + sums,
        scratch_shapes=[
            pltpu.VMEM((2 * tokens, width), bf16),
            pltpu.VMEM((2 * tokens, width), bf16),
            pltpu.VMEM((2, 2, 2 * units, width), bf16),
            pltpu.VMEM(hidden[0].shape, bf16),
            pltpu.VMEM(hidden[0].shape, bf16),
            pltpu.VMEM((2, 2, tokens, width), f32),
            dma((4 + 4 * parts,)),
            dma((2 * parts + 2,)),
        ],
        cost_estimate=tiny,
        compiler_params=pltpu.CompilerParams(vmem_limit_bytes=60 * MIB),
        name="feed_forward",
    )(own_in, met_in, bias, *pieces)


def fc_grad_kernel(parts, act_ref, back_ref, own_ref, met_ref, *refs):
    grads, (x, acts, backs, products, ins, outs) = refs[: 2 * parts], refs[2 * parts :]
    half, units = own_ref.shape[1], grads[0].shape[1]
    copy = pltpu.make_async_copy
    inputs = []
    for k, ref in enumerate((own_ref, met_ref)):
        for m in range(2):
            inputs.append(copy(ref.at[m], x.at[m, pl.ds(k * half, half)], ins.at[2 * k + m]))
    loads = [
        [
            copy(act_ref.at[n], acts.at[n], ins.at[4 + 2 * n]),
            copy(back_ref.at[n], backs.at[n], ins.at[5 + 2 * n]),
        ]
        for n in range(parts)
    ]
    for item in inputs + [item for pair in loads for item in pair]:
        item.start()
    stores = []
    for n in range(parts):
        for item in (inputs if n == 0 else []) + loads[n]:
            item.wait()
        if n >= 2:
            for item in stores[n - 2]:
                item.wait()
        stores.append([])
        for kind, left, right in ((0, backs, 0), (1, acts, 1)):
            products[n % 2, kind] = dot(left[n], x[right], 0, 0).astype(bf16)
            for side in range(2):
                stores[n].append(
                    copy(
                        products.at[n % 2, kind, pl.ds(side * units, units)],
                        grads[2 * n + side].at[kind],
                        outs.at[4 * n + 2 * kind + side],
                    )
                )
                stores[n][-1].start()
    for pair in stores[-2:]:
        for item in pair:
            item.wait()


def fc_grads_of(acts, backs, own_in, met_in):
    parts, tokens, columns = acts.shape
    width = own_in.shape[2]
    dma = pltpu.SemaphoreType.DMA
    return pl.pallas_call(
        functools.partial(fc_grad_kernel, parts),
        grid=(1,),
        in_specs=[any_spec] * 4,
        out_specs=[any_spec] * (2 * parts),
        out_shape=[pltpu.HBM((2, columns // 2, width), bf16)] * (2 * parts),
        scratch_shapes=[
            pltpu.VMEM((2, tokens, width), bf16),
            pltpu.VMEM(acts.shape, bf16),
            pltpu.VMEM(acts.shape, bf16),
            pltpu.VMEM((2, 2, columns, width), bf16),
            dma((4 + 2 * parts,)),
            dma((4 * parts,)),
        ],
        cost_estimate=tiny,
        compiler_params=pltpu.CompilerParams(vmem_limit_bytes=60 * MIB),
        name="fc_grads",
    )(acts, backs, own_in, met_in)


def on_device(
    tokens,
    cond,
    segment_ids,
    crop_slot,
    ada_weight,
    ada_bias,
    attn_weight,
    fc_in,
    fc_out,
    biases,
    out_grad,
):
    net = Net()
    tok_len, width = tokens.shape[1:]
    head_dim = width // HEADS
    mod_rank, core, chips = net.mod_rank, net.core, net.chips
    device_count = net.dp * net.mod
    crop_count = crop_slot.shape[1] // net.mod
    shard = attn_weight.shape[0]
    third = shard // 3
    chunks_of = [range(chips // 2), range(chips // 2, chips)]
    halves = [(n, side) for n in range(3) for side in range(2)]
    aligned = shard % (2 * head_dim) == 0 and third % 16 == 0 and width % (2 * net.mod * shard) == 0

    g_attn = Gather(net, attn_weight[None])
    g_fc = Gather(net, jnp.stack([fc_in, fc_out]))
    silu_cond, mod_own = modulate(cond, ada_weight, ada_bias.reshape(1, -1).astype(f32))
    slot_count, own_cols = cond.shape[0], width // net.dp
    to_dp = jnp.moveaxis(silu_cond.reshape(slot_count, net.dp, own_cols), 1, 0).reshape(net.dp, 1, -1)
    to_all = jnp.broadcast_to(to_dp, (net.dp, net.mod, slot_count * own_cols)).reshape(device_count, -1)
    sent = jnp.concatenate([jnp.broadcast_to(biases[None], (device_count, biases.shape[0])), to_all], axis=1)
    for n in range(g_attn.count):
        g_attn.start()
        g_attn.got = [after(g_attn.got[0], mod_own, sent)]
        g_attn.finish()
    g_attn.start()
    first = g_attn.value
    for n in range(g_fc.count):
        g_fc.start(*first)
        if n < g_fc.count - 1:
            g_fc.finish()
    g_attn.finish().start()
    second = g_attn.value
    g_attn.finish().start()
    third_phase = g_attn.value
    g_fc.got = [after(g_fc.got[0], *third_phase)]
    g_fc.finish().start(*g_attn.got)
    attn_pieces = [(g_attn.value, g_attn.got)[side][n] for n, side in halves]

    mod_other = net.swap(after(mod_own, *first), "mod")
    modulation = jnp.concatenate(
        [jnp.where(mod_rank == 0, mod_own, mod_other), jnp.where(mod_rank == 0, mod_other, mod_own)], axis=1
    )
    seg_ids = segment_ids[0]
    slots = lax.dynamic_slice_in_dim(crop_slot[0], mod_rank * crop_count, crop_count)
    crop_onehot = seg_ids[:, None] == jnp.arange(crop_count, dtype=jnp.int32)[None, :]
    token_slot = jnp.sum(jnp.where(crop_onehot, slots[None, :], 0), axis=1)
    slot_pick = token_slot[:, None] == jnp.arange(cond.shape[0], dtype=jnp.int32)[None, :]
    slot_pick = slot_pick.astype(bf16)
    modulation = after(modulation, *third_phase)
    mods = [modulation[:, n * width : (n + 1) * width] for n in range(6)]
    shift_a, scale_a, gate_a, shift_m, scale_m, gate_m = [times(slot_pick, block) for block in mods]

    sent = after(sent, *second)
    met = lax.all_to_all(sent, ("dp", "mod"), split_axis=0, concat_axis=0, tiled=True)
    met = after(met, *third_phase)
    ada_order = list(range(net.bits - 1, -1, -1))
    dp_order = net.ranks(ada_order, range(net.dp))[0]
    dp_pick = (dp_order[:, None] == jnp.arange(net.dp)[None, :]).astype(bf16)
    cond_cols = times(dp_pick, met.reshape(net.dp, net.mod, -1)[:, 0, biases.shape[0] :]).astype(bf16)
    cond_cols = cond_cols.reshape(-1, own_cols)
    bias_all = met[:, : biases.shape[0]].reshape(-1, width)
    bias_query, bias_value, bias_proj, bias_out = [bias_all[n].astype(f32) for n in range(4)]
    bias_in = bias_all[4:].reshape(device_count, 3, third)
    picks = []
    for n, side in halves:
        devices = net.devices(net.orders[n], chunks_of[side])
        picks.append((devices[:, None] == jnp.arange(device_count)[None, :]).astype(bf16))
    picks = jnp.stack(picks).reshape(3, 2, chips // 2, device_count)
    bias_pieces = jnp.einsum("nsjd,dnr->nsjr", picks, bias_in, preferred_element_type=f32).reshape(3, -1)

    def join(own, other):
        own, other = [a.reshape(-1, 1, net.mod * shard, a.shape[-1]) for a in (own, other)]
        both = jnp.where(core == 0, jnp.concatenate([own, other], 1), jnp.concatenate([other, own], 1))
        return both.reshape(-1, both.shape[-1])

    def part(whole):
        whole = whole.reshape(-1, 2, net.mod * shard, whole.shape[-1])
        return [
            jnp.where(core == c, whole[:, 0], whole[:, 1]).reshape(-1, whole.shape[-1]) for c in range(2)
        ]

    resid = tokens[0].astype(f32)
    normed_a, _ = layer_norm(resid)
    attn_in = (normed_a * (1.0 + scale_a) + shift_a).astype(bf16)
    if aligned:
        index = jnp.concatenate([net.local(net.orders[n], chunks_of[side]) * 3 + n for n, side in halves])
        own_weight = assemble(attn_pieces, index, third)
        qkv_rows = own_weight.shape[0] * 3 // 4
        qkv_weight = own_weight[:qkv_rows]
        proj_own = own_weight[qkv_rows:]
        proj_weight = join(proj_own, net.swap(proj_own, 0))
        ids = jnp.stack([seg_ids, net.swap(seg_ids, 0)])
        attn_in = after(attn_in, *third_phase)
        attn_both = jnp.concatenate([attn_in, net.swap(attn_in, 0)], axis=0)
        own_query, own_value = part(bias_query[:, None])[0], part(bias_value[:, None])[0]
        qkv_bias = jnp.concatenate([own_query, jnp.zeros_like(own_query), own_value], axis=0)
        attn_both = after(attn_both, *g_fc.got)
        g_fc.finish().start()
        qkv = (times_rows(qkv_weight, attn_both) + qkv_bias).astype(bf16)
        qkv = qkv.reshape(3, -1, 2 * head_dim, 2 * tok_len)
        context_both = attention(qkv, ids, head_dim).reshape(-1, 2 * tok_len)
        context = join(context_both[:, :tok_len], net.swap(context_both[:, tok_len:], 0))
        attn_out = dot(context, proj_weight, 0, 1) + bias_proj
    else:
        arrays = attn_pieces + [net.swap(piece, 0) for piece in attn_pieces]
        places = jnp.concatenate(
            [net.devices(net.orders[n], chunks_of[side], c) * 3 + n for c in range(2) for n, side in halves]
        )
        spread = jnp.concatenate(arrays, axis=1)[0]

        def place(n, whole):
            block = lax.dynamic_slice_in_dim(spread, n * third, third)
            return lax.dynamic_update_slice_in_dim(whole, block, places[n] * third, 0)

        attn_w = lax.fori_loop(0, places.shape[0], place, jnp.zeros_like(spread))
        g_fc.finish().start()
        g_fc.finish().start()
        qkv_weight, proj_weight = attn_w[: 3 * width], attn_w[3 * width :]
        qkv_bias = jnp.concatenate([bias_query, jnp.zeros_like(bias_query), bias_value])
        qkv = (times_rows(qkv_weight, attn_in) + qkv_bias[:, None]).astype(bf16)
        qkv = qkv.reshape(3, -1, 2 * head_dim, tok_len)
        context = attention(qkv, seg_ids[None], head_dim).reshape(-1, tok_len)
        attn_out = dot(context, proj_weight, 0, 1) + bias_proj
    mid = resid + gate_a * attn_out
    normed_m, _ = layer_norm(mid)
    mlp_in = (normed_m * (1.0 + scale_m) + shift_m).astype(bf16)
    if aligned:
        mlp_in = after(mlp_in, *g_fc.got)
        g_fc.finish().start()
    grad_mlp = (gate_m * out_grad[0].astype(f32)).astype(bf16)

    mlp_own = jnp.stack([mlp_in, grad_mlp])
    mlp_met = after(net.swap(mlp_own, 0), cond_cols, bias_pieces)
    grad_bias_out = jnp.sum(grad_mlp.astype(f32), axis=0, keepdims=True)
    fc_pieces = [(g_fc.value, g_fc.got)[side][n] for n, side in halves]
    acts, backs, columns, own_sums, other_sums = feed_forward(mlp_own, mlp_met, bias_pieces, fc_pieces)
    sums_met = net.swap(other_sums, 0)
    fc_grads = fc_grads_of(acts, backs, mlp_own, mlp_met)
    sums_met = after(sums_met, *fc_grads)
    back_way = Scatter(net, fc_grads[0::2], fc_grads[1::2])

    result, pair_m, grad_mid, grad_attn, grad_bias_proj, *parts = middle(
        core,
        net.mod * shard if aligned else None,
        own_sums,
        sums_met,
        mid,
        out_grad[0],
        slot_pick,
        modulation,
        bias_out[None],
        proj_weight,
        context,
    )
    if aligned:
        mine, other, proj_mine, proj_other = parts
        context_grads = [a.reshape(-1, 2 * head_dim, tok_len) for a in (mine, net.swap(other, 0))]
        proj_met = net.swap(after(proj_other, *context_grads), 0)
        grad_qkv = attention(qkv, ids, head_dim, context_grads)
        grad_qkv = grad_qkv.reshape(-1, 2 * tok_len)
        back_own, back_other = attn_in_grads(grad_qkv, own_weight)
        back_met = net.swap(back_other, 0)
        grad_qkv = after(grad_qkv, back_own)
        places = jnp.sum(
            jnp.where(
                index[None, :] == jnp.arange(index.shape[0], dtype=index.dtype)[:, None],
                jnp.arange(index.shape[0], dtype=index.dtype)[None, :],
                0,
            ),
            axis=1,
        )
        pieces = weight_grad(grad_qkv, attn_both, proj_mine, proj_met, places, third)
        back_met = after(back_met, pieces)
    else:
        grad_context, grad_proj = parts
        grad_qkv = attention(
            qkv, seg_ids[None], head_dim, [grad_context.reshape(-1, 2 * head_dim, tok_len)]
        ).reshape(-1, tok_len)
        attn_grad = jnp.concatenate([times(grad_qkv, attn_in).astype(bf16), grad_proj], axis=0)

        def take(n, whole):
            block = lax.dynamic_slice_in_dim(attn_grad, places[n] * third, third)
            return lax.dynamic_update_slice_in_dim(whole, block, n * third, 0)

        grads = lax.fori_loop(0, places.shape[0], take, jnp.zeros_like(attn_grad))
        grads = jnp.split(grads[None], 12, axis=1)
        pieces = jnp.concatenate([summed(a, net.swap(b, 0)) for a, b in zip(grads[:6], grads[6:])], axis=1)
        back_own = contract_rows(grad_qkv, qkv_weight)
        back_met = jnp.zeros_like(back_own)
    grad_tokens, pair_a = end_call(
        attn_end_kernel, f32, slot_count, back_own, back_met, tokens[0], grad_mid, attn_out, slot_pick, modulation
    )
    pair_a, *back_way.got = lax.optimization_barrier((pair_a, *back_way.got))
    pair_own = jnp.where(mod_rank == 0, pair_a, pair_m)
    pair_send = jnp.where(mod_rank == 0, pair_m, pair_a)
    grad_mod = summed(pair_own, net.swap(pair_send, "mod"))
    sends = [back_way.join(0, pieces)]
    mod_rows = jnp.concatenate([grad_mod, net.swap(grad_mod, ada_order[0])], axis=0)
    back_way.hold(2, grad_mod)
    sends.append(back_way.join(2, pieces))
    back_way.hold(1, mod_rows)
    sends.append(back_way.join(1, pieces))
    grad_qkv, columns = lax.optimization_barrier((grad_qkv, columns, *sends))[:2]

    grad_silu = times_rows(grad_mod, ada_weight)
    silu_own = jnp.where(mod_rank == 0, grad_silu[:crop_count], grad_silu[crop_count:])
    silu_send = jnp.where(mod_rank == 0, grad_silu[crop_count:], grad_silu[:crop_count]).astype(bf16)

    column = jnp.sum(grad_qkv.astype(f32), axis=1, keepdims=True).reshape(3, -1, 1)
    if aligned:
        none = jnp.zeros_like(column[0])
        column = [join(column[0], none), None, join(column[2], none)]
    columns = columns.reshape(3, 2, chips // 2, third)
    grad_bias_in = jnp.einsum("nsjd,nsjr->dnr", picks.astype(f32), columns, precision=lax.Precision.HIGHEST)
    grad_bias = stack_rows(
        column[0].reshape(1, -1),
        column[2].reshape(1, -1),
        grad_bias_proj,
        grad_bias_out,
        grad_bias_in.reshape(-1, width),
    )
    bias_rows = lax.all_to_all(
        grad_bias.reshape(device_count, -1), ("dp", "mod"), split_axis=0, concat_axis=0, tiled=True
    )
    bias_sum = jnp.sum(bias_rows, axis=0)
    for n in range(3):
        back_way.hold(n, silu_send, bias_sum)
    sends = [back_way.second(n) for n in range(3)]
    back_way.second_attn(sends)
    back_way.third()
    silu_send, mod_rows = lax.optimization_barrier((silu_send, mod_rows, back_way.fc_sent))[:2]
    grad_silu = silu_own + net.swap(silu_send, "mod").astype(f32)
    own_cond = lax.dynamic_slice_in_dim(cond, mod_rank * crop_count, crop_count, 0).astype(f32)
    silu_back = jax.vjp(jax.nn.silu, own_cond)[1]
    grad_cond = silu_back(grad_silu)[0]
    for dim in ada_order[1:]:
        mod_rows = jnp.concatenate([mod_rows, net.swap(mod_rows, dim)], axis=0)
    ada_w_sum = contract_rows(cond_cols, mod_rows)
    ada_b_sum = jnp.sum(mod_rows.astype(f32), axis=0).reshape(ada_bias.shape[0], width)
    ada_b_sum = lax.dynamic_slice_in_dim(ada_b_sum, net.dp_rank * own_cols, own_cols, 1)
    back_way.after_fc()
    back_way.third_attn()
    fc_sum, attn_sum = back_way.last()

    return (
        result[None],
        grad_tokens[None],
        grad_cond,
        ada_w_sum,
        ada_b_sum,
        attn_sum[0],
        fc_sum[0],
        fc_sum[1],
        bias_sum,
    )


def solution(mesh):
    placed = (
        P(("dp", "mod"), None, None),
        P("dp", None),
        P(("dp", "mod"), None),
        P("dp", None),
        P(None, "mod"),
        P("mod", None),
        P(("dp", "mod"), None),
        P(("dp", "mod"), None),
        P(("dp", "mod"), None),
        P(("dp", "mod")),
        P(("dp", "mod"), None, None),
    )
    return jax.shard_map(
        on_device,
        mesh=mesh,
        in_specs=placed,
        out_specs=(
            P(("dp", "mod"), None, None),
            P(("dp", "mod"), None, None),
            P(("dp", "mod"), None),
            P("dp", "mod"),
            P("mod", "dp"),
            P(("dp", "mod"), None),
            P(("dp", "mod"), None),
            P(("dp", "mod"), None),
            P(("dp", "mod")),
        ),
        check_vma=False,
    )
```
